32 devices in a mesh: sess: 4 (over z), tile: 8 (over y, x, core).
Axes of the slice: x: 2, y: 2, z: 4, core: 2. Of those that a mesh axis runs over, the one named last changes fastest.
Arguments:
- features: bfloat16 [24, 16, 320, 128], P('sess', 'tile'), parts along dimension 0, may hold values from -6 to 6
- dec_weight: bfloat16 [9, 128, 128], replicated, may hold values from -0.1875 to 0.1875
- dec_bias: float32 [128], replicated, may hold values from -3 to 3
- first_weight: bfloat16 [9, 128, 128], replicated, may hold values from -0.1875 to 0.1875
- first_bias: float32 [128], replicated, may hold values from -3 to 3
- second_weight: bfloat16 [9, 128, 128], replicated, may hold values from -0.1875 to 0.1875
- second_bias: float32 [128], replicated, may hold values from -3 to 3
- boxes: int32 [3, 32], P(None, 'sess'), parts along dimension 1, may hold values from 0 to 272, as said below
- slots: int32 [64], P('sess'), parts along dimension 0, may hold values from -1 to 7, as said below
Outputs:
- finished: bfloat16 [24, 16, 320, 128], P('sess', 'tile'), parts along dimension 0
- restorations: bfloat16 [64, 64, 64, 128], P(('sess', 'tile')), parts along dimension 0
The draws below stay inside these ranges and needn't reach their ends.
There are 4 independent parts, one for each index of `sess`. The reference program is written for one: setup_inputs(seed, part) draws one part's arguments, and reference() takes and returns one part's arrays. A program takes and returns all parts, laid end to end along the dimension named above; an argument that names none is the same for every part. Nothing has to cross between parts.
Inputs may be any that keep to these rules, and one draw needn't show every extreme that they name: Column k of boxes is crop k: its first row r, its first column w and its size class c; the box has side 12 * (c + 2), and the square of side 48 at rows r, columns w lies inside the frame; some crop has class 3 - 1. `slots`: entries w * 2 to w * 2 + 1 are the crops that worker w restores, -1 marking an empty entry; each crop appears exactly once; some worker has 2 crops.
All inputs are finite; a program needn't handle non-finite values.
Results may differ from the reference program's by a relative error of at most 0.0057.
Values may be sent and summed in bfloat16 or wider, within the bound.
No kernel may reach another device: no remote copies, remote signals or barrier semaphores. Data moves between devices by JAX's collectives and lax.ppermute only.
A program may use at most 64 MiB of HBM per device.

```python
import jax
import jax.numpy as jnp
from jax import lax

C = 128
S = 64
UNIT = 12
NCLS = 3
CAP = 2
BANDS = 6
COLS = 320
BAND_ROWS = 16
H = 96
CROPS = 8
SLOTS = 16


def draw_boxes(key, part):
    keys = jax.random.split(key, 4)
    span = UNIT * (NCLS + 1)
    row0 = jax.random.randint(keys[0], (CROPS,), 0, H - span + 1)
    col0 = jax.random.randint(keys[1], (CROPS,), 0, COLS - span + 1)
    size_class = jax.random.randint(keys[2], (CROPS,), 0, NCLS)
    chosen = jax.random.randint(keys[3], (), 0, CROPS)
    index = jnp.arange(CROPS)
    neighbour = (chosen + 1) % CROPS
    size_class = jnp.where(index == chosen, NCLS - 1, size_class)
    row0 = jnp.where(index == chosen, H - span, row0)
    col0 = jnp.where(index == chosen, 0, col0)
    col0 = jnp.where(index == neighbour, COLS - span, col0)
    return jnp.stack([row0, col0, size_class]).astype(jnp.int32)


def draw_slots(key, part):
    keys = jax.random.split(key, 2)
    workers = SLOTS // CAP
    owner = jax.random.randint(keys[0], (), 0, workers)
    index = jnp.arange(SLOTS, dtype=jnp.int32)
    score = jax.random.randint(keys[1], (SLOTS,), 0, 1 << 20) * SLOTS + index
    score = jnp.where(index // CAP == owner, -1 - index, score)
    order = jnp.argsort(score, stable=True)
    filled = jnp.full((SLOTS,), -1, jnp.int32)
    return filled.at[order[:CROPS]].set(jnp.arange(CROPS, dtype=jnp.int32))


def block_levels(rng, dims, cuts, low, high):
    loudness = 1.0
    for axis_at, shards_of in cuts:
        steps = jax.random.uniform(jax.random.fold_in(jax.random.fold_in(rng, 6), axis_at), (shards_of,), jnp.float32, low / len(cuts), high / len(cuts))
        loudness = loudness * jnp.repeat(jnp.exp(steps), dims[axis_at] // shards_of).reshape((-1,) + (1,) * (len(dims) - 1 - axis_at))
    return loudness


def gaussian(rng, extent, deviation, most, shards=(), kind=jnp.bfloat16):
    result = jax.random.normal(rng, extent, jnp.float32) * deviation
    if len(shards) > 0:
        result = block_levels(rng, extent, shards, -0.22, 0.18) * result
    return jnp.clip(result, min=-most, max=most).astype(kind)


def setup_inputs(seed: int = 0, part: int = 0) -> dict:
    key_of = jax.random.split(jax.random.key(seed), 10)
    part_keys = jax.random.split(jax.random.fold_in(key_of[9], part), 10)
    return {
        "features": gaussian(part_keys[0], (BANDS, BAND_ROWS, COLS, C), 1.0, 6.0, ((1, 8),)),
        "dec_weight": gaussian(key_of[1], (9, C, C), (9 * C) ** -0.5, 0.1875),
        "dec_bias": gaussian(key_of[2], (C,), 0.5, 3.0, (), jnp.float32),
        "first_weight": gaussian(key_of[3], (9, C, C), (9 * C) ** -0.5, 0.1875),
        "first_bias": gaussian(key_of[4], (C,), 0.5, 3.0, (), jnp.float32),
        "second_weight": gaussian(key_of[5], (9, C, C), (9 * C) ** -0.5, 0.1875),
        "second_bias": gaussian(key_of[6], (C,), 0.5, 3.0, (), jnp.float32),
        "boxes": draw_boxes(jax.random.fold_in(jax.random.fold_in(key_of[9], part), 71), part),
        "slots": draw_slots(jax.random.fold_in(jax.random.fold_in(key_of[9], part), 71), part),
    }


def hat_down(length, cells, size_out):
    lenf = length.astype(jnp.float32)
    spots = (jnp.arange(size_out, dtype=jnp.float32) + 0.5) * lenf / size_out - 0.5
    spots = jnp.clip(spots, 0.0, lenf - 1.0)
    return jnp.maximum(0.0, 1.0 - jnp.abs(spots[:, None] - cells[None, :]))


def hat_up(length, cells, size_in):
    lenf = length.astype(jnp.float32)
    spots = (cells + 0.5) * size_in / lenf - 0.5
    spots = jnp.clip(spots, 0.0, size_in - 1.0)
    inside = ((cells >= 0.0) & (cells < lenf)).astype(jnp.float32)
    grid = jnp.arange(size_in, dtype=jnp.float32)
    return jnp.maximum(0.0, 1.0 - jnp.abs(spots[:, None] - grid[None, :])) * inside[:, None]


def conv_ref(padded, weight):
    height = padded.shape[-3] - 2
    width = padded.shape[-2] - 2
    total = None
    for tap in range(9):
        down, right = tap // 3, tap % 3
        part = padded[..., down:down + height, right:right + width, :]
        term = jnp.einsum('...hwk,kd->...hwd', part.astype(jnp.float32), weight[tap].astype(jnp.float32))
        total = term if total is None else total + term
    return total


def restore_ref(crops, first_weight, first_bias, second_weight, second_bias):
    padded = jnp.pad(crops, ((0, 0), (1, 1), (1, 1), (0, 0)))
    inner = jax.nn.silu(conv_ref(padded, first_weight) + first_bias).astype(jnp.bfloat16)
    padded = jnp.pad(inner, ((0, 0), (1, 1), (1, 1), (0, 0)))
    return (conv_ref(padded, second_weight) + second_bias).astype(jnp.bfloat16)


def reference(features, dec_weight, dec_bias, first_weight, first_bias, second_weight, second_bias, boxes, slots):
    span = UNIT * (NCLS + 1)
    bands, band_rows, cols, chans = features.shape
    height = bands * band_rows
    frame = features.reshape(height, cols, chans)
    padded = jnp.pad(frame, ((1, 1), (1, 1), (0, 0)))
    decoded = (frame.astype(jnp.float32) + jax.nn.silu(conv_ref(padded, dec_weight) + dec_bias)).astype(jnp.bfloat16)
    cells = jnp.arange(span, dtype=jnp.float32)
    highest = lax.Precision.HIGHEST
    anchor = jnp.zeros((), jnp.int32)

    def cut(index):
        row0 = boxes[0, index].astype(jnp.int32)
        col0 = boxes[1, index].astype(jnp.int32)
        length = UNIT * (boxes[2, index] + 2)
        region = lax.dynamic_slice(decoded, (row0, col0, anchor), (span, span, chans))
        across = hat_down(length, cells, S)
        colcut = jnp.einsum('tw,hwc->htc', across, region.astype(jnp.float32), precision=highest).astype(jnp.bfloat16)
        return jnp.einsum('sh,htc->stc', across, colcut.astype(jnp.float32), precision=highest).astype(jnp.bfloat16)

    crops = lax.map(cut, jnp.arange(CROPS, dtype=jnp.int32))
    deltas = restore_ref(crops, first_weight, first_bias, second_weight, second_bias)
    picked = deltas[jnp.maximum(slots, 0)]
    restorations = jnp.where((slots >= 0)[:, None, None, None], picked, jnp.zeros_like(picked))

    def paste(index, canvas):
        row0 = boxes[0, index].astype(jnp.int32)
        col0 = boxes[1, index].astype(jnp.int32)
        length = UNIT * (boxes[2, index] + 2)
        lift = hat_up(length, cells, S)
        upper = jnp.einsum('hs,stc->htc', lift, deltas[index].astype(jnp.float32), precision=highest).astype(jnp.bfloat16)
        patch = jnp.einsum('wt,htc->hwc', lift, upper.astype(jnp.float32), precision=highest).astype(jnp.bfloat16)
        old = lax.dynamic_slice(canvas, (row0, col0, anchor), (span, span, chans))
        return lax.dynamic_update_slice(canvas, old + patch.astype(jnp.float32), (row0, col0, anchor))

    canvas = lax.fori_loop(0, CROPS, paste, jnp.zeros((height + span, cols + span, chans), jnp.float32))
    finished = (decoded.astype(jnp.float32) + canvas[:height, :cols]).astype(jnp.bfloat16)
    return (finished.reshape(bands, band_rows, cols, chans), restorations)
```

```python
import functools

import jax
import jax.numpy as jnp
from jax import lax
from jax.experimental import pallas as pl
from jax.experimental.pallas import tpu as pltpu
from jax.sharding import PartitionSpec as P

S = 64
UNIT = 12
NCLS = 3
CAP = 2
SPAN = UNIT * (NCLS + 1)
BF16 = jnp.bfloat16
F32 = jnp.float32
VMEM_LIMIT = 48 * 1024 * 1024


def rows_within(window, band_rows, stride):
    return band_rows * (window // stride) + min(band_rows, window % stride)


def first_local(row, tile, band_rows, stride):
    whole = lax.div(row, stride) * band_rows
    return whole + jnp.clip(lax.rem(row, stride) - tile * band_rows, 0, band_rows)


def global_row(local, tile, band_rows, stride):
    return lax.div(local, band_rows) * stride + tile * band_rows + lax.rem(local, band_rows)


def silu(v):
    half = 0.5 * v
    return half + half * jnp.tanh(half)


def doubled_weight(weight):
    chans = weight.shape[-1]
    taps = weight.reshape(3, 3, chans, chans)
    none = jnp.zeros_like(taps[:1])
    upper = jnp.concatenate([taps, none], 0)
    lower = jnp.concatenate([none, taps], 0)
    return jnp.concatenate([upper, lower], -1).reshape(12 * chans, 2 * chans)


def three_columns(x, width, left, right):
    count = x.shape[0]
    at = lax.rem(lax.broadcasted_iota(jnp.int32, x.shape, 0), width)
    before = jnp.where(at == 0, left, pltpu.roll(x, 1, 0))
    after = jnp.where(at == width - 1, right, pltpu.roll(x, count - 1, 0))
    return before.astype(BF16), x.astype(BF16), after.astype(BF16)


def conv_pairs(src, first, count, weight):
    parts = [
        src[pl.ds(first, count), 0],
        src[pl.ds(first, count), 1],
        src[pl.ds(first + 1, count), 0],
        src[pl.ds(first + 1, count), 1],
    ]
    wide = jnp.concatenate(parts, -1)
    wide = wide.reshape(wide.shape[0] * wide.shape[1], wide.shape[2])
    return jnp.dot(wide, weight[...], preferred_element_type=F32)


def pack_kernel(dims, boxes, slots, feat, sent_main, sent_extra, table, canvas, rim, seconds):
    tiles, band_rows, stride, local_rows, cols, chans, rows = dims
    me = lax.axis_index("tile")

    def first_pass(w, count):
        one = slots[CAP * w]
        two = slots[CAP * w + 1]
        both = (one >= 0) & (two >= 0)
        second = jnp.where(both, two, -1)
        table[0, w] = jnp.where(one >= 0, one, two)
        table[1, w] = second
        seconds[count] = second
        return count + both.astype(jnp.int32)

    lax.fori_loop(0, tiles, first_pass, jnp.int32(0))

    def second_pass(w, count):
        idle = table[0, w] < 0

        @pl.when(idle)
        def _():
            table[0, w] = seconds[count]

        return count + idle.astype(jnp.int32)

    lax.fori_loop(0, tiles, second_pass, jnp.int32(0))

    edge = jnp.zeros((8, chans), F32)
    for row in range(local_rows):
        canvas[row, 0:8, :] = edge
        canvas[row, 8 + cols : 16 + cols, :] = edge
        canvas[row, 8 : 8 + cols, :] = feat[row].astype(F32)
    rim[...] = jnp.zeros_like(rim)

    def pack(crop, w, out):
        row0 = boxes[0, crop]
        col0 = boxes[1, crop]
        start = first_local(jnp.maximum(row0 - 1, 0), me, band_rows, stride)
        for i in range(rows):
            row = jnp.minimum(start + i, local_rows - 1)
            out[w, i * SPAN : (i + 1) * SPAN, :] = canvas[row, pl.ds(col0 + 8, SPAN), :].astype(BF16)
            rim[2 * i : 2 * i + 1, :] = canvas[row, pl.ds(col0 + 7, 1), :]
            rim[2 * i + 1 : 2 * i + 2, :] = canvas[row, pl.ds(col0 + 8 + SPAN, 1), :]
        out[w, rows * SPAN :, :] = rim[...].astype(BF16)

    @pl.loop(0, tiles)
    def _(w):
        pack(table[0, w], w, sent_main)
        extra = table[1, w]

        @pl.when(extra >= 0)
        def _():
            pack(extra, w, sent_extra)


def restore(dims, crop, boxes, got, dec_w, dec_b, one_w, one_b, two_w, two_b, raw, cut, wide, inner, delta):
    tiles, band_rows, stride, local_rows, cols, chans, rows = dims
    row0 = boxes[0, crop]
    length = UNIT * (boxes[2, crop] + 2)
    above = row0 - 1
    pairs = SPAN // 2
    nothing = jnp.zeros((SPAN, 3 * chans), BF16)
    raw[0, 0] = nothing
    raw[pairs, 1] = nothing

    @pl.loop(0, tiles)
    def _(e):
        start = first_local(jnp.maximum(above, 0), e, band_rows, stride)
        rim = got[e, rows * SPAN :, :].astype(F32)
        for i in range(rows):
            local = start + i
            place = global_row(local, e, band_rows, stride) - above
            place = jnp.where((local < local_rows) & (place < SPAN + 2), place, SPAN + 2)
            main = got[e, i * SPAN : (i + 1) * SPAN, :].astype(F32)
            trio = three_columns(main, SPAN, rim[2 * i : 2 * i + 1], rim[2 * i + 1 : 2 * i + 2])
            for b in range(3):
                raw[lax.div(place, 2), lax.rem(place, 2), :, b * chans : (b + 1) * chans] = trio[b]

    lengthf = length.astype(F32)
    t = lax.broadcasted_iota(jnp.int32, (S, SPAN), 0).astype(F32)
    j = lax.broadcasted_iota(jnp.int32, (S, SPAN), 1).astype(F32)
    spots = jnp.clip((t + 0.5) * lengthf / S - 0.5, 0.0, lengthf - 1.0)
    across = jnp.maximum(0.0, 1.0 - jnp.abs(spots - j)).astype(BF16)

    n = 8
    for first in range(0, pairs, n):
        total = silu(conv_pairs(raw, first, n, dec_w) + dec_b[...])
        for k in range(n):
            feat = jnp.concatenate(
                [raw[first + k, 1, :, chans : 2 * chans], raw[first + k + 1, 0, :, chans : 2 * chans]], -1
            )
            decoded = (feat.astype(F32) + total[k * SPAN : (k + 1) * SPAN]).astype(BF16)
            both = jnp.dot(across, decoded, preferred_element_type=F32).astype(BF16)
            cut[2 * (first + k)] = both[:, :chans]
            cut[2 * (first + k) + 1] = both[:, chans:]

    empty = jnp.zeros((S, 3 * chans), BF16)
    for store in (wide, inner):
        store[0, 0] = empty
        store[S // 2, 1] = empty

    @pl.loop(0, S // 2)
    def _(m):
        for parity in range(2):
            s = 2 * m + parity
            spot = jnp.clip((2 * s + 1) * length - S, 0, (length - 1) * 2 * S)
            low = lax.div(spot, 2 * S)
            part = lax.rem(spot, 2 * S).astype(F32) * (1.0 / (2 * S))
            high = jnp.minimum(low + 1, SPAN - 1)
            line = (1.0 - part) * cut[low].astype(F32) + part * cut[high].astype(F32)
            trio = three_columns(line, S, 0.0, 0.0)
            for b in range(3):
                wide[m + parity, 1 - parity, :, b * chans : (b + 1) * chans] = trio[b]

    for first in range(0, S // 2, n):
        total = silu(conv_pairs(wide, first, n, one_w) + one_b[...])
        for half in range(2):
            trio = three_columns(total[:, half * chans : (half + 1) * chans], S, 0.0, 0.0)
            for b in range(3):
                inner[first + half : first + half + n, 1 - half, :, b * chans : (b + 1) * chans] = trio[b].reshape(
                    n, S, chans
                )

    for first in range(0, S // 2, n):
        total = (conv_pairs(inner, first, n, two_w) + two_b[...]).astype(BF16).reshape(n, S, 2 * chans)
        for k in range(n):
            delta[2 * (first + k)] = total[k, :, :chans]
            delta[2 * (first + k) + 1] = total[k, :, chans:]


def main_kernel(
    dims, table, boxes, slots, got, dec_w, dec_b, one_w, one_b, two_w, two_b,
    back, restored, raw, cut, wide, inner, delta, sem,
):
    tiles, band_rows, stride, local_rows, cols, chans, rows = dims
    me = lax.axis_index("tile")
    crop = table[0, me]
    restore(dims, crop, boxes, got, dec_w, dec_b, one_w, one_b, two_w, two_b, raw, cut, wide, inner, delta)
    place = jnp.where(slots[CAP * me] >= 0, 0, 1)
    own = (slots[CAP * me] >= 0) | (slots[CAP * me + 1] >= 0)

    @pl.when(own)
    def _():
        pltpu.make_async_copy(delta, restored.at[place], sem).start()

    row0 = boxes[0, crop]
    length = UNIT * (boxes[2, crop] + 2)
    lengthf = length.astype(F32)
    t = lax.broadcasted_iota(jnp.int32, (SPAN, S), 0).astype(F32)
    s = lax.broadcasted_iota(jnp.int32, (SPAN, S), 1).astype(F32)
    spots = jnp.clip((t + 0.5) * S / lengthf - 0.5, 0.0, S - 1.0)
    lift = jnp.where(t < lengthf, jnp.maximum(0.0, 1.0 - jnp.abs(spots - s)), 0.0)
    coarse = lift.astype(BF16)
    lift = jnp.concatenate([coarse, (lift - coarse.astype(F32)).astype(BF16)], 0)
    scale = 1.0 / (2.0 * lengthf)

    @pl.loop(0, SPAN // 2)
    def _(m):
        lines = []
        for parity in range(2):
            h = 2 * m + parity
            spot = jnp.clip((2 * h + 1) * S - length, 0, (S - 1) * 2 * length)
            low = ((spot.astype(F32) + 0.5) * scale).astype(jnp.int32)
            part = (spot - low * 2 * length).astype(F32) * scale
            high = jnp.minimum(low + 1, S - 1)
            lines.append(((1.0 - part) * delta[low].astype(F32) + part * delta[high].astype(F32)).astype(BF16))
        upper = jnp.concatenate(lines, -1)
        patch = jnp.dot(lift, upper, preferred_element_type=F32)
        patch = (patch[:SPAN] + patch[SPAN:]).astype(BF16)
        for parity in range(2):
            row = row0 + 2 * m + parity
            within = lax.rem(row, stride)
            dest = lax.div(within, band_rows)
            local = lax.div(row, stride) * band_rows + lax.rem(within, band_rows)
            place = local - first_local(row0, dest, band_rows, stride)
            back[dest, place] = patch[:, parity * chans : (parity + 1) * chans]

    @pl.when(own)
    def _():
        pltpu.make_async_copy(delta, restored.at[place], sem).wait()


def extra_kernel(
    dims, table, boxes, slots, got, dec_w, dec_b, one_w, one_b, two_w, two_b, partial,
    restored, raw, cut, wide, inner, delta, sem,
):
    me = lax.axis_index("tile")
    extra = table[1, me]
    one = slots[CAP * me] >= 0
    two = slots[CAP * me + 1] >= 0

    @pl.when(extra >= 0)
    def _():
        restore(dims, extra, boxes, got, dec_w, dec_b, one_w, one_b, two_w, two_b, raw, cut, wide, inner, delta)
        copy = pltpu.make_async_copy(delta, restored.at[1], sem)
        copy.start()
        copy.wait()

    @pl.when(extra < 0)
    def _():
        delta[...] = jnp.zeros_like(delta)

        @pl.when(jnp.logical_not(one))
        def _():
            copy = pltpu.make_async_copy(delta, restored.at[0], sem)
            copy.start()
            copy.wait()

        @pl.when(jnp.logical_not(two))
        def _():
            copy = pltpu.make_async_copy(delta, restored.at[1], sem)
            copy.start()
            copy.wait()


def decode_kernel(dims, feat, above, below, weight, bias, decoded, wide):
    tiles, band_rows, stride, local_rows, cols, chans, rows = dims
    me = lax.axis_index("tile")
    bands = local_rows // band_rows
    top = (me == 0).astype(jnp.int32)
    bottom = (me == tiles - 1).astype(jnp.int32)
    for j in range(bands):
        up = above[jnp.maximum(j - top, 0)].astype(F32)
        down = below[jnp.minimum(j + bottom, bands - 1)].astype(F32)
        if j == 0:
            up = jnp.where(top == 1, 0.0, up)
        if j == bands - 1:
            down = jnp.where(bottom == 1, 0.0, down)
        lines = [up, feat[2 * j].astype(F32), feat[2 * j + 1].astype(F32), down]
        for a in range(4):
            trio = three_columns(lines[a], cols, 0.0, 0.0)
            for b in range(3):
                at = (3 * a + b) * chans
                wide[j % 2, :, at : at + chans] = trio[b]
        total = silu(jnp.dot(wide[j % 2], weight[...], preferred_element_type=F32) + bias[...])
        decoded[2 * j] = (lines[1] + total[:, :chans]).astype(BF16)
        decoded[2 * j + 1] = (lines[2] + total[:, chans:]).astype(BF16)


def paste_kernel(dims, table, boxes, decoded, back, finished, canvas):
    tiles, band_rows, stride, local_rows, cols, chans, rows = dims
    me = lax.axis_index("tile")
    count = back.shape[1]
    for row in range(local_rows):
        canvas[row] = decoded[row].astype(F32)

    @pl.loop(0, tiles)
    def _(e):
        crop = table[0, e]
        row0 = boxes[0, crop]
        col0 = boxes[1, crop]
        length = UNIT * (boxes[2, crop] + 2)
        start = first_local(row0, me, band_rows, stride)
        for i in range(count):
            local = start + i

            @pl.when((local < local_rows) & (global_row(local, me, band_rows, stride) - row0 < length))
            def _():
                canvas[local, pl.ds(col0, SPAN), :] += back[e, i].astype(F32)

    for row in range(local_rows):
        finished[row] = canvas[row].astype(BF16)


def shards(features, dec_weight, dec_bias, first_weight, first_bias, second_weight, second_bias, boxes, slots):
    bands, band_rows, cols, chans = features.shape
    tiles = lax.axis_size("tile")
    assert band_rows == 2 and slots.shape[0] == CAP * tiles and boxes.shape[1] == tiles
    stride = tiles * band_rows
    local_rows = bands * band_rows
    rows = rows_within(SPAN + 2, band_rows, stride)
    back_rows = rows_within(SPAN, band_rows, stride)
    message = rows * SPAN + -(-2 * rows // 16) * 16
    dims = (tiles, band_rows, stride, local_rows, cols, chans, rows)
    frame = features.reshape(local_rows, cols, chans)

    smem = pl.BlockSpec(memory_space=pltpu.SMEM)
    vmem = pl.BlockSpec(memory_space=pltpu.VMEM)
    hbm = pl.BlockSpec(memory_space=pl.ANY)
    params = pltpu.CompilerParams(vmem_limit_bytes=VMEM_LIMIT)

    def cost(flops, moved):
        return pl.CostEstimate(flops=int(flops), bytes_accessed=int(moved), transcendentals=0)

    sent = jax.ShapeDtypeStruct((tiles, message, chans), BF16)
    sent_main, sent_extra, table = pl.pallas_call(
        functools.partial(pack_kernel, dims),
        out_shape=(sent, sent, jax.ShapeDtypeStruct((2, tiles), jnp.int32)),
        in_specs=[smem, smem, vmem],
        out_specs=(vmem, vmem, smem),
        scratch_shapes=[
            pltpu.VMEM((local_rows, cols + 16, chans), F32),
            pltpu.VMEM((message - rows * SPAN, chans), F32),
            pltpu.SMEM((tiles + 1,), jnp.int32),
        ],
        compiler_params=params,
        cost_estimate=cost(0, 6e6),
        name="pack",
    )(boxes, slots, frame)

    got_main = lax.all_to_all(sent_main, "tile", split_axis=0, concat_axis=0, tiled=True)
    got_extra = lax.all_to_all(sent_extra, "tile", split_axis=0, concat_axis=0, tiled=True)

    last = features[:, band_rows - 1]
    leading = features[:, 0]
    last, leading, got_main = lax.optimization_barrier((last, leading, got_main))
    up = [(i, (i + 1) % tiles) for i in range(tiles)]
    above = lax.ppermute(last, "tile", up)
    below = lax.ppermute(leading, "tile", [(j, i) for i, j in up])

    def twice(bias):
        return jnp.concatenate([bias, bias])[None]

    weights = (
        doubled_weight(dec_weight), twice(dec_bias),
        doubled_weight(first_weight), twice(first_bias),
        doubled_weight(second_weight), twice(second_bias),
    )
    scratch = [
        pltpu.VMEM((SPAN // 2 + 2, 2, SPAN, 3 * chans), BF16),
        pltpu.VMEM((SPAN, S, chans), BF16),
        pltpu.VMEM((S // 2 + 1, 2, S, 3 * chans), BF16),
        pltpu.VMEM((S // 2 + 1, 2, S, 3 * chans), BF16),
        pltpu.VMEM((S, S, chans), BF16),
        pltpu.SemaphoreType.DMA,
    ]
    restored_shape = jax.ShapeDtypeStruct((CAP, S, S, chans), BF16)
    back, partial = pl.pallas_call(
        functools.partial(main_kernel, dims),
        out_shape=(jax.ShapeDtypeStruct((tiles, back_rows, SPAN, chans), BF16), restored_shape),
        in_specs=[smem, smem, smem] + [vmem] * 7,
        out_specs=(vmem, hbm),
        scratch_shapes=scratch,
        compiler_params=params,
        cost_estimate=cost(7e9, 8e6),
        name="restore_main",
    )(table, boxes, slots, got_main, *weights)

    got_back = lax.all_to_all(back, "tile", split_axis=0, concat_axis=0, tiled=True)

    restorations = pl.pallas_call(
        functools.partial(extra_kernel, dims),
        out_shape=restored_shape,
        in_specs=[smem, smem, smem] + [vmem] * 7 + [hbm],
        out_specs=hbm,
        scratch_shapes=scratch,
        input_output_aliases={10: 0},
        compiler_params=params,
        cost_estimate=cost(6e9, 8e6),
        name="restore_extra",
    )(table, boxes, slots, got_extra, *weights, partial)

    decoded = pl.pallas_call(
        functools.partial(decode_kernel, dims),
        out_shape=jax.ShapeDtypeStruct((local_rows, cols, chans), BF16),
        in_specs=[vmem] * 5,
        out_specs=vmem,
        scratch_shapes=[pltpu.VMEM((2, cols, 12 * chans), BF16)],
        compiler_params=params,
        cost_estimate=cost(3e9, 6e6),
        name="decode",
    )(frame, above, below, weights[0], weights[1])

    finished = pl.pallas_call(
        functools.partial(paste_kernel, dims),
        out_shape=jax.ShapeDtypeStruct((local_rows, cols, chans), BF16),
        in_specs=[smem, smem, vmem, vmem],
        out_specs=vmem,
        scratch_shapes=[pltpu.VMEM((local_rows, cols, chans), F32)],
        compiler_params=params,
        cost_estimate=cost(0, 6e6),
        name="paste",
    )(table, boxes, decoded, got_back)
    return finished.reshape(bands, band_rows, cols, chans), restorations


def solution(mesh):
    return jax.shard_map(
        shards,
        mesh=mesh,
        in_specs=(
            P("sess", "tile", None, None),
            P(),
            P(),
            P(),
            P(),
            P(),
            P(),
            P(None, "sess"),
            P("sess"),
        ),
        out_specs=(P("sess", "tile", None, None), P(("sess", "tile"), None, None, None)),
        check_vma=False,
    )
```

```python
import functools

import jax
import jax.numpy as jnp
from jax import lax
from jax.experimental import pallas as pl
from jax.experimental.pallas import tpu as pltpu
from jax.sharding import PartitionSpec as P

S = 64
UNIT = 12
NCLS = 3
CAP = 2
SPAN = UNIT * (NCLS + 1)
BF16 = jnp.bfloat16
F32 = jnp.float32
I32 = jnp.int32
VMEM_LIMIT = 40 * 1024 * 1024
ROW, COL, SIDE, ROW2, COL2, SIDE2, PLACE = range(7)


def rows_within(window, band_rows, stride):
    return band_rows * (window // stride) + min(band_rows, window % stride)


def first_local(row, tile, dims):
    whole = lax.div(row, dims.stride) * dims.band_rows
    return whole + jnp.clip(lax.rem(row, dims.stride) - tile * dims.band_rows, 0, dims.band_rows)


def global_row(local, tile, dims):
    return lax.div(local, dims.band_rows) * dims.stride + tile * dims.band_rows + lax.rem(local, dims.band_rows)


class Dims:
    def __init__(self, features, tiles):
        self.bands, self.band_rows, self.cols, self.chans = features.shape
        self.tiles = tiles
        self.stride = tiles * self.band_rows
        self.local_rows = self.bands * self.band_rows
        self.rows = rows_within(SPAN + 2, self.band_rows, self.stride)
        self.back_rows = rows_within(SPAN, self.band_rows, self.stride)
        self.rim = -(-2 * self.rows // 16) * 16
        self.message = self.rows * SPAN + self.rim


def silu(v):
    half = 0.5 * v
    return half + half * jnp.tanh(half)


def three_columns(x, left, right):
    axis = x.ndim - 2
    width = x.shape[axis]
    at = lax.broadcasted_iota(I32, x.shape, axis)
    flat = x.reshape(-1, x.shape[-1])
    count = flat.shape[0]
    before = jnp.where(at == 0, left, pltpu.roll(flat, 1, 0).reshape(x.shape))
    after = jnp.where(at == width - 1, right, pltpu.roll(flat, count - 1, 0).reshape(x.shape))
    return before.astype(BF16), x.astype(BF16), after.astype(BF16)


def both(bias):
    return jnp.concatenate([bias[...], bias[...]], -1)


class Taps:
    def __init__(self, source, store, sems):
        chans = source.shape[-1]
        self.store = store
        self.copies = (
            pltpu.make_async_copy(source, store.at[0:9, :, 0:chans], sems.at[0]),
            pltpu.make_async_copy(source, store.at[3:12, :, chans : 2 * chans], sems.at[1]),
        )

    def start(self):
        for copy in self.copies:
            copy.start()
        chans = self.store.shape[1]
        none = jnp.zeros((3, chans, chans), BF16)
        self.store[9:12, :, 0:chans] = none
        self.store[0:3, :, chans : 2 * chans] = none

    def wait(self):
        for copy in self.copies:
            copy.wait()

    def value(self):
        shape = self.store.shape
        return self.store[...].reshape(shape[0] * shape[1], shape[2])


def conv_pairs(src, first, count, taps):
    parts = [
        src[first : first + count, 0],
        src[first : first + count, 1],
        src[first + 1 : first + count + 1, 0],
        src[first + 1 : first + count + 1, 1],
    ]
    wide = jnp.concatenate(parts, -1)
    wide = wide.reshape(wide.shape[0] * wide.shape[1], wide.shape[2])
    return jnp.dot(wide, taps.value(), preferred_element_type=F32)


def fill_canvas(dims, feat, held, canvas, sems):
    for band in range(dims.bands):
        at = pl.ds(band * dims.band_rows, dims.band_rows)
        pltpu.make_async_copy(feat.at[at], held.at[at], sems.at[band]).start()

    def finish():
        edge = jnp.zeros((8, dims.chans), F32)
        for band in range(dims.bands):
            at = pl.ds(band * dims.band_rows, dims.band_rows)
            pltpu.make_async_copy(feat.at[at], held.at[at], sems.at[band]).wait()
            for i in range(dims.band_rows):
                row = band * dims.band_rows + i
                canvas[row, 0:8, :] = edge
                canvas[row, 8 + dims.cols : 16 + dims.cols, :] = edge
                canvas[row, 8 : 8 + dims.cols, :] = held[row].astype(F32)

    return finish


def pack_crops(dims, table, row_at, col_at, canvas, rim, staged, sent, sems):
    me = lax.axis_index("tile")
    rim[...] = jnp.zeros_like(rim)
    for s in reversed(range(dims.tiles)):
        w = me ^ s
        row0 = table[row_at, w]
        col0 = table[col_at, w]
        start = first_local(jnp.maximum(row0 - 1, 0), me, dims)
        for i in range(dims.rows):
            row = jnp.minimum(start + i, dims.local_rows - 1)
            staged[s, i * SPAN : (i + 1) * SPAN, :] = canvas[row, pl.ds(col0 + 8, SPAN), :].astype(BF16)
            rim[2 * i : 2 * i + 1, :] = canvas[row, pl.ds(col0 + 7, 1), :]
            rim[2 * i + 1 : 2 * i + 2, :] = canvas[row, pl.ds(col0 + 8 + SPAN, 1), :]
        staged[s, dims.rows * SPAN :, :] = rim[...].astype(BF16)
        pltpu.make_async_copy(staged.at[s], sent[s], sems.at[s]).start()
    for s in range(dims.tiles):
        pltpu.make_async_copy(staged.at[s], sent[s], sems.at[s]).wait()


def pack_main_kernel(dims, boxes_in, slots_in, feat, *refs):
    sent, refs = refs[: dims.tiles], refs[dims.tiles :]
    table, boxes, slots, main, extra, seconds, held, canvas, rim, staged, sems, feat_sems, sent_sems = refs
    finish = fill_canvas(dims, feat, held, canvas, feat_sems)
    copies = (
        pltpu.make_async_copy(boxes_in, boxes, sems.at[0]),
        pltpu.make_async_copy(slots_in, slots, sems.at[1]),
    )
    for copy in copies:
        copy.start()
    for copy in copies:
        copy.wait()

    def first_pass(w, count):
        one = slots[CAP * w]
        two = slots[CAP * w + 1]
        full = (one >= 0) & (two >= 0)
        second = jnp.where(full, two, -1)
        main[w] = jnp.where(one >= 0, one, two)
        extra[w] = second
        seconds[count] = second
        return count + full.astype(I32)

    lax.fori_loop(0, dims.tiles, first_pass, jnp.int32(0))

    def second_pass(w, count):
        own = main[w]
        idle = own < 0
        crop = jnp.where(idle, seconds[count], own)
        table[ROW, w] = boxes[0, crop]
        table[COL, w] = boxes[1, crop]
        table[SIDE, w] = UNIT * (boxes[2, crop] + 2)
        other = jnp.maximum(extra[w], 0)
        table[ROW2, w] = boxes[0, other]
        table[COL2, w] = boxes[1, other]
        table[SIDE2, w] = jnp.where(extra[w] >= 0, UNIT * (boxes[2, other] + 2), 0)
        table[PLACE, w] = jnp.where(idle, 2, jnp.where(slots[CAP * w] >= 0, 0, 1))
        return count + idle.astype(I32)

    lax.fori_loop(0, dims.tiles, second_pass, jnp.int32(0))
    finish()
    pack_crops(dims, table, ROW, COL, canvas, rim, staged, sent, sent_sems)


def pack_extra_kernel(dims, table, feat, *refs):
    sent, refs = refs[: dims.tiles], refs[dims.tiles :]
    last, leading, held, canvas, rim, staged, sems, feat_sems, sent_sems = refs
    finish = fill_canvas(dims, feat, held, canvas, feat_sems)
    finish()
    copies = []
    for band in range(dims.bands):
        row = band * dims.band_rows
        copies.append(pltpu.make_async_copy(held.at[row + dims.band_rows - 1], last.at[band], sems.at[2 * band]))
        copies.append(pltpu.make_async_copy(held.at[row], leading.at[band], sems.at[2 * band + 1]))
    for copy in copies:
        copy.start()
    pack_crops(dims, table, ROW2, COL2, canvas, rim, staged, sent, sent_sems)
    for copy in copies:
        copy.wait()


def restore(dims, row0, length, arrivals, got, taps, biases, raw, decoded, wide, inner, delta):
    chans = dims.chans
    me = lax.axis_index("tile")
    above = row0 - 1
    pairs = SPAN // 2
    nothing = jnp.zeros((SPAN, 3 * chans), BF16)
    raw[0, 0] = nothing
    raw[pairs, 1] = nothing
    empty = jnp.zeros((S, 3 * chans), BF16)
    for store in (wide, inner):
        store[0, 0] = empty
        store[S // 2, 1] = empty

    for s in range(dims.tiles):
        arrivals[s].wait()
        e = me ^ s
        start = first_local(jnp.maximum(above, 0), e, dims)
        rim = got[s, dims.rows * SPAN :, :].astype(F32)
        for i in range(dims.rows):
            local = start + i
            place = global_row(local, e, dims) - above
            place = jnp.where((local < dims.local_rows) & (place < SPAN + 2), place, SPAN + 2)
            main = got[s, i * SPAN : (i + 1) * SPAN, :].astype(F32)
            trio = three_columns(main, rim[2 * i : 2 * i + 1], rim[2 * i + 1 : 2 * i + 2])
            for b in range(3):
                raw[place >> 1, place & 1, :, b * chans : (b + 1) * chans] = trio[b]

    lengthf = length.astype(F32)
    t = lax.broadcasted_iota(I32, (S, SPAN), 0)
    j = lax.broadcasted_iota(I32, (S, SPAN), 1).astype(F32)
    across = []
    for b in range(3):
        at = t + (b - 1)
        spots = jnp.clip((at.astype(F32) + 0.5) * lengthf / S - 0.5, 0.0, lengthf - 1.0)
        hat = jnp.maximum(0.0, 1.0 - jnp.abs(spots - j))
        across.append(jnp.where((at >= 0) & (at < S), hat, 0.0))
    across = jnp.concatenate(across, 0).astype(BF16)

    n = 8
    taps[0].wait()
    for first in range(0, pairs, n):
        total = silu(conv_pairs(raw, first, n, taps[0]) + both(biases[0]))
        for k in range(n):
            part = total[k * SPAN : (k + 1) * SPAN]
            at = 2 * (first + k)
            upper = raw[first + k, 1, :, chans : 2 * chans].astype(F32) + part[:, :chans]
            lower = raw[first + k + 1, 0, :, chans : 2 * chans].astype(F32) + part[:, chans:]
            decoded[at] = upper.astype(BF16).astype(F32)
            decoded[at + 1] = lower.astype(BF16).astype(F32)

    for m in range(S // 2):
        lines = []
        for parity in range(2):
            s = 2 * m + parity
            spot = jnp.clip((2 * s + 1) * length - S, 0, (length - 1) * 2 * S)
            low = spot >> 7
            part = (spot & 127).astype(F32) * (1.0 / (2 * S))
            high = jnp.minimum(low + 1, SPAN - 1)
            lines.append(((1.0 - part) * decoded[low] + part * decoded[high]).astype(BF16))
        cells = jnp.dot(across, jnp.concatenate(lines, -1), preferred_element_type=F32).astype(BF16)
        for parity in range(2):
            for b in range(3):
                wide[m + parity, 1 - parity, :, b * chans : (b + 1) * chans] = cells[
                    b * S : (b + 1) * S, parity * chans : (parity + 1) * chans
                ]

    taps[1].wait()
    for first in range(0, S // 2, n):
        total = silu(conv_pairs(wide, first, n, taps[1]) + both(biases[1])).reshape(n, S, 2 * chans)
        trio = three_columns(total, 0.0, 0.0)
        for half in range(2):
            for b in range(3):
                inner[first + half : first + half + n, 1 - half, :, b * chans : (b + 1) * chans] = trio[b][
                    :, :, half * chans : (half + 1) * chans
                ]

    taps[2].wait()
    for first in range(0, S // 2, n):
        total = (conv_pairs(inner, first, n, taps[2]) + both(biases[2])).astype(BF16).reshape(n, S, 2 * chans)
        for k in range(n):
            delta[2 * (first + k)] = total[k, :, :chans]
            delta[2 * (first + k) + 1] = total[k, :, chans:]


def begin(dims, arrived, weights, scratch):
    got, stores, got_sems, tap_sems = scratch
    arrivals = [pltpu.make_async_copy(arrived[s], got.at[s], got_sems.at[s]) for s in range(dims.tiles)]
    taps = [Taps(weights[i], stores.at[i], tap_sems.at[i]) for i in range(3)]
    for arrival in arrivals:
        arrival.start()
    for tap in taps:
        tap.start()
    return arrivals, taps


def main_kernel(dims, *refs):
    tiles, chans = dims.tiles, dims.chans
    arrived, refs = refs[:tiles], refs[tiles:]
    table, weights, biases, refs = refs[0], refs[1:4], refs[4:7], refs[7:]
    sent, refs = refs[:tiles], refs[tiles:]
    restored, got, stores, got_sems, tap_sems, raw, decoded, wide, inner, delta, sem, back, back_sems = refs
    me = lax.axis_index("tile")
    row0 = table[ROW, me]
    length = table[SIDE, me]
    place = table[PLACE, me]
    arrivals, taps = begin(dims, arrived, weights, (got, stores, got_sems, tap_sems))
    restore(dims, row0, length, arrivals, got, taps, biases, raw, decoded, wide, inner, delta)

    @pl.when(place < CAP)
    def _():
        pltpu.make_async_copy(delta, restored.at[place], sem).start()

    lengthf = length.astype(F32)
    t = lax.broadcasted_iota(I32, (SPAN, S), 0).astype(F32)
    s = lax.broadcasted_iota(I32, (SPAN, S), 1).astype(F32)
    spots = jnp.clip((t + 0.5) * S / lengthf - 0.5, 0.0, S - 1.0)
    lift = jnp.where(t < lengthf, jnp.maximum(0.0, 1.0 - jnp.abs(spots - s)), 0.0)
    coarse = lift.astype(BF16)
    lift = jnp.concatenate([coarse, (lift - coarse.astype(F32)).astype(BF16)], 0)
    scale = 1.0 / (2.0 * lengthf)

    for m in range(SPAN // 2):
        lines = []
        for parity in range(2):
            h = 2 * m + parity
            spot = jnp.clip((2 * h + 1) * S - length, 0, (S - 1) * 2 * length)
            low = ((spot.astype(F32) + 0.5) * scale).astype(I32)
            part = (spot - low * 2 * length).astype(F32) * scale
            high = jnp.minimum(low + 1, S - 1)
            lines.append(((1.0 - part) * delta[low].astype(F32) + part * delta[high].astype(F32)).astype(BF16))
        patch = jnp.dot(lift, jnp.concatenate(lines, -1), preferred_element_type=F32)
        patch = (patch[:SPAN] + patch[SPAN:]).astype(BF16)
        for parity in range(2):
            row = row0 + 2 * m + parity
            within = lax.rem(row, dims.stride)
            dest = lax.div(within, dims.band_rows)
            local = lax.div(row, dims.stride) * dims.band_rows + lax.rem(within, dims.band_rows)
            back[dest ^ me, local - first_local(row0, dest, dims)] = patch[:, parity * chans : (parity + 1) * chans]

    copies = [pltpu.make_async_copy(back.at[s], sent[s], back_sems.at[s]) for s in range(tiles)]
    for copy in copies:
        copy.start()
    for copy in copies:
        copy.wait()

    @pl.when(place < CAP)
    def _():
        pltpu.make_async_copy(delta, restored.at[place], sem).wait()


def extra_kernel(dims, *refs):
    tiles = dims.tiles
    arrived, refs = refs[:tiles], refs[tiles:]
    table, weights, biases, refs = refs[0], refs[1:4], refs[4:7], refs[8:]
    restored, got, stores, got_sems, tap_sems, raw, decoded, wide, inner, delta, sem = refs
    me = lax.axis_index("tile")
    row0 = table[ROW2, me]
    length = table[SIDE2, me]
    place = table[PLACE, me]

    def write(slot):
        copy = pltpu.make_async_copy(delta, restored.at[slot], sem)
        copy.start()
        copy.wait()

    @pl.when(length > 0)
    def _():
        arrivals, taps = begin(dims, arrived, weights, (got, stores, got_sems, tap_sems))
        restore(dims, row0, length, arrivals, got, taps, biases, raw, decoded, wide, inner, delta)
        write(1)

    @pl.when(length == 0)
    def _():
        delta[...] = jnp.zeros_like(delta)

        @pl.when(place != 0)
        def _():
            write(0)

        @pl.when(place != 1)
        def _():
            write(1)


def decode_kernel(dims, feat, above, below, weight, bias, decoded, held, up, down, store, wide, sems, tap_sems):
    me = lax.axis_index("tile")
    bands, chans = dims.bands, dims.chans
    taps = Taps(weight, store, tap_sems)
    copies = []
    for band in range(bands):
        at = pl.ds(band * 2, 2)
        copies.append(
            (
                pltpu.make_async_copy(feat.at[at], held.at[at], sems.at[3 * band]),
                pltpu.make_async_copy(above.at[band], up.at[band], sems.at[3 * band + 1]),
                pltpu.make_async_copy(below.at[band], down.at[band], sems.at[3 * band + 2]),
            )
        )
    for trio in copies:
        for copy in trio:
            copy.start()
    taps.start()
    for trio in copies:
        for copy in trio:
            copy.wait()
    taps.wait()
    top = (me == 0).astype(I32)
    bottom = (me == dims.tiles - 1).astype(I32)
    for j in range(bands):
        over = up[jnp.maximum(j - top, 0)].astype(F32)
        under = down[jnp.minimum(j + bottom, bands - 1)].astype(F32)
        if j == 0:
            over = jnp.where(top == 1, 0.0, over)
        if j == bands - 1:
            under = jnp.where(bottom == 1, 0.0, under)
        lines = [over, held[2 * j].astype(F32), held[2 * j + 1].astype(F32), under]
        for a in range(4):
            trio = three_columns(lines[a], 0.0, 0.0)
            for b in range(3):
                at = (3 * a + b) * chans
                wide[j % 2, :, at : at + chans] = trio[b]
        total = silu(jnp.dot(wide[j % 2], taps.value(), preferred_element_type=F32) + both(bias))
        decoded[2 * j] = (lines[1] + total[:, :chans]).astype(BF16)
        decoded[2 * j + 1] = (lines[2] + total[:, chans:]).astype(BF16)


def paste_kernel(dims, table, decoded, *refs):
    back, (finished, canvas, out, sems) = refs[: dims.tiles], refs[dims.tiles :]
    me = lax.axis_index("tile")
    for row in range(dims.local_rows):
        canvas[row] = decoded[row].astype(F32)

    for s in range(dims.tiles):
        e = me ^ s
        row0 = table[ROW, e]
        col0 = table[COL, e]
        length = table[SIDE, e]
        start = first_local(row0, me, dims)
        for i in range(dims.back_rows):
            local = start + i

            @pl.when((local < dims.local_rows) & (global_row(local, me, dims) - row0 < length))
            def _():
                canvas[local, pl.ds(col0, SPAN), :] += back[s][i].astype(F32)

    copies = [pltpu.make_async_copy(out.at[row], finished.at[row], sems.at[row]) for row in range(dims.local_rows)]
    for row in range(dims.local_rows):
        out[row] = canvas[row].astype(BF16)
        copies[row].start()
    for copy in copies:
        copy.wait()


def shards(features, dec_weight, dec_bias, first_weight, first_bias, second_weight, second_bias, boxes, slots):
    tiles = lax.axis_size("tile")
    dims = Dims(features, tiles)
    cols, chans, local_rows = dims.cols, dims.chans, dims.local_rows
    assert dims.band_rows == 2 and slots.shape[0] == CAP * tiles and boxes.shape[1] == tiles
    assert tiles & (tiles - 1) == 0
    frame = features.reshape(local_rows, cols, chans)

    smem = pl.BlockSpec(memory_space=pltpu.SMEM)
    vmem = pl.BlockSpec(memory_space=pltpu.VMEM)
    hbm = pl.BlockSpec(memory_space=pltpu.HBM)
    params = pltpu.CompilerParams(vmem_limit_bytes=VMEM_LIMIT)
    dma = pltpu.SemaphoreType.DMA

    def cost(flops, moved):
        return pl.CostEstimate(flops=int(flops), bytes_accessed=int(moved), transcendentals=0)

    def shaped(*shape, kind=BF16):
        return jax.ShapeDtypeStruct(shape, kind)

    def swap(arrays):
        moved = [arrays[0]] + [None] * (tiles - 1)
        for s in reversed(range(1, tiles)):
            moved[s] = lax.ppermute(arrays[s], "tile", [(i, i ^ s) for i in range(tiles)])
        return moved

    pack_scratch = [
        pltpu.VMEM((local_rows, cols, chans), BF16),
        pltpu.VMEM((local_rows, cols + 16, chans), F32),
        pltpu.VMEM((dims.rim, chans), F32),
        pltpu.VMEM((tiles, dims.message, chans), BF16),
        dma((2 * dims.bands,)),
        dma((dims.bands,)),
        dma((tiles,)),
    ]
    *sent_main, table = pl.pallas_call(
        functools.partial(pack_main_kernel, dims),
        out_shape=[shaped(dims.message, chans)] * tiles + [shaped(7, tiles, kind=I32)],
        in_specs=[hbm, hbm, hbm],
        out_specs=[hbm] * tiles + [smem],
        scratch_shapes=[
            pltpu.SMEM(boxes.shape, I32),
            pltpu.SMEM(slots.shape, I32),
            pltpu.SMEM((tiles,), I32),
            pltpu.SMEM((tiles,), I32),
            pltpu.SMEM((tiles + 1,), I32),
        ]
        + pack_scratch,
        compiler_params=params,
        cost_estimate=cost(0, 6e6),
        name="pack_main",
    )(boxes, slots, frame)
    got_main = swap(sent_main)

    *sent_extra, last, leading = pl.pallas_call(
        functools.partial(pack_extra_kernel, dims),
        out_shape=[shaped(dims.message, chans)] * tiles + [shaped(dims.bands, cols, chans)] * 2,
        in_specs=[smem, hbm],
        out_specs=[hbm] * (tiles + 2),
        scratch_shapes=pack_scratch,
        compiler_params=params,
        cost_estimate=cost(0, 6e6),
        name="pack_extra",
    )(table, frame)
    up = [(i, (i + 1) % tiles) for i in range(tiles)]
    above = lax.ppermute(last, "tile", up)
    below = lax.ppermute(leading, "tile", [(j, i) for i, j in up])
    got_extra = swap(sent_extra)

    weights = (dec_weight, first_weight, second_weight)
    biases = (dec_bias[None], first_bias[None], second_bias[None])
    restore_scratch = [
        pltpu.VMEM((tiles, dims.message, chans), BF16),
        pltpu.VMEM((3, 12, chans, 2 * chans), BF16),
        dma((tiles,)),
        dma((3, 2)),
        pltpu.VMEM((SPAN // 2 + 2, 2, SPAN, 3 * chans), BF16),
        pltpu.VMEM((SPAN, SPAN, chans), F32),
        pltpu.VMEM((S // 2 + 1, 2, S, 3 * chans), BF16),
        pltpu.VMEM((S // 2 + 1, 2, S, 3 * chans), BF16),
        pltpu.VMEM((S, S, chans), BF16),
        dma,
    ]
    *sent_back, partial = pl.pallas_call(
        functools.partial(main_kernel, dims),
        out_shape=[shaped(dims.back_rows, SPAN, chans)] * tiles + [shaped(CAP, S, S, chans)],
        in_specs=[hbm] * tiles + [smem] + [hbm] * 3 + [vmem] * 3,
        out_specs=[hbm] * (tiles + 1),
        scratch_shapes=restore_scratch
        + [pltpu.VMEM((tiles, dims.back_rows, SPAN, chans), BF16), dma((tiles,))],
        compiler_params=params,
        cost_estimate=cost(7e9, 8e6),
        name="restore_main",
    )(*got_main, table, *weights, *biases)
    got_back = swap(sent_back)

    restorations = pl.pallas_call(
        functools.partial(extra_kernel, dims),
        out_shape=shaped(CAP, S, S, chans),
        in_specs=[hbm] * tiles + [smem] + [hbm] * 3 + [vmem] * 3 + [hbm],
        out_specs=hbm,
        scratch_shapes=restore_scratch,
        input_output_aliases={tiles + 7: 0},
        compiler_params=params,
        cost_estimate=cost(6e9, 8e6),
        name="restore_extra",
    )(*got_extra, table, *weights, *biases, partial)

    above, below, _ = lax.optimization_barrier((above, below, sent_back[0]))
    decoded = pl.pallas_call(
        functools.partial(decode_kernel, dims),
        out_shape=shaped(local_rows, cols, chans),
        in_specs=[hbm] * 4 + [vmem],
        out_specs=vmem,
        scratch_shapes=[
            pltpu.VMEM((local_rows, cols, chans), BF16),
            pltpu.VMEM((dims.bands, cols, chans), BF16),
            pltpu.VMEM((dims.bands, cols, chans), BF16),
            pltpu.VMEM((12, chans, 2 * chans), BF16),
            pltpu.VMEM((2, cols, 12 * chans), BF16),
            dma((3 * dims.bands,)),
            dma((2,)),
        ],
        compiler_params=params,
        cost_estimate=cost(3e9, 6e6),
        name="decode",
    )(frame, above, below, weights[0], biases[0])

    finished = pl.pallas_call(
        functools.partial(paste_kernel, dims),
        out_shape=shaped(local_rows, cols, chans),
        in_specs=[smem, vmem] + [vmem] * tiles,
        out_specs=hbm,
        scratch_shapes=[
            pltpu.VMEM((local_rows, cols, chans), F32),
            pltpu.VMEM((local_rows, cols, chans), BF16),
            dma((local_rows,)),
        ],
        compiler_params=params,
        cost_estimate=cost(0, 6e6),
        name="paste",
    )(table, decoded, *got_back)
    return finished.reshape(features.shape), restorations


def solution(mesh):
    return jax.shard_map(
        shards,
        mesh=mesh,
        in_specs=(
            P("sess", "tile", None, None),
            P(),
            P(),
            P(),
            P(),
            P(),
            P(),
            P(None, "sess"),
            P("sess"),
        ),
        out_specs=(P("sess", "tile", None, None), P(("sess", "tile"), None, None, None)),
        check_vma=False,
    )
```

```python
import functools

import jax
import jax.numpy as jnp
from jax import lax
from jax.experimental import pallas as pl
from jax.experimental.pallas import tpu as pltpu
from jax.sharding import PartitionSpec as P

S = 64
UNIT = 12
NCLS = 3
CAP = 2
SPAN = UNIT * (NCLS + 1)
BF16 = jnp.bfloat16
F32 = jnp.float32
I32 = jnp.int32
FULL_GRANT = 62 * 1024 * 1024
SMALL_GRANT = 32 * 1024 * 1024
ROW, COL, SIDE, ROW2, COL2, SIDE2, PLACE = range(7)


def rows_within(window, band_rows, stride):
    return band_rows * (window // stride) + min(band_rows, window % stride)


class Dims:
    def __init__(self, features, tiles):
        self.bands, self.band_rows, self.cols, self.chans = features.shape
        self.tiles = tiles
        self.stride = tiles * self.band_rows
        self.shift = self.stride.bit_length() - 1
        self.local_rows = self.bands * self.band_rows
        self.rows = rows_within(SPAN + 2, self.band_rows, self.stride)
        self.back_rows = rows_within(SPAN, self.band_rows, self.stride)
        self.rim = -(-2 * self.rows // 16) * 16
        self.message = self.rows * SPAN + self.rim


def first_local(row, tile, dims):
    return ((row >> dims.shift) << 1) + jnp.clip((row & (dims.stride - 1)) - 2 * tile, 0, 2)


def global_row(local, tile, dims):
    return ((local >> 1) << dims.shift) + 2 * tile + (local & 1)


def silu(v):
    half = 0.5 * v
    return half + half * jnp.tanh(half)


def both(bias):
    return jnp.concatenate([bias[...], bias[...]], -1)


class RowTaps:
    def __init__(self, source, store, sems):
        chans = source.shape[-1]
        self.store = store
        self.copies = (
            pltpu.make_async_copy(source, store.at[0:3, :, :, 0:chans], sems.at[0]),
            pltpu.make_async_copy(source, store.at[1:4, :, :, chans : 2 * chans], sems.at[1]),
        )

    def start(self):
        for copy in self.copies:
            copy.start()
        chans = self.store.shape[2]
        none = jnp.zeros((3, chans, chans), BF16)
        self.store[3, :, :, 0:chans] = none
        self.store[0, :, :, chans : 2 * chans] = none

    def wait(self):
        for copy in self.copies:
            copy.wait()

    def value(self):
        return self.store[...].reshape(-1, self.store.shape[-1])


class ColumnTaps(RowTaps):
    def __init__(self, source, store, sems):
        chans = source.shape[-1]
        self.store = store
        self.copies = (
            pltpu.make_async_copy(source, store.at[:, 0:3, :, 0:chans], sems.at[0]),
            pltpu.make_async_copy(source, store.at[:, 1:4, :, chans : 2 * chans], sems.at[1]),
        )

    def start(self):
        for copy in self.copies:
            copy.start()
        chans = self.store.shape[2]
        none = jnp.zeros((3, chans, chans), BF16)
        self.store[:, 3, :, 0:chans] = none
        self.store[:, 0, :, chans : 2 * chans] = none


def row_pairs(src, first, count, taps):
    parts = [
        src[pl.ds(first, count), 0],
        src[pl.ds(first, count), 1],
        src[pl.ds(first + 1, count), 0],
        src[pl.ds(first + 1, count), 1],
    ]
    wide = jnp.concatenate(parts, -1)
    return jnp.dot(wide.reshape(-1, wide.shape[-1]), taps.value(), preferred_element_type=F32)


def column_pairs(src, first, count, taps):
    wide = jnp.concatenate([src[pl.ds(first + a, count)] for a in range(3)], -1)
    return jnp.dot(wide.reshape(-1, wide.shape[-1]), taps.value(), preferred_element_type=F32)


def fill_canvas(dims, feat, held, canvas, sems):
    def copy(band):
        return pltpu.make_async_copy(feat.at[band], held.at[band], sems.at[band])

    for band in range(dims.bands):
        copy(band).start()

    def finish():
        edge = jnp.zeros((8, dims.chans), F32)
        for band in range(dims.bands):
            copy(band).wait()
            for i in range(2):
                row = 2 * band + i
                canvas[row, 0:8, :] = edge
                canvas[row, 8 + dims.cols : 16 + dims.cols, :] = edge
                canvas[row, 8 : 8 + dims.cols, :] = held[band, i].astype(F32)

    return finish


def pack_crops(dims, table, row_at, col_at, canvas, rim, staged, sent, sems):
    me = lax.axis_index("tile")
    rim[...] = jnp.zeros_like(rim)

    @pl.loop(0, dims.tiles)
    def _(w):
        row0 = table[row_at, w]
        col0 = table[col_at, w]
        start = first_local(jnp.maximum(row0 - 1, 0), me, dims)
        for i in range(dims.rows):
            row = jnp.minimum(start + i, dims.local_rows - 1)
            staged[w, i * SPAN : (i + 1) * SPAN, :] = canvas[row, pl.ds(col0 + 8, SPAN), :].astype(BF16)
            rim[2 * i : 2 * i + 1, :] = canvas[row, pl.ds(col0 + 7, 1), :]
            rim[2 * i + 1 : 2 * i + 2, :] = canvas[row, pl.ds(col0 + 8 + SPAN, 1), :]
        staged[w, dims.rows * SPAN :, :] = rim[...].astype(BF16)
        pltpu.make_async_copy(staged.at[w], sent.at[w], sems.at[w]).start()

    @pl.loop(0, dims.tiles)
    def _(w):
        pltpu.make_async_copy(staged.at[w], sent.at[w], sems.at[w]).wait()


def pack_main_kernel(
    dims, boxes_in, slots_in, feat, sent, table, last, leading,
    boxes, slots, main, extra, seconds, held, canvas, rim, staged, sems, feat_sems, sent_sems,
):
    copies = (
        pltpu.make_async_copy(boxes_in, boxes, sems.at[0]),
        pltpu.make_async_copy(slots_in, slots, sems.at[1]),
    )
    for copy in copies:
        copy.start()
    finish = fill_canvas(dims, feat, held, canvas, feat_sems)
    edges = (
        pltpu.make_async_copy(feat.at[:, 1], last, sems.at[2]),
        pltpu.make_async_copy(feat.at[:, 0], leading, sems.at[3]),
    )
    for edge in edges:
        edge.start()
    for copy in copies:
        copy.wait()

    def first_pass(w, count):
        one = slots[CAP * w]
        two = slots[CAP * w + 1]
        full = (one >= 0) & (two >= 0)
        second = jnp.where(full, two, -1)
        main[w] = jnp.where(one >= 0, one, two)
        extra[w] = second
        seconds[count] = second
        return count + full.astype(I32)

    lax.fori_loop(0, dims.tiles, first_pass, jnp.int32(0))

    def second_pass(w, count):
        own = main[w]
        idle = own < 0
        crop = jnp.where(idle, seconds[count], own)
        table[ROW, w] = boxes[0, crop]
        table[COL, w] = boxes[1, crop]
        table[SIDE, w] = UNIT * (boxes[2, crop] + 2)
        other = jnp.maximum(extra[w], 0)
        table[ROW2, w] = boxes[0, other]
        table[COL2, w] = boxes[1, other]
        table[SIDE2, w] = jnp.where(extra[w] >= 0, UNIT * (boxes[2, other] + 2), 0)
        table[PLACE, w] = jnp.where(idle, 2, jnp.where(slots[CAP * w] >= 0, 0, 1))
        return count + idle.astype(I32)

    lax.fori_loop(0, dims.tiles, second_pass, jnp.int32(0))
    finish()
    pack_crops(dims, table, ROW, COL, canvas, rim, staged, sent, sent_sems)
    for edge in edges:
        edge.wait()


def pack_extra_kernel(dims, table, feat, sent, held, canvas, rim, staged, sems, feat_sems, sent_sems):
    fill_canvas(dims, feat, held, canvas, feat_sems)()
    pack_crops(dims, table, ROW2, COL2, canvas, rim, staged, sent, sent_sems)


def restore(dims, row0, length, arrival, got, taps, biases, raw, decoded, wide, inner, mixed, delta):
    chans = dims.chans
    above = row0 - 1
    pairs = SPAN // 2
    half = S // 2
    nothing = jnp.zeros((SPAN, 3 * chans), BF16)
    raw[0, 0] = nothing
    raw[pairs, 1] = nothing
    empty = jnp.zeros((half, 4 * chans), BF16)
    for store in (wide, inner):
        store[0] = empty
        store[S + 1] = empty

    @pl.loop(0, dims.tiles)
    def _(e):
        arrival(e).wait()
        start = first_local(jnp.maximum(above, 0), e, dims)
        rim = got[e, dims.rows * SPAN :, :].astype(F32)
        at = lax.broadcasted_iota(I32, (SPAN, chans), 0)
        for i in range(dims.rows):
            local = start + i
            place = global_row(local, e, dims) - above
            place = jnp.where((local < dims.local_rows) & (place < SPAN + 2), place, SPAN + 2)
            line = got[e, i * SPAN : (i + 1) * SPAN, :]
            wider = line.astype(F32)
            left = jnp.where(at == 0, rim[2 * i : 2 * i + 1], pltpu.roll(wider, 1, 0))
            right = jnp.where(at == SPAN - 1, rim[2 * i + 1 : 2 * i + 2], pltpu.roll(wider, SPAN - 1, 0))
            raw[place >> 1, place & 1] = jnp.concatenate([left.astype(BF16), line, right.astype(BF16)], -1)

    taps[0].wait()
    n = 8

    @pl.loop(0, pairs // n)
    def _(step):
        first = step * n
        total = silu(row_pairs(raw, first, n, taps[0]) + both(biases[0]))
        for k in range(n):
            part = total[k * SPAN : (k + 1) * SPAN]
            at = 2 * (first + k)
            upper = raw[first + k, 1, :, chans : 2 * chans].astype(F32) + part[:, :chans]
            lower = raw[first + k + 1, 0, :, chans : 2 * chans].astype(F32) + part[:, chans:]
            decoded[at] = upper.astype(BF16).astype(F32)
            decoded[at + 1] = lower.astype(BF16).astype(F32)

    lengthf = length.astype(F32)
    block = lax.broadcasted_iota(I32, (4, half, SPAN), 0)
    t = 2 * lax.broadcasted_iota(I32, (4, half, SPAN), 1) + block - 1
    j = lax.broadcasted_iota(I32, (4, half, SPAN), 2).astype(F32)
    spots = jnp.clip((t.astype(F32) + 0.5) * lengthf / S - 0.5, 0.0, lengthf - 1.0)
    across = jnp.where((t >= 0) & (t < S), jnp.maximum(0.0, 1.0 - jnp.abs(spots - j)), 0.0)
    across = across.reshape(4 * half, SPAN).astype(BF16)
    group = 4

    @pl.loop(0, S // 2 // group)
    def _(step):
        for k in range(group):
            lines = []
            for parity in range(2):
                s = 2 * (step * group + k) + parity
                spot = jnp.clip((2 * s + 1) * length - S, 0, (length - 1) * 2 * S)
                low = spot >> 7
                part = (spot & 127).astype(F32) * (1.0 / (2 * S))
                high = jnp.minimum(low + 1, SPAN - 1)
                lines.append(((1.0 - part) * decoded[low] + part * decoded[high]).astype(BF16))
            cells = jnp.dot(across, jnp.concatenate(lines, -1), preferred_element_type=F32).astype(BF16)
            for parity in range(2):
                at = 2 * (step * group + k) + parity + 1
                for b in range(4):
                    wide[at, :, b * chans : (b + 1) * chans] = cells[
                        b * half : (b + 1) * half, parity * chans : (parity + 1) * chans
                    ]

    n = 16
    taps[1].wait()

    @pl.loop(0, S // n)
    def _(step):
        first = step * n
        total = silu(column_pairs(wide, first, n, taps[1]) + both(biases[1]))
        at = lax.broadcasted_iota(I32, (n, half, chans), 1)
        even = pltpu.roll(total[:, :chans], n * half - 1, 0).reshape(n, half, chans)
        odd = pltpu.roll(total[:, chans:], 1, 0).reshape(n, half, chans)
        rows = pl.ds(first + 1, n)
        inner[rows, :, 0:chans] = jnp.where(at == 0, 0.0, odd).astype(BF16)
        inner[rows, :, chans : 3 * chans] = total.astype(BF16).reshape(n, half, 2 * chans)
        inner[rows, :, 3 * chans :] = jnp.where(at == half - 1, 0.0, even).astype(BF16)

    taps[2].wait()

    @pl.loop(0, S // n)
    def _(step):
        first = step * n
        total = column_pairs(inner, first, n, taps[2]) + both(biases[2])
        for k in range(n):
            mixed[k, pl.ds(0, half, stride=2), :] = total[k * half : (k + 1) * half, :chans]
            mixed[k, pl.ds(1, half, stride=2), :] = total[k * half : (k + 1) * half, chans:]
        delta[pl.ds(first, n)] = mixed[...].astype(BF16)


def begin(dims, arrived, weights, scratch):
    got, row_store, column_store, got_sems, tap_sems = scratch

    def arrival(e):
        return pltpu.make_async_copy(arrived.at[e], got.at[e], got_sems.at[e])

    for e in range(dims.tiles):
        arrival(e).start()
    taps = (
        RowTaps(weights[0], row_store, tap_sems.at[0]),
        ColumnTaps(weights[1], column_store.at[0], tap_sems.at[1]),
        ColumnTaps(weights[2], column_store.at[1], tap_sems.at[2]),
    )
    for tap in taps:
        tap.start()
    return arrival, taps


def main_kernel(
    dims, table, arrived, dec_w, one_w, two_w, dec_b, one_b, two_b, sent, restored,
    got, row_store, column_store, got_sems, tap_sems, raw, decoded, wide, inner, mixed, delta, sem, back, back_sems,
):
    tiles, chans = dims.tiles, dims.chans
    me = lax.axis_index("tile")
    row0 = table[ROW, me]
    length = table[SIDE, me]
    place = table[PLACE, me]
    scratch = (got, row_store, column_store, got_sems, tap_sems)
    arrival, taps = begin(dims, arrived, (dec_w, one_w, two_w), scratch)
    restore(dims, row0, length, arrival, got, taps, (dec_b, one_b, two_b), raw, decoded, wide, inner, mixed, delta)

    @pl.when(place < CAP)
    def _():
        pltpu.make_async_copy(delta, restored.at[place], sem).start()

    lengthf = length.astype(F32)
    t = lax.broadcasted_iota(I32, (SPAN, S), 0).astype(F32)
    s = lax.broadcasted_iota(I32, (SPAN, S), 1).astype(F32)
    spots = jnp.clip((t + 0.5) * S / lengthf - 0.5, 0.0, S - 1.0)
    lift = jnp.where(t < lengthf, jnp.maximum(0.0, 1.0 - jnp.abs(spots - s)), 0.0)
    coarse = lift.astype(BF16)
    lift = jnp.concatenate([coarse, (lift - coarse.astype(F32)).astype(BF16)], 0)
    scale = 1.0 / (2.0 * lengthf)
    group = 4

    @pl.loop(0, SPAN // 2 // group)
    def _(step):
        for k in range(group):
            lines = []
            for parity in range(2):
                h = 2 * (step * group + k) + parity
                spot = jnp.clip((2 * h + 1) * S - length, 0, (S - 1) * 2 * length)
                low = ((spot.astype(F32) + 0.5) * scale).astype(I32)
                part = (spot - low * 2 * length).astype(F32) * scale
                high = jnp.minimum(low + 1, S - 1)
                lines.append(((1.0 - part) * delta[low].astype(F32) + part * delta[high].astype(F32)).astype(BF16))
            patch = jnp.dot(lift, jnp.concatenate(lines, -1), preferred_element_type=F32)
            patch = (patch[:SPAN] + patch[SPAN:]).astype(BF16)
            for parity in range(2):
                row = row0 + 2 * (step * group + k) + parity
                dest = (row & (dims.stride - 1)) >> 1
                local = ((row >> dims.shift) << 1) + (row & 1)
                back[dest, local - first_local(row0, dest, dims)] = patch[:, parity * chans : (parity + 1) * chans]

    def leave(e):
        return pltpu.make_async_copy(back.at[e], sent.at[e], back_sems.at[e])

    for e in range(tiles):
        leave(e).start()
    for e in range(tiles):
        leave(e).wait()

    @pl.when(place < CAP)
    def _():
        pltpu.make_async_copy(delta, restored.at[place], sem).wait()


def extra_kernel(
    dims, table, arrived, dec_w, one_w, two_w, dec_b, one_b, two_b, partial, restored,
    got, row_store, column_store, got_sems, tap_sems, raw, decoded, wide, inner, mixed, delta, sem,
):
    me = lax.axis_index("tile")
    row0 = table[ROW2, me]
    length = table[SIDE2, me]
    place = table[PLACE, me]

    def write(slot):
        copy = pltpu.make_async_copy(delta, restored.at[slot], sem)
        copy.start()
        copy.wait()

    @pl.when(length > 0)
    def _():
        scratch = (got, row_store, column_store, got_sems, tap_sems)
        arrival, taps = begin(dims, arrived, (dec_w, one_w, two_w), scratch)
        restore(dims, row0, length, arrival, got, taps, (dec_b, one_b, two_b), raw, decoded, wide, inner, mixed, delta)
        write(1)

    @pl.when(length == 0)
    def _():
        delta[...] = jnp.zeros_like(delta)

        @pl.when(place != 0)
        def _():
            write(0)

        @pl.when(place != 1)
        def _():
            write(1)


def decode_kernel(dims, feat, above, below, weight, bias, decoded, held, up, down, store, lines, wide, mixed, sems, tap_sems):
    me = lax.axis_index("tile")
    bands, chans, cols = dims.bands, dims.chans, dims.cols
    half = cols // 2
    taps = ColumnTaps(weight, store, tap_sems)

    def fetch(band):
        return (
            pltpu.make_async_copy(feat.at[band], held.at[band], sems.at[0, band]),
            pltpu.make_async_copy(above.at[band], up.at[band], sems.at[1, band]),
            pltpu.make_async_copy(below.at[band], down.at[band], sems.at[2, band]),
        )

    for band in range(bands):
        for copy in fetch(band):
            copy.start()
    taps.start()
    top = (me == 0).astype(I32)
    bottom = (me == dims.tiles - 1).astype(I32)
    edge = jnp.zeros((8, chans), F32)
    for a in range(4):
        lines[a, 0:8] = edge
        lines[a, 8 + cols :] = edge
    for band in range(bands):
        for copy in fetch(band):
            copy.wait()
    taps.wait()

    @pl.loop(0, bands)
    def _(j):
        no_top = (top == 1) & (j == 0)
        no_bottom = (bottom == 1) & (j == bands - 1)
        over = up[jnp.maximum(j - top, 0)].astype(F32)
        under = down[jnp.minimum(j + bottom, bands - 1)].astype(F32)
        middle = slice(8, 8 + cols)
        lines[0, middle] = jnp.where(no_top, 0.0, over)
        lines[1, middle] = held[j, 0].astype(F32)
        lines[2, middle] = held[j, 1].astype(F32)
        lines[3, middle] = jnp.where(no_bottom, 0.0, under)
        for a in range(4):
            for b in range(4):
                wide[a, :, b * chans : (b + 1) * chans] = lines[a, pl.ds(7 + b, half, stride=2), :].astype(BF16)
        total = silu(column_pairs(wide, 0, 2, taps) + both(bias))
        for i in range(2):
            part = total[i * half : (i + 1) * half]
            for b in range(2):
                here = lines[i + 1, pl.ds(8 + b, half, stride=2), :]
                mixed[i, pl.ds(b, half, stride=2), :] = here + part[:, b * chans : (b + 1) * chans]
            decoded[2 * j + i] = mixed[i].astype(BF16)


def paste_kernel(dims, table, decoded, back, finished, canvas, out, sems):
    me = lax.axis_index("tile")
    for row in range(dims.local_rows):
        canvas[row] = decoded[row].astype(F32)

    @pl.loop(0, dims.tiles)
    def _(e):
        row0 = table[ROW, e]
        col0 = table[COL, e]
        length = table[SIDE, e]
        start = first_local(row0, me, dims)
        for i in range(dims.back_rows):
            local = start + i

            @pl.when((local < dims.local_rows) & (global_row(local, me, dims) - row0 < length))
            def _():
                canvas[local, pl.ds(col0, SPAN), :] += back[e, i].astype(F32)

    copies = [pltpu.make_async_copy(out.at[row], finished.at[row], sems.at[row]) for row in range(dims.local_rows)]
    for row in range(dims.local_rows):
        out[row] = canvas[row].astype(BF16)
        copies[row].start()
    for copy in copies:
        copy.wait()


def shards(features, dec_weight, dec_bias, first_weight, first_bias, second_weight, second_bias, boxes, slots):
    tiles = lax.axis_size("tile")
    dims = Dims(features, tiles)
    bands, cols, chans, local_rows = dims.bands, dims.cols, dims.chans, dims.local_rows
    assert dims.band_rows == 2 and slots.shape[0] == CAP * tiles and boxes.shape[1] == tiles
    assert tiles & (tiles - 1) == 0

    smem = pl.BlockSpec(memory_space=pltpu.SMEM)
    vmem = pl.BlockSpec(memory_space=pltpu.VMEM)
    hbm = pl.BlockSpec(memory_space=pl.ANY)
    full = pltpu.CompilerParams(vmem_limit_bytes=FULL_GRANT)
    small = pltpu.CompilerParams(vmem_limit_bytes=SMALL_GRANT)
    dma = pltpu.SemaphoreType.DMA

    def cost(flops, moved):
        return pl.CostEstimate(flops=int(flops), bytes_accessed=int(moved), transcendentals=0)

    def shaped(*shape, kind=BF16):
        return jax.ShapeDtypeStruct(shape, kind)

    def swap(array):
        return lax.all_to_all(array, "tile", split_axis=0, concat_axis=0, tiled=True)

    pack_scratch = [
        pltpu.VMEM((bands, 2, cols, chans), BF16),
        pltpu.VMEM((local_rows, cols + 16, chans), F32),
        pltpu.VMEM((dims.rim, chans), F32),
        pltpu.VMEM((tiles, dims.message, chans), BF16),
        dma((4,)),
        dma((bands,)),
        dma((tiles,)),
    ]
    message = shaped(tiles, dims.message, chans)
    sent_main, table, last, leading = pl.pallas_call(
        functools.partial(pack_main_kernel, dims),
        out_shape=[message, shaped(7, tiles, kind=I32), shaped(bands, cols, chans), shaped(bands, cols, chans)],
        in_specs=[hbm, hbm, hbm],
        out_specs=[hbm, smem, hbm, hbm],
        scratch_shapes=[
            pltpu.SMEM(boxes.shape, I32),
            pltpu.SMEM(slots.shape, I32),
            pltpu.SMEM((tiles,), I32),
            pltpu.SMEM((tiles,), I32),
            pltpu.SMEM((tiles + 1,), I32),
        ]
        + pack_scratch,
        compiler_params=full,
        cost_estimate=cost(0, 6e6),
        name="pack_main",
    )(boxes, slots, features)
    got_main = swap(sent_main)
    up = [(i, (i + 1) % tiles) for i in range(tiles)]
    above = lax.ppermute(last, "tile", up)
    below = lax.ppermute(leading, "tile", [(j, i) for i, j in up])

    sent_extra = pl.pallas_call(
        functools.partial(pack_extra_kernel, dims),
        out_shape=message,
        in_specs=[smem, hbm],
        out_specs=hbm,
        scratch_shapes=pack_scratch,
        compiler_params=full,
        cost_estimate=cost(0, 6e6),
        name="pack_extra",
    )(table, features)
    got_extra = swap(sent_extra)

    weights = tuple(w.reshape(3, 3, chans, chans) for w in (dec_weight, first_weight, second_weight))
    biases = (dec_bias[None], first_bias[None], second_bias[None])
    restore_scratch = [
        pltpu.VMEM((tiles, dims.message, chans), BF16),
        pltpu.VMEM((4, 3, chans, 2 * chans), BF16),
        pltpu.VMEM((2, 3, 4, chans, 2 * chans), BF16),
        dma((tiles,)),
        dma((3, 2)),
        pltpu.VMEM((SPAN // 2 + 2, 2, SPAN, 3 * chans), BF16),
        pltpu.VMEM((SPAN, SPAN, chans), F32),
        pltpu.VMEM((S + 2, S // 2, 4 * chans), BF16),
        pltpu.VMEM((S + 2, S // 2, 4 * chans), BF16),
        pltpu.VMEM((16, S, chans), F32),
        pltpu.VMEM((S, S, chans), BF16),
        dma,
    ]
    restored_shape = shaped(CAP, S, S, chans)
    sent_back, partial = pl.pallas_call(
        functools.partial(main_kernel, dims),
        out_shape=[shaped(tiles, dims.back_rows, SPAN, chans), restored_shape],
        in_specs=[smem] + [hbm] * 4 + [vmem] * 3,
        out_specs=[hbm, hbm],
        scratch_shapes=restore_scratch
        + [pltpu.VMEM((tiles, dims.back_rows, SPAN, chans), BF16), dma((tiles,))],
        compiler_params=full,
        cost_estimate=cost(7e9, 8e6),
        name="restore_main",
    )(table, got_main, *weights, *biases)
    got_back = swap(sent_back)

    restorations = pl.pallas_call(
        functools.partial(extra_kernel, dims),
        out_shape=restored_shape,
        in_specs=[smem] + [hbm] * 4 + [vmem] * 3 + [hbm],
        out_specs=hbm,
        scratch_shapes=restore_scratch,
        input_output_aliases={8: 0},
        compiler_params=full,
        cost_estimate=cost(6e9, 8e6),
        name="restore_extra",
    )(table, got_extra, *weights, *biases, partial)

    above, below, restorations = lax.optimization_barrier((above, below, restorations))
    decoded = pl.pallas_call(
        functools.partial(decode_kernel, dims),
        out_shape=shaped(local_rows, cols, chans),
        in_specs=[hbm] * 4 + [vmem],
        out_specs=vmem,
        scratch_shapes=[
            pltpu.VMEM((bands, 2, cols, chans), BF16),
            pltpu.VMEM((bands, cols, chans), BF16),
            pltpu.VMEM((bands, cols, chans), BF16),
            pltpu.VMEM((3, 4, chans, 2 * chans), BF16),
            pltpu.VMEM((4, cols + 16, chans), F32),
            pltpu.VMEM((4, cols // 2, 4 * chans), BF16),
            pltpu.VMEM((2, cols, chans), F32),
            dma((3, bands)),
            dma((2,)),
        ],
        compiler_params=small,
        cost_estimate=cost(3e9, 6e6),
        name="decode",
    )(features, above, below, weights[0], biases[0])

    finished = pl.pallas_call(
        functools.partial(paste_kernel, dims),
        out_shape=shaped(local_rows, cols, chans),
        in_specs=[smem, vmem, vmem],
        out_specs=hbm,
        scratch_shapes=[
            pltpu.VMEM((local_rows, cols, chans), F32),
            pltpu.VMEM((local_rows, cols, chans), BF16),
            dma((local_rows,)),
        ],
        compiler_params=small,
        cost_estimate=cost(0, 6e6),
        name="paste",
    )(table, decoded, got_back)
    return finished.reshape(features.shape), restorations


def solution(mesh):
    return jax.shard_map(
        shards,
        mesh=mesh,
        in_specs=(
            P("sess", "tile", None, None),
            P(),
            P(),
            P(),
            P(),
            P(),
            P(),
            P(None, "sess"),
            P("sess"),
        ),
        out_specs=(P("sess", "tile", None, None), P(("sess", "tile"), None, None, None)),
        check_vma=False,
    )
```

```python
import functools

import jax
import jax.numpy as jnp
from jax import lax
from jax.experimental import pallas as pl
from jax.experimental.pallas import tpu as pltpu
from jax.sharding import PartitionSpec as P

S = 64
UNIT = 12
NCLS = 3
CAP = 2
SPAN = UNIT * (NCLS + 1)
BF16 = jnp.bfloat16
F32 = jnp.float32
I32 = jnp.int32
FULL_GRANT = 62 * 1024 * 1024
SMALL_GRANT = 32 * 1024 * 1024
ROW, COL, SIDE, ROW2, COL2, SIDE2, PLACE = range(7)


def rows_within(window, band_rows, stride):
    return band_rows * (window // stride) + min(band_rows, window % stride)


class Dims:
    def __init__(self, features, tiles):
        self.bands, self.band_rows, self.cols, self.chans = features.shape
        self.tiles = tiles
        self.stride = tiles * self.band_rows
        self.shift = self.stride.bit_length() - 1
        self.local_rows = self.bands * self.band_rows
        self.rows = rows_within(SPAN + 2, self.band_rows, self.stride)
        self.back_rows = rows_within(SPAN, self.band_rows, self.stride)
        self.rim = -(-2 * self.rows // 16) * 16
        self.message = self.rows * SPAN + self.rim


def first_local(row, tile, dims):
    return ((row >> dims.shift) << 1) + jnp.clip((row & (dims.stride - 1)) - 2 * tile, 0, 2)


def global_row(local, tile, dims):
    return ((local >> 1) << dims.shift) + 2 * tile + (local & 1)


def silu(v):
    half = 0.5 * v
    return half + half * jnp.tanh(half)


def both(bias):
    return jnp.concatenate([bias[...], bias[...]], -1)


class RowTaps:
    def __init__(self, source, store, sems):
        chans = source.shape[-1]
        self.store = store
        self.copies = (
            pltpu.make_async_copy(source, store.at[0:3, :, :, 0:chans], sems.at[0]),
            pltpu.make_async_copy(source, store.at[1:4, :, :, chans : 2 * chans], sems.at[1]),
        )

    def start(self):
        for copy in self.copies:
            copy.start()
        chans = self.store.shape[2]
        none = jnp.zeros((3, chans, chans), BF16)
        self.store[3, :, :, 0:chans] = none
        self.store[0, :, :, chans : 2 * chans] = none

    def wait(self):
        for copy in self.copies:
            copy.wait()

    def value(self):
        return self.store[...].reshape(-1, self.store.shape[-1])


class ColumnTaps(RowTaps):
    def __init__(self, source, store, sems):
        chans = source.shape[-1]
        self.store = store
        self.copies = (
            pltpu.make_async_copy(source, store.at[:, 0:3, :, 0:chans], sems.at[0]),
            pltpu.make_async_copy(source, store.at[:, 1:4, :, chans : 2 * chans], sems.at[1]),
        )

    def start(self):
        for copy in self.copies:
            copy.start()
        chans = self.store.shape[2]
        none = jnp.zeros((3, chans, chans), BF16)
        self.store[:, 3, :, 0:chans] = none
        self.store[:, 0, :, chans : 2 * chans] = none


def two_chains(wide, taps):
    wide = wide.reshape(-1, wide.shape[-1])
    weight = taps.value()
    middle = weight.shape[0] // 2
    one = jnp.dot(wide[:, :middle], weight[:middle], preferred_element_type=F32)
    two = jnp.dot(wide[:, middle:], weight[middle:], preferred_element_type=F32)
    return one + two


def row_pairs(src, first, count, taps):
    parts = [
        src[pl.ds(first, count), 0],
        src[pl.ds(first, count), 1],
        src[pl.ds(first + 1, count), 0],
        src[pl.ds(first + 1, count), 1],
    ]
    return two_chains(jnp.concatenate(parts, -1), taps)


def column_pairs(src, first, count, taps):
    return two_chains(jnp.concatenate([src[pl.ds(first + a, count)] for a in range(3)], -1), taps)


def fill_canvas(dims, feat, held, canvas, sems):
    def copy(band):
        return pltpu.make_async_copy(feat.at[band], held.at[band], sems.at[band])

    for band in range(dims.bands):
        copy(band).start()

    def finish():
        edge = jnp.zeros((8, dims.chans), F32)
        for band in range(dims.bands):
            copy(band).wait()
            for i in range(2):
                row = 2 * band + i
                canvas[row, 0:8, :] = edge
                canvas[row, 8 + dims.cols : 16 + dims.cols, :] = edge
                canvas[row, 8 : 8 + dims.cols, :] = held[band, i].astype(F32)

    return finish


def pack_crops(dims, table, row_at, col_at, canvas, rim, staged, sent, sems):
    me = lax.axis_index("tile")
    rim[...] = jnp.zeros_like(rim)

    @pl.loop(0, dims.tiles)
    def _(w):
        row0 = table[row_at, w]
        col0 = table[col_at, w]
        start = first_local(jnp.maximum(row0 - 1, 0), me, dims)
        for i in range(dims.rows):
            row = jnp.minimum(start + i, dims.local_rows - 1)
            staged[w, i * SPAN : (i + 1) * SPAN, :] = canvas[row, pl.ds(col0 + 8, SPAN), :].astype(BF16)
            rim[2 * i : 2 * i + 1, :] = canvas[row, pl.ds(col0 + 7, 1), :]
            rim[2 * i + 1 : 2 * i + 2, :] = canvas[row, pl.ds(col0 + 8 + SPAN, 1), :]
        staged[w, dims.rows * SPAN :, :] = rim[...].astype(BF16)
        pltpu.make_async_copy(staged.at[w], sent.at[w], sems.at[w]).start()

    @pl.loop(0, dims.tiles)
    def _(w):
        pltpu.make_async_copy(staged.at[w], sent.at[w], sems.at[w]).wait()


def pack_main_kernel(
    dims, boxes_in, slots_in, feat, sent, table, last, leading,
    boxes, slots, main, extra, seconds, held, canvas, rim, staged, sems, feat_sems, sent_sems,
):
    copies = (
        pltpu.make_async_copy(boxes_in, boxes, sems.at[0]),
        pltpu.make_async_copy(slots_in, slots, sems.at[1]),
    )
    for copy in copies:
        copy.start()
    finish = fill_canvas(dims, feat, held, canvas, feat_sems)
    for copy in copies:
        copy.wait()

    def first_pass(w, count):
        one = slots[CAP * w]
        two = slots[CAP * w + 1]
        full = (one >= 0) & (two >= 0)
        second = jnp.where(full, two, -1)
        main[w] = jnp.where(one >= 0, one, two)
        extra[w] = second
        seconds[count] = second
        return count + full.astype(I32)

    lax.fori_loop(0, dims.tiles, first_pass, jnp.int32(0))

    def second_pass(w, count):
        own = main[w]
        idle = own < 0
        crop = jnp.where(idle, seconds[count], own)
        table[ROW, w] = boxes[0, crop]
        table[COL, w] = boxes[1, crop]
        table[SIDE, w] = UNIT * (boxes[2, crop] + 2)
        other = jnp.maximum(extra[w], 0)
        table[ROW2, w] = boxes[0, other]
        table[COL2, w] = boxes[1, other]
        table[SIDE2, w] = jnp.where(extra[w] >= 0, UNIT * (boxes[2, other] + 2), 0)
        table[PLACE, w] = jnp.where(idle, 2, jnp.where(slots[CAP * w] >= 0, 0, 1))
        return count + idle.astype(I32)

    lax.fori_loop(0, dims.tiles, second_pass, jnp.int32(0))
    finish()
    edges = (
        pltpu.make_async_copy(held.at[:, 1], last, sems.at[2]),
        pltpu.make_async_copy(held.at[:, 0], leading, sems.at[3]),
    )
    for edge in edges:
        edge.start()
    pack_crops(dims, table, ROW, COL, canvas, rim, staged, sent, sent_sems)
    for edge in edges:
        edge.wait()


def pack_extra_kernel(dims, table, feat, sent, held, canvas, rim, staged, sems, feat_sems, sent_sems):
    fill_canvas(dims, feat, held, canvas, feat_sems)()
    pack_crops(dims, table, ROW2, COL2, canvas, rim, staged, sent, sent_sems)


def restore(dims, row0, length, arrival, got, taps, biases, raw, decoded, wide, inner, mixed, delta):
    chans = dims.chans
    above = row0 - 1
    pairs = SPAN // 2
    half = S // 2
    nothing = jnp.zeros((SPAN, 3 * chans), BF16)
    raw[0, 0] = nothing
    raw[pairs, 1] = nothing
    empty = jnp.zeros((half, 4 * chans), BF16)
    for store in (wide, inner):
        store[0] = empty
        store[S + 1] = empty

    @pl.loop(0, dims.tiles)
    def _(e):
        arrival(e).wait()
        start = first_local(jnp.maximum(above, 0), e, dims)
        rim = got[e, dims.rows * SPAN :, :].astype(F32)
        at = lax.broadcasted_iota(I32, (SPAN, chans), 0)
        for i in range(dims.rows):
            local = start + i
            place = global_row(local, e, dims) - above
            place = jnp.where((local < dims.local_rows) & (place < SPAN + 2), place, SPAN + 2)
            line = got[e, i * SPAN : (i + 1) * SPAN, :]
            wider = line.astype(F32)
            left = jnp.where(at == 0, rim[2 * i : 2 * i + 1], pltpu.roll(wider, 1, 0))
            right = jnp.where(at == SPAN - 1, rim[2 * i + 1 : 2 * i + 2], pltpu.roll(wider, SPAN - 1, 0))
            raw[place >> 1, place & 1] = jnp.concatenate([left.astype(BF16), line, right.astype(BF16)], -1)

    taps[0].wait()
    n = 12

    @pl.loop(0, pairs // n)
    def _(step):
        first = step * n
        total = silu(row_pairs(raw, first, n, taps[0]) + both(biases[0]))
        for k in range(n):
            part = total[k * SPAN : (k + 1) * SPAN]
            at = 2 * (first + k)
            upper = raw[first + k, 1, :, chans : 2 * chans].astype(F32) + part[:, :chans]
            lower = raw[first + k + 1, 0, :, chans : 2 * chans].astype(F32) + part[:, chans:]
            decoded[at] = upper.astype(BF16).astype(F32)
            decoded[at + 1] = lower.astype(BF16).astype(F32)

    lengthf = length.astype(F32)
    block = lax.broadcasted_iota(I32, (4, half, SPAN), 0)
    t = 2 * lax.broadcasted_iota(I32, (4, half, SPAN), 1) + block - 1
    j = lax.broadcasted_iota(I32, (4, half, SPAN), 2).astype(F32)
    spots = jnp.clip((t.astype(F32) + 0.5) * lengthf / S - 0.5, 0.0, lengthf - 1.0)
    across = jnp.where((t >= 0) & (t < S), jnp.maximum(0.0, 1.0 - jnp.abs(spots - j)), 0.0)
    across = across.reshape(4 * half, SPAN).astype(BF16)
    group = 4

    @pl.loop(0, S // 2 // group)
    def _(step):
        for k in range(group):
            lines = []
            for parity in range(2):
                s = 2 * (step * group + k) + parity
                spot = jnp.clip((2 * s + 1) * length - S, 0, (length - 1) * 2 * S)
                low = spot >> 7
                part = (spot & 127).astype(F32) * (1.0 / (2 * S))
                high = jnp.minimum(low + 1, SPAN - 1)
                lines.append(((1.0 - part) * decoded[low] + part * decoded[high]).astype(BF16))
            cells = jnp.dot(across, jnp.concatenate(lines, -1), preferred_element_type=F32).astype(BF16)
            for parity in range(2):
                at = 2 * (step * group + k) + parity + 1
                for b in range(4):
                    wide[at, :, b * chans : (b + 1) * chans] = cells[
                        b * half : (b + 1) * half, parity * chans : (parity + 1) * chans
                    ]

    n = 32
    taps[1].wait()

    @pl.loop(0, S // n)
    def _(step):
        first = step * n
        total = silu(column_pairs(wide, first, n, taps[1]) + both(biases[1]))
        at = lax.broadcasted_iota(I32, (n, half, chans), 1)
        even = pltpu.roll(total[:, :chans], n * half - 1, 0).reshape(n, half, chans)
        odd = pltpu.roll(total[:, chans:], 1, 0).reshape(n, half, chans)
        rows = pl.ds(first + 1, n)
        inner[rows, :, 0:chans] = jnp.where(at == 0, 0.0, odd).astype(BF16)
        inner[rows, :, chans : 3 * chans] = total.astype(BF16).reshape(n, half, 2 * chans)
        inner[rows, :, 3 * chans :] = jnp.where(at == half - 1, 0.0, even).astype(BF16)

    taps[2].wait()

    @pl.loop(0, S // n)
    def _(step):
        first = step * n
        total = column_pairs(inner, first, n, taps[2]) + both(biases[2])
        for k in range(n):
            mixed[k, pl.ds(0, half, stride=2), :] = total[k * half : (k + 1) * half, :chans]
            mixed[k, pl.ds(1, half, stride=2), :] = total[k * half : (k + 1) * half, chans:]
        delta[pl.ds(first, n)] = mixed[...].astype(BF16)


def begin(dims, arrived, weights, scratch):
    got, row_store, column_store, got_sems, tap_sems = scratch

    def arrival(e):
        return pltpu.make_async_copy(arrived.at[e], got.at[e], got_sems.at[e])

    for e in range(dims.tiles):
        arrival(e).start()
    taps = (
        RowTaps(weights[0], row_store, tap_sems.at[0]),
        ColumnTaps(weights[1], column_store.at[0], tap_sems.at[1]),
        ColumnTaps(weights[2], column_store.at[1], tap_sems.at[2]),
    )
    for tap in taps:
        tap.start()
    return arrival, taps


def main_kernel(
    dims, table, arrived, dec_w, one_w, two_w, dec_b, one_b, two_b, sent, restored,
    got, row_store, column_store, got_sems, tap_sems, raw, decoded, wide, inner, mixed, delta, sem, back, back_sems,
):
    tiles, chans = dims.tiles, dims.chans
    me = lax.axis_index("tile")
    row0 = table[ROW, me]
    length = table[SIDE, me]
    place = table[PLACE, me]
    scratch = (got, row_store, column_store, got_sems, tap_sems)
    arrival, taps = begin(dims, arrived, (dec_w, one_w, two_w), scratch)
    restore(dims, row0, length, arrival, got, taps, (dec_b, one_b, two_b), raw, decoded, wide, inner, mixed, delta)

    @pl.when(place < CAP)
    def _():
        pltpu.make_async_copy(delta, restored.at[place], sem).start()

    lengthf = length.astype(F32)
    t = lax.broadcasted_iota(I32, (SPAN, S), 0).astype(F32)
    s = lax.broadcasted_iota(I32, (SPAN, S), 1).astype(F32)
    spots = jnp.clip((t + 0.5) * S / lengthf - 0.5, 0.0, S - 1.0)
    lift = jnp.where(t < lengthf, jnp.maximum(0.0, 1.0 - jnp.abs(spots - s)), 0.0)
    coarse = lift.astype(BF16)
    lift = jnp.concatenate([coarse, (lift - coarse.astype(F32)).astype(BF16)], 0)
    scale = 1.0 / (2.0 * lengthf)
    group = 4

    @pl.loop(0, SPAN // 2 // group)
    def _(step):
        for k in range(group):
            lines = []
            for parity in range(2):
                h = 2 * (step * group + k) + parity
                spot = jnp.clip((2 * h + 1) * S - length, 0, (S - 1) * 2 * length)
                low = ((spot.astype(F32) + 0.5) * scale).astype(I32)
                part = (spot - low * 2 * length).astype(F32) * scale
                high = jnp.minimum(low + 1, S - 1)
                lines.append(((1.0 - part) * delta[low].astype(F32) + part * delta[high].astype(F32)).astype(BF16))
            patch = jnp.dot(lift, jnp.concatenate(lines, -1), preferred_element_type=F32)
            patch = (patch[:SPAN] + patch[SPAN:]).astype(BF16)
            for parity in range(2):
                row = row0 + 2 * (step * group + k) + parity
                dest = (row & (dims.stride - 1)) >> 1
                local = ((row >> dims.shift) << 1) + (row & 1)
                back[dest, local - first_local(row0, dest, dims)] = patch[:, parity * chans : (parity + 1) * chans]

    def leave(e):
        return pltpu.make_async_copy(back.at[e], sent.at[e], back_sems.at[e])

    for e in range(tiles):
        leave(e).start()
    for e in range(tiles):
        leave(e).wait()

    @pl.when(place < CAP)
    def _():
        pltpu.make_async_copy(delta, restored.at[place], sem).wait()


def extra_kernel(
    dims, table, arrived, dec_w, one_w, two_w, dec_b, one_b, two_b, partial, restored,
    got, row_store, column_store, got_sems, tap_sems, raw, decoded, wide, inner, mixed, delta, sem,
):
    me = lax.axis_index("tile")
    row0 = table[ROW2, me]
    length = table[SIDE2, me]
    place = table[PLACE, me]

    def write(slot):
        copy = pltpu.make_async_copy(delta, restored.at[slot], sem)
        copy.start()
        copy.wait()

    @pl.when(length > 0)
    def _():
        scratch = (got, row_store, column_store, got_sems, tap_sems)
        arrival, taps = begin(dims, arrived, (dec_w, one_w, two_w), scratch)
        restore(dims, row0, length, arrival, got, taps, (dec_b, one_b, two_b), raw, decoded, wide, inner, mixed, delta)
        write(1)

    @pl.when(length == 0)
    def _():
        delta[...] = jnp.zeros_like(delta)

        @pl.when(place != 0)
        def _():
            write(0)

        @pl.when(place != 1)
        def _():
            write(1)


def decode_kernel(dims, feat, above, below, weight, bias, decoded, held, up, down, store, lines, wide, mixed, sems, tap_sems):
    me = lax.axis_index("tile")
    bands, chans, cols = dims.bands, dims.chans, dims.cols
    half = cols // 2
    taps = ColumnTaps(weight, store, tap_sems)

    def fetch(band):
        return (
            pltpu.make_async_copy(feat.at[band], held.at[band], sems.at[0, band]),
            pltpu.make_async_copy(above.at[band], up.at[band], sems.at[1, band]),
            pltpu.make_async_copy(below.at[band], down.at[band], sems.at[2, band]),
        )

    for band in range(bands):
        for copy in fetch(band):
            copy.start()
    taps.start()
    top = (me == 0).astype(I32)
    bottom = (me == dims.tiles - 1).astype(I32)
    edge = jnp.zeros((8, chans), F32)
    for a in range(4):
        lines[a, 0:8] = edge
        lines[a, 8 + cols :] = edge
    for band in range(bands):
        for copy in fetch(band):
            copy.wait()
    taps.wait()

    @pl.loop(0, bands)
    def _(j):
        no_top = (top == 1) & (j == 0)
        no_bottom = (bottom == 1) & (j == bands - 1)
        over = up[jnp.maximum(j - top, 0)].astype(F32)
        under = down[jnp.minimum(j + bottom, bands - 1)].astype(F32)
        middle = slice(8, 8 + cols)
        lines[0, middle] = jnp.where(no_top, 0.0, over)
        lines[1, middle] = held[j, 0].astype(F32)
        lines[2, middle] = held[j, 1].astype(F32)
        lines[3, middle] = jnp.where(no_bottom, 0.0, under)
        for a in range(4):
            for b in range(4):
                wide[a, :, b * chans : (b + 1) * chans] = lines[a, pl.ds(7 + b, half, stride=2), :].astype(BF16)
        total = silu(column_pairs(wide, 0, 2, taps) + both(bias))
        for i in range(2):
            part = total[i * half : (i + 1) * half]
            for b in range(2):
                here = lines[i + 1, pl.ds(8 + b, half, stride=2), :]
                mixed[i, pl.ds(b, half, stride=2), :] = here + part[:, b * chans : (b + 1) * chans]
            decoded[2 * j + i] = mixed[i].astype(BF16)


def paste_kernel(dims, table, decoded, back, finished, canvas, out, sems):
    me = lax.axis_index("tile")
    for row in range(dims.local_rows):
        canvas[row] = decoded[row].astype(F32)

    @pl.loop(0, dims.tiles)
    def _(e):
        row0 = table[ROW, e]
        col0 = table[COL, e]
        length = table[SIDE, e]
        start = first_local(row0, me, dims)
        for i in range(dims.back_rows):
            local = start + i

            @pl.when((local < dims.local_rows) & (global_row(local, me, dims) - row0 < length))
            def _():
                canvas[local, pl.ds(col0, SPAN), :] += back[e, i].astype(F32)

    copies = [pltpu.make_async_copy(out.at[row], finished.at[row], sems.at[row]) for row in range(dims.local_rows)]
    for row in range(dims.local_rows):
        out[row] = canvas[row].astype(BF16)
        copies[row].start()
    for copy in copies:
        copy.wait()


def shards(features, dec_weight, dec_bias, first_weight, first_bias, second_weight, second_bias, boxes, slots):
    tiles = lax.axis_size("tile")
    dims = Dims(features, tiles)
    bands, cols, chans, local_rows = dims.bands, dims.cols, dims.chans, dims.local_rows
    assert dims.band_rows == 2 and slots.shape[0] == CAP * tiles and boxes.shape[1] == tiles
    assert tiles & (tiles - 1) == 0

    smem = pl.BlockSpec(memory_space=pltpu.SMEM)
    vmem = pl.BlockSpec(memory_space=pltpu.VMEM)
    hbm = pl.BlockSpec(memory_space=pl.ANY)
    full = pltpu.CompilerParams(vmem_limit_bytes=FULL_GRANT)
    small = pltpu.CompilerParams(vmem_limit_bytes=SMALL_GRANT)
    dma = pltpu.SemaphoreType.DMA

    def cost(flops, moved):
        return pl.CostEstimate(flops=int(flops), bytes_accessed=int(moved), transcendentals=0)

    def shaped(*shape, kind=BF16):
        return jax.ShapeDtypeStruct(shape, kind)

    def swap(array):
        return lax.all_to_all(array, "tile", split_axis=0, concat_axis=0, tiled=True)

    pack_scratch = [
        pltpu.VMEM((bands, 2, cols, chans), BF16),
        pltpu.VMEM((local_rows, cols + 16, chans), F32),
        pltpu.VMEM((dims.rim, chans), F32),
        pltpu.VMEM((tiles, dims.message, chans), BF16),
        dma((4,)),
        dma((bands,)),
        dma((tiles,)),
    ]
    message = shaped(tiles, dims.message, chans)
    sent_main, table, last, leading = pl.pallas_call(
        functools.partial(pack_main_kernel, dims),
        out_shape=[message, shaped(7, tiles, kind=I32), shaped(bands, cols, chans), shaped(bands, cols, chans)],
        in_specs=[hbm, hbm, hbm],
        out_specs=[hbm, smem, hbm, hbm],
        scratch_shapes=[
            pltpu.SMEM(boxes.shape, I32),
            pltpu.SMEM(slots.shape, I32),
            pltpu.SMEM((tiles,), I32),
            pltpu.SMEM((tiles,), I32),
            pltpu.SMEM((tiles + 1,), I32),
        ]
        + pack_scratch,
        compiler_params=full,
        cost_estimate=cost(0, 6e6),
        name="pack_main",
    )(boxes, slots, features)
    got_main = swap(sent_main)
    up = [(i, (i + 1) % tiles) for i in range(tiles)]
    above = lax.ppermute(last, "tile", up)
    below = lax.ppermute(leading, "tile", [(j, i) for i, j in up])

    sent_extra = pl.pallas_call(
        functools.partial(pack_extra_kernel, dims),
        out_shape=message,
        in_specs=[smem, hbm],
        out_specs=hbm,
        scratch_shapes=pack_scratch,
        compiler_params=full,
        cost_estimate=cost(0, 6e6),
        name="pack_extra",
    )(table, features)
    got_extra = swap(sent_extra)

    weights = tuple(w.reshape(3, 3, chans, chans) for w in (dec_weight, first_weight, second_weight))
    biases = (dec_bias[None], first_bias[None], second_bias[None])
    restore_scratch = [
        pltpu.VMEM((tiles, dims.message, chans), BF16),
        pltpu.VMEM((4, 3, chans, 2 * chans), BF16),
        pltpu.VMEM((2, 3, 4, chans, 2 * chans), BF16),
        dma((tiles,)),
        dma((3, 2)),
        pltpu.VMEM((SPAN // 2 + 2, 2, SPAN, 3 * chans), BF16),
        pltpu.VMEM((SPAN, SPAN, chans), F32),
        pltpu.VMEM((S + 2, S // 2, 4 * chans), BF16),
        pltpu.VMEM((S + 2, S // 2, 4 * chans), BF16),
        pltpu.VMEM((32, S, chans), F32),
        pltpu.VMEM((S, S, chans), BF16),
        dma,
    ]
    restored_shape = shaped(CAP, S, S, chans)
    sent_back, partial = pl.pallas_call(
        functools.partial(main_kernel, dims),
        out_shape=[shaped(tiles, dims.back_rows, SPAN, chans), restored_shape],
        in_specs=[smem] + [hbm] * 4 + [vmem] * 3,
        out_specs=[hbm, hbm],
        scratch_shapes=restore_scratch
        + [pltpu.VMEM((tiles, dims.back_rows, SPAN, chans), BF16), dma((tiles,))],
        compiler_params=full,
        cost_estimate=cost(7e9, 8e6),
        name="restore_main",
    )(table, got_main, *weights, *biases)
    got_back = swap(sent_back)

    restorations = pl.pallas_call(
        functools.partial(extra_kernel, dims),
        out_shape=restored_shape,
        in_specs=[smem] + [hbm] * 4 + [vmem] * 3 + [hbm],
        out_specs=hbm,
        scratch_shapes=restore_scratch,
        input_output_aliases={8: 0},
        compiler_params=full,
        cost_estimate=cost(6e9, 8e6),
        name="restore_extra",
    )(table, got_extra, *weights, *biases, partial)

    above, below, restorations = lax.optimization_barrier((above, below, restorations))
    decoded = pl.pallas_call(
        functools.partial(decode_kernel, dims),
        out_shape=shaped(local_rows, cols, chans),
        in_specs=[hbm] * 4 + [vmem],
        out_specs=vmem,
        scratch_shapes=[
            pltpu.VMEM((bands, 2, cols, chans), BF16),
            pltpu.VMEM((bands, cols, chans), BF16),
            pltpu.VMEM((bands, cols, chans), BF16),
            pltpu.VMEM((3, 4, chans, 2 * chans), BF16),
            pltpu.VMEM((4, cols + 16, chans), F32),
            pltpu.VMEM((4, cols // 2, 4 * chans), BF16),
            pltpu.VMEM((2, cols, chans), F32),
            dma((3, bands)),
            dma((2,)),
        ],
        compiler_params=small,
        cost_estimate=cost(3e9, 6e6),
        name="decode",
    )(features, above, below, weights[0], biases[0])

    finished = pl.pallas_call(
        functools.partial(paste_kernel, dims),
        out_shape=shaped(local_rows, cols, chans),
        in_specs=[smem, vmem, vmem],
        out_specs=hbm,
        scratch_shapes=[
            pltpu.VMEM((local_rows, cols, chans), F32),
            pltpu.VMEM((local_rows, cols, chans), BF16),
            dma((local_rows,)),
        ],
        compiler_params=small,
        cost_estimate=cost(0, 6e6),
        name="paste",
    )(table, decoded, got_back)
    return finished.reshape(features.shape), restorations


def solution(mesh):
    return jax.shard_map(
        shards,
        mesh=mesh,
        in_specs=(
            P("sess", "tile", None, None),
            P(),
            P(),
            P(),
            P(),
            P(),
            P(),
            P(None, "sess"),
            P("sess"),
        ),
        out_specs=(P("sess", "tile", None, None), P(("sess", "tile"), None, None, None)),
        check_vma=False,
    )
```

```python
import functools

import jax
import jax.numpy as jnp
from jax import lax
from jax.experimental import pallas as pl
from jax.experimental.pallas import tpu as pltpu
from jax.sharding import PartitionSpec as P

S = 64
UNIT = 12
NCLS = 3
CAP = 2
SPAN = UNIT * (NCLS + 1)
BF16 = jnp.bfloat16
F32 = jnp.float32
I32 = jnp.int32
FULL_GRANT = 66500000
SMALL_GRANT = 32 * 1024 * 1024
ROW, COL, SIDE, ROW2, COL2, SIDE2, PLACE = range(7)


def rows_within(window, band_rows, stride):
    return band_rows * (window // stride) + min(band_rows, window % stride)


class Dims:
    def __init__(self, features, tiles):
        self.bands, self.band_rows, self.cols, self.chans = features.shape
        self.tiles = tiles
        self.stride = tiles * self.band_rows
        self.shift = self.stride.bit_length() - 1
        self.local_rows = self.bands * self.band_rows
        self.rows = rows_within(SPAN + 2, self.band_rows, self.stride)
        self.back_rows = rows_within(SPAN, self.band_rows, self.stride)
        self.rim = -(-2 * self.rows // 16) * 16
        self.message = self.rows * SPAN + self.rim


def first_local(row, tile, dims):
    return ((row >> dims.shift) << 1) + jnp.clip((row & (dims.stride - 1)) - 2 * tile, 0, 2)


def global_row(local, tile, dims):
    return ((local >> 1) << dims.shift) + 2 * tile + (local & 1)


def silu(v):
    half = 0.5 * v
    return half + half * jnp.tanh(half)


def both(bias):
    return jnp.concatenate([bias[...], bias[...]], -1)


class RowTaps:
    def __init__(self, source, store, sems):
        chans = source.shape[-1]
        self.store = store
        self.copies = (
            pltpu.make_async_copy(source, store.at[0:3, :, :, 0:chans], sems.at[0]),
            pltpu.make_async_copy(source, store.at[1:4, :, :, chans : 2 * chans], sems.at[1]),
        )

    def start(self):
        for copy in self.copies:
            copy.start()
        chans = self.store.shape[2]
        none = jnp.zeros((3, chans, chans), BF16)
        self.store[3, :, :, 0:chans] = none
        self.store[0, :, :, chans : 2 * chans] = none

    def wait(self):
        for copy in self.copies:
            copy.wait()

    def value(self):
        return self.store[...].reshape(-1, self.store.shape[-1])


class ColumnTaps(RowTaps):
    def __init__(self, source, store, sems):
        chans = source.shape[-1]
        self.store = store
        self.copies = (
            pltpu.make_async_copy(source, store.at[:, 0:3, :, 0:chans], sems.at[0]),
            pltpu.make_async_copy(source, store.at[:, 1:4, :, chans : 2 * chans], sems.at[1]),
        )

    def start(self):
        for copy in self.copies:
            copy.start()
        chans = self.store.shape[2]
        none = jnp.zeros((3, chans, chans), BF16)
        self.store[:, 3, :, 0:chans] = none
        self.store[:, 0, :, chans : 2 * chans] = none


def two_chains(wide, taps):
    wide = wide.reshape(-1, wide.shape[-1])
    weight = taps.value()
    middle = weight.shape[0] // 2
    one = jnp.dot(wide[:, :middle], weight[:middle], preferred_element_type=F32)
    two = jnp.dot(wide[:, middle:], weight[middle:], preferred_element_type=F32)
    return one + two


def row_pairs(src, first, count, taps):
    parts = [
        src[pl.ds(first, count), 0],
        src[pl.ds(first, count), 1],
        src[pl.ds(first + 1, count), 0],
        src[pl.ds(first + 1, count), 1],
    ]
    return two_chains(jnp.concatenate(parts, -1), taps)


def column_pairs(src, first, count, taps):
    return two_chains(jnp.concatenate([src[pl.ds(first + a, count)] for a in range(3)], -1), taps)


def fill_canvas(dims, feat, held, canvas, sems):
    def copy(band):
        return pltpu.make_async_copy(feat.at[band], held.at[band], sems.at[band])

    for band in range(dims.bands):
        copy(band).start()

    def finish():
        edge = jnp.zeros((8, dims.chans), F32)
        for band in range(dims.bands):
            copy(band).wait()
            for i in range(2):
                row = 2 * band + i
                canvas[row, 0:8, :] = edge
                canvas[row, 8 + dims.cols : 16 + dims.cols, :] = edge
                canvas[row, 8 : 8 + dims.cols, :] = held[band, i].astype(F32)

    return finish


def pack_crops(dims, table, row_at, col_at, canvas, rim, staged, partner):
    me = lax.axis_index("tile")
    rim[...] = jnp.zeros_like(rim)

    @pl.loop(0, dims.tiles)
    def _(s):
        w = partner(s)
        row0 = table[row_at, w]
        col0 = table[col_at, w]
        start = first_local(jnp.maximum(row0 - 1, 0), me, dims)
        for i in range(dims.rows):
            row = jnp.minimum(start + i, dims.local_rows - 1)
            staged[s, i * SPAN : (i + 1) * SPAN, :] = canvas[row, pl.ds(col0 + 8, SPAN), :].astype(BF16)
            rim[2 * i : 2 * i + 1, :] = canvas[row, pl.ds(col0 + 7, 1), :]
            rim[2 * i + 1 : 2 * i + 2, :] = canvas[row, pl.ds(col0 + 8 + SPAN, 1), :]
        staged[s, dims.rows * SPAN :, :] = rim[...].astype(BF16)


def pack_main_kernel(
    dims, boxes_in, slots_in, feat, *refs
):
    sent, refs = refs[: dims.tiles], refs[dims.tiles :]
    table, last, leading, boxes, slots, main, extra, seconds, held, canvas, rim, staged, sems, feat_sems, sent_sems = refs
    me = lax.axis_index("tile")
    copies = (
        pltpu.make_async_copy(boxes_in, boxes, sems.at[0]),
        pltpu.make_async_copy(slots_in, slots, sems.at[1]),
    )
    for copy in copies:
        copy.start()
    finish = fill_canvas(dims, feat, held, canvas, feat_sems)
    for copy in copies:
        copy.wait()

    def first_pass(w, count):
        one = slots[CAP * w]
        two = slots[CAP * w + 1]
        full = (one >= 0) & (two >= 0)
        second = jnp.where(full, two, -1)
        main[w] = jnp.where(one >= 0, one, two)
        extra[w] = second
        seconds[count] = second
        return count + full.astype(I32)

    lax.fori_loop(0, dims.tiles, first_pass, jnp.int32(0))

    def second_pass(w, count):
        own = main[w]
        idle = own < 0
        crop = jnp.where(idle, seconds[count], own)
        table[ROW, w] = boxes[0, crop]
        table[COL, w] = boxes[1, crop]
        table[SIDE, w] = UNIT * (boxes[2, crop] + 2)
        other = jnp.maximum(extra[w], 0)
        table[ROW2, w] = boxes[0, other]
        table[COL2, w] = boxes[1, other]
        table[SIDE2, w] = jnp.where(extra[w] >= 0, UNIT * (boxes[2, other] + 2), 0)
        table[PLACE, w] = jnp.where(idle, 2, jnp.where(slots[CAP * w] >= 0, 0, 1))
        return count + idle.astype(I32)

    lax.fori_loop(0, dims.tiles, second_pass, jnp.int32(0))
    finish()
    edges = (
        pltpu.make_async_copy(held.at[:, 1], last, sems.at[2]),
        pltpu.make_async_copy(held.at[:, 0], leading, sems.at[3]),
    )
    for edge in edges:
        edge.start()
    pack_crops(dims, table, ROW, COL, canvas, rim, staged, lambda s: me ^ s)
    copies = [pltpu.make_async_copy(staged.at[s], sent[s], sent_sems.at[s]) for s in range(dims.tiles)]
    for copy in copies:
        copy.start()
    for copy in copies:
        copy.wait()
    for edge in edges:
        edge.wait()


def pack_extra_kernel(dims, table, feat, sent, held, canvas, rim, staged, sems, feat_sems, sent_sems):
    fill_canvas(dims, feat, held, canvas, feat_sems)()
    pack_crops(dims, table, ROW2, COL2, canvas, rim, staged, lambda s: s)
    copies = [pltpu.make_async_copy(staged.at[s], sent.at[s], sent_sems.at[s]) for s in range(dims.tiles)]
    for copy in copies:
        copy.start()
    for copy in copies:
        copy.wait()


def restore(dims, row0, length, arrival, source, got, taps, biases, raw, decoded, wide, inner, mixed, delta, finish):
    chans = dims.chans
    above = row0 - 1
    pairs = SPAN // 2
    half = S // 2
    nothing = jnp.zeros((SPAN, 3 * chans), BF16)
    raw[0, 0] = nothing
    raw[pairs, 1] = nothing
    empty = jnp.zeros((half, 4 * chans), BF16)
    for store in (wide, inner):
        store[0] = empty
        store[S + 1] = empty

    @pl.loop(0, dims.tiles)
    def _(s):
        arrival(s).wait()
        e = source(s)
        start = first_local(jnp.maximum(above, 0), e, dims)
        rim = got[s, dims.rows * SPAN :, :].astype(F32)
        at = lax.broadcasted_iota(I32, (SPAN, chans), 0)
        for i in range(dims.rows):
            local = start + i
            place = global_row(local, e, dims) - above
            place = jnp.where((local < dims.local_rows) & (place < SPAN + 2), place, SPAN + 2)
            line = got[s, i * SPAN : (i + 1) * SPAN, :]
            wider = line.astype(F32)
            left = jnp.where(at == 0, rim[2 * i : 2 * i + 1], pltpu.roll(wider, 1, 0))
            right = jnp.where(at == SPAN - 1, rim[2 * i + 1 : 2 * i + 2], pltpu.roll(wider, SPAN - 1, 0))
            raw[place >> 1, place & 1] = jnp.concatenate([left.astype(BF16), line, right.astype(BF16)], -1)

    taps[0].wait()
    n = 12

    @pl.loop(0, pairs // n)
    def _(step):
        first = step * n
        total = silu(row_pairs(raw, first, n, taps[0]) + both(biases[0]))
        for k in range(n):
            part = total[k * SPAN : (k + 1) * SPAN]
            at = 2 * (first + k)
            upper = raw[first + k, 1, :, chans : 2 * chans].astype(F32) + part[:, :chans]
            lower = raw[first + k + 1, 0, :, chans : 2 * chans].astype(F32) + part[:, chans:]
            decoded[at] = upper.astype(BF16).astype(F32)
            decoded[at + 1] = lower.astype(BF16).astype(F32)

    lengthf = length.astype(F32)
    block = lax.broadcasted_iota(I32, (4, half, SPAN), 0)
    t = 2 * lax.broadcasted_iota(I32, (4, half, SPAN), 1) + block - 1
    j = lax.broadcasted_iota(I32, (4, half, SPAN), 2).astype(F32)
    spots = jnp.clip((t.astype(F32) + 0.5) * lengthf / S - 0.5, 0.0, lengthf - 1.0)
    across = jnp.where((t >= 0) & (t < S), jnp.maximum(0.0, 1.0 - jnp.abs(spots - j)), 0.0)
    across = across.reshape(4 * half, SPAN).astype(BF16)
    group = 8

    @pl.loop(0, S // 2 // group)
    def _(step):
        for k in range(group):
            lines = []
            for parity in range(2):
                s = 2 * (step * group + k) + parity
                spot = jnp.clip((2 * s + 1) * length - S, 0, (length - 1) * 2 * S)
                low = spot >> 7
                part = (spot & 127).astype(F32) * (1.0 / (2 * S))
                high = jnp.minimum(low + 1, SPAN - 1)
                lines.append(((1.0 - part) * decoded[low] + part * decoded[high]).astype(BF16))
            cells = jnp.dot(across, jnp.concatenate(lines, -1), preferred_element_type=F32).astype(BF16)
            for parity in range(2):
                at = 2 * (step * group + k) + parity + 1
                for b in range(4):
                    wide[at, :, b * chans : (b + 1) * chans] = cells[
                        b * half : (b + 1) * half, parity * chans : (parity + 1) * chans
                    ]

    n = 32
    taps[1].wait()

    @pl.loop(0, S // n)
    def _(step):
        first = step * n
        total = silu(column_pairs(wide, first, n, taps[1]) + both(biases[1]))
        at = lax.broadcasted_iota(I32, (n, half, chans), 1)
        even = pltpu.roll(total[:, :chans], n * half - 1, 0).reshape(n, half, chans)
        odd = pltpu.roll(total[:, chans:], 1, 0).reshape(n, half, chans)
        rows = pl.ds(first + 1, n)
        inner[rows, :, 0:chans] = jnp.where(at == 0, 0.0, odd).astype(BF16)
        inner[rows, :, chans : 3 * chans] = total.astype(BF16).reshape(n, half, 2 * chans)
        inner[rows, :, 3 * chans :] = jnp.where(at == half - 1, 0.0, even).astype(BF16)

    taps[2].wait()

    @pl.loop(0, S // n)
    def _(step):
        first = step * n
        total = column_pairs(inner, first, n, taps[2]) + both(biases[2])
        for k in range(n):
            mixed[k, pl.ds(0, half, stride=2), :] = total[k * half : (k + 1) * half, :chans]
            mixed[k, pl.ds(1, half, stride=2), :] = total[k * half : (k + 1) * half, chans:]
        delta[pl.ds(first, n)] = mixed[...].astype(BF16)
        finish(step, pl.ds(first, n))


def begin(dims, arrived, weights, scratch):
    got, row_store, column_store, got_sems, tap_sems = scratch

    def arrival(s):
        return pltpu.make_async_copy(arrived[0], got.at[s], got_sems.at[s])

    for s in range(dims.tiles):
        pltpu.make_async_copy(arrived[s], got.at[s], got_sems.at[s]).start()
    taps = (
        RowTaps(weights[0], row_store, tap_sems.at[0]),
        ColumnTaps(weights[1], column_store.at[0], tap_sems.at[1]),
        ColumnTaps(weights[2], column_store.at[1], tap_sems.at[2]),
    )
    for tap in taps:
        tap.start()
    return arrival, taps


def main_kernel(dims, table, *refs):
    tiles, chans = dims.tiles, dims.chans
    arrived, refs = refs[:tiles], refs[tiles:]
    (dec_w, one_w, two_w, dec_b, one_b, two_b, sent, restored, got, row_store, column_store, got_sems, tap_sems) = refs[:13]
    raw, decoded, wide, inner, mixed, delta, sem, back, back_sems = refs[13:]
    me = lax.axis_index("tile")
    row0 = table[ROW, me]
    length = table[SIDE, me]
    place = table[PLACE, me]
    scratch = (got, row_store, column_store, got_sems, tap_sems)
    arrival, taps = begin(dims, arrived, (dec_w, one_w, two_w), scratch)
    restore(
        dims, row0, length, arrival, lambda s: me ^ s, got, taps, (dec_b, one_b, two_b),
        raw, decoded, wide, inner, mixed, delta, lambda step, rows: None,
    )

    @pl.when(place < CAP)
    def _():
        pltpu.make_async_copy(delta, restored.at[place], sem.at[0]).start()

    lengthf = length.astype(F32)
    t = lax.broadcasted_iota(I32, (SPAN, S), 0).astype(F32)
    s = lax.broadcasted_iota(I32, (SPAN, S), 1).astype(F32)
    spots = jnp.clip((t + 0.5) * S / lengthf - 0.5, 0.0, S - 1.0)
    lift = jnp.where(t < lengthf, jnp.maximum(0.0, 1.0 - jnp.abs(spots - s)), 0.0)
    coarse = lift.astype(BF16)
    lift = jnp.concatenate([coarse, (lift - coarse.astype(F32)).astype(BF16)], 0)
    scale = 1.0 / (2.0 * lengthf)
    group = 8

    @pl.loop(0, SPAN // 2 // group)
    def _(step):
        for k in range(group):
            lines = []
            for parity in range(2):
                h = 2 * (step * group + k) + parity
                spot = jnp.clip((2 * h + 1) * S - length, 0, (S - 1) * 2 * length)
                low = ((spot.astype(F32) + 0.5) * scale).astype(I32)
                part = (spot - low * 2 * length).astype(F32) * scale
                high = jnp.minimum(low + 1, S - 1)
                lines.append(((1.0 - part) * delta[low].astype(F32) + part * delta[high].astype(F32)).astype(BF16))
            patch = jnp.dot(lift, jnp.concatenate(lines, -1), preferred_element_type=F32)
            patch = (patch[:SPAN] + patch[SPAN:]).astype(BF16)
            for parity in range(2):
                row = row0 + 2 * (step * group + k) + parity
                dest = (row & (dims.stride - 1)) >> 1
                local = ((row >> dims.shift) << 1) + (row & 1)
                back[dest, local - first_local(row0, dest, dims)] = patch[:, parity * chans : (parity + 1) * chans]

    def leave(e):
        return pltpu.make_async_copy(back.at[e], sent.at[e], back_sems.at[e])

    for e in range(tiles):
        leave(e).start()
    for e in range(tiles):
        leave(e).wait()

    @pl.when(place < CAP)
    def _():
        pltpu.make_async_copy(delta, restored.at[place], sem.at[0]).wait()


def extra_kernel(
    dims, table, arrived, dec_w, one_w, two_w, dec_b, one_b, two_b, partial, restored,
    got, row_store, column_store, got_sems, tap_sems, raw, decoded, wide, inner, mixed, delta, sem,
):
    me = lax.axis_index("tile")
    row0 = table[ROW2, me]
    length = table[SIDE2, me]
    place = table[PLACE, me]

    def write(slot):
        copy = pltpu.make_async_copy(delta, restored.at[slot], sem.at[0])
        copy.start()
        copy.wait()

    @pl.when(length > 0)
    def _():
        scratch = (got, row_store, column_store, got_sems, tap_sems)
        arrival, taps = begin(dims, [arrived.at[s] for s in range(dims.tiles)], (dec_w, one_w, two_w), scratch)

        def leave(step, rows):
            return pltpu.make_async_copy(delta.at[rows], restored.at[1, rows], sem.at[step])

        restore(
            dims, row0, length, arrival, lambda s: s, got, taps, (dec_b, one_b, two_b),
            raw, decoded, wide, inner, mixed, delta, lambda step, rows: leave(step, rows).start(),
        )
        for step in range(2):
            leave(step, pl.ds(step * (S // 2), S // 2)).wait()

    @pl.when(length == 0)
    def _():
        delta[...] = jnp.zeros_like(delta)

        @pl.when(place != 0)
        def _():
            write(0)

        @pl.when(place != 1)
        def _():
            write(1)


def decode_kernel(dims, feat, above, below, weight, bias, decoded, held, up, down, store, lines, wide, mixed, sems, tap_sems):
    me = lax.axis_index("tile")
    bands, chans, cols = dims.bands, dims.chans, dims.cols
    half = cols // 2
    taps = ColumnTaps(weight, store, tap_sems)

    def fetch(band):
        return (
            pltpu.make_async_copy(feat.at[band], held.at[band], sems.at[0, band]),
            pltpu.make_async_copy(above.at[band], up.at[band], sems.at[1, band]),
            pltpu.make_async_copy(below.at[band], down.at[band], sems.at[2, band]),
        )

    taps.start()
    for band in range(bands):
        for copy in fetch(band)[1:]:
            copy.start()
    for band in range(bands):
        fetch(band)[0].start()
    top = (me == 0).astype(I32)
    bottom = (me == dims.tiles - 1).astype(I32)
    edge = jnp.zeros((8, chans), F32)
    for a in range(4):
        lines[a, 0:8] = edge
        lines[a, 8 + cols :] = edge
    taps.wait()
    for band in range(bands):
        for copy in fetch(band)[1:]:
            copy.wait()

    @pl.loop(0, bands)
    def _(j):
        fetch(j)[0].wait()
        no_top = (top == 1) & (j == 0)
        no_bottom = (bottom == 1) & (j == bands - 1)
        over = up[jnp.maximum(j - top, 0)].astype(F32)
        under = down[jnp.minimum(j + bottom, bands - 1)].astype(F32)
        middle = slice(8, 8 + cols)
        lines[0, middle] = jnp.where(no_top, 0.0, over)
        lines[1, middle] = held[j, 0].astype(F32)
        lines[2, middle] = held[j, 1].astype(F32)
        lines[3, middle] = jnp.where(no_bottom, 0.0, under)
        for a in range(4):
            for b in range(4):
                wide[a, :, b * chans : (b + 1) * chans] = lines[a, pl.ds(7 + b, half, stride=2), :].astype(BF16)
        total = silu(column_pairs(wide, 0, 2, taps) + both(bias))
        for i in range(2):
            part = total[i * half : (i + 1) * half]
            for b in range(2):
                here = lines[i + 1, pl.ds(8 + b, half, stride=2), :]
                mixed[i, pl.ds(b, half, stride=2), :] = here + part[:, b * chans : (b + 1) * chans]
            decoded[2 * j + i] = mixed[i].astype(BF16)


def paste_kernel(dims, table, decoded, back, finished, canvas, out, sems):
    me = lax.axis_index("tile")

    def leave(row):
        return pltpu.make_async_copy(out.at[row], finished.at[row], sems.at[row])

    @pl.loop(0, dims.local_rows)
    def _(row):
        canvas[...] = decoded[row].astype(F32)
        place = global_row(row, me, dims)

        @pl.loop(0, dims.tiles)
        def _(e):
            row0 = table[ROW, e]
            offset = place - row0

            @pl.when((offset >= 0) & (offset < table[SIDE, e]))
            def _():
                at = row - first_local(row0, me, dims)
                canvas[pl.ds(table[COL, e], SPAN), :] += back[e, at].astype(F32)

        out[row] = canvas[...].astype(BF16)
        leave(row).start()

    @pl.loop(0, dims.local_rows)
    def _(row):
        leave(row).wait()


def shards(features, dec_weight, dec_bias, first_weight, first_bias, second_weight, second_bias, boxes, slots):
    tiles = lax.axis_size("tile")
    dims = Dims(features, tiles)
    bands, cols, chans, local_rows = dims.bands, dims.cols, dims.chans, dims.local_rows
    assert dims.band_rows == 2 and slots.shape[0] == CAP * tiles and boxes.shape[1] == tiles
    assert tiles & (tiles - 1) == 0

    smem = pl.BlockSpec(memory_space=pltpu.SMEM)
    vmem = pl.BlockSpec(memory_space=pltpu.VMEM)
    hbm = pl.BlockSpec(memory_space=pl.ANY)
    full = pltpu.CompilerParams(vmem_limit_bytes=FULL_GRANT)
    small = pltpu.CompilerParams(vmem_limit_bytes=SMALL_GRANT)
    dma = pltpu.SemaphoreType.DMA

    def cost(flops, moved):
        return pl.CostEstimate(flops=int(flops), bytes_accessed=int(moved), transcendentals=0)

    def shaped(*shape, kind=BF16):
        return jax.ShapeDtypeStruct(shape, kind)

    def swap(array):
        return lax.all_to_all(array, "tile", split_axis=0, concat_axis=0, tiled=True)

    pack_scratch = [
        pltpu.VMEM((bands, 2, cols, chans), BF16),
        pltpu.VMEM((local_rows, cols + 16, chans), F32),
        pltpu.VMEM((dims.rim, chans), F32),
        pltpu.VMEM((tiles, dims.message, chans), BF16),
        dma((4,)),
        dma((bands,)),
        dma((tiles,)),
    ]
    message = shaped(tiles, dims.message, chans)
    *sent_main, table, last, leading = pl.pallas_call(
        functools.partial(pack_main_kernel, dims),
        out_shape=[shaped(dims.message, chans)] * tiles
        + [shaped(7, tiles, kind=I32), shaped(bands, cols, chans), shaped(bands, cols, chans)],
        in_specs=[hbm, hbm, hbm],
        out_specs=[hbm] * tiles + [smem, hbm, hbm],
        scratch_shapes=[
            pltpu.SMEM(boxes.shape, I32),
            pltpu.SMEM(slots.shape, I32),
            pltpu.SMEM((tiles,), I32),
            pltpu.SMEM((tiles,), I32),
            pltpu.SMEM((tiles + 1,), I32),
        ]
        + pack_scratch,
        compiler_params=full,
        cost_estimate=cost(0, 6e6),
        name="pack_main",
    )(boxes, slots, features)
    got_main = [sent_main[0]]
    for s in range(1, tiles):
        got_main.append(lax.ppermute(sent_main[s], "tile", [(i, i ^ s) for i in range(tiles)]))
    up = [(i, (i + 1) % tiles) for i in range(tiles)]
    above = lax.ppermute(last, "tile", up)
    below = lax.ppermute(leading, "tile", [(j, i) for i, j in up])

    sent_extra = pl.pallas_call(
        functools.partial(pack_extra_kernel, dims),
        out_shape=message,
        in_specs=[smem, hbm],
        out_specs=hbm,
        scratch_shapes=pack_scratch,
        compiler_params=full,
        cost_estimate=cost(0, 6e6),
        name="pack_extra",
    )(table, features)
    got_extra = swap(sent_extra)

    weights = tuple(w.reshape(3, 3, chans, chans) for w in (dec_weight, first_weight, second_weight))
    biases = (dec_bias[None], first_bias[None], second_bias[None])
    restore_scratch = [
        pltpu.VMEM((tiles, dims.message, chans), BF16),
        pltpu.VMEM((4, 3, chans, 2 * chans), BF16),
        pltpu.VMEM((2, 3, 4, chans, 2 * chans), BF16),
        dma((tiles,)),
        dma((3, 2)),
        pltpu.VMEM((SPAN // 2 + 2, 2, SPAN, 3 * chans), BF16),
        pltpu.VMEM((SPAN, SPAN, chans), F32),
        pltpu.VMEM((S + 2, S // 2, 4 * chans), BF16),
        pltpu.VMEM((S + 2, S // 2, 4 * chans), BF16),
        pltpu.VMEM((32, S, chans), F32),
        pltpu.VMEM((S, S, chans), BF16),
        dma((2,)),
    ]
    restored_shape = shaped(CAP, S, S, chans)
    sent_back, partial = pl.pallas_call(
        functools.partial(main_kernel, dims),
        out_shape=[shaped(tiles, dims.back_rows, SPAN, chans), restored_shape],
        in_specs=[smem] + [hbm] * (tiles + 3) + [vmem] * 3,
        out_specs=[hbm, hbm],
        scratch_shapes=restore_scratch
        + [pltpu.VMEM((tiles, dims.back_rows, SPAN, chans), BF16), dma((tiles,))],
        compiler_params=full,
        cost_estimate=cost(7e9, 8e6),
        name="restore_main",
    )(table, *got_main, *weights, *biases)
    got_back = swap(sent_back)

    restorations = pl.pallas_call(
        functools.partial(extra_kernel, dims),
        out_shape=restored_shape,
        in_specs=[smem] + [hbm] * 4 + [vmem] * 3 + [hbm],
        out_specs=hbm,
        scratch_shapes=restore_scratch,
        input_output_aliases={8: 0},
        compiler_params=full,
        cost_estimate=cost(6e9, 8e6),
        name="restore_extra",
    )(table, got_extra, *weights, *biases, partial)

    above, below, restorations = lax.optimization_barrier((above, below, restorations))
    decoded = pl.pallas_call(
        functools.partial(decode_kernel, dims),
        out_shape=shaped(local_rows, cols, chans),
        in_specs=[hbm] * 4 + [vmem],
        out_specs=vmem,
        scratch_shapes=[
            pltpu.VMEM((bands, 2, cols, chans), BF16),
            pltpu.VMEM((bands, cols, chans), BF16),
            pltpu.VMEM((bands, cols, chans), BF16),
            pltpu.VMEM((3, 4, chans, 2 * chans), BF16),
            pltpu.VMEM((4, cols + 16, chans), F32),
            pltpu.VMEM((4, cols // 2, 4 * chans), BF16),
            pltpu.VMEM((2, cols, chans), F32),
            dma((3, bands)),
            dma((2,)),
        ],
        compiler_params=small,
        cost_estimate=cost(3e9, 6e6),
        name="decode",
    )(features, above, below, weights[0], biases[0])

    finished = pl.pallas_call(
        functools.partial(paste_kernel, dims),
        out_shape=shaped(local_rows, cols, chans),
        in_specs=[smem, vmem, vmem],
        out_specs=hbm,
        scratch_shapes=[
            pltpu.VMEM((cols, chans), F32),
            pltpu.VMEM((local_rows, cols, chans), BF16),
            dma((local_rows,)),
        ],
        compiler_params=small,
        cost_estimate=cost(0, 6e6),
        name="paste",
    )(table, decoded, got_back)
    return finished.reshape(features.shape), restorations


def solution(mesh):
    return jax.shard_map(
        shards,
        mesh=mesh,
        in_specs=(
            P("sess", "tile", None, None),
            P(),
            P(),
            P(),
            P(),
            P(),
            P(),
            P(None, "sess"),
            P("sess"),
        ),
        out_specs=(P("sess", "tile", None, None), P(("sess", "tile"), None, None, None)),
        check_vma=False,
    )
```

```python
import functools

import jax
import jax.numpy as jnp
from jax import lax
from jax.experimental import pallas as pl
from jax.experimental.pallas import tpu as pltpu
from jax.sharding import PartitionSpec as P

S = 64
UNIT = 12
NCLS = 3
CAP = 2
SPAN = UNIT * (NCLS + 1)
BF16 = jnp.bfloat16
F32 = jnp.float32
I32 = jnp.int32
FULL_GRANT = 66500000
ROW, COL, SIDE, ROW2, COL2, SIDE2, PLACE = range(7)


def rows_within(window, band_rows, stride):
    return band_rows * (window // stride) + min(band_rows, window % stride)


class Dims:
    def __init__(self, features, tiles):
        self.bands, self.band_rows, self.cols, self.chans = features.shape
        self.tiles = tiles
        self.stride = tiles * self.band_rows
        self.shift = self.stride.bit_length() - 1
        self.local_rows = self.bands * self.band_rows
        self.rows = rows_within(SPAN + 2, self.band_rows, self.stride)
        self.back_rows = rows_within(SPAN, self.band_rows, self.stride)
        self.rim = -(-2 * self.rows // 16) * 16
        self.message = self.rows * SPAN + self.rim


def first_local(row, tile, dims):
    return ((row >> dims.shift) << 1) + jnp.clip((row & (dims.stride - 1)) - 2 * tile, 0, 2)


def global_row(local, tile, dims):
    return ((local >> 1) << dims.shift) + 2 * tile + (local & 1)


def silu(v):
    half = 0.5 * v
    return half + half * jnp.tanh(half)


def both(bias):
    return jnp.concatenate([bias, bias], -1)


class RowTaps:
    def __init__(self, source, bias, store, held, sems):
        chans = source.shape[-1]
        self.store = store
        self.held = held
        self.copies = (
            pltpu.make_async_copy(bias, held, sems.at[2]),
            pltpu.make_async_copy(source, store.at[0:3, :, :, 0:chans], sems.at[0]),
            pltpu.make_async_copy(source, store.at[1:4, :, :, chans : 2 * chans], sems.at[1]),
        )

    def start(self):
        for copy in self.copies:
            copy.start()
        chans = self.store.shape[2]
        none = jnp.zeros((3, chans, chans), BF16)
        self.store[3, :, :, 0:chans] = none
        self.store[0, :, :, chans : 2 * chans] = none

    def wait(self):
        for copy in self.copies:
            copy.wait()

    def bias(self):
        return both(self.held[...])

    def value(self):
        return self.store[...].reshape(-1, self.store.shape[-1])


class ColumnTaps(RowTaps):
    def __init__(self, source, bias, store, held, sems):
        chans = source.shape[-1]
        self.store = store
        self.held = held
        self.copies = (
            pltpu.make_async_copy(bias, held, sems.at[2]),
            pltpu.make_async_copy(source, store.at[:, 0:3, :, 0:chans], sems.at[0]),
            pltpu.make_async_copy(source, store.at[:, 1:4, :, chans : 2 * chans], sems.at[1]),
        )

    def start(self):
        for copy in self.copies:
            copy.start()
        chans = self.store.shape[2]
        none = jnp.zeros((3, chans, chans), BF16)
        self.store[:, 3, :, 0:chans] = none
        self.store[:, 0, :, chans : 2 * chans] = none


def two_chains(wide, taps):
    wide = wide.reshape(-1, wide.shape[-1])
    weight = taps.value()
    middle = weight.shape[0] // 2
    one = jnp.dot(wide[:, :middle], weight[:middle], preferred_element_type=F32)
    two = jnp.dot(wide[:, middle:], weight[middle:], preferred_element_type=F32)
    return one + two


def row_pairs(src, first, count, taps):
    parts = [
        src[pl.ds(first, count), 0],
        src[pl.ds(first, count), 1],
        src[pl.ds(first + 1, count), 0],
        src[pl.ds(first + 1, count), 1],
    ]
    return two_chains(jnp.concatenate(parts, -1), taps)


def column_pairs(src, first, count, taps):
    return two_chains(jnp.concatenate([src[pl.ds(first + a, count)] for a in range(3)], -1), taps)


def fill_canvas(dims, feat, held, canvas, sems):
    def copy(band):
        return pltpu.make_async_copy(feat.at[band], held.at[band], sems.at[band])

    for band in range(dims.bands):
        copy(band).start()

    def finish():
        edge = jnp.zeros((8, dims.chans), F32)
        for band in range(dims.bands):
            copy(band).wait()
            for i in range(2):
                row = 2 * band + i
                canvas[row, 0:8, :] = edge
                canvas[row, 8 + dims.cols : 16 + dims.cols, :] = edge
                canvas[row, 8 : 8 + dims.cols, :] = held[band, i].astype(F32)

    return finish


def pack_crops(dims, table, row_at, col_at, canvas, rim, staged, partner):
    me = lax.axis_index("tile")
    rim[...] = jnp.zeros_like(rim)

    @pl.loop(0, dims.tiles)
    def _(s):
        w = partner(s)
        row0 = table[row_at, w]
        col0 = table[col_at, w]
        start = first_local(jnp.maximum(row0 - 1, 0), me, dims)
        for i in range(dims.rows):
            row = jnp.minimum(start + i, dims.local_rows - 1)
            staged[s, i * SPAN : (i + 1) * SPAN, :] = canvas[row, pl.ds(col0 + 8, SPAN), :].astype(BF16)
            rim[2 * i : 2 * i + 1, :] = canvas[row, pl.ds(col0 + 7, 1), :]
            rim[2 * i + 1 : 2 * i + 2, :] = canvas[row, pl.ds(col0 + 8 + SPAN, 1), :]
        staged[s, dims.rows * SPAN :, :] = rim[...].astype(BF16)


def pack_kernel(
    dims, boxes_in, slots_in, feat, *refs
):
    sent, refs = refs[: dims.tiles], refs[dims.tiles :]
    sent_extra, table, last, leading, boxes, slots, main, extra, seconds, held, canvas, rim, staged, staged_extra, sems, feat_sems, sent_sems = refs
    me = lax.axis_index("tile")
    copies = (
        pltpu.make_async_copy(boxes_in, boxes, sems.at[0]),
        pltpu.make_async_copy(slots_in, slots, sems.at[1]),
    )
    for copy in copies:
        copy.start()
    finish = fill_canvas(dims, feat, held, canvas, feat_sems)
    for copy in copies:
        copy.wait()

    def first_pass(w, count):
        one = slots[CAP * w]
        two = slots[CAP * w + 1]
        full = (one >= 0) & (two >= 0)
        second = jnp.where(full, two, -1)
        main[w] = jnp.where(one >= 0, one, two)
        extra[w] = second
        seconds[count] = second
        return count + full.astype(I32)

    lax.fori_loop(0, dims.tiles, first_pass, jnp.int32(0))

    def second_pass(w, count):
        own = main[w]
        idle = own < 0
        crop = jnp.where(idle, seconds[count], own)
        table[ROW, w] = boxes[0, crop]
        table[COL, w] = boxes[1, crop]
        table[SIDE, w] = UNIT * (boxes[2, crop] + 2)
        other = jnp.maximum(extra[w], 0)
        table[ROW2, w] = boxes[0, other]
        table[COL2, w] = boxes[1, other]
        table[SIDE2, w] = jnp.where(extra[w] >= 0, UNIT * (boxes[2, other] + 2), 0)
        table[PLACE, w] = jnp.where(idle, 2, jnp.where(slots[CAP * w] >= 0, 0, 1))
        return count + idle.astype(I32)

    lax.fori_loop(0, dims.tiles, second_pass, jnp.int32(0))
    finish()
    edges = (
        pltpu.make_async_copy(held.at[:, 1], last, sems.at[2]),
        pltpu.make_async_copy(held.at[:, 0], leading, sems.at[3]),
    )
    for edge in edges:
        edge.start()
    pack_crops(dims, table, ROW, COL, canvas, rim, staged, lambda s: me ^ s)
    copies = [pltpu.make_async_copy(staged.at[s], sent[s], sent_sems.at[s]) for s in range(dims.tiles)]
    for copy in copies:
        copy.start()
    pack_crops(dims, table, ROW2, COL2, canvas, rim, staged_extra, lambda s: s)
    later = pltpu.make_async_copy(staged_extra, sent_extra, sems.at[0])
    later.start()
    for copy in copies:
        copy.wait()
    later.wait()
    for edge in edges:
        edge.wait()


def restore(dims, row0, length, arrival, source, got, taps, raw, decoded, wide, inner, mixed, delta, finish):
    chans = dims.chans
    above = row0 - 1
    pairs = SPAN // 2
    half = S // 2
    nothing = jnp.zeros((SPAN, 3 * chans), BF16)
    raw[0, 0] = nothing
    raw[pairs, 1] = nothing
    empty = jnp.zeros((half, 4 * chans), BF16)
    for store in (wide, inner):
        store[0] = empty
        store[S + 1] = empty

    @pl.loop(0, dims.tiles)
    def _(s):
        arrival(s).wait()
        e = source(s)
        start = first_local(jnp.maximum(above, 0), e, dims)
        rim = got[s, dims.rows * SPAN :, :].astype(F32)
        at = lax.broadcasted_iota(I32, (SPAN, chans), 0)
        for i in range(dims.rows):
            local = start + i
            place = global_row(local, e, dims) - above
            place = jnp.where((local < dims.local_rows) & (place < SPAN + 2), place, SPAN + 2)
            line = got[s, i * SPAN : (i + 1) * SPAN, :]
            wider = line.astype(F32)
            left = jnp.where(at == 0, rim[2 * i : 2 * i + 1], pltpu.roll(wider, 1, 0))
            right = jnp.where(at == SPAN - 1, rim[2 * i + 1 : 2 * i + 2], pltpu.roll(wider, SPAN - 1, 0))
            raw[place >> 1, place & 1] = jnp.concatenate([left.astype(BF16), line, right.astype(BF16)], -1)

    taps[0].wait()
    n = 12

    @pl.loop(0, pairs // n)
    def _(step):
        first = step * n
        total = silu(row_pairs(raw, first, n, taps[0]) + taps[0].bias())
        for k in range(n):
            part = total[k * SPAN : (k + 1) * SPAN]
            at = 2 * (first + k)
            upper = raw[first + k, 1, :, chans : 2 * chans].astype(F32) + part[:, :chans]
            lower = raw[first + k + 1, 0, :, chans : 2 * chans].astype(F32) + part[:, chans:]
            decoded[at] = upper.astype(BF16).astype(F32)
            decoded[at + 1] = lower.astype(BF16).astype(F32)

    lengthf = length.astype(F32)
    block = lax.broadcasted_iota(I32, (4, half, SPAN), 0)
    t = 2 * lax.broadcasted_iota(I32, (4, half, SPAN), 1) + block - 1
    j = lax.broadcasted_iota(I32, (4, half, SPAN), 2).astype(F32)
    spots = jnp.clip((t.astype(F32) + 0.5) * lengthf / S - 0.5, 0.0, lengthf - 1.0)
    across = jnp.where((t >= 0) & (t < S), jnp.maximum(0.0, 1.0 - jnp.abs(spots - j)), 0.0)
    across = across.reshape(4 * half, SPAN).astype(BF16)
    group = 16

    @pl.loop(0, S // 2 // group)
    def _(step):
        for k in range(group):
            lines = []
            for parity in range(2):
                s = 2 * (step * group + k) + parity
                spot = jnp.clip((2 * s + 1) * length - S, 0, (length - 1) * 2 * S)
                low = spot >> 7
                part = (spot & 127).astype(F32) * (1.0 / (2 * S))
                high = jnp.minimum(low + 1, SPAN - 1)
                lines.append(((1.0 - part) * decoded[low] + part * decoded[high]).astype(BF16))
            cells = jnp.dot(across, jnp.concatenate(lines, -1), preferred_element_type=F32).astype(BF16)
            for parity in range(2):
                at = 2 * (step * group + k) + parity + 1
                for b in range(4):
                    wide[at, :, b * chans : (b + 1) * chans] = cells[
                        b * half : (b + 1) * half, parity * chans : (parity + 1) * chans
                    ]

    n = 32
    taps[1].wait()

    @pl.loop(0, S // n)
    def _(step):
        first = step * n
        total = silu(column_pairs(wide, first, n, taps[1]) + taps[1].bias())
        at = lax.broadcasted_iota(I32, (n, half, chans), 1)
        even = pltpu.roll(total[:, :chans], n * half - 1, 0).reshape(n, half, chans)
        odd = pltpu.roll(total[:, chans:], 1, 0).reshape(n, half, chans)
        rows = pl.ds(first + 1, n)
        inner[rows, :, 0:chans] = jnp.where(at == 0, 0.0, odd).astype(BF16)
        inner[rows, :, chans : 3 * chans] = total.astype(BF16).reshape(n, half, 2 * chans)
        inner[rows, :, 3 * chans :] = jnp.where(at == half - 1, 0.0, even).astype(BF16)

    taps[2].wait()

    @pl.loop(0, S // n)
    def _(step):
        first = step * n
        total = column_pairs(inner, first, n, taps[2]) + taps[2].bias()
        for k in range(n):
            mixed[k, pl.ds(0, half, stride=2), :] = total[k * half : (k + 1) * half, :chans]
            mixed[k, pl.ds(1, half, stride=2), :] = total[k * half : (k + 1) * half, chans:]
        delta[pl.ds(first, n)] = mixed[...].astype(BF16)
        finish(step, pl.ds(first, n))


def begin(dims, arrived, weights, biases, scratch):
    got, row_store, column_store, held, got_sems, tap_sems = scratch

    def arrival(s):
        return pltpu.make_async_copy(arrived[0], got.at[s], got_sems.at[s])

    for s in range(dims.tiles):
        pltpu.make_async_copy(arrived[s], got.at[s], got_sems.at[s]).start()
    taps = (
        RowTaps(weights[0], biases[0], row_store, held.at[0], tap_sems.at[0]),
        ColumnTaps(weights[1], biases[1], column_store.at[0], held.at[1], tap_sems.at[1]),
        ColumnTaps(weights[2], biases[2], column_store.at[1], held.at[2], tap_sems.at[2]),
    )
    for tap in taps:
        tap.start()
    return arrival, taps


def main_kernel(dims, table, *refs):
    tiles, chans = dims.tiles, dims.chans
    arrived, refs = refs[:tiles], refs[tiles:]
    (dec_w, one_w, two_w, dec_b, one_b, two_b, sent, restored, got, row_store, column_store, held) = refs[:12]
    got_sems, tap_sems, raw, decoded, wide, inner, mixed, delta, sem, back, back_sems = refs[12:]
    me = lax.axis_index("tile")
    row0 = table[ROW, me]
    length = table[SIDE, me]
    place = table[PLACE, me]
    scratch = (got, row_store, column_store, held, got_sems, tap_sems)
    arrival, taps = begin(dims, arrived, (dec_w, one_w, two_w), (dec_b, one_b, two_b), scratch)
    restore(
        dims, row0, length, arrival, lambda s: me ^ s, got, taps,
        raw, decoded, wide, inner, mixed, delta, lambda step, rows: None,
    )

    @pl.when(place < CAP)
    def _():
        pltpu.make_async_copy(delta, restored.at[place], sem.at[0]).start()

    lengthf = length.astype(F32)
    t = lax.broadcasted_iota(I32, (SPAN, S), 0).astype(F32)
    s = lax.broadcasted_iota(I32, (SPAN, S), 1).astype(F32)
    spots = jnp.clip((t + 0.5) * S / lengthf - 0.5, 0.0, S - 1.0)
    lift = jnp.where(t < lengthf, jnp.maximum(0.0, 1.0 - jnp.abs(spots - s)), 0.0)
    coarse = lift.astype(BF16)
    lift = jnp.concatenate([coarse, (lift - coarse.astype(F32)).astype(BF16)], 0)
    scale = 1.0 / (2.0 * lengthf)
    group = 12

    @pl.loop(0, SPAN // 2 // group)
    def _(step):
        for k in range(group):
            lines = []
            for parity in range(2):
                h = 2 * (step * group + k) + parity
                spot = jnp.clip((2 * h + 1) * S - length, 0, (S - 1) * 2 * length)
                low = ((spot.astype(F32) + 0.5) * scale).astype(I32)
                part = (spot - low * 2 * length).astype(F32) * scale
                high = jnp.minimum(low + 1, S - 1)
                lines.append(((1.0 - part) * delta[low].astype(F32) + part * delta[high].astype(F32)).astype(BF16))
            patch = jnp.dot(lift, jnp.concatenate(lines, -1), preferred_element_type=F32)
            patch = (patch[:SPAN] + patch[SPAN:]).astype(BF16)
            for parity in range(2):
                row = row0 + 2 * (step * group + k) + parity
                dest = (row & (dims.stride - 1)) >> 1
                local = ((row >> dims.shift) << 1) + (row & 1)
                back[dest, local - first_local(row0, dest, dims)] = patch[:, parity * chans : (parity + 1) * chans]

    def leave(e):
        return pltpu.make_async_copy(back.at[e], sent.at[e], back_sems.at[e])

    for e in range(tiles):
        leave(e).start()
    for e in range(tiles):
        leave(e).wait()

    @pl.when(place < CAP)
    def _():
        pltpu.make_async_copy(delta, restored.at[place], sem.at[0]).wait()


def extra_kernel(
    dims, table, arrived, dec_w, one_w, two_w, dec_b, one_b, two_b, partial, restored,
    got, row_store, column_store, held, got_sems, tap_sems, raw, decoded, wide, inner, mixed, delta, sem,
):
    me = lax.axis_index("tile")
    row0 = table[ROW2, me]
    length = table[SIDE2, me]
    place = table[PLACE, me]

    def write(slot):
        copy = pltpu.make_async_copy(delta, restored.at[slot], sem.at[0])
        copy.start()
        copy.wait()

    @pl.when(length > 0)
    def _():
        scratch = (got, row_store, column_store, held, got_sems, tap_sems)
        arrival, taps = begin(dims, [arrived.at[s] for s in range(dims.tiles)], (dec_w, one_w, two_w), (dec_b, one_b, two_b), scratch)

        def leave(step, rows):
            return pltpu.make_async_copy(delta.at[rows], restored.at[1, rows], sem.at[step])

        restore(
            dims, row0, length, arrival, lambda s: s, got, taps,
            raw, decoded, wide, inner, mixed, delta, lambda step, rows: leave(step, rows).start(),
        )
        for step in range(2):
            leave(step, pl.ds(step * (S // 2), S // 2)).wait()

    @pl.when(length == 0)
    def _():
        delta[...] = jnp.zeros_like(delta)

        @pl.when(place != 0)
        def _():
            write(0)

        @pl.when(place != 1)
        def _():
            write(1)


def finish_kernel(
    dims, table, back, feat, above, below, weight, bias, finished,
    got, held, up, down, store, held_bias, lines, wide, canvas, out, sems, tap_sems,
):
    me = lax.axis_index("tile")
    bands, chans, cols = dims.bands, dims.chans, dims.cols
    half = cols // 2
    taps = ColumnTaps(weight, bias, store, held_bias, tap_sems)
    patches = pltpu.make_async_copy(back, got, sems.at[0])
    patches.start()
    loads = (
        pltpu.make_async_copy(above, up, sems.at[1]),
        pltpu.make_async_copy(below, down, sems.at[2]),
        pltpu.make_async_copy(feat, held, sems.at[3]),
    )
    for load in loads:
        load.start()
    taps.start()

    def leave(band):
        return pltpu.make_async_copy(out.at[band], finished.at[band], sems.at[4 + band])

    top = (me == 0).astype(I32)
    bottom = (me == dims.tiles - 1).astype(I32)
    edge = jnp.zeros((8, chans), F32)
    for k in range(lines.shape[0]):
        for a in range(4):
            lines[k, a, 0:8] = edge
            lines[k, a, 8 + cols :] = edge
    canvas[...] = jnp.zeros_like(canvas)
    patches.wait()

    @pl.loop(0, dims.tiles)
    def _(e):
        row0 = table[ROW, e]
        col0 = table[COL, e]
        length = table[SIDE, e]
        start = first_local(row0, me, dims)
        for i in range(dims.back_rows):
            local = start + i

            @pl.when((local < dims.local_rows) & (global_row(local, me, dims) - row0 < length))
            def _():
                canvas[local, pl.ds(col0, SPAN), :] += got[e, i].astype(F32)

    for load in loads:
        load.wait()
    taps.wait()

    def band(j, lines, wide):
        no_top = (top == 1) & (j == 0)
        no_bottom = (bottom == 1) & (j == bands - 1)
        over = up[jnp.maximum(j - top, 0)].astype(F32)
        under = down[jnp.minimum(j + bottom, bands - 1)].astype(F32)
        middle = slice(8, 8 + cols)
        lines[0, middle] = jnp.where(no_top, 0.0, over)
        lines[1, middle] = held[j, 0].astype(F32)
        lines[2, middle] = held[j, 1].astype(F32)
        lines[3, middle] = jnp.where(no_bottom, 0.0, under)
        for a in range(4):
            for b in range(4):
                wide[a, :, b * chans : (b + 1) * chans] = lines[a, pl.ds(7 + b, half, stride=2), :].astype(BF16)
        total = silu(column_pairs(wide, 0, 2, taps) + taps.bias())
        for i in range(2):
            part = total[i * half : (i + 1) * half]
            for b in range(2):
                here = lines[i + 1, pl.ds(8 + b, half, stride=2), :]
                decoded = (here + part[:, b * chans : (b + 1) * chans]).astype(BF16).astype(F32)
                at = pl.ds(b, half, stride=2)
                canvas[2 * j + i, at, :] = canvas[2 * j + i, at, :] + decoded
            out[j, i] = canvas[2 * j + i].astype(BF16)
        leave(j).start()

    @pl.loop(0, bands // 2)
    def _(step):
        for k in range(2):
            band(2 * step + k, lines.at[k], wide.at[k])

    for j in range(bands):
        leave(j).wait()


def shards(features, dec_weight, dec_bias, first_weight, first_bias, second_weight, second_bias, boxes, slots):
    tiles = lax.axis_size("tile")
    dims = Dims(features, tiles)
    bands, cols, chans, local_rows = dims.bands, dims.cols, dims.chans, dims.local_rows
    assert dims.band_rows == 2 and slots.shape[0] == CAP * tiles and boxes.shape[1] == tiles
    assert tiles & (tiles - 1) == 0

    smem = pl.BlockSpec(memory_space=pltpu.SMEM)
    hbm = pl.BlockSpec(memory_space=pl.ANY)
    full = pltpu.CompilerParams(vmem_limit_bytes=FULL_GRANT)
    dma = pltpu.SemaphoreType.DMA

    def cost(flops, moved):
        return pl.CostEstimate(flops=int(flops), bytes_accessed=int(moved), transcendentals=0)

    def shaped(*shape, kind=BF16):
        return jax.ShapeDtypeStruct(shape, kind)

    def swap(array):
        return lax.all_to_all(array, "tile", split_axis=0, concat_axis=0, tiled=True)

    pack_scratch = [
        pltpu.VMEM((bands, 2, cols, chans), BF16),
        pltpu.VMEM((local_rows, cols + 16, chans), F32),
        pltpu.VMEM((dims.rim, chans), F32),
        pltpu.VMEM((tiles, dims.message, chans), BF16),
        pltpu.VMEM((tiles, dims.message, chans), BF16),
        dma((4,)),
        dma((bands,)),
        dma((tiles,)),
    ]
    message = shaped(tiles, dims.message, chans)
    *sent_main, sent_extra, table, last, leading = pl.pallas_call(
        functools.partial(pack_kernel, dims),
        out_shape=[shaped(dims.message, chans)] * tiles
        + [message, shaped(7, tiles, kind=I32), shaped(bands, cols, chans), shaped(bands, cols, chans)],
        in_specs=[hbm, hbm, hbm],
        out_specs=[hbm] * (tiles + 1) + [smem, hbm, hbm],
        scratch_shapes=[
            pltpu.SMEM(boxes.shape, I32),
            pltpu.SMEM(slots.shape, I32),
            pltpu.SMEM((tiles,), I32),
            pltpu.SMEM((tiles,), I32),
            pltpu.SMEM((tiles + 1,), I32),
        ]
        + pack_scratch,
        compiler_params=full,
        cost_estimate=cost(0, 6e6),
        name="pack",
    )(boxes, slots, features)
    got_main = [sent_main[0]]
    for s in range(1, tiles):
        got_main.append(lax.ppermute(sent_main[s], "tile", [(i, i ^ s) for i in range(tiles)]))
    up = [(i, (i + 1) % tiles) for i in range(tiles)]
    above = lax.ppermute(last, "tile", up)
    below = lax.ppermute(leading, "tile", [(j, i) for i, j in up])

    got_extra = swap(sent_extra)

    weights = tuple(w.reshape(3, 3, chans, chans) for w in (dec_weight, first_weight, second_weight))
    biases = (dec_bias[None], first_bias[None], second_bias[None])
    restore_scratch = [
        pltpu.VMEM((tiles, dims.message, chans), BF16),
        pltpu.VMEM((4, 3, chans, 2 * chans), BF16),
        pltpu.VMEM((2, 3, 4, chans, 2 * chans), BF16),
        pltpu.VMEM((3, 1, chans), F32),
        dma((tiles,)),
        dma((3, 3)),
        pltpu.VMEM((SPAN // 2 + 2, 2, SPAN, 3 * chans), BF16),
        pltpu.VMEM((SPAN, SPAN, chans), F32),
        pltpu.VMEM((S + 2, S // 2, 4 * chans), BF16),
        pltpu.VMEM((S + 2, S // 2, 4 * chans), BF16),
        pltpu.VMEM((32, S, chans), F32),
        pltpu.VMEM((S, S, chans), BF16),
        dma((2,)),
    ]
    restored_shape = shaped(CAP, S, S, chans)
    sent_back, partial = pl.pallas_call(
        functools.partial(main_kernel, dims),
        out_shape=[shaped(tiles, dims.back_rows, SPAN, chans), restored_shape],
        in_specs=[smem] + [hbm] * (tiles + 6),
        out_specs=[hbm, hbm],
        scratch_shapes=restore_scratch
        + [pltpu.VMEM((tiles, dims.back_rows, SPAN, chans), BF16), dma((tiles,))],
        compiler_params=full,
        cost_estimate=cost(7e9, 8e6),
        name="restore_main",
    )(table, *got_main, *weights, *biases)
    got_back = swap(sent_back)

    restorations = pl.pallas_call(
        functools.partial(extra_kernel, dims),
        out_shape=restored_shape,
        in_specs=[smem] + [hbm] * 8,
        out_specs=hbm,
        scratch_shapes=restore_scratch,
        input_output_aliases={8: 0},
        compiler_params=full,
        cost_estimate=cost(6e9, 8e6),
        name="restore_extra",
    )(table, got_extra, *weights, *biases, partial)

    above, below, restorations = lax.optimization_barrier((above, below, restorations))
    assert bands % 2 == 0
    finished = pl.pallas_call(
        functools.partial(finish_kernel, dims),
        out_shape=shaped(*features.shape),
        in_specs=[smem] + [hbm] * 6,
        out_specs=hbm,
        scratch_shapes=[
            pltpu.VMEM((tiles, dims.back_rows, SPAN, chans), BF16),
            pltpu.VMEM((bands, 2, cols, chans), BF16),
            pltpu.VMEM((bands, cols, chans), BF16),
            pltpu.VMEM((bands, cols, chans), BF16),
            pltpu.VMEM((3, 4, chans, 2 * chans), BF16),
            pltpu.VMEM((1, chans), F32),
            pltpu.VMEM((2, 4, cols + 16, chans), F32),
            pltpu.VMEM((2, 4, cols // 2, 4 * chans), BF16),
            pltpu.VMEM((local_rows, cols, chans), F32),
            pltpu.VMEM((bands, 2, cols, chans), BF16),
            dma((4 + bands,)),
            dma((3,)),
        ],
        compiler_params=full,
        cost_estimate=cost(3e9, 6e6),
        name="finish",
    )(table, got_back, features, above, below, weights[0], biases[0])
    return finished, restorations


def solution(mesh):
    return jax.shard_map(
        shards,
        mesh=mesh,
        in_specs=(
            P("sess", "tile", None, None),
            P(),
            P(),
            P(),
            P(),
            P(),
            P(),
            P(None, "sess"),
            P("sess"),
        ),
        out_specs=(P("sess", "tile", None, None), P(("sess", "tile"), None, None, None)),
        check_vma=False,
    )
```

```python
import functools

import jax
import jax.numpy as jnp
from jax import lax
from jax.experimental import pallas as pl
from jax.experimental.pallas import tpu as pltpu
from jax.sharding import PartitionSpec as P

S = 64
UNIT = 12
NCLS = 3
CAP = 2
PIECE = 16
SPAN = UNIT * (NCLS + 1)
BF16 = jnp.bfloat16
F32 = jnp.float32
I32 = jnp.int32
FULL_GRANT = 66500000
ROW, COL, SIDE, ROW2, COL2, SIDE2, PLACE = range(7)


def rows_within(window, band_rows, stride):
    return band_rows * (window // stride) + min(band_rows, window % stride)


class Dims:
    def __init__(self, features, tiles):
        self.bands, self.band_rows, self.cols, self.chans = features.shape
        self.tiles = tiles
        self.stride = tiles * self.band_rows
        self.shift = self.stride.bit_length() - 1
        self.local_rows = self.bands * self.band_rows
        self.rows = rows_within(SPAN + 2, self.band_rows, self.stride)
        self.back_rows = rows_within(SPAN, self.band_rows, self.stride)
        self.rim = -(-2 * self.rows // 16) * 16
        self.message = self.rows * SPAN + self.rim


def first_local(row, tile, dims):
    return ((row >> dims.shift) << 1) + jnp.clip((row & (dims.stride - 1)) - 2 * tile, 0, 2)


def global_row(local, tile, dims):
    return ((local >> 1) << dims.shift) + 2 * tile + (local & 1)


def silu(v):
    half = 0.5 * v
    return half + half * jnp.tanh(half)


def both(bias):
    return jnp.concatenate([bias, bias], -1)


class RowTaps:
    def __init__(self, source, bias, store, held, sems):
        chans = source.shape[-1]
        self.store = store
        self.held = held
        self.copies = (
            pltpu.make_async_copy(bias, held, sems.at[2]),
            pltpu.make_async_copy(source, store.at[0:3, :, :, 0:chans], sems.at[0]),
            pltpu.make_async_copy(source, store.at[1:4, :, :, chans : 2 * chans], sems.at[1]),
        )

    def start(self):
        for copy in self.copies:
            copy.start()
        chans = self.store.shape[2]
        none = jnp.zeros((3, chans, chans), BF16)
        self.store[3, :, :, 0:chans] = none
        self.store[0, :, :, chans : 2 * chans] = none

    def wait(self):
        for copy in self.copies:
            copy.wait()

    def bias(self):
        return both(self.held[...])

    def value(self):
        return self.store[...].reshape(-1, self.store.shape[-1])


class ColumnTaps(RowTaps):
    def __init__(self, source, bias, store, held, sems):
        chans = source.shape[-1]
        self.store = store
        self.held = held
        self.copies = (
            pltpu.make_async_copy(bias, held, sems.at[2]),
            pltpu.make_async_copy(source, store.at[:, 0:3, :, 0:chans], sems.at[0]),
            pltpu.make_async_copy(source, store.at[:, 1:4, :, chans : 2 * chans], sems.at[1]),
        )

    def start(self):
        for copy in self.copies:
            copy.start()
        chans = self.store.shape[2]
        none = jnp.zeros((3, chans, chans), BF16)
        self.store[:, 3, :, 0:chans] = none
        self.store[:, 0, :, chans : 2 * chans] = none


def two_chains(wide, taps):
    wide = wide.reshape(-1, wide.shape[-1])
    weight = taps.value()
    middle = weight.shape[0] // 2
    one = jnp.dot(wide[:, :middle], weight[:middle], preferred_element_type=F32)
    two = jnp.dot(wide[:, middle:], weight[middle:], preferred_element_type=F32)
    return one + two


def row_pairs(src, first, count, taps):
    parts = [
        src[pl.ds(first, count), 0],
        src[pl.ds(first, count), 1],
        src[pl.ds(first + 1, count), 0],
        src[pl.ds(first + 1, count), 1],
    ]
    return two_chains(jnp.concatenate(parts, -1), taps)


def column_pairs(src, first, count, taps):
    return two_chains(jnp.concatenate([src[pl.ds(first + a, count)] for a in range(3)], -1), taps)


def fill_canvas(dims, feat, held, canvas, sems):
    def copy(band):
        return pltpu.make_async_copy(feat.at[band], held.at[band], sems.at[band])

    for band in range(dims.bands):
        copy(band).start()

    def finish():
        edge = jnp.zeros((8, dims.chans), F32)
        for band in range(dims.bands):
            copy(band).wait()
            for i in range(2):
                row = 2 * band + i
                canvas[row, 0:8, :] = edge
                canvas[row, 8 + dims.cols : 16 + dims.cols, :] = edge
                canvas[row, 8 : 8 + dims.cols, :] = held[band, i].astype(F32)

    return finish


def pack_crops(dims, table, row_at, col_at, canvas, rim, staged, partner):
    me = lax.axis_index("tile")
    rim[...] = jnp.zeros_like(rim)

    @pl.loop(0, dims.tiles)
    def _(s):
        w = partner(s)
        row0 = table[row_at, w]
        col0 = table[col_at, w]
        start = first_local(jnp.maximum(row0 - 1, 0), me, dims)
        for i in range(dims.rows):
            row = jnp.minimum(start + i, dims.local_rows - 1)
            staged[s, i * SPAN : (i + 1) * SPAN, :] = canvas[row, pl.ds(col0 + 8, SPAN), :].astype(BF16)
            rim[2 * i : 2 * i + 1, :] = canvas[row, pl.ds(col0 + 7, 1), :]
            rim[2 * i + 1 : 2 * i + 2, :] = canvas[row, pl.ds(col0 + 8 + SPAN, 1), :]
        staged[s, dims.rows * SPAN :, :] = rim[...].astype(BF16)


def pack_kernel(
    dims, boxes_in, slots_in, feat, *refs
):
    sent, refs = refs[: dims.tiles], refs[dims.tiles :]
    sent_extra, table, last, leading, boxes, slots, main, extra, seconds, held, canvas, rim, staged, staged_extra, sems, feat_sems, sent_sems = refs
    me = lax.axis_index("tile")
    copies = (
        pltpu.make_async_copy(boxes_in, boxes, sems.at[0]),
        pltpu.make_async_copy(slots_in, slots, sems.at[1]),
    )
    for copy in copies:
        copy.start()
    finish = fill_canvas(dims, feat, held, canvas, feat_sems)
    for copy in copies:
        copy.wait()

    def first_pass(w, count):
        one = slots[CAP * w]
        two = slots[CAP * w + 1]
        full = (one >= 0) & (two >= 0)
        second = jnp.where(full, two, -1)
        main[w] = jnp.where(one >= 0, one, two)
        extra[w] = second
        seconds[count] = second
        return count + full.astype(I32)

    lax.fori_loop(0, dims.tiles, first_pass, jnp.int32(0))

    def second_pass(w, count):
        own = main[w]
        idle = own < 0
        crop = jnp.where(idle, seconds[count], own)
        table[ROW, w] = boxes[0, crop]
        table[COL, w] = boxes[1, crop]
        table[SIDE, w] = UNIT * (boxes[2, crop] + 2)
        other = jnp.maximum(extra[w], 0)
        table[ROW2, w] = boxes[0, other]
        table[COL2, w] = boxes[1, other]
        table[SIDE2, w] = jnp.where(extra[w] >= 0, UNIT * (boxes[2, other] + 2), 0)
        table[PLACE, w] = jnp.where(idle, 2, jnp.where(slots[CAP * w] >= 0, 0, 1))
        return count + idle.astype(I32)

    lax.fori_loop(0, dims.tiles, second_pass, jnp.int32(0))
    finish()
    edges = (
        pltpu.make_async_copy(held.at[:, 1], last, sems.at[2]),
        pltpu.make_async_copy(held.at[:, 0], leading, sems.at[3]),
    )
    for edge in edges:
        edge.start()
    pack_crops(dims, table, ROW, COL, canvas, rim, staged, lambda s: me ^ s)
    copies = [pltpu.make_async_copy(staged.at[s], sent[s], sent_sems.at[s]) for s in range(dims.tiles)]
    for copy in copies:
        copy.start()
    pack_crops(dims, table, ROW2, COL2, canvas, rim, staged_extra, lambda s: s)
    later = pltpu.make_async_copy(staged_extra, sent_extra, sems.at[0])
    later.start()
    for copy in copies:
        copy.wait()
    later.wait()
    for edge in edges:
        edge.wait()


def restore(dims, row0, length, arrival, source, got, taps, raw, decoded, wide, inner, mixed, delta, finish):
    chans = dims.chans
    above = row0 - 1
    pairs = SPAN // 2
    half = S // 2
    nothing = jnp.zeros((SPAN, 3 * chans), BF16)
    raw[0, 0] = nothing
    raw[pairs, 1] = nothing
    empty = jnp.zeros((half, 4 * chans), BF16)
    for store in (wide, inner):
        store[0] = empty
        store[S + 1] = empty

    @pl.loop(0, dims.tiles)
    def _(s):
        arrival(s).wait()
        e = source(s)
        start = first_local(jnp.maximum(above, 0), e, dims)
        rim = got[s, dims.rows * SPAN :, :].astype(F32)
        at = lax.broadcasted_iota(I32, (SPAN, chans), 0)
        for i in range(dims.rows):
            local = start + i
            place = global_row(local, e, dims) - above
            place = jnp.where((local < dims.local_rows) & (place < SPAN + 2), place, SPAN + 2)
            line = got[s, i * SPAN : (i + 1) * SPAN, :]
            wider = line.astype(F32)
            left = jnp.where(at == 0, rim[2 * i : 2 * i + 1], pltpu.roll(wider, 1, 0))
            right = jnp.where(at == SPAN - 1, rim[2 * i + 1 : 2 * i + 2], pltpu.roll(wider, SPAN - 1, 0))
            raw[place >> 1, place & 1] = jnp.concatenate([left.astype(BF16), line, right.astype(BF16)], -1)

    taps[1].start()
    taps[2].start()
    taps[0].wait()
    n = 12

    @pl.loop(0, pairs // n)
    def _(step):
        first = step * n
        total = silu(row_pairs(raw, first, n, taps[0]) + taps[0].bias())
        for k in range(n):
            part = total[k * SPAN : (k + 1) * SPAN]
            at = 2 * (first + k)
            upper = raw[first + k, 1, :, chans : 2 * chans].astype(F32) + part[:, :chans]
            lower = raw[first + k + 1, 0, :, chans : 2 * chans].astype(F32) + part[:, chans:]
            decoded[at] = upper.astype(BF16).astype(F32)
            decoded[at + 1] = lower.astype(BF16).astype(F32)

    lengthf = length.astype(F32)
    block = lax.broadcasted_iota(I32, (4, half, SPAN), 0)
    t = 2 * lax.broadcasted_iota(I32, (4, half, SPAN), 1) + block - 1
    j = lax.broadcasted_iota(I32, (4, half, SPAN), 2).astype(F32)
    spots = jnp.clip((t.astype(F32) + 0.5) * lengthf / S - 0.5, 0.0, lengthf - 1.0)
    across = jnp.where((t >= 0) & (t < S), jnp.maximum(0.0, 1.0 - jnp.abs(spots - j)), 0.0)
    across = across.reshape(4 * half, SPAN).astype(BF16)
    group = 16

    @pl.loop(0, S // 2 // group)
    def _(step):
        for k in range(group):
            lines = []
            for parity in range(2):
                s = 2 * (step * group + k) + parity
                spot = jnp.clip((2 * s + 1) * length - S, 0, (length - 1) * 2 * S)
                low = spot >> 7
                part = (spot & 127).astype(F32) * (1.0 / (2 * S))
                high = jnp.minimum(low + 1, SPAN - 1)
                lines.append(((1.0 - part) * decoded[low] + part * decoded[high]).astype(BF16))
            cells = jnp.dot(across, jnp.concatenate(lines, -1), preferred_element_type=F32).astype(BF16)
            for parity in range(2):
                at = 2 * (step * group + k) + parity + 1
                for b in range(4):
                    wide[at, :, b * chans : (b + 1) * chans] = cells[
                        b * half : (b + 1) * half, parity * chans : (parity + 1) * chans
                    ]

    n = 32
    taps[1].wait()

    @pl.loop(0, S // n)
    def _(step):
        first = step * n
        total = silu(column_pairs(wide, first, n, taps[1]) + taps[1].bias())
        at = lax.broadcasted_iota(I32, (n, half, chans), 1)
        even = pltpu.roll(total[:, :chans], n * half - 1, 0).reshape(n, half, chans)
        odd = pltpu.roll(total[:, chans:], 1, 0).reshape(n, half, chans)
        rows = pl.ds(first + 1, n)
        inner[rows, :, 0:chans] = jnp.where(at == 0, 0.0, odd).astype(BF16)
        inner[rows, :, chans : 3 * chans] = total.astype(BF16).reshape(n, half, 2 * chans)
        inner[rows, :, 3 * chans :] = jnp.where(at == half - 1, 0.0, even).astype(BF16)

    taps[2].wait()

    @pl.loop(0, S // n)
    def _(step):
        first = step * n
        total = column_pairs(inner, first, n, taps[2]) + taps[2].bias()
        for k in range(n):
            mixed[k, pl.ds(0, half, stride=2), :] = total[k * half : (k + 1) * half, :chans]
            mixed[k, pl.ds(1, half, stride=2), :] = total[k * half : (k + 1) * half, chans:]
            if k % PIECE == PIECE - 1:
                at = pl.ds(first + k + 1 - PIECE, PIECE)
                delta[at] = mixed[k + 1 - PIECE : k + 1].astype(BF16)
                finish(step * (n // PIECE) + k // PIECE)


def begin(dims, arrived, weights, biases, scratch):
    got, row_store, column_store, held, got_sems, tap_sems = scratch

    def arrival(s):
        return pltpu.make_async_copy(arrived[0], got.at[s], got_sems.at[s])

    for s in range(dims.tiles):
        pltpu.make_async_copy(arrived[s], got.at[s], got_sems.at[s]).start()
    taps = (
        RowTaps(weights[0], biases[0], row_store, held.at[0], tap_sems.at[0]),
        ColumnTaps(weights[1], biases[1], column_store.at[0], held.at[1], tap_sems.at[1]),
        ColumnTaps(weights[2], biases[2], column_store.at[1], held.at[2], tap_sems.at[2]),
    )
    taps[0].start()
    return arrival, taps


def main_kernel(dims, table, *refs):
    tiles, chans = dims.tiles, dims.chans
    arrived, refs = refs[:tiles], refs[tiles:]
    (dec_w, one_w, two_w, dec_b, one_b, two_b, sent, restored, got, row_store, column_store, held) = refs[:12]
    got_sems, tap_sems, raw, decoded, wide, inner, mixed, delta, sem, back, back_sems = refs[12:]
    me = lax.axis_index("tile")
    row0 = table[ROW, me]
    length = table[SIDE, me]
    place = table[PLACE, me]
    scratch = (got, row_store, column_store, held, got_sems, tap_sems)
    arrival, taps = begin(dims, arrived, (dec_w, one_w, two_w), (dec_b, one_b, two_b), scratch)
    restore(
        dims, row0, length, arrival, lambda s: me ^ s, got, taps,
        raw, decoded, wide, inner, mixed, delta, lambda piece: None,
    )

    @pl.when(place < CAP)
    def _():
        pltpu.make_async_copy(delta, restored.at[place], sem.at[0]).start()

    lengthf = length.astype(F32)
    t = lax.broadcasted_iota(I32, (SPAN, S), 0).astype(F32)
    s = lax.broadcasted_iota(I32, (SPAN, S), 1).astype(F32)
    spots = jnp.clip((t + 0.5) * S / lengthf - 0.5, 0.0, S - 1.0)
    lift = jnp.where(t < lengthf, jnp.maximum(0.0, 1.0 - jnp.abs(spots - s)), 0.0)
    coarse = lift.astype(BF16)
    lift = jnp.concatenate([coarse, (lift - coarse.astype(F32)).astype(BF16)], 0)
    scale = 1.0 / (2.0 * lengthf)
    group = 12

    @pl.loop(0, SPAN // 2 // group)
    def _(step):
        for k in range(group):
            lines = []
            for parity in range(2):
                h = 2 * (step * group + k) + parity
                spot = jnp.clip((2 * h + 1) * S - length, 0, (S - 1) * 2 * length)
                low = ((spot.astype(F32) + 0.5) * scale).astype(I32)
                part = (spot - low * 2 * length).astype(F32) * scale
                high = jnp.minimum(low + 1, S - 1)
                lines.append(((1.0 - part) * delta[low].astype(F32) + part * delta[high].astype(F32)).astype(BF16))
            patch = jnp.dot(lift, jnp.concatenate(lines, -1), preferred_element_type=F32)
            patch = (patch[:SPAN] + patch[SPAN:]).astype(BF16)
            for parity in range(2):
                row = row0 + 2 * (step * group + k) + parity
                dest = (row & (dims.stride - 1)) >> 1
                local = ((row >> dims.shift) << 1) + (row & 1)
                back[dest, local - first_local(row0, dest, dims)] = patch[:, parity * chans : (parity + 1) * chans]

    def leave(e):
        return pltpu.make_async_copy(back.at[e], sent.at[e], back_sems.at[e])

    for e in range(tiles):
        leave(e).start()
    for e in range(tiles):
        leave(e).wait()

    @pl.when(place < CAP)
    def _():
        pltpu.make_async_copy(delta, restored.at[place], sem.at[0]).wait()


def extra_kernel(
    dims, table, arrived, dec_w, one_w, two_w, dec_b, one_b, two_b, partial, restored,
    got, row_store, column_store, held, got_sems, tap_sems, raw, decoded, wide, inner, mixed, delta, sem,
):
    me = lax.axis_index("tile")
    row0 = table[ROW2, me]
    length = table[SIDE2, me]
    place = table[PLACE, me]

    def write(slot):
        copy = pltpu.make_async_copy(delta, restored.at[slot], sem.at[0])
        copy.start()
        copy.wait()

    @pl.when(length > 0)
    def _():
        scratch = (got, row_store, column_store, held, got_sems, tap_sems)
        arrival, taps = begin(dims, [arrived.at[s] for s in range(dims.tiles)], (dec_w, one_w, two_w), (dec_b, one_b, two_b), scratch)

        def leave(piece):
            rows = pl.ds(piece * PIECE, PIECE)
            return pltpu.make_async_copy(delta.at[rows], restored.at[1, rows], sem.at[piece])

        restore(
            dims, row0, length, arrival, lambda s: s, got, taps,
            raw, decoded, wide, inner, mixed, delta, lambda piece: leave(piece).start(),
        )
        for piece in range(S // PIECE):
            leave(piece).wait()

    @pl.when(length == 0)
    def _():
        delta[...] = jnp.zeros_like(delta)

        @pl.when(place != 0)
        def _():
            write(0)

        @pl.when(place != 1)
        def _():
            write(1)


def finish_kernel(
    dims, table, back, feat, above, below, weight, bias, finished,
    got, held, up, down, store, held_bias, lines, wide, canvas, out, sems, load_sems, tap_sems,
):
    me = lax.axis_index("tile")
    bands, chans, cols = dims.bands, dims.chans, dims.cols
    half = cols // 2
    taps = ColumnTaps(weight, bias, store, held_bias, tap_sems)
    patches = pltpu.make_async_copy(back, got, sems.at[0])
    patches.start()
    def from_feat(band):
        return pltpu.make_async_copy(feat.at[band], held.at[band], load_sems.at[0, band])

    def from_above(band):
        return pltpu.make_async_copy(above.at[band], up.at[band], load_sems.at[1, band])

    def from_below(band):
        return pltpu.make_async_copy(below.at[band], down.at[band], load_sems.at[2, band])

    taps.start()
    from_below(0).start()
    for j in range(bands):
        from_feat(j).start()
        from_above(j).start()
        if j + 1 < bands:
            from_below(j + 1).start()

    def leave(band):
        return pltpu.make_async_copy(out.at[band], finished.at[band], sems.at[1 + band])

    top = (me == 0).astype(I32)
    bottom = (me == dims.tiles - 1).astype(I32)
    edge = jnp.zeros((8, chans), F32)
    for k in range(lines.shape[0]):
        for a in range(4):
            lines[k, a, 0:8] = edge
            lines[k, a, 8 + cols :] = edge
    canvas[...] = jnp.zeros_like(canvas)
    patches.wait()

    @pl.loop(0, dims.tiles)
    def _(e):
        row0 = table[ROW, e]
        col0 = table[COL, e]
        length = table[SIDE, e]
        start = first_local(row0, me, dims)
        for i in range(dims.back_rows):
            local = start + i

            @pl.when((local < dims.local_rows) & (global_row(local, me, dims) - row0 < length))
            def _():
                canvas[local, pl.ds(col0, SPAN), :] += got[e, i].astype(F32)

    from_below(0).wait()
    taps.wait()

    def band(j, lines, wide):
        from_feat(j).wait()
        from_above(j).wait()

        @pl.when(j + 1 < bands)
        def _():
            from_below(j + 1).wait()

        no_top = (top == 1) & (j == 0)
        no_bottom = (bottom == 1) & (j == bands - 1)
        over = up[jnp.maximum(j - top, 0)].astype(F32)
        under = down[jnp.minimum(j + bottom, bands - 1)].astype(F32)
        middle = slice(8, 8 + cols)
        lines[0, middle] = jnp.where(no_top, 0.0, over)
        lines[1, middle] = held[j, 0].astype(F32)
        lines[2, middle] = held[j, 1].astype(F32)
        lines[3, middle] = jnp.where(no_bottom, 0.0, under)
        for a in range(4):
            for b in range(4):
                wide[a, :, b * chans : (b + 1) * chans] = lines[a, pl.ds(7 + b, half, stride=2), :].astype(BF16)
        total = silu(column_pairs(wide, 0, 2, taps) + taps.bias())
        for i in range(2):
            part = total[i * half : (i + 1) * half]
            for b in range(2):
                here = lines[i + 1, pl.ds(8 + b, half, stride=2), :]
                decoded = (here + part[:, b * chans : (b + 1) * chans]).astype(BF16).astype(F32)
                at = pl.ds(b, half, stride=2)
                canvas[2 * j + i, at, :] = canvas[2 * j + i, at, :] + decoded
            out[j, i] = canvas[2 * j + i].astype(BF16)
        leave(j).start()

    @pl.loop(0, bands // 2)
    def _(step):
        for k in range(2):
            band(2 * step + k, lines.at[k], wide.at[k])

    for j in range(bands):
        leave(j).wait()


def shards(features, dec_weight, dec_bias, first_weight, first_bias, second_weight, second_bias, boxes, slots):
    tiles = lax.axis_size("tile")
    dims = Dims(features, tiles)
    bands, cols, chans, local_rows = dims.bands, dims.cols, dims.chans, dims.local_rows
    assert dims.band_rows == 2 and slots.shape[0] == CAP * tiles and boxes.shape[1] == tiles
    assert tiles & (tiles - 1) == 0

    smem = pl.BlockSpec(memory_space=pltpu.SMEM)
    hbm = pl.BlockSpec(memory_space=pl.ANY)
    full = pltpu.CompilerParams(vmem_limit_bytes=FULL_GRANT)
    dma = pltpu.SemaphoreType.DMA

    def cost(flops, moved):
        return pl.CostEstimate(flops=int(flops), bytes_accessed=int(moved), transcendentals=0)

    def shaped(*shape, kind=BF16):
        return jax.ShapeDtypeStruct(shape, kind)

    def swap(array):
        return lax.all_to_all(array, "tile", split_axis=0, concat_axis=0, tiled=True)

    pack_scratch = [
        pltpu.VMEM((bands, 2, cols, chans), BF16),
        pltpu.VMEM((local_rows, cols + 16, chans), F32),
        pltpu.VMEM((dims.rim, chans), F32),
        pltpu.VMEM((tiles, dims.message, chans), BF16),
        pltpu.VMEM((tiles, dims.message, chans), BF16),
        dma((4,)),
        dma((bands,)),
        dma((tiles,)),
    ]
    message = shaped(tiles, dims.message, chans)
    *sent_main, sent_extra, table, last, leading = pl.pallas_call(
        functools.partial(pack_kernel, dims),
        out_shape=[shaped(dims.message, chans)] * tiles
        + [message, shaped(7, tiles, kind=I32), shaped(bands, cols, chans), shaped(bands, cols, chans)],
        in_specs=[hbm, hbm, hbm],
        out_specs=[hbm] * (tiles + 1) + [smem, hbm, hbm],
        scratch_shapes=[
            pltpu.SMEM(boxes.shape, I32),
            pltpu.SMEM(slots.shape, I32),
            pltpu.SMEM((tiles,), I32),
            pltpu.SMEM((tiles,), I32),
            pltpu.SMEM((tiles + 1,), I32),
        ]
        + pack_scratch,
        compiler_params=full,
        cost_estimate=cost(0, 6e6),
        name="pack",
    )(boxes, slots, features)
    got_main = [sent_main[0]] + [None] * (tiles - 1)
    for s in [1] + sorted(range(2, tiles), key=lambda s: (-(s >> 1).bit_count(), -(s >> 1), s)):
        got_main[s] = lax.ppermute(sent_main[s], "tile", [(i, i ^ s) for i in range(tiles)])
    up = [(i, (i + 1) % tiles) for i in range(tiles)]
    above = lax.ppermute(last, "tile", up)
    below = lax.ppermute(leading, "tile", [(j, i) for i, j in up])

    got_extra = swap(sent_extra)

    weights = tuple(w.reshape(3, 3, chans, chans) for w in (dec_weight, first_weight, second_weight))
    biases = (dec_bias[None], first_bias[None], second_bias[None])
    restore_scratch = [
        pltpu.VMEM((tiles, dims.message, chans), BF16),
        pltpu.VMEM((4, 3, chans, 2 * chans), BF16),
        pltpu.VMEM((2, 3, 4, chans, 2 * chans), BF16),
        pltpu.VMEM((3, 1, chans), F32),
        dma((tiles,)),
        dma((3, 3)),
        pltpu.VMEM((SPAN // 2 + 2, 2, SPAN, 3 * chans), BF16),
        pltpu.VMEM((SPAN, SPAN, chans), F32),
        pltpu.VMEM((S + 2, S // 2, 4 * chans), BF16),
        pltpu.VMEM((S + 2, S // 2, 4 * chans), BF16),
        pltpu.VMEM((32, S, chans), F32),
        pltpu.VMEM((S, S, chans), BF16),
        dma((S // PIECE,)),
    ]
    restored_shape = shaped(CAP, S, S, chans)
    sent_back, partial = pl.pallas_call(
        functools.partial(main_kernel, dims),
        out_shape=[shaped(tiles, dims.back_rows, SPAN, chans), restored_shape],
        in_specs=[smem] + [hbm] * (tiles + 6),
        out_specs=[hbm, hbm],
        scratch_shapes=restore_scratch
        + [pltpu.VMEM((tiles, dims.back_rows, SPAN, chans), BF16), dma((tiles,))],
        compiler_params=full,
        cost_estimate=cost(7e9, 8e6),
        name="restore_main",
    )(table, *got_main, *weights, *biases)
    got_back = swap(sent_back)

    restorations = pl.pallas_call(
        functools.partial(extra_kernel, dims),
        out_shape=restored_shape,
        in_specs=[smem] + [hbm] * 8,
        out_specs=hbm,
        scratch_shapes=restore_scratch,
        input_output_aliases={8: 0},
        compiler_params=full,
        cost_estimate=cost(6e9, 8e6),
        name="restore_extra",
    )(table, got_extra, *weights, *biases, partial)

    above, below, restorations = lax.optimization_barrier((above, below, restorations))
    assert bands % 2 == 0
    finished = pl.pallas_call(
        functools.partial(finish_kernel, dims),
        out_shape=shaped(*features.shape),
        in_specs=[smem] + [hbm] * 6,
        out_specs=hbm,
        scratch_shapes=[
            pltpu.VMEM((tiles, dims.back_rows, SPAN, chans), BF16),
            pltpu.VMEM((bands, 2, cols, chans), BF16),
            pltpu.VMEM((bands, cols, chans), BF16),
            pltpu.VMEM((bands, cols, chans), BF16),
            pltpu.VMEM((3, 4, chans, 2 * chans), BF16),
            pltpu.VMEM((1, chans), F32),
            pltpu.VMEM((2, 4, cols + 16, chans), F32),
            pltpu.VMEM((2, 4, cols // 2, 4 * chans), BF16),
            pltpu.VMEM((local_rows, cols, chans), F32),
            pltpu.VMEM((bands, 2, cols, chans), BF16),
            dma((1 + bands,)),
            dma((3, bands)),
            dma((3,)),
        ],
        compiler_params=full,
        cost_estimate=cost(3e9, 6e6),
        name="finish",
    )(table, got_back, features, above, below, weights[0], biases[0])
    return finished, restorations


def solution(mesh):
    return jax.shard_map(
        shards,
        mesh=mesh,
        in_specs=(
            P("sess", "tile", None, None),
            P(),
            P(),
            P(),
            P(),
            P(),
            P(),
            P(None, "sess"),
            P("sess"),
        ),
        out_specs=(P("sess", "tile", None, None), P(("sess", "tile"), None, None, None)),
        check_vma=False,
    )
```

```python
import functools

import jax
import jax.numpy as jnp
from jax import lax
from jax.experimental import pallas as pl
from jax.experimental.pallas import tpu as pltpu
from jax.sharding import PartitionSpec as P

S = 64
UNIT = 12
NCLS = 3
CAP = 2
PIECE = 16
BANDS_AT_ONCE = 3
SPAN = UNIT * (NCLS + 1)
BF16 = jnp.bfloat16
F32 = jnp.float32
I32 = jnp.int32
FULL_GRANT = 66500000
ROW, COL, SIDE, ROW2, COL2, SIDE2, PLACE = range(7)


def rows_within(window, band_rows, stride):
    return band_rows * (window // stride) + min(band_rows, window % stride)


class Dims:
    def __init__(self, features, tiles):
        self.bands, self.band_rows, self.cols, self.chans = features.shape
        self.tiles = tiles
        self.stride = tiles * self.band_rows
        self.shift = self.stride.bit_length() - 1
        self.local_rows = self.bands * self.band_rows
        self.rows = rows_within(SPAN + 2, self.band_rows, self.stride)
        self.back_rows = rows_within(SPAN, self.band_rows, self.stride)
        self.rim = -(-2 * self.rows // 16) * 16
        self.message = self.rows * SPAN + self.rim


def first_local(row, tile, dims):
    return ((row >> dims.shift) << 1) + jnp.clip((row & (dims.stride - 1)) - 2 * tile, 0, 2)


def global_row(local, tile, dims):
    return ((local >> 1) << dims.shift) + 2 * tile + (local & 1)


def silu(v):
    half = 0.5 * v
    return half + half * jnp.tanh(half)


def both(bias):
    return jnp.concatenate([bias, bias], -1)


class RowTaps:
    def __init__(self, source, bias, store, held, sems):
        chans = source.shape[-1]
        self.store = store
        self.held = held
        self.copies = (
            pltpu.make_async_copy(bias, held, sems.at[2]),
            pltpu.make_async_copy(source, store.at[0:3, :, :, 0:chans], sems.at[0]),
            pltpu.make_async_copy(source, store.at[1:4, :, :, chans : 2 * chans], sems.at[1]),
        )

    def start(self):
        for copy in self.copies:
            copy.start()
        chans = self.store.shape[2]
        none = jnp.zeros((3, chans, chans), BF16)
        self.store[3, :, :, 0:chans] = none
        self.store[0, :, :, chans : 2 * chans] = none

    def wait(self):
        for copy in self.copies:
            copy.wait()

    def bias(self):
        return both(self.held[...])

    def value(self):
        return self.store[...].reshape(-1, self.store.shape[-1])


class ColumnTaps(RowTaps):
    def __init__(self, source, bias, store, held, sems):
        chans = source.shape[-1]
        self.store = store
        self.held = held
        self.copies = (
            pltpu.make_async_copy(bias, held, sems.at[2]),
            pltpu.make_async_copy(source, store.at[:, 0:3, :, 0:chans], sems.at[0]),
            pltpu.make_async_copy(source, store.at[:, 1:4, :, chans : 2 * chans], sems.at[1]),
        )

    def start(self):
        for copy in self.copies:
            copy.start()
        chans = self.store.shape[2]
        none = jnp.zeros((3, chans, chans), BF16)
        self.store[:, 3, :, 0:chans] = none
        self.store[:, 0, :, chans : 2 * chans] = none


def two_chains(wide, taps):
    wide = wide.reshape(-1, wide.shape[-1])
    weight = taps.value()
    middle = weight.shape[0] // 2
    one = jnp.dot(wide[:, :middle], weight[:middle], preferred_element_type=F32)
    two = jnp.dot(wide[:, middle:], weight[middle:], preferred_element_type=F32)
    return one + two


def row_pairs(src, first, count, taps):
    parts = [
        src[pl.ds(first, count), 0],
        src[pl.ds(first, count), 1],
        src[pl.ds(first + 1, count), 0],
        src[pl.ds(first + 1, count), 1],
    ]
    return two_chains(jnp.concatenate(parts, -1), taps)


def column_pairs(src, first, count, taps):
    return two_chains(jnp.concatenate([src[pl.ds(first + a, count)] for a in range(3)], -1), taps)


def fill_canvas(dims, feat, held, canvas, sems):
    def copy(band):
        return pltpu.make_async_copy(feat.at[band], held.at[band], sems.at[band])

    for band in range(dims.bands):
        copy(band).start()

    def finish():
        edge = jnp.zeros((8, dims.chans), F32)
        for band in range(dims.bands):
            copy(band).wait()
            for i in range(2):
                row = 2 * band + i
                canvas[row, 0:8, :] = edge
                canvas[row, 8 + dims.cols : 16 + dims.cols, :] = edge
                canvas[row, 8 : 8 + dims.cols, :] = held[band, i].astype(F32)

    return finish


def pack_crops(dims, table, row_at, col_at, canvas, rim, staged, partner):
    me = lax.axis_index("tile")
    rim[...] = jnp.zeros_like(rim)

    @pl.loop(0, dims.tiles)
    def _(s):
        w = partner(s)
        row0 = table[row_at, w]
        col0 = table[col_at, w]
        start = first_local(jnp.maximum(row0 - 1, 0), me, dims)
        for i in range(dims.rows):
            row = jnp.minimum(start + i, dims.local_rows - 1)
            staged[s, i * SPAN : (i + 1) * SPAN, :] = canvas[row, pl.ds(col0 + 8, SPAN), :].astype(BF16)
            rim[2 * i : 2 * i + 1, :] = canvas[row, pl.ds(col0 + 7, 1), :]
            rim[2 * i + 1 : 2 * i + 2, :] = canvas[row, pl.ds(col0 + 8 + SPAN, 1), :]
        staged[s, dims.rows * SPAN :, :] = rim[...].astype(BF16)


def pack_kernel(
    dims, boxes_in, slots_in, feat, *refs
):
    sent, refs = refs[: dims.tiles], refs[dims.tiles :]
    sent_extra, table, last, leading, boxes, slots, main, extra, seconds, held, canvas, rim, staged, staged_extra, sems, feat_sems, sent_sems = refs
    me = lax.axis_index("tile")
    copies = (
        pltpu.make_async_copy(boxes_in, boxes, sems.at[0]),
        pltpu.make_async_copy(slots_in, slots, sems.at[1]),
    )
    for copy in copies:
        copy.start()
    finish = fill_canvas(dims, feat, held, canvas, feat_sems)
    for copy in copies:
        copy.wait()

    def first_pass(w, count):
        one = slots[CAP * w]
        two = slots[CAP * w + 1]
        full = (one >= 0) & (two >= 0)
        second = jnp.where(full, two, -1)
        main[w] = jnp.where(one >= 0, one, two)
        extra[w] = second
        seconds[count] = second
        return count + full.astype(I32)

    lax.fori_loop(0, dims.tiles, first_pass, jnp.int32(0))

    def second_pass(w, count):
        own = main[w]
        idle = own < 0
        crop = jnp.where(idle, seconds[count], own)
        table[ROW, w] = boxes[0, crop]
        table[COL, w] = boxes[1, crop]
        table[SIDE, w] = UNIT * (boxes[2, crop] + 2)
        other = jnp.maximum(extra[w], 0)
        table[ROW2, w] = boxes[0, other]
        table[COL2, w] = boxes[1, other]
        table[SIDE2, w] = jnp.where(extra[w] >= 0, UNIT * (boxes[2, other] + 2), 0)
        table[PLACE, w] = jnp.where(idle, 2, jnp.where(slots[CAP * w] >= 0, 0, 1))
        return count + idle.astype(I32)

    lax.fori_loop(0, dims.tiles, second_pass, jnp.int32(0))
    finish()
    edges = (
        pltpu.make_async_copy(held.at[:, 1], last, sems.at[2]),
        pltpu.make_async_copy(held.at[:, 0], leading, sems.at[3]),
    )
    for edge in edges:
        edge.start()
    pack_crops(dims, table, ROW, COL, canvas, rim, staged, lambda s: me ^ s)
    copies = [pltpu.make_async_copy(staged.at[s], sent[s], sent_sems.at[s]) for s in range(dims.tiles)]
    for copy in copies:
        copy.start()
    pack_crops(dims, table, ROW2, COL2, canvas, rim, staged_extra, lambda s: s)
    later = pltpu.make_async_copy(staged_extra, sent_extra, sems.at[0])
    later.start()
    for copy in copies:
        copy.wait()
    later.wait()
    for edge in edges:
        edge.wait()


def restore(dims, row0, length, arrival, source, got, taps, raw, decoded, wide, inner, mixed, delta, finish):
    chans = dims.chans
    above = row0 - 1
    pairs = SPAN // 2
    half = S // 2
    nothing = jnp.zeros((SPAN, 3 * chans), BF16)
    raw[0, 0] = nothing
    raw[pairs, 1] = nothing
    empty = jnp.zeros((half, 4 * chans), BF16)
    for store in (wide, inner):
        store[0] = empty
        store[S + 1] = empty

    @pl.loop(0, dims.tiles)
    def _(s):
        arrival(s).wait()
        e = source(s)
        start = first_local(jnp.maximum(above, 0), e, dims)
        rim = got[s, dims.rows * SPAN :, :].astype(F32)
        at = lax.broadcasted_iota(I32, (SPAN, chans), 0)
        for i in range(dims.rows):
            local = start + i
            place = global_row(local, e, dims) - above
            place = jnp.where((local < dims.local_rows) & (place < SPAN + 2), place, SPAN + 2)
            line = got[s, i * SPAN : (i + 1) * SPAN, :]
            wider = line.astype(F32)
            left = jnp.where(at == 0, rim[2 * i : 2 * i + 1], pltpu.roll(wider, 1, 0))
            right = jnp.where(at == SPAN - 1, rim[2 * i + 1 : 2 * i + 2], pltpu.roll(wider, SPAN - 1, 0))
            raw[place >> 1, place & 1] = jnp.concatenate([left.astype(BF16), line, right.astype(BF16)], -1)

    taps[1].start()
    taps[2].start()
    taps[0].wait()
    n = 8
    for first in range(0, pairs, n):
        total = silu(row_pairs(raw, first, n, taps[0]) + taps[0].bias())
        for k in range(n):
            part = total[k * SPAN : (k + 1) * SPAN]
            at = 2 * (first + k)
            upper = raw[first + k, 1, :, chans : 2 * chans].astype(F32) + part[:, :chans]
            lower = raw[first + k + 1, 0, :, chans : 2 * chans].astype(F32) + part[:, chans:]
            decoded[at] = upper.astype(BF16).astype(F32)
            decoded[at + 1] = lower.astype(BF16).astype(F32)

    lengthf = length.astype(F32)
    block = lax.broadcasted_iota(I32, (4, half, SPAN), 0)
    t = 2 * lax.broadcasted_iota(I32, (4, half, SPAN), 1) + block - 1
    j = lax.broadcasted_iota(I32, (4, half, SPAN), 2).astype(F32)
    spots = jnp.clip((t.astype(F32) + 0.5) * lengthf / S - 0.5, 0.0, lengthf - 1.0)
    across = jnp.where((t >= 0) & (t < S), jnp.maximum(0.0, 1.0 - jnp.abs(spots - j)), 0.0)
    across = across.reshape(4 * half, SPAN).astype(BF16)
    taps[1].wait()
    taps[2].wait()
    for m in range(S // 2):
        lines = []
        for parity in range(2):
            s = 2 * m + parity
            spot = jnp.clip((2 * s + 1) * length - S, 0, (length - 1) * 2 * S)
            low = spot >> 7
            part = (spot & 127).astype(F32) * (1.0 / (2 * S))
            high = jnp.minimum(low + 1, SPAN - 1)
            lines.append(((1.0 - part) * decoded[low] + part * decoded[high]).astype(BF16))
        cells = jnp.dot(across, jnp.concatenate(lines, -1), preferred_element_type=F32).astype(BF16)
        for parity in range(2):
            at = 2 * m + parity + 1
            for b in range(4):
                wide[at, :, b * chans : (b + 1) * chans] = cells[
                    b * half : (b + 1) * half, parity * chans : (parity + 1) * chans
                ]

    n = PIECE
    for first in range(0, S, n):
        total = silu(column_pairs(wide, first, n, taps[1]) + taps[1].bias())
        at = lax.broadcasted_iota(I32, (n, half, chans), 1)
        even = pltpu.roll(total[:, :chans], n * half - 1, 0).reshape(n, half, chans)
        odd = pltpu.roll(total[:, chans:], 1, 0).reshape(n, half, chans)
        rows = pl.ds(first + 1, n)
        inner[rows, :, 0:chans] = jnp.where(at == 0, 0.0, odd).astype(BF16)
        inner[rows, :, chans : 3 * chans] = total.astype(BF16).reshape(n, half, 2 * chans)
        inner[rows, :, 3 * chans :] = jnp.where(at == half - 1, 0.0, even).astype(BF16)

    for first in range(0, S, n):
        total = column_pairs(inner, first, n, taps[2]) + taps[2].bias()
        for k in range(n):
            mixed[first + k, pl.ds(0, half, stride=2), :] = total[k * half : (k + 1) * half, :chans]
            mixed[first + k, pl.ds(1, half, stride=2), :] = total[k * half : (k + 1) * half, chans:]
        delta[first : first + n] = mixed[first : first + n].astype(BF16)
        finish(first // PIECE)


def begin(dims, arrived, weights, biases, scratch):
    got, row_store, column_store, held, got_sems, tap_sems = scratch

    def arrival(s):
        return pltpu.make_async_copy(arrived[0], got.at[s], got_sems.at[s])

    for s in range(dims.tiles):
        pltpu.make_async_copy(arrived[s], got.at[s], got_sems.at[s]).start()
    taps = (
        RowTaps(weights[0], biases[0], row_store, held.at[0], tap_sems.at[0]),
        ColumnTaps(weights[1], biases[1], column_store.at[0], held.at[1], tap_sems.at[1]),
        ColumnTaps(weights[2], biases[2], column_store.at[1], held.at[2], tap_sems.at[2]),
    )
    taps[0].start()
    return arrival, taps


def main_kernel(dims, table, *refs):
    tiles, chans = dims.tiles, dims.chans
    arrived, refs = refs[:tiles], refs[tiles:]
    (dec_w, one_w, two_w, dec_b, one_b, two_b, sent, restored, got, row_store, column_store, held) = refs[:12]
    got_sems, tap_sems, raw, decoded, wide, inner, mixed, delta, sem, back, back_sems = refs[12:]
    me = lax.axis_index("tile")
    row0 = table[ROW, me]
    length = table[SIDE, me]
    place = table[PLACE, me]
    scratch = (got, row_store, column_store, held, got_sems, tap_sems)
    arrival, taps = begin(dims, arrived, (dec_w, one_w, two_w), (dec_b, one_b, two_b), scratch)
    restore(
        dims, row0, length, arrival, lambda s: me ^ s, got, taps,
        raw, decoded, wide, inner, mixed, delta, lambda piece: None,
    )

    @pl.when(place < CAP)
    def _():
        pltpu.make_async_copy(delta, restored.at[place], sem.at[0]).start()

    lengthf = length.astype(F32)
    t = lax.broadcasted_iota(I32, (SPAN, S), 0).astype(F32)
    s = lax.broadcasted_iota(I32, (SPAN, S), 1).astype(F32)
    spots = jnp.clip((t + 0.5) * S / lengthf - 0.5, 0.0, S - 1.0)
    lift = jnp.where(t < lengthf, jnp.maximum(0.0, 1.0 - jnp.abs(spots - s)), 0.0)
    coarse = lift.astype(BF16)
    lift = jnp.concatenate([coarse, (lift - coarse.astype(F32)).astype(BF16)], 0)
    scale = 1.0 / (2.0 * lengthf)
    group = 12

    @pl.loop(0, SPAN // 2 // group)
    def _(step):
        for k in range(group):
            lines = []
            for parity in range(2):
                h = 2 * (step * group + k) + parity
                spot = jnp.clip((2 * h + 1) * S - length, 0, (S - 1) * 2 * length)
                low = ((spot.astype(F32) + 0.5) * scale).astype(I32)
                part = (spot - low * 2 * length).astype(F32) * scale
                high = jnp.minimum(low + 1, S - 1)
                lines.append(((1.0 - part) * delta[low].astype(F32) + part * delta[high].astype(F32)).astype(BF16))
            patch = jnp.dot(lift, jnp.concatenate(lines, -1), preferred_element_type=F32)
            patch = (patch[:SPAN] + patch[SPAN:]).astype(BF16)
            for parity in range(2):
                row = row0 + 2 * (step * group + k) + parity
                dest = (row & (dims.stride - 1)) >> 1
                local = ((row >> dims.shift) << 1) + (row & 1)
                back[dest, local - first_local(row0, dest, dims)] = patch[:, parity * chans : (parity + 1) * chans]

    def leave(e):
        return pltpu.make_async_copy(back.at[e], sent.at[e], back_sems.at[e])

    for e in range(tiles):
        leave(e).start()
    for e in range(tiles):
        leave(e).wait()

    @pl.when(place < CAP)
    def _():
        pltpu.make_async_copy(delta, restored.at[place], sem.at[0]).wait()


def extra_kernel(
    dims, table, arrived, dec_w, one_w, two_w, dec_b, one_b, two_b, partial, restored,
    got, row_store, column_store, held, got_sems, tap_sems, raw, decoded, wide, inner, mixed, delta, sem,
):
    me = lax.axis_index("tile")
    row0 = table[ROW2, me]
    length = table[SIDE2, me]
    place = table[PLACE, me]

    def write(slot):
        copy = pltpu.make_async_copy(delta, restored.at[slot], sem.at[0])
        copy.start()
        copy.wait()

    @pl.when(length > 0)
    def _():
        scratch = (got, row_store, column_store, held, got_sems, tap_sems)
        arrival, taps = begin(dims, [arrived.at[s] for s in range(dims.tiles)], (dec_w, one_w, two_w), (dec_b, one_b, two_b), scratch)

        def leave(piece):
            rows = pl.ds(piece * PIECE, PIECE)
            return pltpu.make_async_copy(delta.at[rows], restored.at[1, rows], sem.at[piece])

        restore(
            dims, row0, length, arrival, lambda s: s, got, taps,
            raw, decoded, wide, inner, mixed, delta, lambda piece: leave(piece).start(),
        )
        for piece in range(S // PIECE):
            leave(piece).wait()

    @pl.when(length == 0)
    def _():
        delta[...] = jnp.zeros_like(delta)

        @pl.when(place != 0)
        def _():
            write(0)

        @pl.when(place != 1)
        def _():
            write(1)


def finish_kernel(
    dims, table, back, feat, above, below, weight, bias, finished,
    got, held, up, down, store, held_bias, lines, wide, canvas, out, sems, load_sems, tap_sems,
):
    me = lax.axis_index("tile")
    bands, chans, cols = dims.bands, dims.chans, dims.cols
    half = cols // 2
    taps = ColumnTaps(weight, bias, store, held_bias, tap_sems)
    patches = pltpu.make_async_copy(back, got, sems.at[0])
    patches.start()
    def from_feat(band):
        return pltpu.make_async_copy(feat.at[band], held.at[band], load_sems.at[0, band])

    def from_above(band):
        return pltpu.make_async_copy(above.at[band], up.at[band], load_sems.at[1, band])

    def from_below(band):
        return pltpu.make_async_copy(below.at[band], down.at[band], load_sems.at[2, band])

    taps.start()
    from_below(0).start()
    for j in range(bands):
        from_feat(j).start()
        from_above(j).start()
        if j + 1 < bands:
            from_below(j + 1).start()

    def leave(band):
        return pltpu.make_async_copy(out.at[band], finished.at[band], sems.at[1 + band])

    top = (me == 0).astype(I32)
    bottom = (me == dims.tiles - 1).astype(I32)
    edge = jnp.zeros((8, chans), F32)
    for k in range(lines.shape[0]):
        for a in range(4):
            lines[k, a, 0:8] = edge
            lines[k, a, 8 + cols :] = edge
    canvas[...] = jnp.zeros_like(canvas)
    patches.wait()

    @pl.loop(0, dims.tiles)
    def _(e):
        row0 = table[ROW, e]
        col0 = table[COL, e]
        length = table[SIDE, e]
        start = first_local(row0, me, dims)
        for i in range(dims.back_rows):
            local = start + i

            @pl.when((local < dims.local_rows) & (global_row(local, me, dims) - row0 < length))
            def _():
                canvas[local, pl.ds(col0, SPAN), :] += got[e, i].astype(F32)

    from_below(0).wait()
    taps.wait()

    def band(j, lines, wide):
        no_top = (top == 1) & (j == 0)
        no_bottom = (bottom == 1) & (j == bands - 1)
        over = up[jnp.maximum(j - top, 0)].astype(F32)
        under = down[jnp.minimum(j + bottom, bands - 1)].astype(F32)
        middle = slice(8, 8 + cols)
        lines[0, middle] = jnp.where(no_top, 0.0, over)
        lines[1, middle] = held[j, 0].astype(F32)
        lines[2, middle] = held[j, 1].astype(F32)
        lines[3, middle] = jnp.where(no_bottom, 0.0, under)
        for a in range(4):
            for b in range(4):
                wide[a, :, b * chans : (b + 1) * chans] = lines[a, pl.ds(7 + b, half, stride=2), :].astype(BF16)
        total = silu(column_pairs(wide, 0, 2, taps) + taps.bias())
        for i in range(2):
            part = total[i * half : (i + 1) * half]
            for b in range(2):
                here = lines[i + 1, pl.ds(8 + b, half, stride=2), :]
                decoded = (here + part[:, b * chans : (b + 1) * chans]).astype(BF16).astype(F32)
                at = pl.ds(b, half, stride=2)
                canvas[2 * j + i, at, :] = canvas[2 * j + i, at, :] + decoded
            out[j, i] = canvas[2 * j + i].astype(BF16)

    @pl.loop(0, bands // BANDS_AT_ONCE)
    def _(step):
        first = BANDS_AT_ONCE * step
        for k in range(BANDS_AT_ONCE):
            from_feat(first + k).wait()
            from_above(first + k).wait()
            if k + 1 < BANDS_AT_ONCE:
                from_below(first + k + 1).wait()

        @pl.when(first + BANDS_AT_ONCE < bands)
        def _():
            from_below(first + BANDS_AT_ONCE).wait()

        for k in range(BANDS_AT_ONCE):
            band(first + k, lines.at[k], wide.at[k])
        for k in range(BANDS_AT_ONCE):
            leave(first + k).start()

    for j in range(bands):
        leave(j).wait()


def shards(features, dec_weight, dec_bias, first_weight, first_bias, second_weight, second_bias, boxes, slots):
    tiles = lax.axis_size("tile")
    dims = Dims(features, tiles)
    bands, cols, chans, local_rows = dims.bands, dims.cols, dims.chans, dims.local_rows
    assert dims.band_rows == 2 and slots.shape[0] == CAP * tiles and boxes.shape[1] == tiles
    assert tiles & (tiles - 1) == 0

    smem = pl.BlockSpec(memory_space=pltpu.SMEM)
    hbm = pl.BlockSpec(memory_space=pl.ANY)
    full = pltpu.CompilerParams(vmem_limit_bytes=FULL_GRANT)
    dma = pltpu.SemaphoreType.DMA

    def cost(flops, moved):
        return pl.CostEstimate(flops=int(flops), bytes_accessed=int(moved), transcendentals=0)

    def shaped(*shape, kind=BF16):
        return jax.ShapeDtypeStruct(shape, kind)

    def swap(array):
        return lax.all_to_all(array, "tile", split_axis=0, concat_axis=0, tiled=True)

    pack_scratch = [
        pltpu.VMEM((bands, 2, cols, chans), BF16),
        pltpu.VMEM((local_rows, cols + 16, chans), F32),
        pltpu.VMEM((dims.rim, chans), F32),
        pltpu.VMEM((tiles, dims.message, chans), BF16),
        pltpu.VMEM((tiles, dims.message, chans), BF16),
        dma((4,)),
        dma((bands,)),
        dma((tiles,)),
    ]
    message = shaped(tiles, dims.message, chans)
    *sent_main, sent_extra, table, last, leading = pl.pallas_call(
        functools.partial(pack_kernel, dims),
        out_shape=[shaped(dims.message, chans)] * tiles
        + [message, shaped(7, tiles, kind=I32), shaped(bands, cols, chans), shaped(bands, cols, chans)],
        in_specs=[hbm, hbm, hbm],
        out_specs=[hbm] * (tiles + 1) + [smem, hbm, hbm],
        scratch_shapes=[
            pltpu.SMEM(boxes.shape, I32),
            pltpu.SMEM(slots.shape, I32),
            pltpu.SMEM((tiles,), I32),
            pltpu.SMEM((tiles,), I32),
            pltpu.SMEM((tiles + 1,), I32),
        ]
        + pack_scratch,
        compiler_params=full,
        cost_estimate=cost(0, 6e6),
        name="pack",
    )(boxes, slots, features)
    got_main = [sent_main[0]] + [None] * (tiles - 1)
    for s in [1] + sorted(range(2, tiles), key=lambda s: (-(s >> 1).bit_count(), -(s >> 1), s)):
        got_main[s] = lax.ppermute(sent_main[s], "tile", [(i, i ^ s) for i in range(tiles)])
    up = [(i, (i + 1) % tiles) for i in range(tiles)]
    above = lax.ppermute(last, "tile", up)
    below = lax.ppermute(leading, "tile", [(j, i) for i, j in up])

    got_extra = swap(sent_extra)

    weights = tuple(w.reshape(3, 3, chans, chans) for w in (dec_weight, first_weight, second_weight))
    biases = (dec_bias[None], first_bias[None], second_bias[None])
    restore_scratch = [
        pltpu.VMEM((tiles, dims.message, chans), BF16),
        pltpu.VMEM((4, 3, chans, 2 * chans), BF16),
        pltpu.VMEM((2, 3, 4, chans, 2 * chans), BF16),
        pltpu.VMEM((3, 1, chans), F32),
        dma((tiles,)),
        dma((3, 3)),
        pltpu.VMEM((SPAN // 2 + 2, 2, SPAN, 3 * chans), BF16),
        pltpu.VMEM((SPAN, SPAN, chans), F32),
        pltpu.VMEM((S + 2, S // 2, 4 * chans), BF16),
        pltpu.VMEM((S + 2, S // 2, 4 * chans), BF16),
        pltpu.VMEM((S, S, chans), F32),
        pltpu.VMEM((S, S, chans), BF16),
        dma((S // PIECE,)),
    ]
    restored_shape = shaped(CAP, S, S, chans)
    sent_back, partial = pl.pallas_call(
        functools.partial(main_kernel, dims),
        out_shape=[shaped(tiles, dims.back_rows, SPAN, chans), restored_shape],
        in_specs=[smem] + [hbm] * (tiles + 6),
        out_specs=[hbm, hbm],
        scratch_shapes=restore_scratch
        + [pltpu.VMEM((tiles, dims.back_rows, SPAN, chans), BF16), dma((tiles,))],
        compiler_params=full,
        cost_estimate=cost(7e9, 8e6),
        name="restore_main",
    )(table, *got_main, *weights, *biases)
    got_back = swap(sent_back)

    restorations = pl.pallas_call(
        functools.partial(extra_kernel, dims),
        out_shape=restored_shape,
        in_specs=[smem] + [hbm] * 8,
        out_specs=hbm,
        scratch_shapes=restore_scratch,
        input_output_aliases={8: 0},
        compiler_params=full,
        cost_estimate=cost(6e9, 8e6),
        name="restore_extra",
    )(table, got_extra, *weights, *biases, partial)

    above, below, restorations = lax.optimization_barrier((above, below, restorations))
    assert bands % BANDS_AT_ONCE == 0
    finished = pl.pallas_call(
        functools.partial(finish_kernel, dims),
        out_shape=shaped(*features.shape),
        in_specs=[smem] + [hbm] * 6,
        out_specs=hbm,
        scratch_shapes=[
            pltpu.VMEM((tiles, dims.back_rows, SPAN, chans), BF16),
            pltpu.VMEM((bands, 2, cols, chans), BF16),
            pltpu.VMEM((bands, cols, chans), BF16),
            pltpu.VMEM((bands, cols, chans), BF16),
            pltpu.VMEM((3, 4, chans, 2 * chans), BF16),
            pltpu.VMEM((1, chans), F32),
            pltpu.VMEM((BANDS_AT_ONCE, 4, cols + 16, chans), F32),
            pltpu.VMEM((BANDS_AT_ONCE, 4, cols // 2, 4 * chans), BF16),
            pltpu.VMEM((local_rows, cols, chans), F32),
            pltpu.VMEM((bands, 2, cols, chans), BF16),
            dma((1 + bands,)),
            dma((3, bands)),
            dma((3,)),
        ],
        compiler_params=full,
        cost_estimate=cost(3e9, 6e6),
        name="finish",
    )(table, got_back, features, above, below, weights[0], biases[0])
    return finished, restorations


def solution(mesh):
    return jax.shard_map(
        shards,
        mesh=mesh,
        in_specs=(
            P("sess", "tile", None, None),
            P(),
            P(),
            P(),
            P(),
            P(),
            P(),
            P(None, "sess"),
            P("sess"),
        ),
        out_specs=(P("sess", "tile", None, None), P(("sess", "tile"), None, None, None)),
        check_vma=False,
    )
```

```python
import functools

import jax
import jax.numpy as jnp
from jax import lax
from jax.experimental import pallas as pl
from jax.experimental.pallas import tpu as pltpu
from jax.sharding import PartitionSpec as P

S = 64
UNIT = 12
NCLS = 3
CAP = 2
PIECE = 16
BANDS_AT_ONCE = 3
SPAN = UNIT * (NCLS + 1)
BF16 = jnp.bfloat16
F32 = jnp.float32
I32 = jnp.int32
FULL_GRANT = 66500000
ROW, COL, SIDE, ROW2, COL2, SIDE2, PLACE = range(7)


def rows_within(window, band_rows, stride):
    return band_rows * (window // stride) + min(band_rows, window % stride)


class Dims:
    def __init__(self, features, tiles):
        self.bands, self.band_rows, self.cols, self.chans = features.shape
        self.tiles = tiles
        self.stride = tiles * self.band_rows
        self.shift = self.stride.bit_length() - 1
        self.local_rows = self.bands * self.band_rows
        self.rows = rows_within(SPAN + 2, self.band_rows, self.stride)
        self.back_rows = rows_within(SPAN, self.band_rows, self.stride)
        self.rim = -(-2 * self.rows // 16) * 16
        self.message = self.rows * SPAN + self.rim


def first_local(row, tile, dims):
    return ((row >> dims.shift) << 1) + jnp.clip((row & (dims.stride - 1)) - 2 * tile, 0, 2)


def global_row(local, tile, dims):
    return ((local >> 1) << dims.shift) + 2 * tile + (local & 1)


def silu(v):
    half = 0.5 * v
    return half + half * jnp.tanh(half)


def both(bias):
    return jnp.concatenate([bias, bias], -1)


class RowTaps:
    def __init__(self, source, bias, store, held, sems):
        chans = source.shape[-1]
        self.store = store
        self.held = held
        self.copies = (
            pltpu.make_async_copy(bias, held, sems.at[2]),
            pltpu.make_async_copy(source, store.at[0:3, :, :, 0:chans], sems.at[0]),
            pltpu.make_async_copy(source, store.at[1:4, :, :, chans : 2 * chans], sems.at[1]),
        )

    def start(self):
        for copy in self.copies:
            copy.start()
        chans = self.store.shape[2]
        none = jnp.zeros((3, chans, chans), BF16)
        self.store[3, :, :, 0:chans] = none
        self.store[0, :, :, chans : 2 * chans] = none

    def wait(self):
        for copy in self.copies:
            copy.wait()

    def bias(self):
        return both(self.held[...])

    def value(self):
        return self.store[...].reshape(-1, self.store.shape[-1])


class ColumnTaps(RowTaps):
    def __init__(self, source, bias, store, held, sems):
        chans = source.shape[-1]
        self.store = store
        self.held = held
        self.copies = (
            pltpu.make_async_copy(bias, held, sems.at[2]),
            pltpu.make_async_copy(source, store.at[:, 0:3, :, 0:chans], sems.at[0]),
            pltpu.make_async_copy(source, store.at[:, 1:4, :, chans : 2 * chans], sems.at[1]),
        )

    def start(self):
        for copy in self.copies:
            copy.start()
        chans = self.store.shape[2]
        none = jnp.zeros((3, chans, chans), BF16)
        self.store[:, 3, :, 0:chans] = none
        self.store[:, 0, :, chans : 2 * chans] = none


def two_chains(wide, taps):
    wide = wide.reshape(-1, wide.shape[-1])
    weight = taps.value()
    middle = weight.shape[0] // 2
    one = jnp.dot(wide[:, :middle], weight[:middle], preferred_element_type=F32)
    two = jnp.dot(wide[:, middle:], weight[middle:], preferred_element_type=F32)
    return one + two


def row_pairs(src, first, count, taps):
    parts = [
        src[pl.ds(first, count), 0],
        src[pl.ds(first, count), 1],
        src[pl.ds(first + 1, count), 0],
        src[pl.ds(first + 1, count), 1],
    ]
    return two_chains(jnp.concatenate(parts, -1), taps)


def column_pairs(src, first, count, taps):
    return two_chains(jnp.concatenate([src[pl.ds(first + a, count)] for a in range(3)], -1), taps)


def fill_canvas(dims, feat, held, canvas, sems):
    def copy(band):
        return pltpu.make_async_copy(feat.at[band], held.at[band], sems.at[band])

    for band in range(dims.bands):
        copy(band).start()

    def finish():
        edge = jnp.zeros((8, dims.chans), F32)
        for band in range(dims.bands):
            copy(band).wait()
            for i in range(2):
                row = 2 * band + i
                canvas[row, 0:8, :] = edge
                canvas[row, 8 + dims.cols : 16 + dims.cols, :] = edge
                canvas[row, 8 : 8 + dims.cols, :] = held[band, i].astype(F32)

    return finish


def pack_crops(dims, table, row_at, col_at, side_at, canvas, rim, staged, partner):
    me = lax.axis_index("tile")
    rim[...] = jnp.zeros_like(rim)

    @pl.loop(0, dims.tiles)
    def _(s):
        w = partner(s)

        @pl.when(table[side_at, w] > 0)
        def _():
            row0 = table[row_at, w]
            col0 = table[col_at, w]
            start = first_local(jnp.maximum(row0 - 1, 0), me, dims)
            for i in range(dims.rows):
                row = jnp.minimum(start + i, dims.local_rows - 1)
                staged[s, i * SPAN : (i + 1) * SPAN, :] = canvas[row, pl.ds(col0 + 8, SPAN), :].astype(BF16)
                rim[2 * i : 2 * i + 1, :] = canvas[row, pl.ds(col0 + 7, 1), :]
                rim[2 * i + 1 : 2 * i + 2, :] = canvas[row, pl.ds(col0 + 8 + SPAN, 1), :]
            staged[s, dims.rows * SPAN :, :] = rim[...].astype(BF16)


def pack_kernel(
    dims, boxes_in, slots_in, feat, *refs
):
    sent, refs = refs[: dims.tiles], refs[dims.tiles :]
    sent_extra, table, last, leading, boxes, slots, main, extra, seconds, held, canvas, rim, staged, staged_extra, sems, feat_sems, sent_sems = refs
    me = lax.axis_index("tile")
    copies = (
        pltpu.make_async_copy(boxes_in, boxes, sems.at[0]),
        pltpu.make_async_copy(slots_in, slots, sems.at[1]),
    )
    for copy in copies:
        copy.start()
    finish = fill_canvas(dims, feat, held, canvas, feat_sems)
    for copy in copies:
        copy.wait()

    def first_pass(w, count):
        one = slots[CAP * w]
        two = slots[CAP * w + 1]
        full = (one >= 0) & (two >= 0)
        second = jnp.where(full, two, -1)
        main[w] = jnp.where(one >= 0, one, two)
        extra[w] = second
        seconds[count] = second
        return count + full.astype(I32)

    lax.fori_loop(0, dims.tiles, first_pass, jnp.int32(0))

    def second_pass(w, count):
        own = main[w]
        idle = own < 0
        crop = jnp.where(idle, seconds[count], own)
        table[ROW, w] = boxes[0, crop]
        table[COL, w] = boxes[1, crop]
        table[SIDE, w] = UNIT * (boxes[2, crop] + 2)
        other = jnp.maximum(extra[w], 0)
        table[ROW2, w] = boxes[0, other]
        table[COL2, w] = boxes[1, other]
        table[SIDE2, w] = jnp.where(extra[w] >= 0, UNIT * (boxes[2, other] + 2), 0)
        table[PLACE, w] = jnp.where(idle, 2, jnp.where(slots[CAP * w] >= 0, 0, 1))
        return count + idle.astype(I32)

    lax.fori_loop(0, dims.tiles, second_pass, jnp.int32(0))
    finish()
    edges = (
        pltpu.make_async_copy(held.at[:, 1], last, sems.at[2]),
        pltpu.make_async_copy(held.at[:, 0], leading, sems.at[3]),
    )
    for edge in edges:
        edge.start()
    pack_crops(dims, table, ROW, COL, SIDE, canvas, rim, staged, lambda s: me ^ s)
    copies = [pltpu.make_async_copy(staged.at[s], sent[s], sent_sems.at[s]) for s in range(dims.tiles)]
    for copy in copies:
        copy.start()
    pack_crops(dims, table, ROW2, COL2, SIDE2, canvas, rim, staged_extra, lambda s: s)
    later = pltpu.make_async_copy(staged_extra, sent_extra, sems.at[0])
    later.start()
    for copy in copies:
        copy.wait()
    later.wait()
    for edge in edges:
        edge.wait()


def restore(dims, row0, length, arrival, source, got, taps, raw, decoded, wide, inner, mixed, delta, finish):
    chans = dims.chans
    above = row0 - 1
    pairs = SPAN // 2
    half = S // 2
    nothing = jnp.zeros((SPAN, 3 * chans), BF16)
    raw[0, 0] = nothing
    raw[pairs, 1] = nothing
    empty = jnp.zeros((half, 4 * chans), BF16)
    for store in (wide, inner):
        store[0] = empty
        store[S + 1] = empty

    column = lax.broadcasted_iota(I32, (SPAN, chans), 0)

    def lay(s):
        e = source(s)
        start = first_local(jnp.maximum(above, 0), e, dims)
        rim = got[s, dims.rows * SPAN :, :].astype(F32)
        for i in range(dims.rows):
            local = start + i
            place = global_row(local, e, dims) - above
            place = jnp.where((local < dims.local_rows) & (place < SPAN + 2), place, SPAN + 2)
            line = got[s, i * SPAN : (i + 1) * SPAN, :]
            wider = line.astype(F32)
            left = jnp.where(column == 0, rim[2 * i : 2 * i + 1], pltpu.roll(wider, 1, 0))
            right = jnp.where(column == SPAN - 1, rim[2 * i + 1 : 2 * i + 2], pltpu.roll(wider, SPAN - 1, 0))
            raw[place >> 1, place & 1] = jnp.concatenate([left.astype(BF16), line, right.astype(BF16)], -1)

    @pl.loop(0, dims.tiles // 4)
    def _(step):
        for k in range(4):
            arrival(4 * step + k).wait()
        for k in range(4):
            lay(4 * step + k)

    taps[1].start()
    taps[2].start()
    taps[0].wait()
    n = 8
    for first in range(0, pairs, n):
        total = silu(row_pairs(raw, first, n, taps[0]) + taps[0].bias())
        for k in range(n):
            part = total[k * SPAN : (k + 1) * SPAN]
            at = 2 * (first + k)
            upper = raw[first + k, 1, :, chans : 2 * chans].astype(F32) + part[:, :chans]
            lower = raw[first + k + 1, 0, :, chans : 2 * chans].astype(F32) + part[:, chans:]
            decoded[at] = upper.astype(BF16).astype(F32)
            decoded[at + 1] = lower.astype(BF16).astype(F32)

    lengthf = length.astype(F32)
    block = lax.broadcasted_iota(I32, (4, half, SPAN), 0)
    t = 2 * lax.broadcasted_iota(I32, (4, half, SPAN), 1) + block - 1
    j = lax.broadcasted_iota(I32, (4, half, SPAN), 2).astype(F32)
    spots = jnp.clip((t.astype(F32) + 0.5) * lengthf / S - 0.5, 0.0, lengthf - 1.0)
    across = jnp.where((t >= 0) & (t < S), jnp.maximum(0.0, 1.0 - jnp.abs(spots - j)), 0.0)
    across = across.reshape(4 * half, SPAN).astype(BF16)
    taps[1].wait()
    taps[2].wait()
    for m in range(S // 2):
        lines = []
        for parity in range(2):
            s = 2 * m + parity
            spot = jnp.clip((2 * s + 1) * length - S, 0, (length - 1) * 2 * S)
            low = spot >> 7
            part = (spot & 127).astype(F32) * (1.0 / (2 * S))
            high = jnp.minimum(low + 1, SPAN - 1)
            lines.append(((1.0 - part) * decoded[low] + part * decoded[high]).astype(BF16))
        cells = jnp.dot(across, jnp.concatenate(lines, -1), preferred_element_type=F32).astype(BF16)
        for parity in range(2):
            at = 2 * m + parity + 1
            for b in range(4):
                wide[at, :, b * chans : (b + 1) * chans] = cells[
                    b * half : (b + 1) * half, parity * chans : (parity + 1) * chans
                ]

    n = PIECE
    for first in range(0, S, n):
        total = silu(column_pairs(wide, first, n, taps[1]) + taps[1].bias())
        at = lax.broadcasted_iota(I32, (n, half, chans), 1)
        even = pltpu.roll(total[:, :chans], n * half - 1, 0).reshape(n, half, chans)
        odd = pltpu.roll(total[:, chans:], 1, 0).reshape(n, half, chans)
        rows = pl.ds(first + 1, n)
        inner[rows, :, 0:chans] = jnp.where(at == 0, 0.0, odd).astype(BF16)
        inner[rows, :, chans : 3 * chans] = total.astype(BF16).reshape(n, half, 2 * chans)
        inner[rows, :, 3 * chans :] = jnp.where(at == half - 1, 0.0, even).astype(BF16)

    for first in range(0, S, n):
        total = column_pairs(inner, first, n, taps[2]) + taps[2].bias()
        for k in range(n):
            mixed[first + k, pl.ds(0, half, stride=2), :] = total[k * half : (k + 1) * half, :chans]
            mixed[first + k, pl.ds(1, half, stride=2), :] = total[k * half : (k + 1) * half, chans:]
        delta[first : first + n] = mixed[first : first + n].astype(BF16)
        finish(first // PIECE)


def begin(dims, arrived, weights, biases, scratch):
    got, row_store, column_store, held, got_sems, tap_sems = scratch

    def arrival(s):
        return pltpu.make_async_copy(arrived[0], got.at[s], got_sems.at[s])

    for s in range(dims.tiles):
        pltpu.make_async_copy(arrived[s], got.at[s], got_sems.at[s]).start()
    taps = (
        RowTaps(weights[0], biases[0], row_store, held.at[0], tap_sems.at[0]),
        ColumnTaps(weights[1], biases[1], column_store.at[0], held.at[1], tap_sems.at[1]),
        ColumnTaps(weights[2], biases[2], column_store.at[1], held.at[2], tap_sems.at[2]),
    )
    taps[0].start()
    return arrival, taps


def main_kernel(dims, table, *refs):
    tiles, chans = dims.tiles, dims.chans
    arrived, refs = refs[:tiles], refs[tiles:]
    (dec_w, one_w, two_w, dec_b, one_b, two_b, sent, restored, got, row_store, column_store, held) = refs[:12]
    got_sems, tap_sems, raw, decoded, wide, inner, mixed, delta, sem, back, back_sems = refs[12:]
    me = lax.axis_index("tile")
    row0 = table[ROW, me]
    length = table[SIDE, me]
    place = table[PLACE, me]
    scratch = (got, row_store, column_store, held, got_sems, tap_sems)
    arrival, taps = begin(dims, arrived, (dec_w, one_w, two_w), (dec_b, one_b, two_b), scratch)
    restore(
        dims, row0, length, arrival, lambda s: me ^ s, got, taps,
        raw, decoded, wide, inner, mixed, delta, lambda piece: None,
    )

    @pl.when(place < CAP)
    def _():
        pltpu.make_async_copy(delta, restored.at[place], sem.at[0]).start()

    lengthf = length.astype(F32)
    t = lax.broadcasted_iota(I32, (SPAN, S), 0).astype(F32)
    s = lax.broadcasted_iota(I32, (SPAN, S), 1).astype(F32)
    spots = jnp.clip((t + 0.5) * S / lengthf - 0.5, 0.0, S - 1.0)
    lift = jnp.where(t < lengthf, jnp.maximum(0.0, 1.0 - jnp.abs(spots - s)), 0.0)
    coarse = lift.astype(BF16)
    lift = jnp.concatenate([coarse, (lift - coarse.astype(F32)).astype(BF16)], 0)
    scale = 1.0 / (2.0 * lengthf)
    for m in range(SPAN // 2):
        lines = []
        for parity in range(2):
            h = 2 * m + parity
            spot = jnp.clip((2 * h + 1) * S - length, 0, (S - 1) * 2 * length)
            low = ((spot.astype(F32) + 0.5) * scale).astype(I32)
            part = (spot - low * 2 * length).astype(F32) * scale
            high = jnp.minimum(low + 1, S - 1)
            lines.append(((1.0 - part) * delta[low].astype(F32) + part * delta[high].astype(F32)).astype(BF16))
        patch = jnp.dot(lift, jnp.concatenate(lines, -1), preferred_element_type=F32)
        patch = (patch[:SPAN] + patch[SPAN:]).astype(BF16)
        for parity in range(2):
            row = row0 + 2 * m + parity
            dest = (row & (dims.stride - 1)) >> 1
            local = ((row >> dims.shift) << 1) + (row & 1)
            back[dest, local - first_local(row0, dest, dims)] = patch[:, parity * chans : (parity + 1) * chans]

    def leave(e):
        return pltpu.make_async_copy(back.at[e], sent.at[e], back_sems.at[e])

    for e in range(tiles):
        leave(e).start()
    for e in range(tiles):
        leave(e).wait()

    @pl.when(place < CAP)
    def _():
        pltpu.make_async_copy(delta, restored.at[place], sem.at[0]).wait()


def extra_kernel(
    dims, table, arrived, dec_w, one_w, two_w, dec_b, one_b, two_b, partial, restored,
    got, row_store, column_store, held, got_sems, tap_sems, raw, decoded, wide, inner, mixed, delta, sem,
):
    me = lax.axis_index("tile")
    row0 = table[ROW2, me]
    length = table[SIDE2, me]
    place = table[PLACE, me]

    def write(slot):
        copy = pltpu.make_async_copy(delta, restored.at[slot], sem.at[0])
        copy.start()
        copy.wait()

    @pl.when(length > 0)
    def _():
        scratch = (got, row_store, column_store, held, got_sems, tap_sems)
        arrival, taps = begin(dims, [arrived.at[s] for s in range(dims.tiles)], (dec_w, one_w, two_w), (dec_b, one_b, two_b), scratch)

        def leave(piece):
            rows = pl.ds(piece * PIECE, PIECE)
            return pltpu.make_async_copy(delta.at[rows], restored.at[1, rows], sem.at[piece])

        restore(
            dims, row0, length, arrival, lambda s: s, got, taps,
            raw, decoded, wide, inner, mixed, delta, lambda piece: leave(piece).start(),
        )
        for piece in range(S // PIECE):
            leave(piece).wait()

    @pl.when(length == 0)
    def _():
        delta[...] = jnp.zeros_like(delta)

        @pl.when(place != 0)
        def _():
            write(0)

        @pl.when(place != 1)
        def _():
            write(1)


def finish_kernel(
    dims, table, back, feat, above, below, weight, bias, finished,
    got, held, up, down, store, held_bias, lines, wide, canvas, out, sems, load_sems, tap_sems,
):
    me = lax.axis_index("tile")
    bands, chans, cols = dims.bands, dims.chans, dims.cols
    half = cols // 2
    taps = ColumnTaps(weight, bias, store, held_bias, tap_sems)
    patches = pltpu.make_async_copy(back, got, sems.at[0])
    patches.start()
    def from_feat(band):
        return pltpu.make_async_copy(feat.at[band], held.at[band], load_sems.at[0, band])

    def from_above(band):
        return pltpu.make_async_copy(above.at[band], up.at[band], load_sems.at[1, band])

    def from_below(band):
        return pltpu.make_async_copy(below.at[band], down.at[band], load_sems.at[2, band])

    taps.start()
    from_below(0).start()
    for j in range(bands):
        from_feat(j).start()
        from_above(j).start()
        if j + 1 < bands:
            from_below(j + 1).start()

    def leave(band):
        return pltpu.make_async_copy(out.at[band], finished.at[band], sems.at[1 + band])

    top = (me == 0).astype(I32)
    bottom = (me == dims.tiles - 1).astype(I32)
    edge = jnp.zeros((8, chans), F32)
    for k in range(lines.shape[0]):
        for a in range(4):
            lines[k, a, 0:8] = edge
            lines[k, a, 8 + cols :] = edge
    canvas[...] = jnp.zeros_like(canvas)
    patches.wait()

    @pl.loop(0, dims.tiles)
    def _(e):
        row0 = table[ROW, e]
        col0 = table[COL, e]
        length = table[SIDE, e]
        start = first_local(row0, me, dims)
        for i in range(dims.back_rows):
            local = start + i

            @pl.when((local < dims.local_rows) & (global_row(local, me, dims) - row0 < length))
            def _():
                canvas[local, pl.ds(col0, SPAN), :] += got[e, i].astype(F32)

    from_below(0).wait()
    taps.wait()

    def band(j, lines, wide):
        no_top = (top == 1) & (j == 0)
        no_bottom = (bottom == 1) & (j == bands - 1)
        over = up[jnp.maximum(j - top, 0)].astype(F32)
        under = down[jnp.minimum(j + bottom, bands - 1)].astype(F32)
        middle = slice(8, 8 + cols)
        lines[0, middle] = jnp.where(no_top, 0.0, over)
        lines[1, middle] = held[j, 0].astype(F32)
        lines[2, middle] = held[j, 1].astype(F32)
        lines[3, middle] = jnp.where(no_bottom, 0.0, under)
        for a in range(4):
            for b in range(4):
                wide[a, :, b * chans : (b + 1) * chans] = lines[a, pl.ds(7 + b, half, stride=2), :].astype(BF16)
        total = silu(column_pairs(wide, 0, 2, taps) + taps.bias())
        for i in range(2):
            part = total[i * half : (i + 1) * half]
            for b in range(2):
                here = lines[i + 1, pl.ds(8 + b, half, stride=2), :]
                decoded = (here + part[:, b * chans : (b + 1) * chans]).astype(BF16).astype(F32)
                at = pl.ds(b, half, stride=2)
                canvas[2 * j + i, at, :] = canvas[2 * j + i, at, :] + decoded
            out[j, i] = canvas[2 * j + i].astype(BF16)

    @pl.loop(0, bands // BANDS_AT_ONCE)
    def _(step):
        first = BANDS_AT_ONCE * step
        for k in range(BANDS_AT_ONCE):
            from_feat(first + k).wait()
            from_above(first + k).wait()
            if k + 1 < BANDS_AT_ONCE:
                from_below(first + k + 1).wait()

        @pl.when(first + BANDS_AT_ONCE < bands)
        def _():
            from_below(first + BANDS_AT_ONCE).wait()

        for k in range(BANDS_AT_ONCE):
            band(first + k, lines.at[k], wide.at[k])
        for k in range(BANDS_AT_ONCE):
            leave(first + k).start()

    for j in range(bands):
        leave(j).wait()


def shards(features, dec_weight, dec_bias, first_weight, first_bias, second_weight, second_bias, boxes, slots):
    tiles = lax.axis_size("tile")
    dims = Dims(features, tiles)
    bands, cols, chans, local_rows = dims.bands, dims.cols, dims.chans, dims.local_rows
    assert dims.band_rows == 2 and slots.shape[0] == CAP * tiles and boxes.shape[1] == tiles
    assert tiles & (tiles - 1) == 0

    smem = pl.BlockSpec(memory_space=pltpu.SMEM)
    hbm = pl.BlockSpec(memory_space=pl.ANY)
    full = pltpu.CompilerParams(vmem_limit_bytes=FULL_GRANT)
    dma = pltpu.SemaphoreType.DMA

    def cost(flops, moved):
        return pl.CostEstimate(flops=int(flops), bytes_accessed=int(moved), transcendentals=0)

    def shaped(*shape, kind=BF16):
        return jax.ShapeDtypeStruct(shape, kind)

    def swap(array):
        return lax.all_to_all(array, "tile", split_axis=0, concat_axis=0, tiled=True)

    pack_scratch = [
        pltpu.VMEM((bands, 2, cols, chans), BF16),
        pltpu.VMEM((local_rows, cols + 16, chans), F32),
        pltpu.VMEM((dims.rim, chans), F32),
        pltpu.VMEM((tiles, dims.message, chans), BF16),
        pltpu.VMEM((tiles, dims.message, chans), BF16),
        dma((4,)),
        dma((bands,)),
        dma((tiles,)),
    ]
    message = shaped(tiles, dims.message, chans)
    *sent_main, sent_extra, table, last, leading = pl.pallas_call(
        functools.partial(pack_kernel, dims),
        out_shape=[shaped(dims.message, chans)] * tiles
        + [message, shaped(7, tiles, kind=I32), shaped(bands, cols, chans), shaped(bands, cols, chans)],
        in_specs=[hbm, hbm, hbm],
        out_specs=[hbm] * (tiles + 1) + [smem, hbm, hbm],
        scratch_shapes=[
            pltpu.SMEM(boxes.shape, I32),
            pltpu.SMEM(slots.shape, I32),
            pltpu.SMEM((tiles,), I32),
            pltpu.SMEM((tiles,), I32),
            pltpu.SMEM((tiles + 1,), I32),
        ]
        + pack_scratch,
        compiler_params=full,
        cost_estimate=cost(0, 6e6),
        name="pack",
    )(boxes, slots, features)
    got_main = [sent_main[0]] + [None] * (tiles - 1)
    for s in [1] + sorted(range(2, tiles), key=lambda s: (-(s >> 1).bit_count(), -(s >> 1), s)):
        got_main[s] = lax.ppermute(sent_main[s], "tile", [(i, i ^ s) for i in range(tiles)])
    up = [(i, (i + 1) % tiles) for i in range(tiles)]
    above = lax.ppermute(last, "tile", up)
    below = lax.ppermute(leading, "tile", [(j, i) for i, j in up])

    got_extra = swap(sent_extra)

    weights = tuple(w.reshape(3, 3, chans, chans) for w in (dec_weight, first_weight, second_weight))
    biases = (dec_bias[None], first_bias[None], second_bias[None])
    restore_scratch = [
        pltpu.VMEM((tiles, dims.message, chans), BF16),
        pltpu.VMEM((4, 3, chans, 2 * chans), BF16),
        pltpu.VMEM((2, 3, 4, chans, 2 * chans), BF16),
        pltpu.VMEM((3, 1, chans), F32),
        dma((tiles,)),
        dma((3, 3)),
        pltpu.VMEM((SPAN // 2 + 2, 2, SPAN, 3 * chans), BF16),
        pltpu.VMEM((SPAN, SPAN, chans), F32),
        pltpu.VMEM((S + 2, S // 2, 4 * chans), BF16),
        pltpu.VMEM((S + 2, S // 2, 4 * chans), BF16),
        pltpu.VMEM((S, S, chans), F32),
        pltpu.VMEM((S, S, chans), BF16),
        dma((S // PIECE,)),
    ]
    restored_shape = shaped(CAP, S, S, chans)
    sent_back, partial = pl.pallas_call(
        functools.partial(main_kernel, dims),
        out_shape=[shaped(tiles, dims.back_rows, SPAN, chans), restored_shape],
        in_specs=[smem] + [hbm] * (tiles + 6),
        out_specs=[hbm, hbm],
        scratch_shapes=restore_scratch
        + [pltpu.VMEM((tiles, dims.back_rows, SPAN, chans), BF16), dma((tiles,))],
        compiler_params=pltpu.CompilerParams(vmem_limit_bytes=62 * 1024 * 1024),
        cost_estimate=cost(7e9, 8e6),
        name="restore_main",
    )(table, *got_main, *weights, *biases)
    got_back = swap(sent_back)

    restorations = pl.pallas_call(
        functools.partial(extra_kernel, dims),
        out_shape=restored_shape,
        in_specs=[smem] + [hbm] * 8,
        out_specs=hbm,
        scratch_shapes=restore_scratch,
        input_output_aliases={8: 0},
        compiler_params=full,
        cost_estimate=cost(6e9, 8e6),
        name="restore_extra",
    )(table, got_extra, *weights, *biases, partial)

    above, below, restorations = lax.optimization_barrier((above, below, restorations))
    assert bands % BANDS_AT_ONCE == 0
    finished = pl.pallas_call(
        functools.partial(finish_kernel, dims),
        out_shape=shaped(*features.shape),
        in_specs=[smem] + [hbm] * 6,
        out_specs=hbm,
        scratch_shapes=[
            pltpu.VMEM((tiles, dims.back_rows, SPAN, chans), BF16),
            pltpu.VMEM((bands, 2, cols, chans), BF16),
            pltpu.VMEM((bands, cols, chans), BF16),
            pltpu.VMEM((bands, cols, chans), BF16),
            pltpu.VMEM((3, 4, chans, 2 * chans), BF16),
            pltpu.VMEM((1, chans), F32),
            pltpu.VMEM((BANDS_AT_ONCE, 4, cols + 16, chans), F32),
            pltpu.VMEM((BANDS_AT_ONCE, 4, cols // 2, 4 * chans), BF16),
            pltpu.VMEM((local_rows, cols, chans), F32),
            pltpu.VMEM((bands, 2, cols, chans), BF16),
            dma((1 + bands,)),
            dma((3, bands)),
            dma((3,)),
        ],
        compiler_params=full,
        cost_estimate=cost(3e9, 6e6),
        name="finish",
    )(table, got_back, features, above, below, weights[0], biases[0])
    return finished, restorations


def solution(mesh):
    return jax.shard_map(
        shards,
        mesh=mesh,
        in_specs=(
            P("sess", "tile", None, None),
            P(),
            P(),
            P(),
            P(),
            P(),
            P(),
            P(None, "sess"),
            P("sess"),
        ),
        out_specs=(P("sess", "tile", None, None), P(("sess", "tile"), None, None, None)),
        check_vma=False,
    )
```

```python
import functools

import jax
import jax.numpy as jnp
from jax import lax
from jax.experimental import pallas as pl
from jax.experimental.pallas import tpu as pltpu
from jax.sharding import PartitionSpec as P

S = 64
UNIT = 12
NCLS = 3
CAP = 2
PIECE = 16
BANDS_AT_ONCE = 3
SPAN = UNIT * (NCLS + 1)
BF16 = jnp.bfloat16
F32 = jnp.float32
I32 = jnp.int32
FULL_GRANT = 66500000
ROW, COL, SIDE, ROW2, COL2, SIDE2, PLACE = range(7)


def rows_within(window, band_rows, stride):
    return band_rows * (window // stride) + min(band_rows, window % stride)


class Dims:
    def __init__(self, features, tiles):
        self.bands, self.band_rows, self.cols, self.chans = features.shape
        self.tiles = tiles
        self.stride = tiles * self.band_rows
        self.shift = self.stride.bit_length() - 1
        self.local_rows = self.bands * self.band_rows
        self.rows = rows_within(SPAN + 2, self.band_rows, self.stride)
        self.back_rows = rows_within(SPAN, self.band_rows, self.stride)
        self.rim = -(-2 * self.rows // 16) * 16
        self.message = self.rows * SPAN + self.rim


def first_local(row, tile, dims):
    return ((row >> dims.shift) << 1) + jnp.clip((row & (dims.stride - 1)) - 2 * tile, 0, 2)


def global_row(local, tile, dims):
    return ((local >> 1) << dims.shift) + 2 * tile + (local & 1)


def partner_order(tiles):
    far = sorted(range(3, tiles), key=lambda s: (-(s >> 1).bit_count(), s))
    return [0, 1, 2] + far


def partner(place, tiles):
    me = lax.axis_index("tile")
    other = jnp.int32(0)
    for k, s in enumerate(partner_order(tiles)):
        other = jnp.where(place == k, s, other)
    return me ^ other


def silu(v):
    half = 0.5 * v
    return half + half * jnp.tanh(half)


def both(bias):
    return jnp.concatenate([bias, bias], -1)


class RowTaps:
    def __init__(self, source, bias, store, held, sems):
        chans = source.shape[-1]
        self.store = store
        self.held = held
        self.copies = (
            pltpu.make_async_copy(bias, held, sems.at[2]),
            pltpu.make_async_copy(source, store.at[0:3, :, :, 0:chans], sems.at[0]),
            pltpu.make_async_copy(source, store.at[1:4, :, :, chans : 2 * chans], sems.at[1]),
        )

    def start(self):
        for copy in self.copies:
            copy.start()
        chans = self.store.shape[2]
        none = jnp.zeros((3, chans, chans), BF16)
        self.store[3, :, :, 0:chans] = none
        self.store[0, :, :, chans : 2 * chans] = none

    def wait(self):
        for copy in self.copies:
            copy.wait()

    def bias(self):
        return both(self.held[...])

    def value(self):
        return self.store[...].reshape(-1, self.store.shape[-1])


class ColumnTaps(RowTaps):
    def __init__(self, source, bias, store, held, sems):
        chans = source.shape[-1]
        self.store = store
        self.held = held
        self.copies = (
            pltpu.make_async_copy(bias, held, sems.at[2]),
            pltpu.make_async_copy(source, store.at[:, 0:3, :, 0:chans], sems.at[0]),
            pltpu.make_async_copy(source, store.at[:, 1:4, :, chans : 2 * chans], sems.at[1]),
        )

    def start(self):
        for copy in self.copies:
            copy.start()
        chans = self.store.shape[2]
        none = jnp.zeros((3, chans, chans), BF16)
        self.store[:, 3, :, 0:chans] = none
        self.store[:, 0, :, chans : 2 * chans] = none


def two_chains(wide, taps):
    wide = wide.reshape(-1, wide.shape[-1])
    weight = taps.value()
    middle = weight.shape[0] // 2
    one = jnp.dot(wide[:, :middle], weight[:middle], preferred_element_type=F32)
    two = jnp.dot(wide[:, middle:], weight[middle:], preferred_element_type=F32)
    return one + two


def row_pairs(src, first, count, taps):
    parts = [
        src[pl.ds(first, count), 0],
        src[pl.ds(first, count), 1],
        src[pl.ds(first + 1, count), 0],
        src[pl.ds(first + 1, count), 1],
    ]
    return two_chains(jnp.concatenate(parts, -1), taps)


def column_pairs(src, first, count, taps):
    return two_chains(jnp.concatenate([src[pl.ds(first + a, count)] for a in range(3)], -1), taps)


def fill_canvas(dims, feat, held, canvas, sems):
    def copy(band):
        return pltpu.make_async_copy(feat.at[band], held.at[band], sems.at[band])

    for band in range(dims.bands):
        copy(band).start()

    def finish():
        edge = jnp.zeros((8, dims.chans), F32)
        for band in range(dims.bands):
            copy(band).wait()
            for i in range(2):
                row = 2 * band + i
                canvas[row, 0:8, :] = edge
                canvas[row, 8 + dims.cols : 16 + dims.cols, :] = edge
                canvas[row, 8 : 8 + dims.cols, :] = held[band, i].astype(F32)

    return finish


def pack_crops(dims, table, row_at, col_at, canvas, rim, staged, worker):
    me = lax.axis_index("tile")
    rim[...] = jnp.zeros_like(rim)

    @pl.loop(0, dims.tiles)
    def _(s):
        w = worker(s)
        row0 = table[row_at, w]
        col0 = table[col_at, w]
        start = first_local(jnp.maximum(row0 - 1, 0), me, dims)
        for i in range(dims.rows):
            row = jnp.minimum(start + i, dims.local_rows - 1)
            staged[s, i * SPAN : (i + 1) * SPAN, :] = canvas[row, pl.ds(col0 + 8, SPAN), :].astype(BF16)
            rim[2 * i : 2 * i + 1, :] = canvas[row, pl.ds(col0 + 7, 1), :]
            rim[2 * i + 1 : 2 * i + 2, :] = canvas[row, pl.ds(col0 + 8 + SPAN, 1), :]
        staged[s, dims.rows * SPAN :, :] = rim[...].astype(BF16)


def pack_kernel(
    dims, boxes_in, slots_in, feat, *refs
):
    sent, refs = refs[: dims.tiles], refs[dims.tiles :]
    sent_extra, table, last, leading, boxes, slots, main, extra, seconds, held, canvas, rim, staged, staged_extra, sems, feat_sems, sent_sems = refs
    me = lax.axis_index("tile")
    copies = (
        pltpu.make_async_copy(boxes_in, boxes, sems.at[0]),
        pltpu.make_async_copy(slots_in, slots, sems.at[1]),
    )
    for copy in copies:
        copy.start()
    finish = fill_canvas(dims, feat, held, canvas, feat_sems)
    for copy in copies:
        copy.wait()

    def first_pass(w, count):
        one = slots[CAP * w]
        two = slots[CAP * w + 1]
        full = (one >= 0) & (two >= 0)
        second = jnp.where(full, two, -1)
        main[w] = jnp.where(one >= 0, one, two)
        extra[w] = second
        seconds[count] = second
        return count + full.astype(I32)

    lax.fori_loop(0, dims.tiles, first_pass, jnp.int32(0))

    def second_pass(w, count):
        own = main[w]
        idle = own < 0
        crop = jnp.where(idle, seconds[count], own)
        table[ROW, w] = boxes[0, crop]
        table[COL, w] = boxes[1, crop]
        table[SIDE, w] = UNIT * (boxes[2, crop] + 2)
        other = jnp.maximum(extra[w], 0)
        table[ROW2, w] = boxes[0, other]
        table[COL2, w] = boxes[1, other]
        table[SIDE2, w] = jnp.where(extra[w] >= 0, UNIT * (boxes[2, other] + 2), 0)
        table[PLACE, w] = jnp.where(idle, 2, jnp.where(slots[CAP * w] >= 0, 0, 1))
        return count + idle.astype(I32)

    lax.fori_loop(0, dims.tiles, second_pass, jnp.int32(0))
    finish()
    edges = (
        pltpu.make_async_copy(held.at[:, 1], last, sems.at[2]),
        pltpu.make_async_copy(held.at[:, 0], leading, sems.at[3]),
    )
    for edge in edges:
        edge.start()
    pack_crops(dims, table, ROW, COL, canvas, rim, staged, lambda s: partner(s, dims.tiles))
    copies = [pltpu.make_async_copy(staged.at[s], sent[s], sent_sems.at[s]) for s in range(dims.tiles)]
    for copy in copies:
        copy.start()
    pack_crops(dims, table, ROW2, COL2, canvas, rim, staged_extra, lambda s: s)
    later = pltpu.make_async_copy(staged_extra, sent_extra, sems.at[0])
    later.start()
    for copy in copies:
        copy.wait()
    later.wait()
    for edge in edges:
        edge.wait()


def restore(dims, row0, length, arrival, source, got, taps, raw, decoded, wide, inner, mixed, delta, finish):
    chans = dims.chans
    above = row0 - 1
    pairs = SPAN // 2
    half = S // 2
    nothing = jnp.zeros((SPAN, 3 * chans), BF16)
    raw[0, 0] = nothing
    raw[pairs, 1] = nothing
    empty = jnp.zeros((half, 4 * chans), BF16)
    for store in (wide, inner):
        store[0] = empty
        store[S + 1] = empty

    @pl.loop(0, dims.tiles)
    def _(s):
        arrival(s).wait()
        e = source(s)
        start = first_local(jnp.maximum(above, 0), e, dims)
        rim = got[s, dims.rows * SPAN :, :].astype(F32)
        at = lax.broadcasted_iota(I32, (SPAN, chans), 0)
        for i in range(dims.rows):
            local = start + i
            place = global_row(local, e, dims) - above
            place = jnp.where((local < dims.local_rows) & (place < SPAN + 2), place, SPAN + 2)
            line = got[s, i * SPAN : (i + 1) * SPAN, :]
            wider = line.astype(F32)
            left = jnp.where(at == 0, rim[2 * i : 2 * i + 1], pltpu.roll(wider, 1, 0))
            right = jnp.where(at == SPAN - 1, rim[2 * i + 1 : 2 * i + 2], pltpu.roll(wider, SPAN - 1, 0))
            raw[place >> 1, place & 1] = jnp.concatenate([left.astype(BF16), line, right.astype(BF16)], -1)

    taps[1].start()
    taps[2].start()
    taps[0].wait()
    n = 8
    for first in range(0, pairs, n):
        total = silu(row_pairs(raw, first, n, taps[0]) + taps[0].bias())
        for k in range(n):
            part = total[k * SPAN : (k + 1) * SPAN]
            at = 2 * (first + k)
            upper = raw[first + k, 1, :, chans : 2 * chans].astype(F32) + part[:, :chans]
            lower = raw[first + k + 1, 0, :, chans : 2 * chans].astype(F32) + part[:, chans:]
            decoded[at] = upper.astype(BF16).astype(F32)
            decoded[at + 1] = lower.astype(BF16).astype(F32)

    lengthf = length.astype(F32)
    block = lax.broadcasted_iota(I32, (4, half, SPAN), 0)
    t = 2 * lax.broadcasted_iota(I32, (4, half, SPAN), 1) + block - 1
    j = lax.broadcasted_iota(I32, (4, half, SPAN), 2).astype(F32)
    spots = jnp.clip((t.astype(F32) + 0.5) * lengthf / S - 0.5, 0.0, lengthf - 1.0)
    across = jnp.where((t >= 0) & (t < S), jnp.maximum(0.0, 1.0 - jnp.abs(spots - j)), 0.0)
    across = across.reshape(4 * half, SPAN).astype(BF16)
    taps[1].wait()
    taps[2].wait()
    for m in range(S // 2):
        lines = []
        for parity in range(2):
            s = 2 * m + parity
            spot = jnp.clip((2 * s + 1) * length - S, 0, (length - 1) * 2 * S)
            low = spot >> 7
            part = (spot & 127).astype(F32) * (1.0 / (2 * S))
            high = jnp.minimum(low + 1, SPAN - 1)
            lines.append(((1.0 - part) * decoded[low] + part * decoded[high]).astype(BF16))
        cells = jnp.dot(across, jnp.concatenate(lines, -1), preferred_element_type=F32).astype(BF16)
        for parity in range(2):
            at = 2 * m + parity + 1
            for b in range(4):
                wide[at, :, b * chans : (b + 1) * chans] = cells[
                    b * half : (b + 1) * half, parity * chans : (parity + 1) * chans
                ]

    n = PIECE
    for first in range(0, S, n):
        total = silu(column_pairs(wide, first, n, taps[1]) + taps[1].bias())
        at = lax.broadcasted_iota(I32, (n, half, chans), 1)
        even = pltpu.roll(total[:, :chans], n * half - 1, 0).reshape(n, half, chans)
        odd = pltpu.roll(total[:, chans:], 1, 0).reshape(n, half, chans)
        rows = pl.ds(first + 1, n)
        inner[rows, :, 0:chans] = jnp.where(at == 0, 0.0, odd).astype(BF16)
        inner[rows, :, chans : 3 * chans] = total.astype(BF16).reshape(n, half, 2 * chans)
        inner[rows, :, 3 * chans :] = jnp.where(at == half - 1, 0.0, even).astype(BF16)

    for first in range(0, S, n):
        total = column_pairs(inner, first, n, taps[2]) + taps[2].bias()
        for k in range(n):
            mixed[first + k, pl.ds(0, half, stride=2), :] = total[k * half : (k + 1) * half, :chans]
            mixed[first + k, pl.ds(1, half, stride=2), :] = total[k * half : (k + 1) * half, chans:]
        delta[first : first + n] = mixed[first : first + n].astype(BF16)
        finish(first // PIECE)


def begin(dims, arrived, weights, biases, scratch):
    got, row_store, column_store, held, got_sems, tap_sems = scratch

    def arrival(s):
        return pltpu.make_async_copy(arrived[0], got.at[s], got_sems.at[s])

    for s in range(dims.tiles):
        pltpu.make_async_copy(arrived[s], got.at[s], got_sems.at[s]).start()
    taps = (
        RowTaps(weights[0], biases[0], row_store, held.at[0], tap_sems.at[0]),
        ColumnTaps(weights[1], biases[1], column_store.at[0], held.at[1], tap_sems.at[1]),
        ColumnTaps(weights[2], biases[2], column_store.at[1], held.at[2], tap_sems.at[2]),
    )
    taps[0].start()
    return arrival, taps


def main_kernel(dims, table, *refs):
    tiles, chans = dims.tiles, dims.chans
    arrived, refs = refs[:tiles], refs[tiles:]
    (dec_w, one_w, two_w, dec_b, one_b, two_b, sent, restored, got, row_store, column_store, held) = refs[:12]
    got_sems, tap_sems, raw, decoded, wide, inner, mixed, delta, sem, back, back_sems = refs[12:]
    me = lax.axis_index("tile")
    row0 = table[ROW, me]
    length = table[SIDE, me]
    place = table[PLACE, me]
    scratch = (got, row_store, column_store, held, got_sems, tap_sems)
    arrival, taps = begin(dims, arrived, (dec_w, one_w, two_w), (dec_b, one_b, two_b), scratch)
    restore(
        dims, row0, length, arrival, lambda s: partner(s, tiles), got, taps,
        raw, decoded, wide, inner, mixed, delta, lambda piece: None,
    )

    @pl.when(place < CAP)
    def _():
        pltpu.make_async_copy(delta, restored.at[place], sem.at[0]).start()

    lengthf = length.astype(F32)
    t = lax.broadcasted_iota(I32, (SPAN, S), 0).astype(F32)
    s = lax.broadcasted_iota(I32, (SPAN, S), 1).astype(F32)
    spots = jnp.clip((t + 0.5) * S / lengthf - 0.5, 0.0, S - 1.0)
    lift = jnp.where(t < lengthf, jnp.maximum(0.0, 1.0 - jnp.abs(spots - s)), 0.0)
    coarse = lift.astype(BF16)
    lift = jnp.concatenate([coarse, (lift - coarse.astype(F32)).astype(BF16)], 0)
    scale = 1.0 / (2.0 * lengthf)
    group = 12

    @pl.loop(0, SPAN // 2 // group)
    def _(step):
        for k in range(group):
            lines = []
            for parity in range(2):
                h = 2 * (step * group + k) + parity
                spot = jnp.clip((2 * h + 1) * S - length, 0, (S - 1) * 2 * length)
                low = ((spot.astype(F32) + 0.5) * scale).astype(I32)
                part = (spot - low * 2 * length).astype(F32) * scale
                high = jnp.minimum(low + 1, S - 1)
                lines.append(((1.0 - part) * delta[low].astype(F32) + part * delta[high].astype(F32)).astype(BF16))
            patch = jnp.dot(lift, jnp.concatenate(lines, -1), preferred_element_type=F32)
            patch = (patch[:SPAN] + patch[SPAN:]).astype(BF16)
            for parity in range(2):
                row = row0 + 2 * (step * group + k) + parity
                dest = (row & (dims.stride - 1)) >> 1
                local = ((row >> dims.shift) << 1) + (row & 1)
                back[dest, local - first_local(row0, dest, dims)] = patch[:, parity * chans : (parity + 1) * chans]

    def leave(e):
        return pltpu.make_async_copy(back.at[e], sent.at[e], back_sems.at[e])

    for e in range(tiles):
        leave(e).start()
    for e in range(tiles):
        leave(e).wait()

    @pl.when(place < CAP)
    def _():
        pltpu.make_async_copy(delta, restored.at[place], sem.at[0]).wait()


def extra_kernel(
    dims, table, arrived, dec_w, one_w, two_w, dec_b, one_b, two_b, partial, restored,
    got, row_store, column_store, held, got_sems, tap_sems, raw, decoded, wide, inner, mixed, delta, sem,
):
    me = lax.axis_index("tile")
    row0 = table[ROW2, me]
    length = table[SIDE2, me]
    place = table[PLACE, me]

    def write(slot):
        copy = pltpu.make_async_copy(delta, restored.at[slot], sem.at[0])
        copy.start()
        copy.wait()

    @pl.when(length > 0)
    def _():
        scratch = (got, row_store, column_store, held, got_sems, tap_sems)
        arrival, taps = begin(dims, [arrived.at[s] for s in range(dims.tiles)], (dec_w, one_w, two_w), (dec_b, one_b, two_b), scratch)

        def leave(piece):
            rows = pl.ds(piece * PIECE, PIECE)
            return pltpu.make_async_copy(delta.at[rows], restored.at[1, rows], sem.at[piece])

        restore(
            dims, row0, length, arrival, lambda s: s, got, taps,
            raw, decoded, wide, inner, mixed, delta, lambda piece: leave(piece).start(),
        )
        for piece in range(S // PIECE):
            leave(piece).wait()

    @pl.when(length == 0)
    def _():
        delta[...] = jnp.zeros_like(delta)

        @pl.when(place != 0)
        def _():
            write(0)

        @pl.when(place != 1)
        def _():
            write(1)


def finish_kernel(
    dims, table, back, feat, above, below, weight, bias, finished,
    got, held, up, down, store, held_bias, lines, wide, canvas, out, sems, load_sems, tap_sems,
):
    me = lax.axis_index("tile")
    bands, chans, cols = dims.bands, dims.chans, dims.cols
    half = cols // 2
    taps = ColumnTaps(weight, bias, store, held_bias, tap_sems)
    patches = pltpu.make_async_copy(back, got, sems.at[0])
    patches.start()
    def from_feat(band):
        return pltpu.make_async_copy(feat.at[band], held.at[band], load_sems.at[0, band])

    def from_above(band):
        return pltpu.make_async_copy(above.at[band], up.at[band], load_sems.at[1, band])

    def from_below(band):
        return pltpu.make_async_copy(below.at[band], down.at[band], load_sems.at[2, band])

    taps.start()
    from_below(0).start()
    for j in range(bands):
        from_feat(j).start()
        from_above(j).start()
        if j + 1 < bands:
            from_below(j + 1).start()

    def leave(band):
        return pltpu.make_async_copy(out.at[band], finished.at[band], sems.at[1 + band])

    top = (me == 0).astype(I32)
    bottom = (me == dims.tiles - 1).astype(I32)
    edge = jnp.zeros((8, chans), F32)
    for k in range(lines.shape[0]):
        for a in range(4):
            lines[k, a, 0:8] = edge
            lines[k, a, 8 + cols :] = edge
    canvas[...] = jnp.zeros_like(canvas)
    patches.wait()

    @pl.loop(0, dims.tiles)
    def _(e):
        row0 = table[ROW, e]
        col0 = table[COL, e]
        length = table[SIDE, e]
        start = first_local(row0, me, dims)
        for i in range(dims.back_rows):
            local = start + i

            @pl.when((local < dims.local_rows) & (global_row(local, me, dims) - row0 < length))
            def _():
                canvas[local, pl.ds(col0, SPAN), :] += got[e, i].astype(F32)

    from_below(0).wait()
    taps.wait()

    def band(j, lines, wide):
        no_top = (top == 1) & (j == 0)
        no_bottom = (bottom == 1) & (j == bands - 1)
        over = up[jnp.maximum(j - top, 0)].astype(F32)
        under = down[jnp.minimum(j + bottom, bands - 1)].astype(F32)
        middle = slice(8, 8 + cols)
        lines[0, middle] = jnp.where(no_top, 0.0, over)
        lines[1, middle] = held[j, 0].astype(F32)
        lines[2, middle] = held[j, 1].astype(F32)
        lines[3, middle] = jnp.where(no_bottom, 0.0, under)
        for a in range(4):
            for b in range(4):
                wide[a, :, b * chans : (b + 1) * chans] = lines[a, pl.ds(7 + b, half, stride=2), :].astype(BF16)
        total = silu(column_pairs(wide, 0, 2, taps) + taps.bias())
        for i in range(2):
            part = total[i * half : (i + 1) * half]
            for b in range(2):
                here = lines[i + 1, pl.ds(8 + b, half, stride=2), :]
                decoded = (here + part[:, b * chans : (b + 1) * chans]).astype(BF16).astype(F32)
                at = pl.ds(b, half, stride=2)
                canvas[2 * j + i, at, :] = canvas[2 * j + i, at, :] + decoded
            out[j, i] = canvas[2 * j + i].astype(BF16)

    @pl.loop(0, bands // BANDS_AT_ONCE)
    def _(step):
        first = BANDS_AT_ONCE * step
        for k in range(BANDS_AT_ONCE):
            from_feat(first + k).wait()
            from_above(first + k).wait()
            if k + 1 < BANDS_AT_ONCE:
                from_below(first + k + 1).wait()

        @pl.when(first + BANDS_AT_ONCE < bands)
        def _():
            from_below(first + BANDS_AT_ONCE).wait()

        for k in range(BANDS_AT_ONCE):
            band(first + k, lines.at[k], wide.at[k])
        for k in range(BANDS_AT_ONCE):
            leave(first + k).start()

    for j in range(bands):
        leave(j).wait()


def shards(features, dec_weight, dec_bias, first_weight, first_bias, second_weight, second_bias, boxes, slots):
    tiles = lax.axis_size("tile")
    dims = Dims(features, tiles)
    bands, cols, chans, local_rows = dims.bands, dims.cols, dims.chans, dims.local_rows
    assert dims.band_rows == 2 and slots.shape[0] == CAP * tiles and boxes.shape[1] == tiles
    assert tiles & (tiles - 1) == 0

    smem = pl.BlockSpec(memory_space=pltpu.SMEM)
    hbm = pl.BlockSpec(memory_space=pl.ANY)
    full = pltpu.CompilerParams(vmem_limit_bytes=FULL_GRANT)
    dma = pltpu.SemaphoreType.DMA

    def cost(flops, moved):
        return pl.CostEstimate(flops=int(flops), bytes_accessed=int(moved), transcendentals=0)

    def shaped(*shape, kind=BF16):
        return jax.ShapeDtypeStruct(shape, kind)

    def swap(array):
        return lax.all_to_all(array, "tile", split_axis=0, concat_axis=0, tiled=True)

    pack_scratch = [
        pltpu.VMEM((bands, 2, cols, chans), BF16),
        pltpu.VMEM((local_rows, cols + 16, chans), F32),
        pltpu.VMEM((dims.rim, chans), F32),
        pltpu.VMEM((tiles, dims.message, chans), BF16),
        pltpu.VMEM((tiles, dims.message, chans), BF16),
        dma((4,)),
        dma((bands,)),
        dma((tiles,)),
    ]
    message = shaped(tiles, dims.message, chans)
    *sent_main, sent_extra, table, last, leading = pl.pallas_call(
        functools.partial(pack_kernel, dims),
        out_shape=[shaped(dims.message, chans)] * tiles
        + [message, shaped(7, tiles, kind=I32), shaped(bands, cols, chans), shaped(bands, cols, chans)],
        in_specs=[hbm, hbm, hbm],
        out_specs=[hbm] * (tiles + 1) + [smem, hbm, hbm],
        scratch_shapes=[
            pltpu.SMEM(boxes.shape, I32),
            pltpu.SMEM(slots.shape, I32),
            pltpu.SMEM((tiles,), I32),
            pltpu.SMEM((tiles,), I32),
            pltpu.SMEM((tiles + 1,), I32),
        ]
        + pack_scratch,
        compiler_params=full,
        cost_estimate=cost(0, 6e6),
        name="pack",
    )(boxes, slots, features)
    got_main = [
        lax.ppermute(message, "tile", [(i, i ^ s) for i in range(tiles)]) if s else message
        for s, message in zip(partner_order(tiles), sent_main)
    ]
    *got_main, sent_extra, last, leading = lax.optimization_barrier((*got_main, sent_extra, last, leading))
    up = [(i, (i + 1) % tiles) for i in range(tiles)]
    above = lax.ppermute(last, "tile", up)
    below = lax.ppermute(leading, "tile", [(j, i) for i, j in up])

    got_extra = swap(sent_extra)

    weights = tuple(w.reshape(3, 3, chans, chans) for w in (dec_weight, first_weight, second_weight))
    biases = (dec_bias[None], first_bias[None], second_bias[None])
    restore_scratch = [
        pltpu.VMEM((tiles, dims.message, chans), BF16),
        pltpu.VMEM((4, 3, chans, 2 * chans), BF16),
        pltpu.VMEM((2, 3, 4, chans, 2 * chans), BF16),
        pltpu.VMEM((3, 1, chans), F32),
        dma((tiles,)),
        dma((3, 3)),
        pltpu.VMEM((SPAN // 2 + 2, 2, SPAN, 3 * chans), BF16),
        pltpu.VMEM((SPAN, SPAN, chans), F32),
        pltpu.VMEM((S + 2, S // 2, 4 * chans), BF16),
        pltpu.VMEM((S + 2, S // 2, 4 * chans), BF16),
        pltpu.VMEM((S, S, chans), F32),
        pltpu.VMEM((S, S, chans), BF16),
        dma((S // PIECE,)),
    ]
    restored_shape = shaped(CAP, S, S, chans)
    sent_back, partial = pl.pallas_call(
        functools.partial(main_kernel, dims),
        out_shape=[shaped(tiles, dims.back_rows, SPAN, chans), restored_shape],
        in_specs=[smem] + [hbm] * (tiles + 6),
        out_specs=[hbm, hbm],
        scratch_shapes=restore_scratch
        + [pltpu.VMEM((tiles, dims.back_rows, SPAN, chans), BF16), dma((tiles,))],
        compiler_params=full,
        cost_estimate=cost(7e9, 8e6),
        name="restore_main",
    )(table, *got_main, *weights, *biases)
    got_back = swap(sent_back)

    restorations = pl.pallas_call(
        functools.partial(extra_kernel, dims),
        out_shape=restored_shape,
        in_specs=[smem] + [hbm] * 8,
        out_specs=hbm,
        scratch_shapes=restore_scratch,
        input_output_aliases={8: 0},
        compiler_params=full,
        cost_estimate=cost(6e9, 8e6),
        name="restore_extra",
    )(table, got_extra, *weights, *biases, partial)

    above, below, restorations = lax.optimization_barrier((above, below, restorations))
    assert bands % BANDS_AT_ONCE == 0
    finished = pl.pallas_call(
        functools.partial(finish_kernel, dims),
        out_shape=shaped(*features.shape),
        in_specs=[smem] + [hbm] * 6,
        out_specs=hbm,
        scratch_shapes=[
            pltpu.VMEM((tiles, dims.back_rows, SPAN, chans), BF16),
            pltpu.VMEM((bands, 2, cols, chans), BF16),
            pltpu.VMEM((bands, cols, chans), BF16),
            pltpu.VMEM((bands, cols, chans), BF16),
            pltpu.VMEM((3, 4, chans, 2 * chans), BF16),
            pltpu.VMEM((1, chans), F32),
            pltpu.VMEM((BANDS_AT_ONCE, 4, cols + 16, chans), F32),
            pltpu.VMEM((BANDS_AT_ONCE, 4, cols // 2, 4 * chans), BF16),
            pltpu.VMEM((local_rows, cols, chans), F32),
            pltpu.VMEM((bands, 2, cols, chans), BF16),
            dma((1 + bands,)),
            dma((3, bands)),
            dma((3,)),
        ],
        compiler_params=full,
        cost_estimate=cost(3e9, 6e6),
        name="finish",
    )(table, got_back, features, above, below, weights[0], biases[0])
    return finished, restorations


def solution(mesh):
    return jax.shard_map(
        shards,
        mesh=mesh,
        in_specs=(
            P("sess", "tile", None, None),
            P(),
            P(),
            P(),
            P(),
            P(),
            P(),
            P(None, "sess"),
            P("sess"),
        ),
        out_specs=(P("sess", "tile", None, None), P(("sess", "tile"), None, None, None)),
        check_vma=False,
    )
```

```python
import functools

import jax
import jax.numpy as jnp
from jax import lax
from jax.experimental import pallas as pl
from jax.experimental.pallas import tpu as pltpu
from jax.sharding import PartitionSpec as P

S = 64
UNIT = 12
NCLS = 3
CAP = 2
PIECE = 16
BANDS_AT_ONCE = 3
SPAN = UNIT * (NCLS + 1)
BF16 = jnp.bfloat16
F32 = jnp.float32
I32 = jnp.int32
FULL_GRANT = 66500000
ROW, COL, SIDE, ROW2, COL2, SIDE2, PLACE = range(7)


def rows_within(window, band_rows, stride):
    return band_rows * (window // stride) + min(band_rows, window % stride)


class Dims:
    def __init__(self, features, tiles):
        self.bands, self.band_rows, self.cols, self.chans = features.shape
        self.tiles = tiles
        self.stride = tiles * self.band_rows
        self.shift = self.stride.bit_length() - 1
        self.local_rows = self.bands * self.band_rows
        self.rows = rows_within(SPAN + 2, self.band_rows, self.stride)
        self.back_rows = rows_within(SPAN, self.band_rows, self.stride)
        self.rim = -(-2 * self.rows // 16) * 16
        self.message = self.rows * SPAN + self.rim


def first_local(row, tile, dims):
    return ((row >> dims.shift) << 1) + jnp.clip((row & (dims.stride - 1)) - 2 * tile, 0, 2)


def global_row(local, tile, dims):
    return ((local >> 1) << dims.shift) + 2 * tile + (local & 1)


def silu(v):
    half = 0.5 * v
    return half + half * jnp.tanh(half)


def both(bias):
    return jnp.concatenate([bias, bias], -1)


class RowTaps:
    def __init__(self, source, bias, store, held, sems):
        chans = source.shape[-1]
        self.store = store
        self.held = held
        self.copies = (
            pltpu.make_async_copy(bias, held, sems.at[2]),
            pltpu.make_async_copy(source, store.at[0:3, :, :, 0:chans], sems.at[0]),
            pltpu.make_async_copy(source, store.at[1:4, :, :, chans : 2 * chans], sems.at[1]),
        )

    def start(self):
        for copy in self.copies:
            copy.start()
        chans = self.store.shape[2]
        none = jnp.zeros((3, chans, chans), BF16)
        self.store[3, :, :, 0:chans] = none
        self.store[0, :, :, chans : 2 * chans] = none

    def wait(self):
        for copy in self.copies:
            copy.wait()

    def bias(self):
        return both(self.held[...])

    def value(self):
        return self.store[...].reshape(-1, self.store.shape[-1])


class ColumnTaps(RowTaps):
    def __init__(self, source, bias, store, held, sems):
        chans = source.shape[-1]
        self.store = store
        self.held = held
        self.copies = (
            pltpu.make_async_copy(bias, held, sems.at[2]),
            pltpu.make_async_copy(source, store.at[:, 0:3, :, 0:chans], sems.at[0]),
            pltpu.make_async_copy(source, store.at[:, 1:4, :, chans : 2 * chans], sems.at[1]),
        )

    def start(self):
        for copy in self.copies:
            copy.start()
        chans = self.store.shape[2]
        none = jnp.zeros((3, chans, chans), BF16)
        self.store[:, 3, :, 0:chans] = none
        self.store[:, 0, :, chans : 2 * chans] = none


def chains(wide, taps, count):
    weight = taps.value()
    depth = weight.shape[0] // count
    total = None
    for k in range(count):
        part = slice(k * depth, (k + 1) * depth)
        term = jnp.dot(wide[:, part], weight[part], preferred_element_type=F32)
        total = term if total is None else total + term
    return total


def row_pairs(src, first, count, taps):
    parts = [
        src[pl.ds(first, count), 0],
        src[pl.ds(first, count), 1],
        src[pl.ds(first + 1, count), 0],
        src[pl.ds(first + 1, count), 1],
    ]
    wide = jnp.concatenate(parts, -1)
    return chains(wide.reshape(-1, wide.shape[-1]), taps, 3)


def column_pairs(src, first, count, taps):
    wide = jnp.concatenate([src[pl.ds(first + a, count)] for a in range(3)], -1)
    return chains(wide.reshape(-1, wide.shape[-1]), taps, 3)


def fill_canvas(dims, feat, held, canvas, sems):
    def copy(band):
        return pltpu.make_async_copy(feat.at[band], held.at[band], sems.at[band])

    for band in range(dims.bands):
        copy(band).start()

    def finish():
        edge = jnp.zeros((8, dims.chans), F32)
        for band in range(dims.bands):
            copy(band).wait()
            for i in range(2):
                row = 2 * band + i
                canvas[row, 0:8, :] = edge
                canvas[row, 8 + dims.cols : 16 + dims.cols, :] = edge
                canvas[row, 8 : 8 + dims.cols, :] = held[band, i].astype(F32)

    return finish


def pack_crops(dims, table, row_at, col_at, canvas, rim, staged, partner):
    me = lax.axis_index("tile")
    rim[...] = jnp.zeros_like(rim)

    @pl.loop(0, dims.tiles)
    def _(s):
        w = partner(s)
        row0 = table[row_at, w]
        col0 = table[col_at, w]
        start = first_local(jnp.maximum(row0 - 1, 0), me, dims)
        for i in range(dims.rows):
            row = jnp.minimum(start + i, dims.local_rows - 1)
            staged[s, i * SPAN : (i + 1) * SPAN, :] = canvas[row, pl.ds(col0 + 8, SPAN), :].astype(BF16)
            rim[2 * i : 2 * i + 1, :] = canvas[row, pl.ds(col0 + 7, 1), :]
            rim[2 * i + 1 : 2 * i + 2, :] = canvas[row, pl.ds(col0 + 8 + SPAN, 1), :]
        staged[s, dims.rows * SPAN :, :] = rim[...].astype(BF16)


def pack_kernel(
    dims, boxes_in, slots_in, feat, *refs
):
    sent, refs = refs[: dims.tiles], refs[dims.tiles :]
    sent_extra, table, last, leading, boxes, slots, main, extra, seconds, held, canvas, rim, staged, staged_extra, sems, feat_sems, sent_sems = refs
    me = lax.axis_index("tile")
    copies = (
        pltpu.make_async_copy(boxes_in, boxes, sems.at[0]),
        pltpu.make_async_copy(slots_in, slots, sems.at[1]),
    )
    for copy in copies:
        copy.start()
    finish = fill_canvas(dims, feat, held, canvas, feat_sems)
    for copy in copies:
        copy.wait()

    def first_pass(w, count):
        one = slots[CAP * w]
        two = slots[CAP * w + 1]
        full = (one >= 0) & (two >= 0)
        second = jnp.where(full, two, -1)
        main[w] = jnp.where(one >= 0, one, two)
        extra[w] = second
        seconds[count] = second
        return count + full.astype(I32)

    lax.fori_loop(0, dims.tiles, first_pass, jnp.int32(0))

    def second_pass(w, count):
        own = main[w]
        idle = own < 0
        crop = jnp.where(idle, seconds[count], own)
        table[ROW, w] = boxes[0, crop]
        table[COL, w] = boxes[1, crop]
        table[SIDE, w] = UNIT * (boxes[2, crop] + 2)
        other = jnp.maximum(extra[w], 0)
        table[ROW2, w] = boxes[0, other]
        table[COL2, w] = boxes[1, other]
        table[SIDE2, w] = jnp.where(extra[w] >= 0, UNIT * (boxes[2, other] + 2), 0)
        table[PLACE, w] = jnp.where(idle, 2, jnp.where(slots[CAP * w] >= 0, 0, 1))
        return count + idle.astype(I32)

    lax.fori_loop(0, dims.tiles, second_pass, jnp.int32(0))
    finish()
    edges = (
        pltpu.make_async_copy(held.at[:, 1], last, sems.at[2]),
        pltpu.make_async_copy(held.at[:, 0], leading, sems.at[3]),
    )
    for edge in edges:
        edge.start()
    pack_crops(dims, table, ROW, COL, canvas, rim, staged, lambda s: me ^ s)
    copies = [pltpu.make_async_copy(staged.at[s], sent[s], sent_sems.at[s]) for s in range(dims.tiles)]
    for copy in copies:
        copy.start()
    pack_crops(dims, table, ROW2, COL2, canvas, rim, staged_extra, lambda s: s)
    later = pltpu.make_async_copy(staged_extra, sent_extra, sems.at[0])
    later.start()
    for copy in copies:
        copy.wait()
    later.wait()
    for edge in edges:
        edge.wait()


def restore(dims, row0, length, arrival, source, got, taps, raw, decoded, wide, inner, mixed, delta, finish):
    chans = dims.chans
    above = row0 - 1
    pairs = SPAN // 2
    half = S // 2
    nothing = jnp.zeros((SPAN, 3 * chans), BF16)
    raw[0, 0] = nothing
    raw[pairs, 1] = nothing
    empty = jnp.zeros((half, 4 * chans), BF16)
    for store in (wide, inner):
        store[0] = empty
        store[S + 1] = empty

    @pl.loop(0, dims.tiles)
    def _(s):
        arrival(s).wait()
        e = source(s)
        start = first_local(jnp.maximum(above, 0), e, dims)
        rim = got[s, dims.rows * SPAN :, :].astype(F32)
        at = lax.broadcasted_iota(I32, (SPAN, chans), 0)
        for i in range(dims.rows):
            local = start + i
            place = global_row(local, e, dims) - above
            place = jnp.where((local < dims.local_rows) & (place < SPAN + 2), place, SPAN + 2)
            line = got[s, i * SPAN : (i + 1) * SPAN, :]
            wider = line.astype(F32)
            left = jnp.where(at == 0, rim[2 * i : 2 * i + 1], pltpu.roll(wider, 1, 0))
            right = jnp.where(at == SPAN - 1, rim[2 * i + 1 : 2 * i + 2], pltpu.roll(wider, SPAN - 1, 0))
            raw[place >> 1, place & 1] = jnp.concatenate([left.astype(BF16), line, right.astype(BF16)], -1)

    lengthf = length.astype(F32)
    block = lax.broadcasted_iota(I32, (4, half, SPAN), 0)
    t = 2 * lax.broadcasted_iota(I32, (4, half, SPAN), 1) + block - 1
    j = lax.broadcasted_iota(I32, (4, half, SPAN), 2).astype(F32)
    spots = jnp.clip((t.astype(F32) + 0.5) * lengthf / S - 0.5, 0.0, lengthf - 1.0)
    across = jnp.where((t >= 0) & (t < S), jnp.maximum(0.0, 1.0 - jnp.abs(spots - j)), 0.0)
    across = across.reshape(4 * half, SPAN).astype(BF16)
    for tap in taps:
        tap.wait()
    n = PIECE

    def region(piece):
        first = piece * (n // 2)
        total = silu(row_pairs(raw, first, n // 2, taps[0]) + taps[0].bias())
        for k in range(n // 2):
            part = total[k * SPAN : (k + 1) * SPAN]
            at = 2 * (first + k)
            upper = raw[first + k, 1, :, chans : 2 * chans].astype(F32) + part[:, :chans]
            lower = raw[first + k + 1, 0, :, chans : 2 * chans].astype(F32) + part[:, chans:]
            decoded[at] = upper.astype(BF16).astype(F32)
            decoded[at + 1] = lower.astype(BF16).astype(F32)

    def resample(piece):
        for m in range(piece * (n // 2), (piece + 1) * (n // 2)):
            lines = []
            for parity in range(2):
                s = 2 * m + parity
                spot = jnp.clip((2 * s + 1) * length - S, 0, (length - 1) * 2 * S)
                low = spot >> 7
                part = (spot & 127).astype(F32) * (1.0 / (2 * S))
                high = jnp.minimum(low + 1, SPAN - 1)
                lines.append(((1.0 - part) * decoded[low] + part * decoded[high]).astype(BF16))
            cells = jnp.dot(across, jnp.concatenate(lines, -1), preferred_element_type=F32).astype(BF16)
            for parity in range(2):
                at = 2 * m + parity + 1
                for b in range(4):
                    wide[at, :, b * chans : (b + 1) * chans] = cells[
                        b * half : (b + 1) * half, parity * chans : (parity + 1) * chans
                    ]

    def first_conv(piece):
        first = piece * n
        total = silu(column_pairs(wide, first, n, taps[1]) + taps[1].bias())
        at = lax.broadcasted_iota(I32, (n, half, chans), 1)
        even = pltpu.roll(total[:, :chans], n * half - 1, 0).reshape(n, half, chans)
        odd = pltpu.roll(total[:, chans:], 1, 0).reshape(n, half, chans)
        rows = slice(first + 1, first + 1 + n)
        inner[rows, :, 0:chans] = jnp.where(at == 0, 0.0, odd).astype(BF16)
        inner[rows, :, chans : 3 * chans] = total.astype(BF16).reshape(n, half, 2 * chans)
        inner[rows, :, 3 * chans :] = jnp.where(at == half - 1, 0.0, even).astype(BF16)

    def second_conv(piece):
        first = piece * n
        total = column_pairs(inner, first, n, taps[2]) + taps[2].bias()
        for k in range(n):
            mixed[first + k, pl.ds(0, half, stride=2), :] = total[k * half : (k + 1) * half, :chans]
            mixed[first + k, pl.ds(1, half, stride=2), :] = total[k * half : (k + 1) * half, chans:]
        delta[first : first + n] = mixed[first : first + n].astype(BF16)

    stages = (
        [(region, 0), (resample, 0), (region, 1), (resample, 1), (first_conv, 0), (region, 2), (resample, 2)]
        + [(first_conv, 1), (second_conv, 0), (resample, 3), (first_conv, 2), (second_conv, 1), (first_conv, 3)]
        + [(second_conv, 2), (second_conv, 3)]
    )
    for stage, piece in stages:
        stage(piece)
        if stage is second_conv:
            finish(piece)


def begin(dims, arrived, weights, biases, scratch):
    got, row_store, column_store, held, got_sems, tap_sems = scratch

    def arrival(s):
        return pltpu.make_async_copy(arrived[0], got.at[s], got_sems.at[s])

    for s in range(dims.tiles):
        pltpu.make_async_copy(arrived[s], got.at[s], got_sems.at[s]).start()
    taps = (
        RowTaps(weights[0], biases[0], row_store, held.at[0], tap_sems.at[0]),
        ColumnTaps(weights[1], biases[1], column_store.at[0], held.at[1], tap_sems.at[1]),
        ColumnTaps(weights[2], biases[2], column_store.at[1], held.at[2], tap_sems.at[2]),
    )
    for tap in taps:
        tap.start()
    return arrival, taps


def main_kernel(dims, table, *refs):
    tiles, chans = dims.tiles, dims.chans
    arrived, refs = refs[:tiles], refs[tiles:]
    (dec_w, one_w, two_w, dec_b, one_b, two_b, sent, restored, got, row_store, column_store, held) = refs[:12]
    got_sems, tap_sems, raw, decoded, wide, inner, mixed, delta, sem, back, back_sems = refs[12:]
    me = lax.axis_index("tile")
    row0 = table[ROW, me]
    length = table[SIDE, me]
    place = table[PLACE, me]
    scratch = (got, row_store, column_store, held, got_sems, tap_sems)
    arrival, taps = begin(dims, arrived, (dec_w, one_w, two_w), (dec_b, one_b, two_b), scratch)
    restore(
        dims, row0, length, arrival, lambda s: me ^ s, got, taps,
        raw, decoded, wide, inner, mixed, delta, lambda piece: None,
    )

    @pl.when(place < CAP)
    def _():
        pltpu.make_async_copy(delta, restored.at[place], sem.at[0]).start()

    lengthf = length.astype(F32)
    t = lax.broadcasted_iota(I32, (SPAN, S), 0).astype(F32)
    s = lax.broadcasted_iota(I32, (SPAN, S), 1).astype(F32)
    spots = jnp.clip((t + 0.5) * S / lengthf - 0.5, 0.0, S - 1.0)
    lift = jnp.where(t < lengthf, jnp.maximum(0.0, 1.0 - jnp.abs(spots - s)), 0.0)
    coarse = lift.astype(BF16)
    lift = jnp.concatenate([coarse, (lift - coarse.astype(F32)).astype(BF16)], 0)
    scale = 1.0 / (2.0 * lengthf)
    group = 12

    @pl.loop(0, SPAN // 2 // group)
    def _(step):
        for k in range(group):
            lines = []
            for parity in range(2):
                h = 2 * (step * group + k) + parity
                spot = jnp.clip((2 * h + 1) * S - length, 0, (S - 1) * 2 * length)
                low = ((spot.astype(F32) + 0.5) * scale).astype(I32)
                part = (spot - low * 2 * length).astype(F32) * scale
                high = jnp.minimum(low + 1, S - 1)
                lines.append(((1.0 - part) * delta[low].astype(F32) + part * delta[high].astype(F32)).astype(BF16))
            patch = jnp.dot(lift, jnp.concatenate(lines, -1), preferred_element_type=F32)
            patch = (patch[:SPAN] + patch[SPAN:]).astype(BF16)
            for parity in range(2):
                row = row0 + 2 * (step * group + k) + parity
                dest = (row & (dims.stride - 1)) >> 1
                local = ((row >> dims.shift) << 1) + (row & 1)
                back[dest, local - first_local(row0, dest, dims)] = patch[:, parity * chans : (parity + 1) * chans]

    def leave(e):
        return pltpu.make_async_copy(back.at[e], sent.at[e], back_sems.at[e])

    for e in range(tiles):
        leave(e).start()
    for e in range(tiles):
        leave(e).wait()

    @pl.when(place < CAP)
    def _():
        pltpu.make_async_copy(delta, restored.at[place], sem.at[0]).wait()


def extra_kernel(
    dims, table, arrived, dec_w, one_w, two_w, dec_b, one_b, two_b, partial, restored,
    got, row_store, column_store, held, got_sems, tap_sems, raw, decoded, wide, inner, mixed, delta, sem,
):
    me = lax.axis_index("tile")
    row0 = table[ROW2, me]
    length = table[SIDE2, me]
    place = table[PLACE, me]

    def write(slot):
        copy = pltpu.make_async_copy(delta, restored.at[slot], sem.at[0])
        copy.start()
        copy.wait()

    @pl.when(length > 0)
    def _():
        scratch = (got, row_store, column_store, held, got_sems, tap_sems)
        arrival, taps = begin(dims, [arrived.at[s] for s in range(dims.tiles)], (dec_w, one_w, two_w), (dec_b, one_b, two_b), scratch)

        def leave(piece):
            rows = pl.ds(piece * PIECE, PIECE)
            return pltpu.make_async_copy(delta.at[rows], restored.at[1, rows], sem.at[piece])

        restore(
            dims, row0, length, arrival, lambda s: s, got, taps,
            raw, decoded, wide, inner, mixed, delta, lambda piece: leave(piece).start(),
        )
        for piece in range(S // PIECE):
            leave(piece).wait()

    @pl.when(length == 0)
    def _():
        delta[...] = jnp.zeros_like(delta)

        @pl.when(place != 0)
        def _():
            write(0)

        @pl.when(place != 1)
        def _():
            write(1)


def finish_kernel(
    dims, table, back, feat, above, below, weight, bias, finished,
    got, held, up, down, store, held_bias, lines, wide, canvas, out, sems, load_sems, tap_sems,
):
    me = lax.axis_index("tile")
    bands, chans, cols = dims.bands, dims.chans, dims.cols
    half = cols // 2
    taps = ColumnTaps(weight, bias, store, held_bias, tap_sems)
    patches = pltpu.make_async_copy(back, got, sems.at[0])
    patches.start()
    def from_feat(band):
        return pltpu.make_async_copy(feat.at[band], held.at[band], load_sems.at[0, band])

    def from_above(band):
        return pltpu.make_async_copy(above.at[band], up.at[band], load_sems.at[1, band])

    def from_below(band):
        return pltpu.make_async_copy(below.at[band], down.at[band], load_sems.at[2, band])

    taps.start()
    from_below(0).start()
    for j in range(bands):
        from_feat(j).start()
        from_above(j).start()
        if j + 1 < bands:
            from_below(j + 1).start()

    def leave(band):
        return pltpu.make_async_copy(out.at[band], finished.at[band], sems.at[1 + band])

    top = (me == 0).astype(I32)
    bottom = (me == dims.tiles - 1).astype(I32)
    edge = jnp.zeros((8, chans), F32)
    for k in range(lines.shape[0]):
        for a in range(4):
            lines[k, a, 0:8] = edge
            lines[k, a, 8 + cols :] = edge
    canvas[...] = jnp.zeros_like(canvas)
    patches.wait()

    @pl.loop(0, dims.tiles)
    def _(e):
        row0 = table[ROW, e]
        col0 = table[COL, e]
        length = table[SIDE, e]
        start = first_local(row0, me, dims)
        for i in range(dims.back_rows):
            local = start + i

            @pl.when((local < dims.local_rows) & (global_row(local, me, dims) - row0 < length))
            def _():
                canvas[local, pl.ds(col0, SPAN), :] += got[e, i].astype(F32)

    from_below(0).wait()
    taps.wait()

    def band(j, lines, wide):
        no_top = (top == 1) & (j == 0)
        no_bottom = (bottom == 1) & (j == bands - 1)
        over = up[jnp.maximum(j - top, 0)].astype(F32)
        under = down[jnp.minimum(j + bottom, bands - 1)].astype(F32)
        middle = slice(8, 8 + cols)
        lines[0, middle] = jnp.where(no_top, 0.0, over)
        lines[1, middle] = held[j, 0].astype(F32)
        lines[2, middle] = held[j, 1].astype(F32)
        lines[3, middle] = jnp.where(no_bottom, 0.0, under)
        for a in range(4):
            for b in range(4):
                wide[a, :, b * chans : (b + 1) * chans] = lines[a, pl.ds(7 + b, half, stride=2), :].astype(BF16)
        total = silu(column_pairs(wide, 0, 2, taps) + taps.bias())
        for i in range(2):
            part = total[i * half : (i + 1) * half]
            for b in range(2):
                here = lines[i + 1, pl.ds(8 + b, half, stride=2), :]
                decoded = (here + part[:, b * chans : (b + 1) * chans]).astype(BF16).astype(F32)
                at = pl.ds(b, half, stride=2)
                canvas[2 * j + i, at, :] = canvas[2 * j + i, at, :] + decoded
            out[j, i] = canvas[2 * j + i].astype(BF16)

    @pl.loop(0, bands // BANDS_AT_ONCE)
    def _(step):
        first = BANDS_AT_ONCE * step
        for k in range(BANDS_AT_ONCE):
            from_feat(first + k).wait()
            from_above(first + k).wait()
            if k + 1 < BANDS_AT_ONCE:
                from_below(first + k + 1).wait()

        @pl.when(first + BANDS_AT_ONCE < bands)
        def _():
            from_below(first + BANDS_AT_ONCE).wait()

        for k in range(BANDS_AT_ONCE):
            band(first + k, lines.at[k], wide.at[k])
        for k in range(BANDS_AT_ONCE):
            leave(first + k).start()

    for j in range(bands):
        leave(j).wait()


def shards(features, dec_weight, dec_bias, first_weight, first_bias, second_weight, second_bias, boxes, slots):
    tiles = lax.axis_size("tile")
    dims = Dims(features, tiles)
    bands, cols, chans, local_rows = dims.bands, dims.cols, dims.chans, dims.local_rows
    assert dims.band_rows == 2 and slots.shape[0] == CAP * tiles and boxes.shape[1] == tiles
    assert tiles & (tiles - 1) == 0

    smem = pl.BlockSpec(memory_space=pltpu.SMEM)
    hbm = pl.BlockSpec(memory_space=pl.ANY)
    full = pltpu.CompilerParams(vmem_limit_bytes=FULL_GRANT)
    dma = pltpu.SemaphoreType.DMA

    def cost(flops, moved):
        return pl.CostEstimate(flops=int(flops), bytes_accessed=int(moved), transcendentals=0)

    def shaped(*shape, kind=BF16):
        return jax.ShapeDtypeStruct(shape, kind)

    def swap(array):
        return lax.all_to_all(array, "tile", split_axis=0, concat_axis=0, tiled=True)

    pack_scratch = [
        pltpu.VMEM((bands, 2, cols, chans), BF16),
        pltpu.VMEM((local_rows, cols + 16, chans), F32),
        pltpu.VMEM((dims.rim, chans), F32),
        pltpu.VMEM((tiles, dims.message, chans), BF16),
        pltpu.VMEM((tiles, dims.message, chans), BF16),
        dma((4,)),
        dma((bands,)),
        dma((tiles,)),
    ]
    message = shaped(tiles, dims.message, chans)
    *sent_main, sent_extra, table, last, leading = pl.pallas_call(
        functools.partial(pack_kernel, dims),
        out_shape=[shaped(dims.message, chans)] * tiles
        + [message, shaped(7, tiles, kind=I32), shaped(bands, cols, chans), shaped(bands, cols, chans)],
        in_specs=[hbm, hbm, hbm],
        out_specs=[hbm] * (tiles + 1) + [smem, hbm, hbm],
        scratch_shapes=[
            pltpu.SMEM(boxes.shape, I32),
            pltpu.SMEM(slots.shape, I32),
            pltpu.SMEM((tiles,), I32),
            pltpu.SMEM((tiles,), I32),
            pltpu.SMEM((tiles + 1,), I32),
        ]
        + pack_scratch,
        compiler_params=full,
        cost_estimate=cost(0, 6e6),
        name="pack",
    )(boxes, slots, features)
    got_main = [sent_main[0]] + [None] * (tiles - 1)
    for s in [1] + sorted(range(2, tiles), key=lambda s: (-(s >> 1).bit_count(), -(s >> 1), s)):
        got_main[s] = lax.ppermute(sent_main[s], "tile", [(i, i ^ s) for i in range(tiles)])
    up = [(i, (i + 1) % tiles) for i in range(tiles)]
    above = lax.ppermute(last, "tile", up)
    below = lax.ppermute(leading, "tile", [(j, i) for i, j in up])

    got_extra = swap(sent_extra)

    weights = tuple(w.reshape(3, 3, chans, chans) for w in (dec_weight, first_weight, second_weight))
    biases = (dec_bias[None], first_bias[None], second_bias[None])
    restore_scratch = [
        pltpu.VMEM((tiles, dims.message, chans), BF16),
        pltpu.VMEM((4, 3, chans, 2 * chans), BF16),
        pltpu.VMEM((2, 3, 4, chans, 2 * chans), BF16),
        pltpu.VMEM((3, 1, chans), F32),
        dma((tiles,)),
        dma((3, 3)),
        pltpu.VMEM((SPAN // 2 + 2, 2, SPAN, 3 * chans), BF16),
        pltpu.VMEM((SPAN, SPAN, chans), F32),
        pltpu.VMEM((S + 2, S // 2, 4 * chans), BF16),
        pltpu.VMEM((S + 2, S // 2, 4 * chans), BF16),
        pltpu.VMEM((S, S, chans), F32),
        pltpu.VMEM((S, S, chans), BF16),
        dma((S // PIECE,)),
    ]
    restored_shape = shaped(CAP, S, S, chans)
    sent_back, partial = pl.pallas_call(
        functools.partial(main_kernel, dims),
        out_shape=[shaped(tiles, dims.back_rows, SPAN, chans), restored_shape],
        in_specs=[smem] + [hbm] * (tiles + 6),
        out_specs=[hbm, hbm],
        scratch_shapes=restore_scratch
        + [pltpu.VMEM((tiles, dims.back_rows, SPAN, chans), BF16), dma((tiles,))],
        compiler_params=full,
        cost_estimate=cost(7e9, 8e6),
        name="restore_main",
    )(table, *got_main, *weights, *biases)
    got_back = swap(sent_back)

    restorations = pl.pallas_call(
        functools.partial(extra_kernel, dims),
        out_shape=restored_shape,
        in_specs=[smem] + [hbm] * 8,
        out_specs=hbm,
        scratch_shapes=restore_scratch,
        input_output_aliases={8: 0},
        compiler_params=full,
        cost_estimate=cost(6e9, 8e6),
        name="restore_extra",
    )(table, got_extra, *weights, *biases, partial)

    above, below, restorations = lax.optimization_barrier((above, below, restorations))
    assert bands % BANDS_AT_ONCE == 0
    finished = pl.pallas_call(
        functools.partial(finish_kernel, dims),
        out_shape=shaped(*features.shape),
        in_specs=[smem] + [hbm] * 6,
        out_specs=hbm,
        scratch_shapes=[
            pltpu.VMEM((tiles, dims.back_rows, SPAN, chans), BF16),
            pltpu.VMEM((bands, 2, cols, chans), BF16),
            pltpu.VMEM((bands, cols, chans), BF16),
            pltpu.VMEM((bands, cols, chans), BF16),
            pltpu.VMEM((3, 4, chans, 2 * chans), BF16),
            pltpu.VMEM((1, chans), F32),
            pltpu.VMEM((BANDS_AT_ONCE, 4, cols + 16, chans), F32),
            pltpu.VMEM((BANDS_AT_ONCE, 4, cols // 2, 4 * chans), BF16),
            pltpu.VMEM((local_rows, cols, chans), F32),
            pltpu.VMEM((bands, 2, cols, chans), BF16),
            dma((1 + bands,)),
            dma((3, bands)),
            dma((3,)),
        ],
        compiler_params=full,
        cost_estimate=cost(3e9, 6e6),
        name="finish",
    )(table, got_back, features, above, below, weights[0], biases[0])
    return finished, restorations


def solution(mesh):
    return jax.shard_map(
        shards,
        mesh=mesh,
        in_specs=(
            P("sess", "tile", None, None),
            P(),
            P(),
            P(),
            P(),
            P(),
            P(),
            P(None, "sess"),
            P("sess"),
        ),
        out_specs=(P("sess", "tile", None, None), P(("sess", "tile"), None, None, None)),
        check_vma=False,
    )
```

```python
import functools

import jax
import jax.numpy as jnp
from jax import lax
from jax.experimental import pallas as pl
from jax.experimental.pallas import tpu as pltpu
from jax.sharding import PartitionSpec as P

S = 64
UNIT = 12
NCLS = 3
CAP = 2
PIECE = 16
BANDS_AT_ONCE = 3
SPAN = UNIT * (NCLS + 1)
BF16 = jnp.bfloat16
F32 = jnp.float32
I32 = jnp.int32
FULL_GRANT = 67000000
ROW, COL, SIDE, ROW2, COL2, SIDE2, PLACE = range(7)


def rows_within(window, band_rows, stride):
    return band_rows * (window // stride) + min(band_rows, window % stride)


class Dims:
    def __init__(self, features, tiles):
        self.bands, self.band_rows, self.cols, self.chans = features.shape
        self.tiles = tiles
        self.stride = tiles * self.band_rows
        self.shift = self.stride.bit_length() - 1
        self.local_rows = self.bands * self.band_rows
        self.rows = rows_within(SPAN + 2, self.band_rows, self.stride)
        self.back_rows = rows_within(SPAN, self.band_rows, self.stride)
        self.rim = -(-2 * self.rows // 16) * 16
        self.message = self.rows * SPAN + self.rim


def first_local(row, tile, dims):
    return ((row >> dims.shift) << 1) + jnp.clip((row & (dims.stride - 1)) - 2 * tile, 0, 2)


def global_row(local, tile, dims):
    return ((local >> 1) << dims.shift) + 2 * tile + (local & 1)


def silu(v):
    half = 0.5 * v
    return half + half * jnp.tanh(half)


def both(bias):
    return jnp.concatenate([bias, bias], -1)


class RowTaps:
    def __init__(self, source, bias, fetched, store, held, sems):
        self.fetched, self.store, self.held = fetched, store, held
        self.copies = (
            pltpu.make_async_copy(source, fetched, sems.at[0]),
            pltpu.make_async_copy(bias, held, sems.at[1]),
        )

    def start(self):
        for copy in self.copies:
            copy.start()

    def wait(self):
        for copy in self.copies:
            copy.wait()
        chans = self.store.shape[2]
        none = jnp.zeros((3, chans, chans), BF16)
        self.store[3, :, :, 0:chans] = none
        self.store[0, :, :, chans : 2 * chans] = none
        self.store[0:3, :, :, 0:chans] = self.fetched[...]
        self.store[1:4, :, :, chans : 2 * chans] = self.fetched[...]

    def bias(self):
        return both(self.held[...])

    def value(self):
        return self.store[...].reshape(-1, self.store.shape[-1])


class ColumnTaps(RowTaps):
    def wait(self):
        for copy in self.copies:
            copy.wait()
        chans = self.store.shape[2]
        none = jnp.zeros((3, chans, chans), BF16)
        self.store[:, 3, :, 0:chans] = none
        self.store[:, 0, :, chans : 2 * chans] = none
        self.store[:, 0:3, :, 0:chans] = self.fetched[...]
        self.store[:, 1:4, :, chans : 2 * chans] = self.fetched[...]


def two_chains(wide, taps):
    wide = wide.reshape(-1, wide.shape[-1])
    weight = taps.value()
    middle = weight.shape[0] // 2
    one = jnp.dot(wide[:, :middle], weight[:middle], preferred_element_type=F32)
    two = jnp.dot(wide[:, middle:], weight[middle:], preferred_element_type=F32)
    return one + two


def row_pairs(src, first, count, taps):
    parts = [
        src[pl.ds(first, count), 0],
        src[pl.ds(first, count), 1],
        src[pl.ds(first + 1, count), 0],
        src[pl.ds(first + 1, count), 1],
    ]
    return two_chains(jnp.concatenate(parts, -1), taps)


def column_pairs(src, first, count, taps):
    return two_chains(jnp.concatenate([src[pl.ds(first + a, count)] for a in range(3)], -1), taps)


def fill_canvas(dims, feat, held, canvas, sems):
    def copy(band):
        return pltpu.make_async_copy(feat.at[band], held.at[band], sems.at[band])

    for band in range(dims.bands):
        copy(band).start()

    def finish():
        edge = jnp.zeros((8, dims.chans), F32)
        for band in range(dims.bands):
            copy(band).wait()
            for i in range(2):
                row = 2 * band + i
                canvas[row, 0:8, :] = edge
                canvas[row, 8 + dims.cols : 16 + dims.cols, :] = edge
                canvas[row, 8 : 8 + dims.cols, :] = held[band, i].astype(F32)

    return finish


def pack_crops(dims, table, row_at, col_at, canvas, rim, staged, partner):
    me = lax.axis_index("tile")
    rim[...] = jnp.zeros_like(rim)

    @pl.loop(0, dims.tiles)
    def _(s):
        w = partner(s)
        row0 = table[row_at, w]
        col0 = table[col_at, w]
        start = first_local(jnp.maximum(row0 - 1, 0), me, dims)
        for i in range(dims.rows):
            row = jnp.minimum(start + i, dims.local_rows - 1)
            staged[s, i * SPAN : (i + 1) * SPAN, :] = canvas[row, pl.ds(col0 + 8, SPAN), :].astype(BF16)
            rim[2 * i : 2 * i + 1, :] = canvas[row, pl.ds(col0 + 7, 1), :]
            rim[2 * i + 1 : 2 * i + 2, :] = canvas[row, pl.ds(col0 + 8 + SPAN, 1), :]
        staged[s, dims.rows * SPAN :, :] = rim[...].astype(BF16)


def pack_kernel(
    dims, boxes_in, slots_in, feat, *refs
):
    sent, refs = refs[: dims.tiles], refs[dims.tiles :]
    sent_extra, table, last, leading, boxes, slots, main, extra, seconds, held, canvas, rim, staged, staged_extra, sems, feat_sems, sent_sems = refs
    me = lax.axis_index("tile")
    copies = (
        pltpu.make_async_copy(boxes_in, boxes, sems.at[0]),
        pltpu.make_async_copy(slots_in, slots, sems.at[1]),
    )
    for copy in copies:
        copy.start()
    finish = fill_canvas(dims, feat, held, canvas, feat_sems)
    for copy in copies:
        copy.wait()

    def first_pass(w, count):
        one = slots[CAP * w]
        two = slots[CAP * w + 1]
        full = (one >= 0) & (two >= 0)
        second = jnp.where(full, two, -1)
        main[w] = jnp.where(one >= 0, one, two)
        extra[w] = second
        seconds[count] = second
        return count + full.astype(I32)

    lax.fori_loop(0, dims.tiles, first_pass, jnp.int32(0))

    def second_pass(w, count):
        own = main[w]
        idle = own < 0
        crop = jnp.where(idle, seconds[count], own)
        table[ROW, w] = boxes[0, crop]
        table[COL, w] = boxes[1, crop]
        table[SIDE, w] = UNIT * (boxes[2, crop] + 2)
        other = jnp.maximum(extra[w], 0)
        table[ROW2, w] = boxes[0, other]
        table[COL2, w] = boxes[1, other]
        table[SIDE2, w] = jnp.where(extra[w] >= 0, UNIT * (boxes[2, other] + 2), 0)
        table[PLACE, w] = jnp.where(idle, 2, jnp.where(slots[CAP * w] >= 0, 0, 1))
        return count + idle.astype(I32)

    lax.fori_loop(0, dims.tiles, second_pass, jnp.int32(0))
    finish()
    edges = (
        pltpu.make_async_copy(held.at[:, 1], last, sems.at[2]),
        pltpu.make_async_copy(held.at[:, 0], leading, sems.at[3]),
    )
    for edge in edges:
        edge.start()
    pack_crops(dims, table, ROW, COL, canvas, rim, staged, lambda s: me ^ s)
    copies = [pltpu.make_async_copy(staged.at[s], sent[s], sent_sems.at[s]) for s in range(dims.tiles)]
    for copy in copies:
        copy.start()
    pack_crops(dims, table, ROW2, COL2, canvas, rim, staged_extra, lambda s: s)
    later = pltpu.make_async_copy(staged_extra, sent_extra, sems.at[0])
    later.start()
    for copy in copies:
        copy.wait()
    later.wait()
    for edge in edges:
        edge.wait()


def restore(dims, row0, length, arrival, source, got, taps, raw, decoded, wide, inner, mixed, delta, finish):
    chans = dims.chans
    above = row0 - 1
    pairs = SPAN // 2
    half = S // 2
    nothing = jnp.zeros((SPAN, 3 * chans), BF16)
    raw[0, 0] = nothing
    raw[pairs, 1] = nothing
    empty = jnp.zeros((half, 4 * chans), BF16)
    for store in (wide, inner):
        store[0] = empty
        store[S + 1] = empty

    @pl.loop(0, dims.tiles)
    def _(s):
        arrival(s).wait()
        e = source(s)
        start = first_local(jnp.maximum(above, 0), e, dims)
        rim = got[s, dims.rows * SPAN :, :].astype(F32)
        at = lax.broadcasted_iota(I32, (SPAN, chans), 0)
        for i in range(dims.rows):
            local = start + i
            place = global_row(local, e, dims) - above
            place = jnp.where((local < dims.local_rows) & (place < SPAN + 2), place, SPAN + 2)
            line = got[s, i * SPAN : (i + 1) * SPAN, :]
            wider = line.astype(F32)
            left = jnp.where(at == 0, rim[2 * i : 2 * i + 1], pltpu.roll(wider, 1, 0))
            right = jnp.where(at == SPAN - 1, rim[2 * i + 1 : 2 * i + 2], pltpu.roll(wider, SPAN - 1, 0))
            raw[place >> 1, place & 1] = jnp.concatenate([left.astype(BF16), line, right.astype(BF16)], -1)

    taps[1].start()
    taps[2].start()
    taps[0].wait()
    n = 8
    for first in range(0, pairs, n):
        total = silu(row_pairs(raw, first, n, taps[0]) + taps[0].bias())
        for k in range(n):
            part = total[k * SPAN : (k + 1) * SPAN]
            at = 2 * (first + k)
            upper = raw[first + k, 1, :, chans : 2 * chans].astype(F32) + part[:, :chans]
            lower = raw[first + k + 1, 0, :, chans : 2 * chans].astype(F32) + part[:, chans:]
            decoded[at] = upper.astype(BF16).astype(F32)
            decoded[at + 1] = lower.astype(BF16).astype(F32)

    lengthf = length.astype(F32)
    block = lax.broadcasted_iota(I32, (4, half, SPAN), 0)
    t = 2 * lax.broadcasted_iota(I32, (4, half, SPAN), 1) + block - 1
    j = lax.broadcasted_iota(I32, (4, half, SPAN), 2).astype(F32)
    spots = jnp.clip((t.astype(F32) + 0.5) * lengthf / S - 0.5, 0.0, lengthf - 1.0)
    across = jnp.where((t >= 0) & (t < S), jnp.maximum(0.0, 1.0 - jnp.abs(spots - j)), 0.0)
    across = across.reshape(4 * half, SPAN).astype(BF16)
    taps[1].wait()
    taps[2].wait()
    for m in range(S // 2):
        lines = []
        for parity in range(2):
            s = 2 * m + parity
            spot = jnp.clip((2 * s + 1) * length - S, 0, (length - 1) * 2 * S)
            low = spot >> 7
            part = (spot & 127).astype(F32) * (1.0 / (2 * S))
            high = jnp.minimum(low + 1, SPAN - 1)
            lines.append(((1.0 - part) * decoded[low] + part * decoded[high]).astype(BF16))
        cells = jnp.dot(across, jnp.concatenate(lines, -1), preferred_element_type=F32).astype(BF16)
        for parity in range(2):
            at = 2 * m + parity + 1
            for b in range(4):
                wide[at, :, b * chans : (b + 1) * chans] = cells[
                    b * half : (b + 1) * half, parity * chans : (parity + 1) * chans
                ]

    n = PIECE
    for first in range(0, S, n):
        total = silu(column_pairs(wide, first, n, taps[1]) + taps[1].bias())
        at = lax.broadcasted_iota(I32, (n, half, chans), 1)
        even = pltpu.roll(total[:, :chans], n * half - 1, 0).reshape(n, half, chans)
        odd = pltpu.roll(total[:, chans:], 1, 0).reshape(n, half, chans)
        rows = pl.ds(first + 1, n)
        inner[rows, :, 0:chans] = jnp.where(at == 0, 0.0, odd).astype(BF16)
        inner[rows, :, chans : 3 * chans] = total.astype(BF16).reshape(n, half, 2 * chans)
        inner[rows, :, 3 * chans :] = jnp.where(at == half - 1, 0.0, even).astype(BF16)

    for first in range(0, S, n):
        total = column_pairs(inner, first, n, taps[2]) + taps[2].bias()
        for k in range(n):
            mixed[first + k, pl.ds(0, half, stride=2), :] = total[k * half : (k + 1) * half, :chans]
            mixed[first + k, pl.ds(1, half, stride=2), :] = total[k * half : (k + 1) * half, chans:]
        delta[first : first + n] = mixed[first : first + n].astype(BF16)
        finish(first // PIECE)


def begin(dims, arrived, weights, biases, scratch):
    got, fetched, row_store, column_store, held, got_sems, tap_sems = scratch

    def arrival(s):
        return pltpu.make_async_copy(arrived[0], got.at[s], got_sems.at[s])

    for s in range(dims.tiles):
        pltpu.make_async_copy(arrived[s], got.at[s], got_sems.at[s]).start()
    taps = (
        RowTaps(weights[0], biases[0], fetched.at[0], row_store, held.at[0], tap_sems.at[0]),
        ColumnTaps(weights[1], biases[1], fetched.at[1], column_store.at[0], held.at[1], tap_sems.at[1]),
        ColumnTaps(weights[2], biases[2], fetched.at[2], column_store.at[1], held.at[2], tap_sems.at[2]),
    )
    taps[0].start()
    return arrival, taps


def main_kernel(dims, table, *refs):
    tiles, chans = dims.tiles, dims.chans
    arrived, refs = refs[:tiles], refs[tiles:]
    (dec_w, one_w, two_w, dec_b, one_b, two_b, sent, restored, got, fetched, row_store, column_store, held) = refs[:13]
    got_sems, tap_sems, raw, decoded, wide, inner, mixed, delta, sem, back, back_sems = refs[13:]
    me = lax.axis_index("tile")
    row0 = table[ROW, me]
    length = table[SIDE, me]
    place = table[PLACE, me]
    scratch = (got, fetched, row_store, column_store, held, got_sems, tap_sems)
    arrival, taps = begin(dims, arrived, (dec_w, one_w, two_w), (dec_b, one_b, two_b), scratch)
    restore(
        dims, row0, length, arrival, lambda s: me ^ s, got, taps,
        raw, decoded, wide, inner, mixed, delta, lambda piece: None,
    )

    @pl.when(place < CAP)
    def _():
        pltpu.make_async_copy(delta, restored.at[place], sem.at[0]).start()

    lengthf = length.astype(F32)
    t = lax.broadcasted_iota(I32, (SPAN, S), 0).astype(F32)
    s = lax.broadcasted_iota(I32, (SPAN, S), 1).astype(F32)
    spots = jnp.clip((t + 0.5) * S / lengthf - 0.5, 0.0, S - 1.0)
    lift = jnp.where(t < lengthf, jnp.maximum(0.0, 1.0 - jnp.abs(spots - s)), 0.0)
    coarse = lift.astype(BF16)
    lift = jnp.concatenate([coarse, (lift - coarse.astype(F32)).astype(BF16)], 0)
    scale = 1.0 / (2.0 * lengthf)
    group = 12

    @pl.loop(0, SPAN // 2 // group)
    def _(step):
        for k in range(group):
            lines = []
            for parity in range(2):
                h = 2 * (step * group + k) + parity
                spot = jnp.clip((2 * h + 1) * S - length, 0, (S - 1) * 2 * length)
                low = ((spot.astype(F32) + 0.5) * scale).astype(I32)
                part = (spot - low * 2 * length).astype(F32) * scale
                high = jnp.minimum(low + 1, S - 1)
                lines.append(((1.0 - part) * delta[low].astype(F32) + part * delta[high].astype(F32)).astype(BF16))
            patch = jnp.dot(lift, jnp.concatenate(lines, -1), preferred_element_type=F32)
            patch = (patch[:SPAN] + patch[SPAN:]).astype(BF16)
            for parity in range(2):
                row = row0 + 2 * (step * group + k) + parity
                dest = (row & (dims.stride - 1)) >> 1
                local = ((row >> dims.shift) << 1) + (row & 1)
                back[dest, local - first_local(row0, dest, dims)] = patch[:, parity * chans : (parity + 1) * chans]

    def leave(e):
        return pltpu.make_async_copy(back.at[e], sent.at[e], back_sems.at[e])

    for e in range(tiles):
        leave(e).start()
    for e in range(tiles):
        leave(e).wait()

    @pl.when(place < CAP)
    def _():
        pltpu.make_async_copy(delta, restored.at[place], sem.at[0]).wait()


def extra_kernel(
    dims, table, arrived, dec_w, one_w, two_w, dec_b, one_b, two_b, partial, restored,
    got, fetched, row_store, column_store, held, got_sems, tap_sems, raw, decoded, wide, inner, mixed, delta, sem,
):
    me = lax.axis_index("tile")
    row0 = table[ROW2, me]
    length = table[SIDE2, me]
    place = table[PLACE, me]

    def write(slot):
        copy = pltpu.make_async_copy(delta, restored.at[slot], sem.at[0])
        copy.start()
        copy.wait()

    @pl.when(length > 0)
    def _():
        scratch = (got, fetched, row_store, column_store, held, got_sems, tap_sems)
        arrival, taps = begin(dims, [arrived.at[s] for s in range(dims.tiles)], (dec_w, one_w, two_w), (dec_b, one_b, two_b), scratch)

        def leave(piece):
            rows = pl.ds(piece * PIECE, PIECE)
            return pltpu.make_async_copy(delta.at[rows], restored.at[1, rows], sem.at[piece])

        restore(
            dims, row0, length, arrival, lambda s: s, got, taps,
            raw, decoded, wide, inner, mixed, delta, lambda piece: leave(piece).start(),
        )
        for piece in range(S // PIECE):
            leave(piece).wait()

    @pl.when(length == 0)
    def _():
        delta[...] = jnp.zeros_like(delta)

        @pl.when(place != 0)
        def _():
            write(0)

        @pl.when(place != 1)
        def _():
            write(1)


def finish_kernel(
    dims, table, back, feat, above, below, weight, bias, finished,
    got, held, up, down, fetched, store, held_bias, lines, wide, canvas, out, sems, load_sems, tap_sems,
):
    me = lax.axis_index("tile")
    bands, chans, cols = dims.bands, dims.chans, dims.cols
    half = cols // 2
    taps = ColumnTaps(weight, bias, fetched, store, held_bias, tap_sems)
    patches = pltpu.make_async_copy(back, got, sems.at[0])
    patches.start()
    def from_feat(band):
        return pltpu.make_async_copy(feat.at[band], held.at[band], load_sems.at[0, band])

    def from_above(band):
        return pltpu.make_async_copy(above.at[band], up.at[band], load_sems.at[1, band])

    def from_below(band):
        return pltpu.make_async_copy(below.at[band], down.at[band], load_sems.at[2, band])

    taps.start()
    from_below(0).start()
    for j in range(bands):
        from_feat(j).start()
        from_above(j).start()
        if j + 1 < bands:
            from_below(j + 1).start()

    def leave(band):
        return pltpu.make_async_copy(out.at[band], finished.at[band], sems.at[1 + band])

    top = (me == 0).astype(I32)
    bottom = (me == dims.tiles - 1).astype(I32)
    edge = jnp.zeros((8, chans), F32)
    for k in range(lines.shape[0]):
        for a in range(4):
            lines[k, a, 0:8] = edge
            lines[k, a, 8 + cols :] = edge
    canvas[...] = jnp.zeros_like(canvas)
    patches.wait()

    @pl.loop(0, dims.tiles)
    def _(e):
        row0 = table[ROW, e]
        col0 = table[COL, e]
        length = table[SIDE, e]
        start = first_local(row0, me, dims)
        for i in range(dims.back_rows):
            local = start + i

            @pl.when((local < dims.local_rows) & (global_row(local, me, dims) - row0 < length))
            def _():
                canvas[local, pl.ds(col0, SPAN), :] += got[e, i].astype(F32)

    from_below(0).wait()
    taps.wait()

    def band(j, lines, wide):
        no_top = (top == 1) & (j == 0)
        no_bottom = (bottom == 1) & (j == bands - 1)
        over = up[jnp.maximum(j - top, 0)].astype(F32)
        under = down[jnp.minimum(j + bottom, bands - 1)].astype(F32)
        middle = slice(8, 8 + cols)
        lines[0, middle] = jnp.where(no_top, 0.0, over)
        lines[1, middle] = held[j, 0].astype(F32)
        lines[2, middle] = held[j, 1].astype(F32)
        lines[3, middle] = jnp.where(no_bottom, 0.0, under)
        for a in range(4):
            for b in range(4):
                wide[a, :, b * chans : (b + 1) * chans] = lines[a, pl.ds(7 + b, half, stride=2), :].astype(BF16)
        total = silu(column_pairs(wide, 0, 2, taps) + taps.bias())
        for i in range(2):
            part = total[i * half : (i + 1) * half]
            for b in range(2):
                here = lines[i + 1, pl.ds(8 + b, half, stride=2), :]
                decoded = (here + part[:, b * chans : (b + 1) * chans]).astype(BF16).astype(F32)
                at = pl.ds(b, half, stride=2)
                canvas[2 * j + i, at, :] = canvas[2 * j + i, at, :] + decoded
            out[j, i] = canvas[2 * j + i].astype(BF16)

    @pl.loop(0, bands // BANDS_AT_ONCE)
    def _(step):
        first = BANDS_AT_ONCE * step
        for k in range(BANDS_AT_ONCE):
            from_feat(first + k).wait()
            from_above(first + k).wait()
            if k + 1 < BANDS_AT_ONCE:
                from_below(first + k + 1).wait()

        @pl.when(first + BANDS_AT_ONCE < bands)
        def _():
            from_below(first + BANDS_AT_ONCE).wait()

        for k in range(BANDS_AT_ONCE):
            band(first + k, lines.at[k], wide.at[k])
        for k in range(BANDS_AT_ONCE):
            leave(first + k).start()

    for j in range(bands):
        leave(j).wait()


def shards(features, dec_weight, dec_bias, first_weight, first_bias, second_weight, second_bias, boxes, slots):
    tiles = lax.axis_size("tile")
    dims = Dims(features, tiles)
    bands, cols, chans, local_rows = dims.bands, dims.cols, dims.chans, dims.local_rows
    assert dims.band_rows == 2 and slots.shape[0] == CAP * tiles and boxes.shape[1] == tiles
    assert tiles & (tiles - 1) == 0

    smem = pl.BlockSpec(memory_space=pltpu.SMEM)
    hbm = pl.BlockSpec(memory_space=pl.ANY)
    full = pltpu.CompilerParams(vmem_limit_bytes=FULL_GRANT)
    dma = pltpu.SemaphoreType.DMA

    def cost(flops, moved):
        return pl.CostEstimate(flops=int(flops), bytes_accessed=int(moved), transcendentals=0)

    def shaped(*shape, kind=BF16):
        return jax.ShapeDtypeStruct(shape, kind)

    def swap(array):
        return lax.all_to_all(array, "tile", split_axis=0, concat_axis=0, tiled=True)

    pack_scratch = [
        pltpu.VMEM((bands, 2, cols, chans), BF16),
        pltpu.VMEM((local_rows, cols + 16, chans), F32),
        pltpu.VMEM((dims.rim, chans), F32),
        pltpu.VMEM((tiles, dims.message, chans), BF16),
        pltpu.VMEM((tiles, dims.message, chans), BF16),
        dma((4,)),
        dma((bands,)),
        dma((tiles,)),
    ]
    message = shaped(tiles, dims.message, chans)
    *sent_main, sent_extra, table, last, leading = pl.pallas_call(
        functools.partial(pack_kernel, dims),
        out_shape=[shaped(dims.message, chans)] * tiles
        + [message, shaped(7, tiles, kind=I32), shaped(bands, cols, chans), shaped(bands, cols, chans)],
        in_specs=[hbm, hbm, hbm],
        out_specs=[hbm] * (tiles + 1) + [smem, hbm, hbm],
        scratch_shapes=[
            pltpu.SMEM(boxes.shape, I32),
            pltpu.SMEM(slots.shape, I32),
            pltpu.SMEM((tiles,), I32),
            pltpu.SMEM((tiles,), I32),
            pltpu.SMEM((tiles + 1,), I32),
        ]
        + pack_scratch,
        compiler_params=full,
        cost_estimate=cost(0, 6e6),
        name="pack",
    )(boxes, slots, features)
    got_main = [sent_main[0]] + [None] * (tiles - 1)
    for s in [1] + sorted(range(2, tiles), key=lambda s: (-(s >> 1).bit_count(), -(s >> 1), s)):
        got_main[s] = lax.ppermute(sent_main[s], "tile", [(i, i ^ s) for i in range(tiles)])
    up = [(i, (i + 1) % tiles) for i in range(tiles)]
    above = lax.ppermute(last, "tile", up)
    below = lax.ppermute(leading, "tile", [(j, i) for i, j in up])

    got_extra = swap(sent_extra)

    weights = tuple(w.reshape(3, 3, chans, chans) for w in (dec_weight, first_weight, second_weight))
    biases = (dec_bias[None], first_bias[None], second_bias[None])
    restore_scratch = [
        pltpu.VMEM((tiles, dims.message, chans), BF16),
        pltpu.VMEM((3, 3, 3, chans, chans), BF16),
        pltpu.VMEM((4, 3, chans, 2 * chans), BF16),
        pltpu.VMEM((2, 3, 4, chans, 2 * chans), BF16),
        pltpu.VMEM((3, 1, chans), F32),
        dma((tiles,)),
        dma((3, 2)),
        pltpu.VMEM((SPAN // 2 + 2, 2, SPAN, 3 * chans), BF16),
        pltpu.VMEM((SPAN, SPAN, chans), F32),
        pltpu.VMEM((S + 2, S // 2, 4 * chans), BF16),
        pltpu.VMEM((S + 2, S // 2, 4 * chans), BF16),
        pltpu.VMEM((S, S, chans), F32),
        pltpu.VMEM((S, S, chans), BF16),
        dma((S // PIECE,)),
    ]
    restored_shape = shaped(CAP, S, S, chans)
    sent_back, partial = pl.pallas_call(
        functools.partial(main_kernel, dims),
        out_shape=[shaped(tiles, dims.back_rows, SPAN, chans), restored_shape],
        in_specs=[smem] + [hbm] * (tiles + 6),
        out_specs=[hbm, hbm],
        scratch_shapes=restore_scratch
        + [pltpu.VMEM((tiles, dims.back_rows, SPAN, chans), BF16), dma((tiles,))],
        compiler_params=full,
        cost_estimate=cost(7e9, 8e6),
        name="restore_main",
    )(table, *got_main, *weights, *biases)
    got_back = swap(sent_back)

    restorations = pl.pallas_call(
        functools.partial(extra_kernel, dims),
        out_shape=restored_shape,
        in_specs=[smem] + [hbm] * 8,
        out_specs=hbm,
        scratch_shapes=restore_scratch,
        input_output_aliases={8: 0},
        compiler_params=full,
        cost_estimate=cost(6e9, 8e6),
        name="restore_extra",
    )(table, got_extra, *weights, *biases, partial)

    above, below, restorations = lax.optimization_barrier((above, below, restorations))
    assert bands % BANDS_AT_ONCE == 0
    finished = pl.pallas_call(
        functools.partial(finish_kernel, dims),
        out_shape=shaped(*features.shape),
        in_specs=[smem] + [hbm] * 6,
        out_specs=hbm,
        scratch_shapes=[
            pltpu.VMEM((tiles, dims.back_rows, SPAN, chans), BF16),
            pltpu.VMEM((bands, 2, cols, chans), BF16),
            pltpu.VMEM((bands, cols, chans), BF16),
            pltpu.VMEM((bands, cols, chans), BF16),
            pltpu.VMEM((3, 3, chans, chans), BF16),
            pltpu.VMEM((3, 4, chans, 2 * chans), BF16),
            pltpu.VMEM((1, chans), F32),
            pltpu.VMEM((BANDS_AT_ONCE, 4, cols + 16, chans), F32),
            pltpu.VMEM((BANDS_AT_ONCE, 4, cols // 2, 4 * chans), BF16),
            pltpu.VMEM((local_rows, cols, chans), F32),
            pltpu.VMEM((bands, 2, cols, chans), BF16),
            dma((1 + bands,)),
            dma((3, bands)),
            dma((2,)),
        ],
        compiler_params=full,
        cost_estimate=cost(3e9, 6e6),
        name="finish",
    )(table, got_back, features, above, below, weights[0], biases[0])
    return finished, restorations


def solution(mesh):
    return jax.shard_map(
        shards,
        mesh=mesh,
        in_specs=(
            P("sess", "tile", None, None),
            P(),
            P(),
            P(),
            P(),
            P(),
            P(),
            P(None, "sess"),
            P("sess"),
        ),
        out_specs=(P("sess", "tile", None, None), P(("sess", "tile"), None, None, None)),
        check_vma=False,
    )
```

```python
import functools

import jax
import jax.numpy as jnp
from jax import lax
from jax.experimental import pallas as pl
from jax.experimental.pallas import tpu as pltpu
from jax.sharding import PartitionSpec as P

S = 64
UNIT = 12
NCLS = 3
CAP = 2
PIECE = 16
BANDS_AT_ONCE = 3
SPAN = UNIT * (NCLS + 1)
BF16 = jnp.bfloat16
F32 = jnp.float32
I32 = jnp.int32
FULL_GRANT = 67000000
ROW, COL, SIDE, ROW2, COL2, SIDE2, PLACE = range(7)


def rows_within(window, band_rows, stride):
    return band_rows * (window // stride) + min(band_rows, window % stride)


class Dims:
    def __init__(self, features, tiles):
        self.bands, self.band_rows, self.cols, self.chans = features.shape
        self.tiles = tiles
        self.stride = tiles * self.band_rows
        self.shift = self.stride.bit_length() - 1
        self.local_rows = self.bands * self.band_rows
        self.rows = rows_within(SPAN + 2, self.band_rows, self.stride)
        self.back_rows = rows_within(SPAN, self.band_rows, self.stride)
        self.rim = -(-2 * self.rows // 16) * 16
        self.message = self.rows * SPAN + self.rim


def first_local(row, tile, dims):
    return ((row >> dims.shift) << 1) + jnp.clip((row & (dims.stride - 1)) - 2 * tile, 0, 2)


def global_row(local, tile, dims):
    return ((local >> 1) << dims.shift) + 2 * tile + (local & 1)


def silu(v):
    half = 0.5 * v
    return half + half * jnp.tanh(half)


def both(bias):
    return jnp.concatenate([bias, bias], -1)


class RowTaps:
    def __init__(self, source, bias, store, held, sems):
        chans = source.shape[-1]
        self.store = store
        self.held = held
        self.copies = (
            pltpu.make_async_copy(bias, held, sems.at[2]),
            pltpu.make_async_copy(source, store.at[0:3, :, :, 0:chans], sems.at[0]),
            pltpu.make_async_copy(source, store.at[1:4, :, :, chans : 2 * chans], sems.at[1]),
        )

    def start(self):
        for copy in self.copies:
            copy.start()
        chans = self.store.shape[2]
        none = jnp.zeros((3, chans, chans), BF16)
        self.store[3, :, :, 0:chans] = none
        self.store[0, :, :, chans : 2 * chans] = none

    def wait(self):
        for copy in self.copies:
            copy.wait()

    def bias(self):
        return both(self.held[...])

    def value(self):
        return self.store[...].reshape(-1, self.store.shape[-1])


class ColumnTaps(RowTaps):
    def __init__(self, source, bias, store, held, sems):
        chans = source.shape[-1]
        self.store = store
        self.held = held
        self.copies = (
            pltpu.make_async_copy(bias, held, sems.at[2]),
            pltpu.make_async_copy(source, store.at[:, 0:3, :, 0:chans], sems.at[0]),
            pltpu.make_async_copy(source, store.at[:, 1:4, :, chans : 2 * chans], sems.at[1]),
        )

    def start(self):
        for copy in self.copies:
            copy.start()
        chans = self.store.shape[2]
        none = jnp.zeros((3, chans, chans), BF16)
        self.store[:, 3, :, 0:chans] = none
        self.store[:, 0, :, chans : 2 * chans] = none


def two_chains(wide, taps):
    wide = wide.reshape(-1, wide.shape[-1])
    weight = taps.value()
    middle = weight.shape[0] // 2
    one = jnp.dot(wide[:, :middle], weight[:middle], preferred_element_type=F32)
    two = jnp.dot(wide[:, middle:], weight[middle:], preferred_element_type=F32)
    return one + two


def row_pairs(src, first, count, taps):
    parts = [
        src[pl.ds(first, count), 0],
        src[pl.ds(first, count), 1],
        src[pl.ds(first + 1, count), 0],
        src[pl.ds(first + 1, count), 1],
    ]
    return two_chains(jnp.concatenate(parts, -1), taps)


def column_pairs(src, first, count, taps):
    return two_chains(jnp.concatenate([src[pl.ds(first + a, count)] for a in range(3)], -1), taps)


def fill_canvas(dims, feat, held, canvas, sems):
    def copy(band):
        return pltpu.make_async_copy(feat.at[band], held.at[band], sems.at[band])

    for band in range(dims.bands):
        copy(band).start()

    def finish():
        edge = jnp.zeros((8, dims.chans), F32)
        for band in range(dims.bands):
            copy(band).wait()
            for i in range(2):
                row = 2 * band + i
                canvas[row, 0:8, :] = edge
                canvas[row, 8 + dims.cols : 16 + dims.cols, :] = edge
                canvas[row, 8 : 8 + dims.cols, :] = held[band, i].astype(F32)

    return finish


def pack_crops(dims, table, row_at, col_at, canvas, rim, staged, partner):
    me = lax.axis_index("tile")
    rim[...] = jnp.zeros_like(rim)

    @pl.loop(0, dims.tiles)
    def _(s):
        w = partner(s)
        row0 = table[row_at, w]
        col0 = table[col_at, w]
        start = first_local(jnp.maximum(row0 - 1, 0), me, dims)
        for i in range(dims.rows):
            row = jnp.minimum(start + i, dims.local_rows - 1)
            staged[s, i * SPAN : (i + 1) * SPAN, :] = canvas[row, pl.ds(col0 + 8, SPAN), :].astype(BF16)
            rim[2 * i : 2 * i + 1, :] = canvas[row, pl.ds(col0 + 7, 1), :]
            rim[2 * i + 1 : 2 * i + 2, :] = canvas[row, pl.ds(col0 + 8 + SPAN, 1), :]
        staged[s, dims.rows * SPAN :, :] = rim[...].astype(BF16)


def pack_kernel(
    dims, boxes_in, slots_in, feat, *refs
):
    sent, refs = refs[: dims.tiles], refs[dims.tiles :]
    sent_extra, table, last, leading, boxes, slots, main, extra, seconds, held, canvas, rim, staged, staged_extra, sems, feat_sems, sent_sems = refs
    me = lax.axis_index("tile")
    copies = (
        pltpu.make_async_copy(boxes_in, boxes, sems.at[0]),
        pltpu.make_async_copy(slots_in, slots, sems.at[1]),
    )
    for copy in copies:
        copy.start()
    finish = fill_canvas(dims, feat, held, canvas, feat_sems)
    for copy in copies:
        copy.wait()

    def first_pass(w, count):
        one = slots[CAP * w]
        two = slots[CAP * w + 1]
        full = (one >= 0) & (two >= 0)
        second = jnp.where(full, two, -1)
        main[w] = jnp.where(one >= 0, one, two)
        extra[w] = second
        seconds[count] = second
        return count + full.astype(I32)

    lax.fori_loop(0, dims.tiles, first_pass, jnp.int32(0))

    def second_pass(w, count):
        own = main[w]
        idle = own < 0
        crop = jnp.where(idle, seconds[count], own)
        table[ROW, w] = boxes[0, crop]
        table[COL, w] = boxes[1, crop]
        table[SIDE, w] = UNIT * (boxes[2, crop] + 2)
        other = jnp.maximum(extra[w], 0)
        table[ROW2, w] = boxes[0, other]
        table[COL2, w] = boxes[1, other]
        table[SIDE2, w] = jnp.where(extra[w] >= 0, UNIT * (boxes[2, other] + 2), 0)
        table[PLACE, w] = jnp.where(idle, 2, jnp.where(slots[CAP * w] >= 0, 0, 1))
        return count + idle.astype(I32)

    lax.fori_loop(0, dims.tiles, second_pass, jnp.int32(0))
    finish()
    edges = (
        pltpu.make_async_copy(held.at[:, 1], last, sems.at[2]),
        pltpu.make_async_copy(held.at[:, 0], leading, sems.at[3]),
    )
    for edge in edges:
        edge.start()
    pack_crops(dims, table, ROW, COL, canvas, rim, staged, lambda s: me ^ s)
    copies = [pltpu.make_async_copy(staged.at[s], sent[s], sent_sems.at[s]) for s in range(dims.tiles)]
    for copy in copies:
        copy.start()
    pack_crops(dims, table, ROW2, COL2, canvas, rim, staged_extra, lambda s: s)
    later = pltpu.make_async_copy(staged_extra, sent_extra, sems.at[0])
    later.start()
    for copy in copies:
        copy.wait()
    later.wait()
    for edge in edges:
        edge.wait()


def restore(dims, row0, length, arrival, source, got, taps, raw, decoded, wide, inner, mixed, delta, finish):
    chans = dims.chans
    above = row0 - 1
    pairs = SPAN // 2
    half = S // 2
    nothing = jnp.zeros((SPAN, 3 * chans), BF16)
    raw[0, 0] = nothing
    raw[pairs, 1] = nothing
    empty = jnp.zeros((half, 4 * chans), BF16)
    for store in (wide, inner):
        store[0] = empty
        store[S + 1] = empty

    @pl.loop(0, dims.tiles)
    def _(s):
        arrival(s).wait()
        e = source(s)
        start = first_local(jnp.maximum(above, 0), e, dims)
        rim = got[s, dims.rows * SPAN :, :].astype(F32)
        at = lax.broadcasted_iota(I32, (SPAN, chans), 0)
        for i in range(dims.rows):
            local = start + i
            place = global_row(local, e, dims) - above
            place = jnp.where((local < dims.local_rows) & (place < SPAN + 2), place, SPAN + 2)
            line = got[s, i * SPAN : (i + 1) * SPAN, :]
            wider = line.astype(F32)
            left = jnp.where(at == 0, rim[2 * i : 2 * i + 1], pltpu.roll(wider, 1, 0))
            right = jnp.where(at == SPAN - 1, rim[2 * i + 1 : 2 * i + 2], pltpu.roll(wider, SPAN - 1, 0))
            raw[place >> 1, place & 1] = jnp.concatenate([left.astype(BF16), line, right.astype(BF16)], -1)

    taps[1].start()
    taps[2].start()
    taps[0].wait()
    n = 8
    for first in range(0, pairs, n):
        total = silu(row_pairs(raw, first, n, taps[0]) + taps[0].bias())
        for k in range(n):
            part = total[k * SPAN : (k + 1) * SPAN]
            at = 2 * (first + k)
            upper = raw[first + k, 1, :, chans : 2 * chans].astype(F32) + part[:, :chans]
            lower = raw[first + k + 1, 0, :, chans : 2 * chans].astype(F32) + part[:, chans:]
            decoded[at] = upper.astype(BF16).astype(F32)
            decoded[at + 1] = lower.astype(BF16).astype(F32)

    lengthf = length.astype(F32)
    block = lax.broadcasted_iota(I32, (4, half, SPAN), 0)
    t = 2 * lax.broadcasted_iota(I32, (4, half, SPAN), 1) + block - 1
    j = lax.broadcasted_iota(I32, (4, half, SPAN), 2).astype(F32)
    spots = jnp.clip((t.astype(F32) + 0.5) * lengthf / S - 0.5, 0.0, lengthf - 1.0)
    across = jnp.where((t >= 0) & (t < S), jnp.maximum(0.0, 1.0 - jnp.abs(spots - j)), 0.0)
    across = across.reshape(4 * half, SPAN).astype(BF16)
    taps[1].wait()
    taps[2].wait()
    for m in range(S // 2):
        lines = []
        for parity in range(2):
            s = 2 * m + parity
            spot = jnp.clip((2 * s + 1) * length - S, 0, (length - 1) * 2 * S)
            low = spot >> 7
            part = (spot & 127).astype(F32) * (1.0 / (2 * S))
            high = jnp.minimum(low + 1, SPAN - 1)
            lines.append(((1.0 - part) * decoded[low] + part * decoded[high]).astype(BF16))
        cells = jnp.dot(across, jnp.concatenate(lines, -1), preferred_element_type=F32).astype(BF16)
        for parity in range(2):
            at = 2 * m + parity + 1
            for b in range(4):
                wide[at, :, b * chans : (b + 1) * chans] = cells[
                    b * half : (b + 1) * half, parity * chans : (parity + 1) * chans
                ]

    n = PIECE
    for first in range(0, S, n):
        total = silu(column_pairs(wide, first, n, taps[1]) + taps[1].bias())
        at = lax.broadcasted_iota(I32, (n, half, chans), 1)
        even = pltpu.roll(total[:, :chans], n * half - 1, 0).reshape(n, half, chans)
        odd = pltpu.roll(total[:, chans:], 1, 0).reshape(n, half, chans)
        rows = pl.ds(first + 1, n)
        inner[rows, :, 0:chans] = jnp.where(at == 0, 0.0, odd).astype(BF16)
        inner[rows, :, chans : 3 * chans] = total.astype(BF16).reshape(n, half, 2 * chans)
        inner[rows, :, 3 * chans :] = jnp.where(at == half - 1, 0.0, even).astype(BF16)

    for first in range(0, S, n):
        total = column_pairs(inner, first, n, taps[2]) + taps[2].bias()
        for k in range(n):
            mixed[first + k, pl.ds(0, half, stride=2), :] = total[k * half : (k + 1) * half, :chans]
            mixed[first + k, pl.ds(1, half, stride=2), :] = total[k * half : (k + 1) * half, chans:]
        delta[first : first + n] = mixed[first : first + n].astype(BF16)
        finish(first // PIECE)


def begin(dims, arrived, weights, biases, scratch):
    got, row_store, column_store, held, got_sems, tap_sems = scratch

    def arrival(s):
        return pltpu.make_async_copy(arrived[0], got.at[s], got_sems.at[s])

    for s in range(dims.tiles):
        pltpu.make_async_copy(arrived[s], got.at[s], got_sems.at[s]).start()
    taps = (
        RowTaps(weights[0], biases[0], row_store, held.at[0], tap_sems.at[0]),
        ColumnTaps(weights[1], biases[1], column_store.at[0], held.at[1], tap_sems.at[1]),
        ColumnTaps(weights[2], biases[2], column_store.at[1], held.at[2], tap_sems.at[2]),
    )
    taps[0].start()
    return arrival, taps


def main_kernel(dims, table, *refs):
    tiles, chans = dims.tiles, dims.chans
    arrived, refs = refs[:tiles], refs[tiles:]
    (dec_w, one_w, two_w, dec_b, one_b, two_b, sent, restored, got, row_store, column_store, held) = refs[:12]
    got_sems, tap_sems, raw, decoded, wide, inner, mixed, delta, sem, back, back_sems = refs[12:]
    me = lax.axis_index("tile")
    row0 = table[ROW, me]
    length = table[SIDE, me]
    place = table[PLACE, me]
    scratch = (got, row_store, column_store, held, got_sems, tap_sems)
    arrival, taps = begin(dims, arrived, (dec_w, one_w, two_w), (dec_b, one_b, two_b), scratch)
    restore(
        dims, row0, length, arrival, lambda s: me ^ s, got, taps,
        raw, decoded, wide, inner, mixed, delta, lambda piece: None,
    )

    @pl.when(place < CAP)
    def _():
        pltpu.make_async_copy(delta, restored.at[place], sem.at[0]).start()

    lengthf = length.astype(F32)
    t = lax.broadcasted_iota(I32, (SPAN, S), 0).astype(F32)
    s = lax.broadcasted_iota(I32, (SPAN, S), 1).astype(F32)
    spots = jnp.clip((t + 0.5) * S / lengthf - 0.5, 0.0, S - 1.0)
    lift = jnp.where(t < lengthf, jnp.maximum(0.0, 1.0 - jnp.abs(spots - s)), 0.0)
    coarse = lift.astype(BF16)
    lift = jnp.concatenate([coarse, (lift - coarse.astype(F32)).astype(BF16)], 0)
    scale = 1.0 / (2.0 * lengthf)
    group = 12

    @pl.loop(0, SPAN // 2 // group)
    def _(step):
        for k in range(group):
            lines = []
            for parity in range(2):
                h = 2 * (step * group + k) + parity
                spot = jnp.clip((2 * h + 1) * S - length, 0, (S - 1) * 2 * length)
                low = ((spot.astype(F32) + 0.5) * scale).astype(I32)
                part = (spot - low * 2 * length).astype(F32) * scale
                high = jnp.minimum(low + 1, S - 1)
                lines.append(((1.0 - part) * delta[low].astype(F32) + part * delta[high].astype(F32)).astype(BF16))
            patch = jnp.dot(lift, jnp.concatenate(lines, -1), preferred_element_type=F32)
            patch = (patch[:SPAN] + patch[SPAN:]).astype(BF16)
            for parity in range(2):
                row = row0 + 2 * (step * group + k) + parity
                dest = (row & (dims.stride - 1)) >> 1
                local = ((row >> dims.shift) << 1) + (row & 1)
                back[dest, local - first_local(row0, dest, dims)] = patch[:, parity * chans : (parity + 1) * chans]

    def leave(e):
        return pltpu.make_async_copy(back.at[e], sent.at[e], back_sems.at[e])

    for e in range(tiles):
        leave(e).start()
    for e in range(tiles):
        leave(e).wait()

    @pl.when(place < CAP)
    def _():
        pltpu.make_async_copy(delta, restored.at[place], sem.at[0]).wait()


def extra_kernel(
    dims, table, arrived, dec_w, one_w, two_w, dec_b, one_b, two_b, partial, restored,
    got, row_store, column_store, held, got_sems, tap_sems, raw, decoded, wide, inner, mixed, delta, sem,
):
    me = lax.axis_index("tile")
    row0 = table[ROW2, me]
    length = table[SIDE2, me]
    place = table[PLACE, me]

    def write(slot):
        copy = pltpu.make_async_copy(delta, restored.at[slot], sem.at[0])
        copy.start()
        copy.wait()

    @pl.when(length > 0)
    def _():
        scratch = (got, row_store, column_store, held, got_sems, tap_sems)
        arrival, taps = begin(dims, [arrived.at[s] for s in range(dims.tiles)], (dec_w, one_w, two_w), (dec_b, one_b, two_b), scratch)

        def leave(piece):
            rows = pl.ds(piece * PIECE, PIECE)
            return pltpu.make_async_copy(delta.at[rows], restored.at[1, rows], sem.at[piece])

        restore(
            dims, row0, length, arrival, lambda s: s, got, taps,
            raw, decoded, wide, inner, mixed, delta, lambda piece: leave(piece).start(),
        )
        for piece in range(S // PIECE):
            leave(piece).wait()

    @pl.when(length == 0)
    def _():
        delta[...] = jnp.zeros_like(delta)

        @pl.when(place != 0)
        def _():
            write(0)

        @pl.when(place != 1)
        def _():
            write(1)


def finish_kernel(
    dims, table, back, feat, above, below, weight, bias, finished,
    got, held, up, down, store, held_bias, lines, wide, canvas, out, sems, load_sems, tap_sems,
):
    me = lax.axis_index("tile")
    bands, chans, cols = dims.bands, dims.chans, dims.cols
    half = cols // 2
    taps = ColumnTaps(weight, bias, store, held_bias, tap_sems)
    patches = pltpu.make_async_copy(back, got, sems.at[0])
    patches.start()
    def from_feat(band):
        return pltpu.make_async_copy(feat.at[band], held.at[band], load_sems.at[0, band])

    def from_above(band):
        return pltpu.make_async_copy(above.at[band], up.at[band], load_sems.at[1, band])

    def from_below(band):
        return pltpu.make_async_copy(below.at[band], down.at[band], load_sems.at[2, band])

    taps.start()
    from_below(0).start()
    for j in range(bands):
        from_feat(j).start()
        from_above(j).start()
        if j + 1 < bands:
            from_below(j + 1).start()

    def leave(band):
        return pltpu.make_async_copy(out.at[band], finished.at[band], sems.at[1 + band])

    top = (me == 0).astype(I32)
    bottom = (me == dims.tiles - 1).astype(I32)
    edge = jnp.zeros((8, chans), F32)
    for k in range(lines.shape[0]):
        for a in range(4):
            lines[k, a, 0:8] = edge
            lines[k, a, 8 + cols :] = edge
    canvas[...] = jnp.zeros_like(canvas)
    patches.wait()

    @pl.loop(0, dims.tiles)
    def _(e):
        row0 = table[ROW, e]
        col0 = table[COL, e]
        length = table[SIDE, e]
        start = first_local(row0, me, dims)
        for i in range(dims.back_rows):
            local = start + i

            @pl.when((local < dims.local_rows) & (global_row(local, me, dims) - row0 < length))
            def _():
                canvas[local, pl.ds(col0, SPAN), :] += got[e, i].astype(F32)

    from_below(0).wait()
    taps.wait()

    def band(j, lines, wide):
        no_top = (top == 1) & (j == 0)
        no_bottom = (bottom == 1) & (j == bands - 1)
        over = up[jnp.maximum(j - top, 0)].astype(F32)
        under = down[jnp.minimum(j + bottom, bands - 1)].astype(F32)
        middle = slice(8, 8 + cols)
        lines[0, middle] = jnp.where(no_top, 0.0, over)
        lines[1, middle] = held[j, 0].astype(F32)
        lines[2, middle] = held[j, 1].astype(F32)
        lines[3, middle] = jnp.where(no_bottom, 0.0, under)
        for a in range(4):
            for b in range(4):
                wide[a, :, b * chans : (b + 1) * chans] = lines[a, pl.ds(7 + b, half, stride=2), :].astype(BF16)
        total = silu(column_pairs(wide, 0, 2, taps) + taps.bias())
        for i in range(2):
            part = total[i * half : (i + 1) * half]
            for b in range(2):
                here = lines[i + 1, pl.ds(8 + b, half, stride=2), :]
                decoded = (here + part[:, b * chans : (b + 1) * chans]).astype(BF16).astype(F32)
                at = pl.ds(b, half, stride=2)
                canvas[2 * j + i, at, :] = canvas[2 * j + i, at, :] + decoded
            out[j, i] = canvas[2 * j + i].astype(BF16)

    @pl.loop(0, bands // BANDS_AT_ONCE)
    def _(step):
        first = BANDS_AT_ONCE * step
        for k in range(BANDS_AT_ONCE):
            from_feat(first + k).wait()
            from_above(first + k).wait()
            if k + 1 < BANDS_AT_ONCE:
                from_below(first + k + 1).wait()

        @pl.when(first + BANDS_AT_ONCE < bands)
        def _():
            from_below(first + BANDS_AT_ONCE).wait()

        for k in range(BANDS_AT_ONCE):
            band(first + k, lines.at[k], wide.at[k])
        for k in range(BANDS_AT_ONCE):
            leave(first + k).start()

    for j in range(bands):
        leave(j).wait()


def shards(features, dec_weight, dec_bias, first_weight, first_bias, second_weight, second_bias, boxes, slots):
    tiles = lax.axis_size("tile")
    dims = Dims(features, tiles)
    bands, cols, chans, local_rows = dims.bands, dims.cols, dims.chans, dims.local_rows
    assert dims.band_rows == 2 and slots.shape[0] == CAP * tiles and boxes.shape[1] == tiles
    assert tiles & (tiles - 1) == 0

    smem = pl.BlockSpec(memory_space=pltpu.SMEM)
    hbm = pl.BlockSpec(memory_space=pl.ANY)
    full = pltpu.CompilerParams(vmem_limit_bytes=FULL_GRANT)
    dma = pltpu.SemaphoreType.DMA

    def cost(flops, moved):
        return pl.CostEstimate(flops=int(flops), bytes_accessed=int(moved), transcendentals=0)

    def shaped(*shape, kind=BF16):
        return jax.ShapeDtypeStruct(shape, kind)

    def swap(array):
        return lax.all_to_all(array, "tile", split_axis=0, concat_axis=0, tiled=True)

    pack_scratch = [
        pltpu.VMEM((bands, 2, cols, chans), BF16),
        pltpu.VMEM((local_rows, cols + 16, chans), F32),
        pltpu.VMEM((dims.rim, chans), F32),
        pltpu.VMEM((tiles, dims.message, chans), BF16),
        pltpu.VMEM((tiles, dims.message, chans), BF16),
        dma((4,)),
        dma((bands,)),
        dma((tiles,)),
    ]
    message = shaped(tiles, dims.message, chans)
    *sent_main, sent_extra, table, last, leading = pl.pallas_call(
        functools.partial(pack_kernel, dims),
        out_shape=[shaped(dims.message, chans)] * tiles
        + [message, shaped(7, tiles, kind=I32), shaped(bands, cols, chans), shaped(bands, cols, chans)],
        in_specs=[hbm, hbm, hbm],
        out_specs=[hbm] * (tiles + 1) + [smem, hbm, hbm],
        scratch_shapes=[
            pltpu.SMEM(boxes.shape, I32),
            pltpu.SMEM(slots.shape, I32),
            pltpu.SMEM((tiles,), I32),
            pltpu.SMEM((tiles,), I32),
            pltpu.SMEM((tiles + 1,), I32),
        ]
        + pack_scratch,
        compiler_params=full,
        cost_estimate=cost(0, 6e6),
        name="pack",
    )(boxes, slots, features)
    got_main = [sent_main[0]] + [None] * (tiles - 1)
    for s in [1] + sorted(range(2, tiles), key=lambda s: (-(s >> 1).bit_count(), -(s >> 1), s)):
        got_main[s] = lax.ppermute(sent_main[s], "tile", [(i, i ^ s) for i in range(tiles)])
    up = [(i, (i + 1) % tiles) for i in range(tiles)]
    above = lax.ppermute(last, "tile", up)
    below = lax.ppermute(leading, "tile", [(j, i) for i, j in up])

    got_extra = swap(sent_extra)

    weights = tuple(w.reshape(3, 3, chans, chans) for w in (dec_weight, first_weight, second_weight))
    biases = (dec_bias[None], first_bias[None], second_bias[None])
    restore_scratch = [
        pltpu.VMEM((tiles, dims.message, chans), BF16),
        pltpu.VMEM((4, 3, chans, 2 * chans), BF16),
        pltpu.VMEM((2, 3, 4, chans, 2 * chans), BF16),
        pltpu.VMEM((3, 1, chans), F32),
        dma((tiles,)),
        dma((3, 3)),
        pltpu.VMEM((SPAN // 2 + 2, 2, SPAN, 3 * chans), BF16),
        pltpu.VMEM((SPAN, SPAN, chans), F32),
        pltpu.VMEM((S + 2, S // 2, 4 * chans), BF16),
        pltpu.VMEM((S + 2, S // 2, 4 * chans), BF16),
        pltpu.VMEM((S, S, chans), F32),
        pltpu.VMEM((S, S, chans), BF16),
        dma((S // PIECE,)),
    ]
    restored_shape = shaped(CAP, S, S, chans)
    sent_back, partial = pl.pallas_call(
        functools.partial(main_kernel, dims),
        out_shape=[shaped(tiles, dims.back_rows, SPAN, chans), restored_shape],
        in_specs=[smem] + [hbm] * (tiles + 6),
        out_specs=[hbm, hbm],
        scratch_shapes=restore_scratch
        + [pltpu.VMEM((tiles, dims.back_rows, SPAN, chans), BF16), dma((tiles,))],
        compiler_params=full,
        cost_estimate=cost(7e9, 8e6),
        name="restore_main",
    )(table, *got_main, *weights, *biases)
    got_back = swap(sent_back)

    restorations = pl.pallas_call(
        functools.partial(extra_kernel, dims),
        out_shape=restored_shape,
        in_specs=[smem] + [hbm] * 8,
        out_specs=hbm,
        scratch_shapes=restore_scratch,
        input_output_aliases={8: 0},
        compiler_params=full,
        cost_estimate=cost(6e9, 8e6),
        name="restore_extra",
    )(table, got_extra, *weights, *biases, partial)

    above, below, restorations = lax.optimization_barrier((above, below, restorations))
    assert bands % BANDS_AT_ONCE == 0
    finished = pl.pallas_call(
        functools.partial(finish_kernel, dims),
        out_shape=shaped(*features.shape),
        in_specs=[smem] + [hbm] * 6,
        out_specs=hbm,
        scratch_shapes=[
            pltpu.VMEM((tiles, dims.back_rows, SPAN, chans), BF16),
            pltpu.VMEM((bands, 2, cols, chans), BF16),
            pltpu.VMEM((bands, cols, chans), BF16),
            pltpu.VMEM((bands, cols, chans), BF16),
            pltpu.VMEM((3, 4, chans, 2 * chans), BF16),
            pltpu.VMEM((1, chans), F32),
            pltpu.VMEM((BANDS_AT_ONCE, 4, cols + 16, chans), F32),
            pltpu.VMEM((BANDS_AT_ONCE, 4, cols // 2, 4 * chans), BF16),
            pltpu.VMEM((local_rows, cols, chans), F32),
            pltpu.VMEM((bands, 2, cols, chans), BF16),
            dma((1 + bands,)),
            dma((3, bands)),
            dma((3,)),
        ],
        compiler_params=full,
        cost_estimate=cost(3e9, 6e6),
        name="finish",
    )(table, got_back, features, above, below, weights[0], biases[0])
    return finished, restorations


def solution(mesh):
    return jax.shard_map(
        shards,
        mesh=mesh,
        in_specs=(
            P("sess", "tile", None, None),
            P(),
            P(),
            P(),
            P(),
            P(),
            P(),
            P(None, "sess"),
            P("sess"),
        ),
        out_specs=(P("sess", "tile", None, None), P(("sess", "tile"), None, None, None)),
        check_vma=False,
    )
```

```python
import functools

import jax
import jax.numpy as jnp
from jax import lax
from jax.experimental import pallas as pl
from jax.experimental.pallas import tpu as pltpu
from jax.sharding import PartitionSpec as P

S = 64
UNIT = 12
NCLS = 3
CAP = 2
PIECE = 16
BANDS_AT_ONCE = 3
SPAN = UNIT * (NCLS + 1)
BF16 = jnp.bfloat16
F32 = jnp.float32
I32 = jnp.int32
FULL_GRANT = 67000000
ROW, COL, SIDE, ROW2, COL2, SIDE2, PLACE = range(7)


def rows_within(window, band_rows, stride):
    return band_rows * (window // stride) + min(band_rows, window % stride)


class Dims:
    def __init__(self, features, tiles):
        self.bands, self.band_rows, self.cols, self.chans = features.shape
        self.tiles = tiles
        self.stride = tiles * self.band_rows
        self.shift = self.stride.bit_length() - 1
        self.local_rows = self.bands * self.band_rows
        self.rows = rows_within(SPAN + 2, self.band_rows, self.stride)
        self.back_rows = rows_within(SPAN, self.band_rows, self.stride)
        self.rim = -(-2 * self.rows // 16) * 16
        self.message = self.rows * SPAN + self.rim


def first_local(row, tile, dims):
    return ((row >> dims.shift) << 1) + jnp.clip((row & (dims.stride - 1)) - 2 * tile, 0, 2)


def global_row(local, tile, dims):
    return ((local >> 1) << dims.shift) + 2 * tile + (local & 1)


def silu(v):
    half = 0.5 * v
    return half + half * jnp.tanh(half)


def both(bias):
    return jnp.concatenate([bias, bias], -1)


class RowTaps:
    def __init__(self, source, bias, store, held, sems):
        chans = source.shape[-1]
        self.store = store
        self.held = held
        self.copies = (
            pltpu.make_async_copy(bias, held, sems.at[2]),
            pltpu.make_async_copy(source, store.at[0:3, :, :, 0:chans], sems.at[0]),
            pltpu.make_async_copy(source, store.at[1:4, :, :, chans : 2 * chans], sems.at[1]),
        )

    def start(self):
        for copy in self.copies:
            copy.start()
        chans = self.store.shape[2]
        none = jnp.zeros((3, chans, chans), BF16)
        self.store[3, :, :, 0:chans] = none
        self.store[0, :, :, chans : 2 * chans] = none

    def wait(self):
        for copy in self.copies:
            copy.wait()

    def bias(self):
        return both(self.held[...])

    def value(self):
        return self.store[...].reshape(-1, self.store.shape[-1])


class ColumnTaps(RowTaps):
    def __init__(self, source, bias, store, held, sems):
        chans = source.shape[-1]
        self.store = store
        self.held = held
        self.copies = (
            pltpu.make_async_copy(bias, held, sems.at[2]),
            pltpu.make_async_copy(source, store.at[:, 0:3, :, 0:chans], sems.at[0]),
            pltpu.make_async_copy(source, store.at[:, 1:4, :, chans : 2 * chans], sems.at[1]),
        )

    def start(self):
        for copy in self.copies:
            copy.start()
        chans = self.store.shape[2]
        none = jnp.zeros((3, chans, chans), BF16)
        self.store[:, 3, :, 0:chans] = none
        self.store[:, 0, :, chans : 2 * chans] = none


def two_chains(wide, taps):
    wide = wide.reshape(-1, wide.shape[-1])
    weight = taps.value()
    middle = weight.shape[0] // 2
    one = jnp.dot(wide[:, :middle], weight[:middle], preferred_element_type=F32)
    two = jnp.dot(wide[:, middle:], weight[middle:], preferred_element_type=F32)
    return one + two


def row_pairs(src, first, count, taps):
    parts = [
        src[pl.ds(first, count), 0],
        src[pl.ds(first, count), 1],
        src[pl.ds(first + 1, count), 0],
        src[pl.ds(first + 1, count), 1],
    ]
    return two_chains(jnp.concatenate(parts, -1), taps)


def column_pairs(src, first, count, taps):
    return two_chains(jnp.concatenate([src[pl.ds(first + a, count)] for a in range(3)], -1), taps)


def fill_canvas(dims, feat, held, canvas, sems):
    def copy(band):
        return pltpu.make_async_copy(feat.at[band], held.at[band], sems.at[band])

    for band in range(dims.bands):
        copy(band).start()

    def finish():
        edge = jnp.zeros((8, dims.chans), F32)
        for band in range(dims.bands):
            copy(band).wait()
            for i in range(2):
                row = 2 * band + i
                canvas[row, 0:8, :] = edge
                canvas[row, 8 + dims.cols : 16 + dims.cols, :] = edge
                canvas[row, 8 : 8 + dims.cols, :] = held[band, i].astype(F32)

    return finish


def pack_crop(dims, row0, col0, canvas, rim, staged):
    me = lax.axis_index("tile")
    start = first_local(jnp.maximum(row0 - 1, 0), me, dims)
    for i in range(dims.rows):
        row = jnp.minimum(start + i, dims.local_rows - 1)
        staged[i * SPAN : (i + 1) * SPAN, :] = canvas[row, pl.ds(col0 + 8, SPAN), :].astype(BF16)
        rim[2 * i : 2 * i + 1, :] = canvas[row, pl.ds(col0 + 7, 1), :]
        rim[2 * i + 1 : 2 * i + 2, :] = canvas[row, pl.ds(col0 + 8 + SPAN, 1), :]
    staged[dims.rows * SPAN :, :] = rim[...].astype(BF16)


def pack_kernel(
    dims, boxes_in, slots_in, feat, *refs
):
    sent, refs = refs[: dims.tiles], refs[dims.tiles :]
    sent_extra, table, last, leading, boxes, slots, main, extra, seconds, held, canvas, rim, staged, staged_extra, sems, feat_sems, sent_sems = refs
    me = lax.axis_index("tile")
    copies = (
        pltpu.make_async_copy(boxes_in, boxes, sems.at[0]),
        pltpu.make_async_copy(slots_in, slots, sems.at[1]),
    )
    for copy in copies:
        copy.start()
    finish = fill_canvas(dims, feat, held, canvas, feat_sems)
    for copy in copies:
        copy.wait()

    def first_pass(w, count):
        one = slots[CAP * w]
        two = slots[CAP * w + 1]
        full = (one >= 0) & (two >= 0)
        second = jnp.where(full, two, -1)
        main[w] = jnp.where(one >= 0, one, two)
        extra[w] = second
        seconds[count] = second
        return count + full.astype(I32)

    lax.fori_loop(0, dims.tiles, first_pass, jnp.int32(0))

    def second_pass(w, count):
        own = main[w]
        idle = own < 0
        crop = jnp.where(idle, seconds[count], own)
        table[ROW, w] = boxes[0, crop]
        table[COL, w] = boxes[1, crop]
        table[SIDE, w] = UNIT * (boxes[2, crop] + 2)
        other = jnp.maximum(extra[w], 0)
        table[ROW2, w] = boxes[0, other]
        table[COL2, w] = boxes[1, other]
        table[SIDE2, w] = jnp.where(extra[w] >= 0, UNIT * (boxes[2, other] + 2), 0)
        table[PLACE, w] = jnp.where(idle, 2, jnp.where(slots[CAP * w] >= 0, 0, 1))
        return count + idle.astype(I32)

    lax.fori_loop(0, dims.tiles, second_pass, jnp.int32(0))
    finish()
    rim[...] = jnp.zeros_like(rim)
    copies = [pltpu.make_async_copy(staged.at[s], sent[s], sent_sems.at[0, s]) for s in range(dims.tiles)]
    half = dims.tiles // 2
    for part in range(2):

        @pl.loop(part * half, (part + 1) * half)
        def _(s):
            pack_crop(dims, table[ROW, me ^ s], table[COL, me ^ s], canvas, rim, staged.at[s])

        for copy in copies[part * half : (part + 1) * half]:
            copy.start()
    edges = (
        pltpu.make_async_copy(held.at[:, 1], last, sems.at[2]),
        pltpu.make_async_copy(held.at[:, 0], leading, sems.at[3]),
    )
    for edge in edges:
        edge.start()

    def later(w):
        return pltpu.make_async_copy(staged_extra.at[w], sent_extra.at[w], sent_sems.at[1, w])

    @pl.loop(0, dims.tiles)
    def _(w):
        @pl.when(table[SIDE2, w] > 0)
        def _():
            pack_crop(dims, table[ROW2, w], table[COL2, w], canvas, rim, staged_extra.at[w])
            later(w).start()

    for copy in copies:
        copy.wait()
    for edge in edges:
        edge.wait()

    @pl.loop(0, dims.tiles)
    def _(w):
        @pl.when(table[SIDE2, w] > 0)
        def _():
            later(w).wait()


def restore(dims, row0, length, arrival, source, got, taps, raw, decoded, wide, inner, mixed, delta, finish):
    chans = dims.chans
    above = row0 - 1
    pairs = SPAN // 2
    half = S // 2
    nothing = jnp.zeros((SPAN, 3 * chans), BF16)
    raw[0, 0] = nothing
    raw[pairs, 1] = nothing
    empty = jnp.zeros((half, 4 * chans), BF16)
    for store in (wide, inner):
        store[0] = empty
        store[S + 1] = empty

    @pl.loop(0, dims.tiles)
    def _(s):
        arrival(s).wait()
        e = source(s)
        start = first_local(jnp.maximum(above, 0), e, dims)
        rim = got[s, dims.rows * SPAN :, :].astype(F32)
        at = lax.broadcasted_iota(I32, (SPAN, chans), 0)
        for i in range(dims.rows):
            local = start + i
            place = global_row(local, e, dims) - above
            place = jnp.where((local < dims.local_rows) & (place < SPAN + 2), place, SPAN + 2)
            line = got[s, i * SPAN : (i + 1) * SPAN, :]
            wider = line.astype(F32)
            left = jnp.where(at == 0, rim[2 * i : 2 * i + 1], pltpu.roll(wider, 1, 0))
            right = jnp.where(at == SPAN - 1, rim[2 * i + 1 : 2 * i + 2], pltpu.roll(wider, SPAN - 1, 0))
            raw[place >> 1, place & 1] = jnp.concatenate([left.astype(BF16), line, right.astype(BF16)], -1)

    taps[1].start()
    taps[2].start()
    taps[0].wait()
    n = 8
    for first in range(0, pairs, n):
        total = silu(row_pairs(raw, first, n, taps[0]) + taps[0].bias())
        for k in range(n):
            part = total[k * SPAN : (k + 1) * SPAN]
            at = 2 * (first + k)
            upper = raw[first + k, 1, :, chans : 2 * chans].astype(F32) + part[:, :chans]
            lower = raw[first + k + 1, 0, :, chans : 2 * chans].astype(F32) + part[:, chans:]
            decoded[at] = upper.astype(BF16).astype(F32)
            decoded[at + 1] = lower.astype(BF16).astype(F32)

    lengthf = length.astype(F32)
    block = lax.broadcasted_iota(I32, (4, half, SPAN), 0)
    t = 2 * lax.broadcasted_iota(I32, (4, half, SPAN), 1) + block - 1
    j = lax.broadcasted_iota(I32, (4, half, SPAN), 2).astype(F32)
    spots = jnp.clip((t.astype(F32) + 0.5) * lengthf / S - 0.5, 0.0, lengthf - 1.0)
    across = jnp.where((t >= 0) & (t < S), jnp.maximum(0.0, 1.0 - jnp.abs(spots - j)), 0.0)
    across = across.reshape(4 * half, SPAN).astype(BF16)
    taps[1].wait()
    taps[2].wait()
    for m in range(S // 2):
        lines = []
        for parity in range(2):
            s = 2 * m + parity
            spot = jnp.clip((2 * s + 1) * length - S, 0, (length - 1) * 2 * S)
            low = spot >> 7
            part = (spot & 127).astype(F32) * (1.0 / (2 * S))
            high = jnp.minimum(low + 1, SPAN - 1)
            lines.append(((1.0 - part) * decoded[low] + part * decoded[high]).astype(BF16))
        cells = jnp.dot(across, jnp.concatenate(lines, -1), preferred_element_type=F32).astype(BF16)
        for parity in range(2):
            at = 2 * m + parity + 1
            for b in range(4):
                wide[at, :, b * chans : (b + 1) * chans] = cells[
                    b * half : (b + 1) * half, parity * chans : (parity + 1) * chans
                ]

    n = PIECE
    for first in range(0, S, n):
        total = silu(column_pairs(wide, first, n, taps[1]) + taps[1].bias())
        at = lax.broadcasted_iota(I32, (n, half, chans), 1)
        even = pltpu.roll(total[:, :chans], n * half - 1, 0).reshape(n, half, chans)
        odd = pltpu.roll(total[:, chans:], 1, 0).reshape(n, half, chans)
        rows = pl.ds(first + 1, n)
        inner[rows, :, 0:chans] = jnp.where(at == 0, 0.0, odd).astype(BF16)
        inner[rows, :, chans : 3 * chans] = total.astype(BF16).reshape(n, half, 2 * chans)
        inner[rows, :, 3 * chans :] = jnp.where(at == half - 1, 0.0, even).astype(BF16)

    for first in range(0, S, n):
        total = column_pairs(inner, first, n, taps[2]) + taps[2].bias()
        for k in range(n):
            mixed[first + k, pl.ds(0, half, stride=2), :] = total[k * half : (k + 1) * half, :chans]
            mixed[first + k, pl.ds(1, half, stride=2), :] = total[k * half : (k + 1) * half, chans:]
        delta[first : first + n] = mixed[first : first + n].astype(BF16)
        finish(first // PIECE)


def begin(dims, arrived, weights, biases, scratch):
    got, row_store, column_store, held, got_sems, tap_sems = scratch

    def arrival(s):
        return pltpu.make_async_copy(arrived[0], got.at[s], got_sems.at[s])

    for s in range(dims.tiles):
        pltpu.make_async_copy(arrived[s], got.at[s], got_sems.at[s]).start()
    taps = (
        RowTaps(weights[0], biases[0], row_store, held.at[0], tap_sems.at[0]),
        ColumnTaps(weights[1], biases[1], column_store.at[0], held.at[1], tap_sems.at[1]),
        ColumnTaps(weights[2], biases[2], column_store.at[1], held.at[2], tap_sems.at[2]),
    )
    taps[0].start()
    return arrival, taps


def main_kernel(dims, table, *refs):
    tiles, chans = dims.tiles, dims.chans
    arrived, refs = refs[:tiles], refs[tiles:]
    (dec_w, one_w, two_w, dec_b, one_b, two_b, sent, restored, got, row_store, column_store, held) = refs[:12]
    got_sems, tap_sems, raw, decoded, wide, inner, mixed, delta, sem, back, back_sems = refs[12:]
    me = lax.axis_index("tile")
    row0 = table[ROW, me]
    length = table[SIDE, me]
    place = table[PLACE, me]
    scratch = (got, row_store, column_store, held, got_sems, tap_sems)
    arrival, taps = begin(dims, arrived, (dec_w, one_w, two_w), (dec_b, one_b, two_b), scratch)
    restore(
        dims, row0, length, arrival, lambda s: me ^ s, got, taps,
        raw, decoded, wide, inner, mixed, delta, lambda piece: None,
    )

    @pl.when(place < CAP)
    def _():
        pltpu.make_async_copy(delta, restored.at[place], sem.at[0]).start()

    lengthf = length.astype(F32)
    t = lax.broadcasted_iota(I32, (SPAN, S), 0).astype(F32)
    s = lax.broadcasted_iota(I32, (SPAN, S), 1).astype(F32)
    spots = jnp.clip((t + 0.5) * S / lengthf - 0.5, 0.0, S - 1.0)
    lift = jnp.where(t < lengthf, jnp.maximum(0.0, 1.0 - jnp.abs(spots - s)), 0.0)
    coarse = lift.astype(BF16)
    lift = jnp.concatenate([coarse, (lift - coarse.astype(F32)).astype(BF16)], 0)
    scale = 1.0 / (2.0 * lengthf)
    group = 12

    @pl.loop(0, SPAN // 2 // group)
    def _(step):
        for k in range(group):
            lines = []
            for parity in range(2):
                h = 2 * (step * group + k) + parity
                spot = jnp.clip((2 * h + 1) * S - length, 0, (S - 1) * 2 * length)
                low = ((spot.astype(F32) + 0.5) * scale).astype(I32)
                part = (spot - low * 2 * length).astype(F32) * scale
                high = jnp.minimum(low + 1, S - 1)
                lines.append(((1.0 - part) * delta[low].astype(F32) + part * delta[high].astype(F32)).astype(BF16))
            patch = jnp.dot(lift, jnp.concatenate(lines, -1), preferred_element_type=F32)
            patch = (patch[:SPAN] + patch[SPAN:]).astype(BF16)
            for parity in range(2):
                row = row0 + 2 * (step * group + k) + parity
                dest = (row & (dims.stride - 1)) >> 1
                local = ((row >> dims.shift) << 1) + (row & 1)
                back[dest, local - first_local(row0, dest, dims)] = patch[:, parity * chans : (parity + 1) * chans]

    def leave(e):
        return pltpu.make_async_copy(back.at[e], sent.at[e], back_sems.at[e])

    for e in range(tiles):
        leave(e).start()
    for e in range(tiles):
        leave(e).wait()

    @pl.when(place < CAP)
    def _():
        pltpu.make_async_copy(delta, restored.at[place], sem.at[0]).wait()


def extra_kernel(
    dims, table, arrived, dec_w, one_w, two_w, dec_b, one_b, two_b, partial, restored,
    got, row_store, column_store, held, got_sems, tap_sems, raw, decoded, wide, inner, mixed, delta, sem,
):
    me = lax.axis_index("tile")
    row0 = table[ROW2, me]
    length = table[SIDE2, me]
    place = table[PLACE, me]

    def write(slot):
        copy = pltpu.make_async_copy(delta, restored.at[slot], sem.at[0])
        copy.start()
        copy.wait()

    @pl.when(length > 0)
    def _():
        scratch = (got, row_store, column_store, held, got_sems, tap_sems)
        arrival, taps = begin(dims, [arrived.at[s] for s in range(dims.tiles)], (dec_w, one_w, two_w), (dec_b, one_b, two_b), scratch)

        def leave(piece):
            rows = pl.ds(piece * PIECE, PIECE)
            return pltpu.make_async_copy(delta.at[rows], restored.at[1, rows], sem.at[piece])

        restore(
            dims, row0, length, arrival, lambda s: s, got, taps,
            raw, decoded, wide, inner, mixed, delta, lambda piece: leave(piece).start(),
        )
        for piece in range(S // PIECE):
            leave(piece).wait()

    @pl.when(length == 0)
    def _():
        delta[...] = jnp.zeros_like(delta)

        @pl.when(place != 0)
        def _():
            write(0)

        @pl.when(place != 1)
        def _():
            write(1)


def finish_kernel(
    dims, table, back, feat, above, below, weight, bias, finished,
    got, held, up, down, store, held_bias, lines, wide, canvas, out, sems, load_sems, tap_sems,
):
    me = lax.axis_index("tile")
    bands, chans, cols = dims.bands, dims.chans, dims.cols
    half = cols // 2
    taps = ColumnTaps(weight, bias, store, held_bias, tap_sems)
    patches = pltpu.make_async_copy(back, got, sems.at[0])
    patches.start()
    def from_feat(band):
        return pltpu.make_async_copy(feat.at[band], held.at[band], load_sems.at[0, band])

    def from_above(band):
        return pltpu.make_async_copy(above.at[band], up.at[band], load_sems.at[1, band])

    def from_below(band):
        return pltpu.make_async_copy(below.at[band], down.at[band], load_sems.at[2, band])

    taps.start()
    from_below(0).start()
    for j in range(bands):
        from_feat(j).start()
        from_above(j).start()
        if j + 1 < bands:
            from_below(j + 1).start()

    def leave(band):
        return pltpu.make_async_copy(out.at[band], finished.at[band], sems.at[1 + band])

    top = (me == 0).astype(I32)
    bottom = (me == dims.tiles - 1).astype(I32)
    edge = jnp.zeros((8, chans), F32)
    for k in range(lines.shape[0]):
        for a in range(4):
            lines[k, a, 0:8] = edge
            lines[k, a, 8 + cols :] = edge
    canvas[...] = jnp.zeros_like(canvas)
    patches.wait()

    @pl.loop(0, dims.tiles)
    def _(e):
        row0 = table[ROW, e]
        col0 = table[COL, e]
        length = table[SIDE, e]
        start = first_local(row0, me, dims)
        for i in range(dims.back_rows):
            local = start + i

            @pl.when((local < dims.local_rows) & (global_row(local, me, dims) - row0 < length))
            def _():
                canvas[local, pl.ds(col0, SPAN), :] += got[e, i].astype(F32)

    from_below(0).wait()
    taps.wait()

    def band(j, lines, wide):
        no_top = (top == 1) & (j == 0)
        no_bottom = (bottom == 1) & (j == bands - 1)
        over = up[jnp.maximum(j - top, 0)].astype(F32)
        under = down[jnp.minimum(j + bottom, bands - 1)].astype(F32)
        middle = slice(8, 8 + cols)
        lines[0, middle] = jnp.where(no_top, 0.0, over)
        lines[1, middle] = held[j, 0].astype(F32)
        lines[2, middle] = held[j, 1].astype(F32)
        lines[3, middle] = jnp.where(no_bottom, 0.0, under)
        for a in range(4):
            for b in range(4):
                wide[a, :, b * chans : (b + 1) * chans] = lines[a, pl.ds(7 + b, half, stride=2), :].astype(BF16)
        total = silu(column_pairs(wide, 0, 2, taps) + taps.bias())
        for i in range(2):
            part = total[i * half : (i + 1) * half]
            for b in range(2):
                here = lines[i + 1, pl.ds(8 + b, half, stride=2), :]
                decoded = (here + part[:, b * chans : (b + 1) * chans]).astype(BF16).astype(F32)
                at = pl.ds(b, half, stride=2)
                canvas[2 * j + i, at, :] = canvas[2 * j + i, at, :] + decoded
            out[j, i] = canvas[2 * j + i].astype(BF16)

    @pl.loop(0, bands // BANDS_AT_ONCE)
    def _(step):
        first = BANDS_AT_ONCE * step
        for k in range(BANDS_AT_ONCE):
            from_feat(first + k).wait()
            from_above(first + k).wait()
            if k + 1 < BANDS_AT_ONCE:
                from_below(first + k + 1).wait()

        @pl.when(first + BANDS_AT_ONCE < bands)
        def _():
            from_below(first + BANDS_AT_ONCE).wait()

        for k in range(BANDS_AT_ONCE):
            band(first + k, lines.at[k], wide.at[k])
        for k in range(BANDS_AT_ONCE):
            leave(first + k).start()

    for j in range(bands):
        leave(j).wait()


def shards(features, dec_weight, dec_bias, first_weight, first_bias, second_weight, second_bias, boxes, slots):
    tiles = lax.axis_size("tile")
    dims = Dims(features, tiles)
    bands, cols, chans, local_rows = dims.bands, dims.cols, dims.chans, dims.local_rows
    assert dims.band_rows == 2 and slots.shape[0] == CAP * tiles and boxes.shape[1] == tiles
    assert tiles & (tiles - 1) == 0

    smem = pl.BlockSpec(memory_space=pltpu.SMEM)
    hbm = pl.BlockSpec(memory_space=pl.ANY)
    full = pltpu.CompilerParams(vmem_limit_bytes=FULL_GRANT)
    dma = pltpu.SemaphoreType.DMA

    def cost(flops, moved):
        return pl.CostEstimate(flops=int(flops), bytes_accessed=int(moved), transcendentals=0)

    def shaped(*shape, kind=BF16):
        return jax.ShapeDtypeStruct(shape, kind)

    def swap(array):
        return lax.all_to_all(array, "tile", split_axis=0, concat_axis=0, tiled=True)

    pack_scratch = [
        pltpu.VMEM((bands, 2, cols, chans), BF16),
        pltpu.VMEM((local_rows, cols + 16, chans), F32),
        pltpu.VMEM((dims.rim, chans), F32),
        pltpu.VMEM((tiles, dims.message, chans), BF16),
        pltpu.VMEM((tiles, dims.message, chans), BF16),
        dma((4,)),
        dma((bands,)),
        dma((2, tiles)),
    ]
    message = shaped(tiles, dims.message, chans)
    *sent_main, sent_extra, table, last, leading = pl.pallas_call(
        functools.partial(pack_kernel, dims),
        out_shape=[shaped(dims.message, chans)] * tiles
        + [message, shaped(7, tiles, kind=I32), shaped(bands, cols, chans), shaped(bands, cols, chans)],
        in_specs=[hbm, hbm, hbm],
        out_specs=[hbm] * (tiles + 1) + [smem, hbm, hbm],
        scratch_shapes=[
            pltpu.SMEM(boxes.shape, I32),
            pltpu.SMEM(slots.shape, I32),
            pltpu.SMEM((tiles,), I32),
            pltpu.SMEM((tiles,), I32),
            pltpu.SMEM((tiles + 1,), I32),
        ]
        + pack_scratch,
        compiler_params=full,
        cost_estimate=cost(0, 6e6),
        name="pack",
    )(boxes, slots, features)
    got_main = [sent_main[0]] + [None] * (tiles - 1)
    for s in [1] + sorted(range(2, tiles), key=lambda s: (-(s >> 1).bit_count(), -(s >> 1), s)):
        got_main[s] = lax.ppermute(sent_main[s], "tile", [(i, i ^ s) for i in range(tiles)])
    up = [(i, (i + 1) % tiles) for i in range(tiles)]
    above = lax.ppermute(last, "tile", up)
    below = lax.ppermute(leading, "tile", [(j, i) for i, j in up])

    got_extra = swap(sent_extra)

    weights = tuple(w.reshape(3, 3, chans, chans) for w in (dec_weight, first_weight, second_weight))
    biases = (dec_bias[None], first_bias[None], second_bias[None])
    restore_scratch = [
        pltpu.VMEM((tiles, dims.message, chans), BF16),
        pltpu.VMEM((4, 3, chans, 2 * chans), BF16),
        pltpu.VMEM((2, 3, 4, chans, 2 * chans), BF16),
        pltpu.VMEM((3, 1, chans), F32),
        dma((tiles,)),
        dma((3, 3)),
        pltpu.VMEM((SPAN // 2 + 2, 2, SPAN, 3 * chans), BF16),
        pltpu.VMEM((SPAN, SPAN, chans), F32),
        pltpu.VMEM((S + 2, S // 2, 4 * chans), BF16),
        pltpu.VMEM((S + 2, S // 2, 4 * chans), BF16),
        pltpu.VMEM((S, S, chans), F32),
        pltpu.VMEM((S, S, chans), BF16),
        dma((S // PIECE,)),
    ]
    restored_shape = shaped(CAP, S, S, chans)
    sent_back, partial = pl.pallas_call(
        functools.partial(main_kernel, dims),
        out_shape=[shaped(tiles, dims.back_rows, SPAN, chans), restored_shape],
        in_specs=[smem] + [hbm] * (tiles + 6),
        out_specs=[hbm, hbm],
        scratch_shapes=restore_scratch
        + [pltpu.VMEM((tiles, dims.back_rows, SPAN, chans), BF16), dma((tiles,))],
        compiler_params=full,
        cost_estimate=cost(7e9, 8e6),
        name="restore_main",
    )(table, *got_main, *weights, *biases)
    got_back = swap(sent_back)

    restorations = pl.pallas_call(
        functools.partial(extra_kernel, dims),
        out_shape=restored_shape,
        in_specs=[smem] + [hbm] * 8,
        out_specs=hbm,
        scratch_shapes=restore_scratch,
        input_output_aliases={8: 0},
        compiler_params=full,
        cost_estimate=cost(6e9, 8e6),
        name="restore_extra",
    )(table, got_extra, *weights, *biases, partial)

    above, below, restorations = lax.optimization_barrier((above, below, restorations))
    assert bands % BANDS_AT_ONCE == 0
    finished = pl.pallas_call(
        functools.partial(finish_kernel, dims),
        out_shape=shaped(*features.shape),
        in_specs=[smem] + [hbm] * 6,
        out_specs=hbm,
        scratch_shapes=[
            pltpu.VMEM((tiles, dims.back_rows, SPAN, chans), BF16),
            pltpu.VMEM((bands, 2, cols, chans), BF16),
            pltpu.VMEM((bands, cols, chans), BF16),
            pltpu.VMEM((bands, cols, chans), BF16),
            pltpu.VMEM((3, 4, chans, 2 * chans), BF16),
            pltpu.VMEM((1, chans), F32),
            pltpu.VMEM((BANDS_AT_ONCE, 4, cols + 16, chans), F32),
            pltpu.VMEM((BANDS_AT_ONCE, 4, cols // 2, 4 * chans), BF16),
            pltpu.VMEM((local_rows, cols, chans), F32),
            pltpu.VMEM((bands, 2, cols, chans), BF16),
            dma((1 + bands,)),
            dma((3, bands)),
            dma((3,)),
        ],
        compiler_params=full,
        cost_estimate=cost(3e9, 6e6),
        name="finish",
    )(table, got_back, features, above, below, weights[0], biases[0])
    return finished, restorations


def solution(mesh):
    return jax.shard_map(
        shards,
        mesh=mesh,
        in_specs=(
            P("sess", "tile", None, None),
            P(),
            P(),
            P(),
            P(),
            P(),
            P(),
            P(None, "sess"),
            P("sess"),
        ),
        out_specs=(P("sess", "tile", None, None), P(("sess", "tile"), None, None, None)),
        check_vma=False,
    )
```

```python
import functools

import jax
import jax.numpy as jnp
from jax import lax
from jax.experimental import pallas as pl
from jax.experimental.pallas import tpu as pltpu
from jax.sharding import PartitionSpec as P

S = 64
UNIT = 12
NCLS = 3
CAP = 2
PIECE = 16
BANDS_AT_ONCE = 3
SPAN = UNIT * (NCLS + 1)
BF16 = jnp.bfloat16
F32 = jnp.float32
I32 = jnp.int32
FULL_GRANT = 67000000
LAST_GRANT = 32 * 1024 * 1024
ROW, COL, SIDE, ROW2, COL2, SIDE2, PLACE = range(7)


def rows_within(window, band_rows, stride):
    return band_rows * (window // stride) + min(band_rows, window % stride)


class Dims:
    def __init__(self, features, tiles):
        self.bands, self.band_rows, self.cols, self.chans = features.shape
        self.tiles = tiles
        self.stride = tiles * self.band_rows
        self.shift = self.stride.bit_length() - 1
        self.local_rows = self.bands * self.band_rows
        self.rows = rows_within(SPAN + 2, self.band_rows, self.stride)
        self.back_rows = rows_within(SPAN, self.band_rows, self.stride)
        self.rim = -(-2 * self.rows // 16) * 16
        self.message = self.rows * SPAN + self.rim


def first_local(row, tile, dims):
    return ((row >> dims.shift) << 1) + jnp.clip((row & (dims.stride - 1)) - 2 * tile, 0, 2)


def global_row(local, tile, dims):
    return ((local >> 1) << dims.shift) + 2 * tile + (local & 1)


def silu(v):
    half = 0.5 * v
    return half + half * jnp.tanh(half)


def both(bias):
    return jnp.concatenate([bias, bias], -1)


class RowTaps:
    def __init__(self, source, bias, store, held, sems):
        chans = source.shape[-1]
        self.store = store
        self.held = held
        self.copies = (
            pltpu.make_async_copy(bias, held, sems.at[2]),
            pltpu.make_async_copy(source, store.at[0:3, :, :, 0:chans], sems.at[0]),
            pltpu.make_async_copy(source, store.at[1:4, :, :, chans : 2 * chans], sems.at[1]),
        )

    def start(self):
        for copy in self.copies:
            copy.start()
        chans = self.store.shape[2]
        none = jnp.zeros((3, chans, chans), BF16)
        self.store[3, :, :, 0:chans] = none
        self.store[0, :, :, chans : 2 * chans] = none

    def wait(self):
        for copy in self.copies:
            copy.wait()

    def bias(self):
        return both(self.held[...])

    def value(self):
        return self.store[...].reshape(-1, self.store.shape[-1])


class ColumnTaps(RowTaps):
    def __init__(self, source, bias, store, held, sems):
        chans = source.shape[-1]
        self.store = store
        self.held = held
        self.copies = (
            pltpu.make_async_copy(bias, held, sems.at[2]),
            pltpu.make_async_copy(source, store.at[:, 0:3, :, 0:chans], sems.at[0]),
            pltpu.make_async_copy(source, store.at[:, 1:4, :, chans : 2 * chans], sems.at[1]),
        )

    def start(self):
        for copy in self.copies:
            copy.start()
        chans = self.store.shape[2]
        none = jnp.zeros((3, chans, chans), BF16)
        self.store[:, 3, :, 0:chans] = none
        self.store[:, 0, :, chans : 2 * chans] = none


def two_chains(wide, taps):
    wide = wide.reshape(-1, wide.shape[-1])
    weight = taps.value()
    middle = weight.shape[0] // 2
    one = jnp.dot(wide[:, :middle], weight[:middle], preferred_element_type=F32)
    two = jnp.dot(wide[:, middle:], weight[middle:], preferred_element_type=F32)
    return one + two


def row_pairs(src, first, count, taps):
    parts = [
        src[pl.ds(first, count), 0],
        src[pl.ds(first, count), 1],
        src[pl.ds(first + 1, count), 0],
        src[pl.ds(first + 1, count), 1],
    ]
    return two_chains(jnp.concatenate(parts, -1), taps)


def column_pairs(src, first, count, taps):
    return two_chains(jnp.concatenate([src[pl.ds(first + a, count)] for a in range(3)], -1), taps)


def fill_canvas(dims, feat, held, canvas, sems):
    def copy(band):
        return pltpu.make_async_copy(feat.at[band], held.at[band], sems.at[band])

    for band in range(dims.bands):
        copy(band).start()

    def finish():
        edge = jnp.zeros((8, dims.chans), F32)
        for band in range(dims.bands):
            copy(band).wait()
            for i in range(2):
                row = 2 * band + i
                canvas[row, 0:8, :] = edge
                canvas[row, 8 + dims.cols : 16 + dims.cols, :] = edge
                canvas[row, 8 : 8 + dims.cols, :] = held[band, i].astype(F32)

    return finish


def pack_crop(dims, row0, col0, canvas, rim, staged):
    me = lax.axis_index("tile")
    start = first_local(jnp.maximum(row0 - 1, 0), me, dims)
    for i in range(dims.rows):
        row = jnp.minimum(start + i, dims.local_rows - 1)
        staged[i * SPAN : (i + 1) * SPAN, :] = canvas[row, pl.ds(col0 + 8, SPAN), :].astype(BF16)
        rim[2 * i : 2 * i + 1, :] = canvas[row, pl.ds(col0 + 7, 1), :]
        rim[2 * i + 1 : 2 * i + 2, :] = canvas[row, pl.ds(col0 + 8 + SPAN, 1), :]
    staged[dims.rows * SPAN :, :] = rim[...].astype(BF16)


def pack_kernel(
    dims, boxes_in, slots_in, feat, *refs
):
    sent, refs = refs[: dims.tiles], refs[dims.tiles :]
    sent_extra, table, last, leading, boxes, slots, main, extra, seconds, held, canvas, rim, staged, staged_extra, sems, feat_sems, sent_sems = refs
    me = lax.axis_index("tile")
    copies = (
        pltpu.make_async_copy(boxes_in, boxes, sems.at[0]),
        pltpu.make_async_copy(slots_in, slots, sems.at[1]),
    )
    for copy in copies:
        copy.start()
    finish = fill_canvas(dims, feat, held, canvas, feat_sems)
    for copy in copies:
        copy.wait()

    def first_pass(w, count):
        one = slots[CAP * w]
        two = slots[CAP * w + 1]
        full = (one >= 0) & (two >= 0)
        second = jnp.where(full, two, -1)
        main[w] = jnp.where(one >= 0, one, two)
        extra[w] = second
        seconds[count] = second
        return count + full.astype(I32)

    lax.fori_loop(0, dims.tiles, first_pass, jnp.int32(0))

    def second_pass(w, count):
        own = main[w]
        idle = own < 0
        crop = jnp.where(idle, seconds[count], own)
        table[ROW, w] = boxes[0, crop]
        table[COL, w] = boxes[1, crop]
        table[SIDE, w] = UNIT * (boxes[2, crop] + 2)
        other = jnp.maximum(extra[w], 0)
        table[ROW2, w] = boxes[0, other]
        table[COL2, w] = boxes[1, other]
        table[SIDE2, w] = jnp.where(extra[w] >= 0, UNIT * (boxes[2, other] + 2), 0)
        table[PLACE, w] = jnp.where(idle, 2, jnp.where(slots[CAP * w] >= 0, 0, 1))
        return count + idle.astype(I32)

    lax.fori_loop(0, dims.tiles, second_pass, jnp.int32(0))
    finish()
    rim[...] = jnp.zeros_like(rim)
    copies = [pltpu.make_async_copy(staged.at[s], sent[s], sent_sems.at[0, s]) for s in range(dims.tiles)]
    half = dims.tiles // 2
    for part in range(2):

        @pl.loop(part * half, (part + 1) * half)
        def _(s):
            pack_crop(dims, table[ROW, me ^ s], table[COL, me ^ s], canvas, rim, staged.at[s])

        for copy in copies[part * half : (part + 1) * half]:
            copy.start()
    edges = (
        pltpu.make_async_copy(held.at[:, 1], last, sems.at[2]),
        pltpu.make_async_copy(held.at[:, 0], leading, sems.at[3]),
    )
    for edge in edges:
        edge.start()

    def later(w):
        return pltpu.make_async_copy(staged_extra.at[w], sent_extra.at[w], sent_sems.at[1, w])

    @pl.loop(0, dims.tiles)
    def _(w):
        @pl.when(table[SIDE2, w] > 0)
        def _():
            pack_crop(dims, table[ROW2, w], table[COL2, w], canvas, rim, staged_extra.at[w])
            later(w).start()

    for copy in copies:
        copy.wait()
    for edge in edges:
        edge.wait()

    @pl.loop(0, dims.tiles)
    def _(w):
        @pl.when(table[SIDE2, w] > 0)
        def _():
            later(w).wait()


def restore(dims, row0, length, arrival, source, got, taps, raw, decoded, wide, inner, mixed, delta, finish):
    chans = dims.chans
    above = row0 - 1
    pairs = SPAN // 2
    half = S // 2
    nothing = jnp.zeros((SPAN, 3 * chans), BF16)
    raw[0, 0] = nothing
    raw[pairs, 1] = nothing
    empty = jnp.zeros((half, 4 * chans), BF16)
    for store in (wide, inner):
        store[0] = empty
        store[S + 1] = empty

    @pl.loop(0, dims.tiles)
    def _(s):
        arrival(s).wait()
        e = source(s)
        start = first_local(jnp.maximum(above, 0), e, dims)
        rim = got[s, dims.rows * SPAN :, :].astype(F32)
        at = lax.broadcasted_iota(I32, (SPAN, chans), 0)
        for i in range(dims.rows):
            local = start + i
            place = global_row(local, e, dims) - above
            place = jnp.where((local < dims.local_rows) & (place < SPAN + 2), place, SPAN + 2)
            line = got[s, i * SPAN : (i + 1) * SPAN, :]
            wider = line.astype(F32)
            left = jnp.where(at == 0, rim[2 * i : 2 * i + 1], pltpu.roll(wider, 1, 0))
            right = jnp.where(at == SPAN - 1, rim[2 * i + 1 : 2 * i + 2], pltpu.roll(wider, SPAN - 1, 0))
            raw[place >> 1, place & 1] = jnp.concatenate([left.astype(BF16), line, right.astype(BF16)], -1)

    taps[1].start()
    taps[2].start()
    taps[0].wait()
    n = 8
    for first in range(0, pairs, n):
        total = silu(row_pairs(raw, first, n, taps[0]) + taps[0].bias())
        for k in range(n):
            part = total[k * SPAN : (k + 1) * SPAN]
            at = 2 * (first + k)
            upper = raw[first + k, 1, :, chans : 2 * chans].astype(F32) + part[:, :chans]
            lower = raw[first + k + 1, 0, :, chans : 2 * chans].astype(F32) + part[:, chans:]
            decoded[at] = upper.astype(BF16).astype(F32)
            decoded[at + 1] = lower.astype(BF16).astype(F32)

    lengthf = length.astype(F32)
    block = lax.broadcasted_iota(I32, (4, half, SPAN), 0)
    t = 2 * lax.broadcasted_iota(I32, (4, half, SPAN), 1) + block - 1
    j = lax.broadcasted_iota(I32, (4, half, SPAN), 2).astype(F32)
    spots = jnp.clip((t.astype(F32) + 0.5) * lengthf / S - 0.5, 0.0, lengthf - 1.0)
    across = jnp.where((t >= 0) & (t < S), jnp.maximum(0.0, 1.0 - jnp.abs(spots - j)), 0.0)
    across = across.reshape(4 * half, SPAN).astype(BF16)
    taps[1].wait()
    taps[2].wait()
    for m in range(S // 2):
        lines = []
        for parity in range(2):
            s = 2 * m + parity
            spot = jnp.clip((2 * s + 1) * length - S, 0, (length - 1) * 2 * S)
            low = spot >> 7
            part = (spot & 127).astype(F32) * (1.0 / (2 * S))
            high = jnp.minimum(low + 1, SPAN - 1)
            lines.append(((1.0 - part) * decoded[low] + part * decoded[high]).astype(BF16))
        cells = jnp.dot(across, jnp.concatenate(lines, -1), preferred_element_type=F32).astype(BF16)
        for parity in range(2):
            at = 2 * m + parity + 1
            for b in range(4):
                wide[at, :, b * chans : (b + 1) * chans] = cells[
                    b * half : (b + 1) * half, parity * chans : (parity + 1) * chans
                ]

    n = PIECE
    for first in range(0, S, n):
        total = silu(column_pairs(wide, first, n, taps[1]) + taps[1].bias())
        at = lax.broadcasted_iota(I32, (n, half, chans), 1)
        even = pltpu.roll(total[:, :chans], n * half - 1, 0).reshape(n, half, chans)
        odd = pltpu.roll(total[:, chans:], 1, 0).reshape(n, half, chans)
        rows = pl.ds(first + 1, n)
        inner[rows, :, 0:chans] = jnp.where(at == 0, 0.0, odd).astype(BF16)
        inner[rows, :, chans : 3 * chans] = total.astype(BF16).reshape(n, half, 2 * chans)
        inner[rows, :, 3 * chans :] = jnp.where(at == half - 1, 0.0, even).astype(BF16)

    for first in range(0, S, n):
        total = column_pairs(inner, first, n, taps[2]) + taps[2].bias()
        for k in range(n):
            mixed[first + k, pl.ds(0, half, stride=2), :] = total[k * half : (k + 1) * half, :chans]
            mixed[first + k, pl.ds(1, half, stride=2), :] = total[k * half : (k + 1) * half, chans:]
        delta[first : first + n] = mixed[first : first + n].astype(BF16)
        finish(first // PIECE)


def begin(dims, arrived, weights, biases, scratch):
    got, row_store, column_store, held, got_sems, tap_sems = scratch

    def arrival(s):
        return pltpu.make_async_copy(arrived[0], got.at[s], got_sems.at[s])

    for s in range(dims.tiles):
        pltpu.make_async_copy(arrived[s], got.at[s], got_sems.at[s]).start()
    taps = (
        RowTaps(weights[0], biases[0], row_store, held.at[0], tap_sems.at[0]),
        ColumnTaps(weights[1], biases[1], column_store.at[0], held.at[1], tap_sems.at[1]),
        ColumnTaps(weights[2], biases[2], column_store.at[1], held.at[2], tap_sems.at[2]),
    )
    taps[0].start()
    return arrival, taps


def main_kernel(dims, table, *refs):
    tiles, chans = dims.tiles, dims.chans
    arrived, refs = refs[:tiles], refs[tiles:]
    (dec_w, one_w, two_w, dec_b, one_b, two_b, sent, restored, got, row_store, column_store, held) = refs[:12]
    got_sems, tap_sems, raw, decoded, wide, inner, mixed, delta, sem, back, back_sems = refs[12:]
    me = lax.axis_index("tile")
    row0 = table[ROW, me]
    length = table[SIDE, me]
    place = table[PLACE, me]
    scratch = (got, row_store, column_store, held, got_sems, tap_sems)
    arrival, taps = begin(dims, arrived, (dec_w, one_w, two_w), (dec_b, one_b, two_b), scratch)
    restore(
        dims, row0, length, arrival, lambda s: me ^ s, got, taps,
        raw, decoded, wide, inner, mixed, delta, lambda piece: None,
    )

    @pl.when(place < CAP)
    def _():
        pltpu.make_async_copy(delta, restored.at[place], sem.at[0]).start()

    lengthf = length.astype(F32)
    t = lax.broadcasted_iota(I32, (SPAN, S), 0).astype(F32)
    s = lax.broadcasted_iota(I32, (SPAN, S), 1).astype(F32)
    spots = jnp.clip((t + 0.5) * S / lengthf - 0.5, 0.0, S - 1.0)
    lift = jnp.where(t < lengthf, jnp.maximum(0.0, 1.0 - jnp.abs(spots - s)), 0.0)
    coarse = lift.astype(BF16)
    lift = jnp.concatenate([coarse, (lift - coarse.astype(F32)).astype(BF16)], 0)
    scale = 1.0 / (2.0 * lengthf)
    group = 12

    @pl.loop(0, SPAN // 2 // group)
    def _(step):
        for k in range(group):
            lines = []
            for parity in range(2):
                h = 2 * (step * group + k) + parity
                spot = jnp.clip((2 * h + 1) * S - length, 0, (S - 1) * 2 * length)
                low = ((spot.astype(F32) + 0.5) * scale).astype(I32)
                part = (spot - low * 2 * length).astype(F32) * scale
                high = jnp.minimum(low + 1, S - 1)
                lines.append(((1.0 - part) * delta[low].astype(F32) + part * delta[high].astype(F32)).astype(BF16))
            patch = jnp.dot(lift, jnp.concatenate(lines, -1), preferred_element_type=F32)
            patch = (patch[:SPAN] + patch[SPAN:]).astype(BF16)
            for parity in range(2):
                row = row0 + 2 * (step * group + k) + parity
                dest = (row & (dims.stride - 1)) >> 1
                local = ((row >> dims.shift) << 1) + (row & 1)
                back[dest, local - first_local(row0, dest, dims)] = patch[:, parity * chans : (parity + 1) * chans]

    def leave(e):
        return pltpu.make_async_copy(back.at[e], sent.at[e], back_sems.at[e])

    for e in range(tiles):
        leave(e).start()
    for e in range(tiles):
        leave(e).wait()

    @pl.when(place < CAP)
    def _():
        pltpu.make_async_copy(delta, restored.at[place], sem.at[0]).wait()


def extra_kernel(
    dims, table, arrived, dec_w, one_w, two_w, dec_b, one_b, two_b, partial, restored,
    got, row_store, column_store, held, got_sems, tap_sems, raw, decoded, wide, inner, mixed, delta, sem,
):
    me = lax.axis_index("tile")
    row0 = table[ROW2, me]
    length = table[SIDE2, me]
    place = table[PLACE, me]

    def write(slot):
        copy = pltpu.make_async_copy(delta, restored.at[slot], sem.at[0])
        copy.start()
        copy.wait()

    @pl.when(length > 0)
    def _():
        scratch = (got, row_store, column_store, held, got_sems, tap_sems)
        arrival, taps = begin(dims, [arrived.at[s] for s in range(dims.tiles)], (dec_w, one_w, two_w), (dec_b, one_b, two_b), scratch)

        def leave(piece):
            rows = pl.ds(piece * PIECE, PIECE)
            return pltpu.make_async_copy(delta.at[rows], restored.at[1, rows], sem.at[piece])

        restore(
            dims, row0, length, arrival, lambda s: s, got, taps,
            raw, decoded, wide, inner, mixed, delta, lambda piece: leave(piece).start(),
        )
        for piece in range(S // PIECE):
            leave(piece).wait()

    @pl.when(length == 0)
    def _():
        delta[...] = jnp.zeros_like(delta)

        @pl.when(place != 0)
        def _():
            write(0)

        @pl.when(place != 1)
        def _():
            write(1)


def finish_kernel(
    dims, table, back, feat, above, below, weight, bias, finished,
    got, held, up, down, store, held_bias, lines, wide, canvas, out, sems, load_sems, tap_sems,
):
    me = lax.axis_index("tile")
    bands, chans, cols = dims.bands, dims.chans, dims.cols
    half = cols // 2
    taps = ColumnTaps(weight, bias, store, held_bias, tap_sems)
    patches = pltpu.make_async_copy(back, got, sems.at[0])
    patches.start()
    def from_feat(band):
        return pltpu.make_async_copy(feat.at[band], held.at[band], load_sems.at[0, band])

    def from_above(band):
        return pltpu.make_async_copy(above.at[band], up.at[band], load_sems.at[1, band])

    def from_below(band):
        return pltpu.make_async_copy(below.at[band], down.at[band], load_sems.at[2, band])

    taps.start()
    from_below(0).start()
    for j in range(bands):
        from_feat(j).start()
        from_above(j).start()
        if j + 1 < bands:
            from_below(j + 1).start()

    def leave(band):
        return pltpu.make_async_copy(out.at[band], finished.at[band], sems.at[1 + band])

    top = (me == 0).astype(I32)
    bottom = (me == dims.tiles - 1).astype(I32)
    edge = jnp.zeros((8, chans), F32)
    for k in range(lines.shape[0]):
        for a in range(4):
            lines[k, a, 0:8] = edge
            lines[k, a, 8 + cols :] = edge
    canvas[...] = jnp.zeros_like(canvas)
    patches.wait()

    @pl.loop(0, dims.tiles)
    def _(e):
        row0 = table[ROW, e]
        col0 = table[COL, e]
        length = table[SIDE, e]
        start = first_local(row0, me, dims)
        for i in range(dims.back_rows):
            local = start + i

            @pl.when((local < dims.local_rows) & (global_row(local, me, dims) - row0 < length))
            def _():
                canvas[local, pl.ds(col0, SPAN), :] += got[e, i].astype(F32)

    from_below(0).wait()
    taps.wait()

    def band(j, lines, wide):
        no_top = (top == 1) & (j == 0)
        no_bottom = (bottom == 1) & (j == bands - 1)
        over = up[jnp.maximum(j - top, 0)].astype(F32)
        under = down[jnp.minimum(j + bottom, bands - 1)].astype(F32)
        middle = slice(8, 8 + cols)
        lines[0, middle] = jnp.where(no_top, 0.0, over)
        lines[1, middle] = held[j, 0].astype(F32)
        lines[2, middle] = held[j, 1].astype(F32)
        lines[3, middle] = jnp.where(no_bottom, 0.0, under)
        for a in range(4):
            for b in range(4):
                wide[a, :, b * chans : (b + 1) * chans] = lines[a, pl.ds(7 + b, half, stride=2), :].astype(BF16)
        total = silu(column_pairs(wide, 0, 2, taps) + taps.bias())
        for i in range(2):
            part = total[i * half : (i + 1) * half]
            for b in range(2):
                here = lines[i + 1, pl.ds(8 + b, half, stride=2), :]
                decoded = (here + part[:, b * chans : (b + 1) * chans]).astype(BF16).astype(F32)
                at = pl.ds(b, half, stride=2)
                canvas[2 * j + i, at, :] = canvas[2 * j + i, at, :] + decoded
            out[j, i] = canvas[2 * j + i].astype(BF16)

    @pl.loop(0, bands // BANDS_AT_ONCE)
    def _(step):
        first = BANDS_AT_ONCE * step
        for k in range(BANDS_AT_ONCE):
            from_feat(first + k).wait()
            from_above(first + k).wait()
            if k + 1 < BANDS_AT_ONCE:
                from_below(first + k + 1).wait()

        @pl.when(first + BANDS_AT_ONCE < bands)
        def _():
            from_below(first + BANDS_AT_ONCE).wait()

        for k in range(BANDS_AT_ONCE):
            band(first + k, lines.at[k], wide.at[k])
        for k in range(BANDS_AT_ONCE):
            leave(first + k).start()

    for j in range(bands):
        leave(j).wait()


def shards(features, dec_weight, dec_bias, first_weight, first_bias, second_weight, second_bias, boxes, slots):
    tiles = lax.axis_size("tile")
    dims = Dims(features, tiles)
    bands, cols, chans, local_rows = dims.bands, dims.cols, dims.chans, dims.local_rows
    assert dims.band_rows == 2 and slots.shape[0] == CAP * tiles and boxes.shape[1] == tiles
    assert tiles & (tiles - 1) == 0

    smem = pl.BlockSpec(memory_space=pltpu.SMEM)
    hbm = pl.BlockSpec(memory_space=pl.ANY)
    full = pltpu.CompilerParams(vmem_limit_bytes=FULL_GRANT)
    dma = pltpu.SemaphoreType.DMA

    def cost(flops, moved):
        return pl.CostEstimate(flops=int(flops), bytes_accessed=int(moved), transcendentals=0)

    def shaped(*shape, kind=BF16):
        return jax.ShapeDtypeStruct(shape, kind)

    def swap(array):
        return lax.all_to_all(array, "tile", split_axis=0, concat_axis=0, tiled=True)

    pack_scratch = [
        pltpu.VMEM((bands, 2, cols, chans), BF16),
        pltpu.VMEM((local_rows, cols + 16, chans), F32),
        pltpu.VMEM((dims.rim, chans), F32),
        pltpu.VMEM((tiles, dims.message, chans), BF16),
        pltpu.VMEM((tiles, dims.message, chans), BF16),
        dma((4,)),
        dma((bands,)),
        dma((2, tiles)),
    ]
    message = shaped(tiles, dims.message, chans)
    *sent_main, sent_extra, table, last, leading = pl.pallas_call(
        functools.partial(pack_kernel, dims),
        out_shape=[shaped(dims.message, chans)] * tiles
        + [message, shaped(7, tiles, kind=I32), shaped(bands, cols, chans), shaped(bands, cols, chans)],
        in_specs=[hbm, hbm, hbm],
        out_specs=[hbm] * (tiles + 1) + [smem, hbm, hbm],
        scratch_shapes=[
            pltpu.SMEM(boxes.shape, I32),
            pltpu.SMEM(slots.shape, I32),
            pltpu.SMEM((tiles,), I32),
            pltpu.SMEM((tiles,), I32),
            pltpu.SMEM((tiles + 1,), I32),
        ]
        + pack_scratch,
        compiler_params=full,
        cost_estimate=cost(0, 6e6),
        name="pack",
    )(boxes, slots, features)
    got_main = [sent_main[0]] + [None] * (tiles - 1)
    for s in [1] + sorted(range(2, tiles), key=lambda s: (-(s >> 1).bit_count(), -(s >> 1), s)):
        got_main[s] = lax.ppermute(sent_main[s], "tile", [(i, i ^ s) for i in range(tiles)])
    up = [(i, (i + 1) % tiles) for i in range(tiles)]
    above = lax.ppermute(last, "tile", up)
    below = lax.ppermute(leading, "tile", [(j, i) for i, j in up])

    got_extra = swap(sent_extra)

    weights = tuple(w.reshape(3, 3, chans, chans) for w in (dec_weight, first_weight, second_weight))
    biases = (dec_bias[None], first_bias[None], second_bias[None])
    restore_scratch = [
        pltpu.VMEM((tiles, dims.message, chans), BF16),
        pltpu.VMEM((4, 3, chans, 2 * chans), BF16),
        pltpu.VMEM((2, 3, 4, chans, 2 * chans), BF16),
        pltpu.VMEM((3, 1, chans), F32),
        dma((tiles,)),
        dma((3, 3)),
        pltpu.VMEM((SPAN // 2 + 2, 2, SPAN, 3 * chans), BF16),
        pltpu.VMEM((SPAN, SPAN, chans), F32),
        pltpu.VMEM((S + 2, S // 2, 4 * chans), BF16),
        pltpu.VMEM((S + 2, S // 2, 4 * chans), BF16),
        pltpu.VMEM((S, S, chans), F32),
        pltpu.VMEM((S, S, chans), BF16),
        dma((S // PIECE,)),
    ]
    restored_shape = shaped(CAP, S, S, chans)
    sent_back, partial = pl.pallas_call(
        functools.partial(main_kernel, dims),
        out_shape=[shaped(tiles, dims.back_rows, SPAN, chans), restored_shape],
        in_specs=[smem] + [hbm] * (tiles + 6),
        out_specs=[hbm, hbm],
        scratch_shapes=restore_scratch
        + [pltpu.VMEM((tiles, dims.back_rows, SPAN, chans), BF16), dma((tiles,))],
        compiler_params=full,
        cost_estimate=cost(7e9, 8e6),
        name="restore_main",
    )(table, *got_main, *weights, *biases)
    got_back = swap(sent_back)

    restorations = pl.pallas_call(
        functools.partial(extra_kernel, dims),
        out_shape=restored_shape,
        in_specs=[smem] + [hbm] * 8,
        out_specs=hbm,
        scratch_shapes=restore_scratch,
        input_output_aliases={8: 0},
        compiler_params=full,
        cost_estimate=cost(6e9, 8e6),
        name="restore_extra",
    )(table, got_extra, *weights, *biases, partial)

    above, below, restorations = lax.optimization_barrier((above, below, restorations))
    assert bands % BANDS_AT_ONCE == 0
    finished = pl.pallas_call(
        functools.partial(finish_kernel, dims),
        out_shape=shaped(*features.shape),
        in_specs=[smem] + [hbm] * 6,
        out_specs=hbm,
        scratch_shapes=[
            pltpu.VMEM((tiles, dims.back_rows, SPAN, chans), BF16),
            pltpu.VMEM((bands, 2, cols, chans), BF16),
            pltpu.VMEM((bands, cols, chans), BF16),
            pltpu.VMEM((bands, cols, chans), BF16),
            pltpu.VMEM((3, 4, chans, 2 * chans), BF16),
            pltpu.VMEM((1, chans), F32),
            pltpu.VMEM((BANDS_AT_ONCE, 4, cols + 16, chans), F32),
            pltpu.VMEM((BANDS_AT_ONCE, 4, cols // 2, 4 * chans), BF16),
            pltpu.VMEM((local_rows, cols, chans), F32),
            pltpu.VMEM((bands, 2, cols, chans), BF16),
            dma((1 + bands,)),
            dma((3, bands)),
            dma((3,)),
        ],
        compiler_params=pltpu.CompilerParams(vmem_limit_bytes=LAST_GRANT),
        cost_estimate=cost(3e9, 6e6),
        name="finish",
    )(table, got_back, features, above, below, weights[0], biases[0])
    return finished, restorations


def solution(mesh):
    return jax.shard_map(
        shards,
        mesh=mesh,
        in_specs=(
            P("sess", "tile", None, None),
            P(),
            P(),
            P(),
            P(),
            P(),
            P(),
            P(None, "sess"),
            P("sess"),
        ),
        out_specs=(P("sess", "tile", None, None), P(("sess", "tile"), None, None, None)),
        check_vma=False,
    )
```

```python
import functools

import jax
import jax.numpy as jnp
from jax import lax
from jax.experimental import pallas as pl
from jax.experimental.pallas import tpu as pltpu
from jax.sharding import PartitionSpec as P

S = 64
UNIT = 12
NCLS = 3
CAP = 2
PIECE = 16
BANDS_AT_ONCE = 3
SPAN = UNIT * (NCLS + 1)
BF16 = jnp.bfloat16
F32 = jnp.float32
I32 = jnp.int32
FULL_GRANT = 67000000
ROW, COL, SIDE, ROW2, COL2, SIDE2, PLACE = range(7)


def rows_within(window, band_rows, stride):
    return band_rows * (window // stride) + min(band_rows, window % stride)


class Dims:
    def __init__(self, features, tiles):
        self.bands, self.band_rows, self.cols, self.chans = features.shape
        self.tiles = tiles
        self.stride = tiles * self.band_rows
        self.shift = self.stride.bit_length() - 1
        self.local_rows = self.bands * self.band_rows
        self.rows = rows_within(SPAN + 2, self.band_rows, self.stride)
        self.back_rows = rows_within(SPAN, self.band_rows, self.stride)
        self.rim = -(-2 * self.rows // 16) * 16
        self.message = self.rows * SPAN + self.rim


def first_local(row, tile, dims):
    return ((row >> dims.shift) << 1) + jnp.clip((row & (dims.stride - 1)) - 2 * tile, 0, 2)


def global_row(local, tile, dims):
    return ((local >> 1) << dims.shift) + 2 * tile + (local & 1)


def silu(v):
    half = 0.5 * v
    return half + half * jnp.tanh(half)


def both(bias):
    return jnp.concatenate([bias, bias], -1)


class RowTaps:
    def __init__(self, source, bias, store, held, sems):
        chans = source.shape[-1]
        self.store = store
        self.held = held
        self.copies = (
            pltpu.make_async_copy(bias, held, sems.at[2]),
            pltpu.make_async_copy(source, store.at[0:3, :, :, 0:chans], sems.at[0]),
            pltpu.make_async_copy(source, store.at[1:4, :, :, chans : 2 * chans], sems.at[1]),
        )

    def start(self):
        for copy in self.copies:
            copy.start()
        chans = self.store.shape[2]
        none = jnp.zeros((3, chans, chans), BF16)
        self.store[3, :, :, 0:chans] = none
        self.store[0, :, :, chans : 2 * chans] = none

    def wait(self):
        for copy in self.copies:
            copy.wait()

    def bias(self):
        return both(self.held[...])

    def value(self):
        return self.store[...].reshape(-1, self.store.shape[-1])


class ColumnTaps(RowTaps):
    def __init__(self, source, bias, store, held, sems):
        chans = source.shape[-1]
        self.store = store
        self.held = held
        self.copies = (
            pltpu.make_async_copy(bias, held, sems.at[2]),
            pltpu.make_async_copy(source, store.at[:, 0:3, :, 0:chans], sems.at[0]),
            pltpu.make_async_copy(source, store.at[:, 1:4, :, chans : 2 * chans], sems.at[1]),
        )

    def start(self):
        for copy in self.copies:
            copy.start()
        chans = self.store.shape[2]
        none = jnp.zeros((3, chans, chans), BF16)
        self.store[:, 3, :, 0:chans] = none
        self.store[:, 0, :, chans : 2 * chans] = none


def two_chains(wide, taps):
    wide = wide.reshape(-1, wide.shape[-1])
    weight = taps.value()
    middle = weight.shape[0] // 2
    one = jnp.dot(wide[:, :middle], weight[:middle], preferred_element_type=F32)
    two = jnp.dot(wide[:, middle:], weight[middle:], preferred_element_type=F32)
    return one + two


def row_pairs(src, first, count, taps):
    parts = [
        src[pl.ds(first, count), 0],
        src[pl.ds(first, count), 1],
        src[pl.ds(first + 1, count), 0],
        src[pl.ds(first + 1, count), 1],
    ]
    return two_chains(jnp.concatenate(parts, -1), taps)


def column_pairs(src, first, count, taps):
    return two_chains(jnp.concatenate([src[pl.ds(first + a, count)] for a in range(3)], -1), taps)


def fill_canvas(dims, feat, held, canvas, sems):
    def copy(band):
        return pltpu.make_async_copy(feat.at[band], held.at[band], sems.at[band])

    for band in range(dims.bands):
        copy(band).start()

    def finish():
        edge = jnp.zeros((8, dims.chans), F32)
        for band in range(dims.bands):
            copy(band).wait()
            for i in range(2):
                row = 2 * band + i
                canvas[row, 0:8, :] = edge
                canvas[row, 8 + dims.cols : 16 + dims.cols, :] = edge
                canvas[row, 8 : 8 + dims.cols, :] = held[band, i].astype(F32)

    return finish


def pack_crops(dims, table, row_at, col_at, canvas, rim, staged, partner):
    me = lax.axis_index("tile")
    rim[...] = jnp.zeros_like(rim)

    @pl.loop(0, dims.tiles)
    def _(s):
        w = partner(s)
        row0 = table[row_at, w]
        col0 = table[col_at, w]
        start = first_local(jnp.maximum(row0 - 1, 0), me, dims)
        for i in range(dims.rows):
            row = jnp.minimum(start + i, dims.local_rows - 1)
            staged[s, i * SPAN : (i + 1) * SPAN, :] = canvas[row, pl.ds(col0 + 8, SPAN), :].astype(BF16)
            rim[2 * i : 2 * i + 1, :] = canvas[row, pl.ds(col0 + 7, 1), :]
            rim[2 * i + 1 : 2 * i + 2, :] = canvas[row, pl.ds(col0 + 8 + SPAN, 1), :]
        staged[s, dims.rows * SPAN :, :] = rim[...].astype(BF16)


def pack_kernel(
    dims, boxes_in, slots_in, feat, *refs
):
    sent, refs = refs[: dims.tiles], refs[dims.tiles :]
    sent_extra, table, last, leading, boxes, slots, main, extra, seconds, held, canvas, rim, staged, staged_extra, sems, feat_sems, sent_sems = refs
    me = lax.axis_index("tile")
    copies = (
        pltpu.make_async_copy(boxes_in, boxes, sems.at[0]),
        pltpu.make_async_copy(slots_in, slots, sems.at[1]),
    )
    for copy in copies:
        copy.start()
    finish = fill_canvas(dims, feat, held, canvas, feat_sems)
    for copy in copies:
        copy.wait()

    def first_pass(w, count):
        one = slots[CAP * w]
        two = slots[CAP * w + 1]
        full = (one >= 0) & (two >= 0)
        second = jnp.where(full, two, -1)
        main[w] = jnp.where(one >= 0, one, two)
        extra[w] = second
        seconds[count] = second
        return count + full.astype(I32)

    lax.fori_loop(0, dims.tiles, first_pass, jnp.int32(0))

    def second_pass(w, count):
        own = main[w]
        idle = own < 0
        crop = jnp.where(idle, seconds[count], own)
        table[ROW, w] = boxes[0, crop]
        table[COL, w] = boxes[1, crop]
        table[SIDE, w] = UNIT * (boxes[2, crop] + 2)
        other = jnp.maximum(extra[w], 0)
        table[ROW2, w] = boxes[0, other]
        table[COL2, w] = boxes[1, other]
        table[SIDE2, w] = jnp.where(extra[w] >= 0, UNIT * (boxes[2, other] + 2), 0)
        table[PLACE, w] = jnp.where(idle, 2, jnp.where(slots[CAP * w] >= 0, 0, 1))
        return count + idle.astype(I32)

    lax.fori_loop(0, dims.tiles, second_pass, jnp.int32(0))
    finish()
    edges = (
        pltpu.make_async_copy(held.at[:, 1], last, sems.at[2]),
        pltpu.make_async_copy(held.at[:, 0], leading, sems.at[3]),
    )
    for edge in edges:
        edge.start()
    pack_crops(dims, table, ROW, COL, canvas, rim, staged, lambda s: me ^ s)
    copies = [pltpu.make_async_copy(staged.at[s], sent[s], sent_sems.at[s]) for s in range(dims.tiles)]
    for copy in copies:
        copy.start()
    pack_crops(dims, table, ROW2, COL2, canvas, rim, staged_extra, lambda s: s)
    later = pltpu.make_async_copy(staged_extra, sent_extra, sems.at[0])
    later.start()
    for copy in copies:
        copy.wait()
    later.wait()
    for edge in edges:
        edge.wait()


def restore(dims, row0, length, arrival, source, got, taps, raw, decoded, wide, inner, mixed, delta, finish):
    chans = dims.chans
    above = row0 - 1
    pairs = SPAN // 2
    half = S // 2
    nothing = jnp.zeros((SPAN, 3 * chans), BF16)
    raw[0, 0] = nothing
    raw[pairs, 1] = nothing
    empty = jnp.zeros((half, 4 * chans), BF16)
    for store in (wide, inner):
        store[0] = empty
        store[S + 1] = empty

    @pl.loop(0, dims.tiles)
    def _(s):
        arrival(s).wait()
        e = source(s)
        start = first_local(jnp.maximum(above, 0), e, dims)
        rim = got[s, dims.rows * SPAN :, :].astype(F32)
        at = lax.broadcasted_iota(I32, (SPAN, chans), 0)
        for i in range(dims.rows):
            local = start + i
            place = global_row(local, e, dims) - above
            place = jnp.where((local < dims.local_rows) & (place < SPAN + 2), place, SPAN + 2)
            line = got[s, i * SPAN : (i + 1) * SPAN, :]
            wider = line.astype(F32)
            left = jnp.where(at == 0, rim[2 * i : 2 * i + 1], pltpu.roll(wider, 1, 0))
            right = jnp.where(at == SPAN - 1, rim[2 * i + 1 : 2 * i + 2], pltpu.roll(wider, SPAN - 1, 0))
            raw[place >> 1, place & 1] = jnp.concatenate([left.astype(BF16), line, right.astype(BF16)], -1)

    taps[1].start()
    taps[2].start()
    taps[0].wait()
    n = 8
    for first in range(0, pairs, n):
        total = silu(row_pairs(raw, first, n, taps[0]) + taps[0].bias())
        for k in range(n):
            part = total[k * SPAN : (k + 1) * SPAN]
            at = 2 * (first + k)
            upper = raw[first + k, 1, :, chans : 2 * chans].astype(F32) + part[:, :chans]
            lower = raw[first + k + 1, 0, :, chans : 2 * chans].astype(F32) + part[:, chans:]
            decoded[at] = upper.astype(BF16).astype(F32)
            decoded[at + 1] = lower.astype(BF16).astype(F32)

    lengthf = length.astype(F32)
    block = lax.broadcasted_iota(I32, (4, half, SPAN), 0)
    t = 2 * lax.broadcasted_iota(I32, (4, half, SPAN), 1) + block - 1
    j = lax.broadcasted_iota(I32, (4, half, SPAN), 2).astype(F32)
    spots = jnp.clip((t.astype(F32) + 0.5) * lengthf / S - 0.5, 0.0, lengthf - 1.0)
    across = jnp.where((t >= 0) & (t < S), jnp.maximum(0.0, 1.0 - jnp.abs(spots - j)), 0.0)
    across = across.reshape(4 * half, SPAN).astype(BF16)
    taps[1].wait()
    taps[2].wait()
    for m in range(S // 2):
        lines = []
        for parity in range(2):
            s = 2 * m + parity
            spot = jnp.clip((2 * s + 1) * length - S, 0, (length - 1) * 2 * S)
            low = spot >> 7
            part = (spot & 127).astype(F32) * (1.0 / (2 * S))
            high = jnp.minimum(low + 1, SPAN - 1)
            lines.append(((1.0 - part) * decoded[low] + part * decoded[high]).astype(BF16))
        cells = jnp.dot(across, jnp.concatenate(lines, -1), preferred_element_type=F32).astype(BF16)
        for parity in range(2):
            at = 2 * m + parity + 1
            for b in range(4):
                wide[at, :, b * chans : (b + 1) * chans] = cells[
                    b * half : (b + 1) * half, parity * chans : (parity + 1) * chans
                ]

    n = PIECE
    for first in range(0, S, n):
        total = silu(column_pairs(wide, first, n, taps[1]) + taps[1].bias())
        at = lax.broadcasted_iota(I32, (n, half, chans), 1)
        even = pltpu.roll(total[:, :chans], n * half - 1, 0).reshape(n, half, chans)
        odd = pltpu.roll(total[:, chans:], 1, 0).reshape(n, half, chans)
        rows = pl.ds(first + 1, n)
        inner[rows, :, 0:chans] = jnp.where(at == 0, 0.0, odd).astype(BF16)
        inner[rows, :, chans : 3 * chans] = total.astype(BF16).reshape(n, half, 2 * chans)
        inner[rows, :, 3 * chans :] = jnp.where(at == half - 1, 0.0, even).astype(BF16)

    for first in range(0, S, n):
        total = column_pairs(inner, first, n, taps[2]) + taps[2].bias()
        for k in range(n):
            mixed[first + k, pl.ds(0, half, stride=2), :] = total[k * half : (k + 1) * half, :chans]
            mixed[first + k, pl.ds(1, half, stride=2), :] = total[k * half : (k + 1) * half, chans:]
        delta[first : first + n] = mixed[first : first + n].astype(BF16)
        finish(first // PIECE)


def begin(dims, arrived, weights, biases, scratch):
    got, row_store, column_store, held, got_sems, tap_sems = scratch

    def arrival(s):
        return pltpu.make_async_copy(arrived[0], got.at[s], got_sems.at[s])

    for s in range(dims.tiles):
        pltpu.make_async_copy(arrived[s], got.at[s], got_sems.at[s]).start()
    taps = (
        RowTaps(weights[0], biases[0], row_store, held.at[0], tap_sems.at[0]),
        ColumnTaps(weights[1], biases[1], column_store.at[0], held.at[1], tap_sems.at[1]),
        ColumnTaps(weights[2], biases[2], column_store.at[1], held.at[2], tap_sems.at[2]),
    )
    taps[0].start()
    return arrival, taps


def main_kernel(dims, table, *refs):
    tiles, chans = dims.tiles, dims.chans
    arrived, refs = refs[:tiles], refs[tiles:]
    (dec_w, one_w, two_w, dec_b, one_b, two_b, sent, restored, got, row_store, column_store, held) = refs[:12]
    got_sems, tap_sems, raw, decoded, wide, inner, mixed, delta, sem, back, back_sems = refs[12:]
    me = lax.axis_index("tile")
    row0 = table[ROW, me]
    length = table[SIDE, me]
    place = table[PLACE, me]
    scratch = (got, row_store, column_store, held, got_sems, tap_sems)
    arrival, taps = begin(dims, arrived, (dec_w, one_w, two_w), (dec_b, one_b, two_b), scratch)
    restore(
        dims, row0, length, arrival, lambda s: me ^ s, got, taps,
        raw, decoded, wide, inner, mixed, delta, lambda piece: None,
    )

    @pl.when(place < CAP)
    def _():
        pltpu.make_async_copy(delta, restored.at[place], sem.at[0]).start()

    lengthf = length.astype(F32)
    t = lax.broadcasted_iota(I32, (SPAN, S), 0).astype(F32)
    s = lax.broadcasted_iota(I32, (SPAN, S), 1).astype(F32)
    spots = jnp.clip((t + 0.5) * S / lengthf - 0.5, 0.0, S - 1.0)
    lift = jnp.where(t < lengthf, jnp.maximum(0.0, 1.0 - jnp.abs(spots - s)), 0.0)
    coarse = lift.astype(BF16)
    lift = jnp.concatenate([coarse, (lift - coarse.astype(F32)).astype(BF16)], 0)
    scale = 1.0 / (2.0 * lengthf)
    group = 12

    @pl.loop(0, SPAN // 2 // group)
    def _(step):
        for k in range(group):
            lines = []
            for parity in range(2):
                h = 2 * (step * group + k) + parity
                spot = jnp.clip((2 * h + 1) * S - length, 0, (S - 1) * 2 * length)
                low = ((spot.astype(F32) + 0.5) * scale).astype(I32)
                part = (spot - low * 2 * length).astype(F32) * scale
                high = jnp.minimum(low + 1, S - 1)
                lines.append(((1.0 - part) * delta[low].astype(F32) + part * delta[high].astype(F32)).astype(BF16))
            patch = jnp.dot(lift, jnp.concatenate(lines, -1), preferred_element_type=F32)
            patch = (patch[:SPAN] + patch[SPAN:]).astype(BF16)
            for parity in range(2):
                row = row0 + 2 * (step * group + k) + parity
                dest = (row & (dims.stride - 1)) >> 1
                local = ((row >> dims.shift) << 1) + (row & 1)
                back[dest, local - first_local(row0, dest, dims)] = patch[:, parity * chans : (parity + 1) * chans]

    def leave(e):
        return pltpu.make_async_copy(back.at[e], sent.at[e], back_sems.at[e])

    for e in range(tiles):
        leave(e).start()
    for e in range(tiles):
        leave(e).wait()

    @pl.when(place < CAP)
    def _():
        pltpu.make_async_copy(delta, restored.at[place], sem.at[0]).wait()


def extra_kernel(
    dims, table, arrived, dec_w, one_w, two_w, dec_b, one_b, two_b, partial, restored,
    got, row_store, column_store, held, got_sems, tap_sems, raw, decoded, wide, inner, mixed, delta, sem,
):
    me = lax.axis_index("tile")
    row0 = table[ROW2, me]
    length = table[SIDE2, me]
    place = table[PLACE, me]

    def write(slot):
        copy = pltpu.make_async_copy(delta, restored.at[slot], sem.at[0])
        copy.start()
        copy.wait()

    @pl.when(length > 0)
    def _():
        scratch = (got, row_store, column_store, held, got_sems, tap_sems)
        arrival, taps = begin(dims, [arrived.at[s] for s in range(dims.tiles)], (dec_w, one_w, two_w), (dec_b, one_b, two_b), scratch)

        def leave(piece):
            rows = pl.ds(piece * PIECE, PIECE)
            return pltpu.make_async_copy(delta.at[rows], restored.at[1, rows], sem.at[piece])

        restore(
            dims, row0, length, arrival, lambda s: s, got, taps,
            raw, decoded, wide, inner, mixed, delta, lambda piece: leave(piece).start(),
        )
        for piece in range(S // PIECE):
            leave(piece).wait()

    @pl.when(length == 0)
    def _():
        delta[...] = jnp.zeros_like(delta)

        @pl.when(place != 0)
        def _():
            write(0)

        @pl.when(place != 1)
        def _():
            write(1)


def decode_kernel(
    dims, feat, above, below, weight, bias, finished,
    held, up, down, store, held_bias, lines, wide, mixed, out, sems, load_sems, tap_sems,
):
    me = lax.axis_index("tile")
    bands, chans, cols = dims.bands, dims.chans, dims.cols
    half = cols // 2
    taps = ColumnTaps(weight, bias, store, held_bias, tap_sems)
    def from_feat(band):
        return pltpu.make_async_copy(feat.at[band], held.at[band], load_sems.at[0, band])

    def from_above(band):
        return pltpu.make_async_copy(above.at[band], up.at[band], load_sems.at[1, band])

    def from_below(band):
        return pltpu.make_async_copy(below.at[band], down.at[band], load_sems.at[2, band])

    taps.start()
    from_below(0).start()
    for j in range(bands):
        from_feat(j).start()
        from_above(j).start()
        if j + 1 < bands:
            from_below(j + 1).start()

    def leave(band):
        return pltpu.make_async_copy(out.at[band], finished.at[band], sems.at[band])

    top = (me == 0).astype(I32)
    bottom = (me == dims.tiles - 1).astype(I32)
    edge = jnp.zeros((8, chans), F32)
    for k in range(lines.shape[0]):
        for a in range(4):
            lines[k, a, 0:8] = edge
            lines[k, a, 8 + cols :] = edge
    from_below(0).wait()
    taps.wait()

    def band(j, lines, wide, mixed):
        no_top = (top == 1) & (j == 0)
        no_bottom = (bottom == 1) & (j == bands - 1)
        over = up[jnp.maximum(j - top, 0)].astype(F32)
        under = down[jnp.minimum(j + bottom, bands - 1)].astype(F32)
        middle = slice(8, 8 + cols)
        lines[0, middle] = jnp.where(no_top, 0.0, over)
        lines[1, middle] = held[j, 0].astype(F32)
        lines[2, middle] = held[j, 1].astype(F32)
        lines[3, middle] = jnp.where(no_bottom, 0.0, under)
        for a in range(4):
            for b in range(4):
                wide[a, :, b * chans : (b + 1) * chans] = lines[a, pl.ds(7 + b, half, stride=2), :].astype(BF16)
        total = silu(column_pairs(wide, 0, 2, taps) + taps.bias())
        for i in range(2):
            part = total[i * half : (i + 1) * half]
            for b in range(2):
                here = lines[i + 1, pl.ds(8 + b, half, stride=2), :]
                mixed[i, pl.ds(b, half, stride=2), :] = here + part[:, b * chans : (b + 1) * chans]
            out[j, i] = mixed[i].astype(BF16)

    @pl.loop(0, bands // BANDS_AT_ONCE)
    def _(step):
        first = BANDS_AT_ONCE * step
        for k in range(BANDS_AT_ONCE):
            from_feat(first + k).wait()
            from_above(first + k).wait()
            if k + 1 < BANDS_AT_ONCE:
                from_below(first + k + 1).wait()

        @pl.when(first + BANDS_AT_ONCE < bands)
        def _():
            from_below(first + BANDS_AT_ONCE).wait()

        for k in range(BANDS_AT_ONCE):
            band(first + k, lines.at[k], wide.at[k], mixed.at[k])
        for k in range(BANDS_AT_ONCE):
            leave(first + k).start()

    for j in range(bands):
        leave(j).wait()


def paste_kernel(dims, table, back, decoded, finished, got, held, canvas, out, sems, load_sems):
    me = lax.axis_index("tile")
    patches = pltpu.make_async_copy(back, got, sems.at[0])
    patches.start()

    def load(band):
        return pltpu.make_async_copy(decoded.at[band], held.at[band], load_sems.at[band])

    def leave(band):
        return pltpu.make_async_copy(out.at[band], finished.at[band], sems.at[1 + band])

    for j in range(dims.bands):
        load(j).start()
    canvas[...] = jnp.zeros_like(canvas)
    patches.wait()

    @pl.loop(0, dims.tiles)
    def _(e):
        row0 = table[ROW, e]
        col0 = table[COL, e]
        length = table[SIDE, e]
        start = first_local(row0, me, dims)
        for i in range(dims.back_rows):
            local = start + i

            @pl.when((local < dims.local_rows) & (global_row(local, me, dims) - row0 < length))
            def _():
                canvas[local, pl.ds(col0, SPAN), :] += got[e, i].astype(F32)

    for j in range(dims.bands):
        load(j).wait()
        for i in range(2):
            out[j, i] = (canvas[2 * j + i] + held[j, i].astype(F32)).astype(BF16)
        leave(j).start()
    for j in range(dims.bands):
        leave(j).wait()


def shards(features, dec_weight, dec_bias, first_weight, first_bias, second_weight, second_bias, boxes, slots):
    tiles = lax.axis_size("tile")
    dims = Dims(features, tiles)
    bands, cols, chans, local_rows = dims.bands, dims.cols, dims.chans, dims.local_rows
    assert dims.band_rows == 2 and slots.shape[0] == CAP * tiles and boxes.shape[1] == tiles
    assert tiles & (tiles - 1) == 0

    smem = pl.BlockSpec(memory_space=pltpu.SMEM)
    hbm = pl.BlockSpec(memory_space=pl.ANY)
    full = pltpu.CompilerParams(vmem_limit_bytes=FULL_GRANT)
    dma = pltpu.SemaphoreType.DMA

    def cost(flops, moved):
        return pl.CostEstimate(flops=int(flops), bytes_accessed=int(moved), transcendentals=0)

    def shaped(*shape, kind=BF16):
        return jax.ShapeDtypeStruct(shape, kind)

    def swap(array):
        return lax.all_to_all(array, "tile", split_axis=0, concat_axis=0, tiled=True)

    pack_scratch = [
        pltpu.VMEM((bands, 2, cols, chans), BF16),
        pltpu.VMEM((local_rows, cols + 16, chans), F32),
        pltpu.VMEM((dims.rim, chans), F32),
        pltpu.VMEM((tiles, dims.message, chans), BF16),
        pltpu.VMEM((tiles, dims.message, chans), BF16),
        dma((4,)),
        dma((bands,)),
        dma((tiles,)),
    ]
    message = shaped(tiles, dims.message, chans)
    *sent_main, sent_extra, table, last, leading = pl.pallas_call(
        functools.partial(pack_kernel, dims),
        out_shape=[shaped(dims.message, chans)] * tiles
        + [message, shaped(7, tiles, kind=I32), shaped(bands, cols, chans), shaped(bands, cols, chans)],
        in_specs=[hbm, hbm, hbm],
        out_specs=[hbm] * (tiles + 1) + [smem, hbm, hbm],
        scratch_shapes=[
            pltpu.SMEM(boxes.shape, I32),
            pltpu.SMEM(slots.shape, I32),
            pltpu.SMEM((tiles,), I32),
            pltpu.SMEM((tiles,), I32),
            pltpu.SMEM((tiles + 1,), I32),
        ]
        + pack_scratch,
        compiler_params=full,
        cost_estimate=cost(0, 6e6),
        name="pack",
    )(boxes, slots, features)
    got_main = [sent_main[0]] + [None] * (tiles - 1)
    for s in [1] + sorted(range(2, tiles), key=lambda s: (-(s >> 1).bit_count(), -(s >> 1), s)):
        got_main[s] = lax.ppermute(sent_main[s], "tile", [(i, i ^ s) for i in range(tiles)])
    up = [(i, (i + 1) % tiles) for i in range(tiles)]
    above = lax.ppermute(last, "tile", up)
    below = lax.ppermute(leading, "tile", [(j, i) for i, j in up])

    got_extra = swap(sent_extra)

    weights = tuple(w.reshape(3, 3, chans, chans) for w in (dec_weight, first_weight, second_weight))
    biases = (dec_bias[None], first_bias[None], second_bias[None])
    restore_scratch = [
        pltpu.VMEM((tiles, dims.message, chans), BF16),
        pltpu.VMEM((4, 3, chans, 2 * chans), BF16),
        pltpu.VMEM((2, 3, 4, chans, 2 * chans), BF16),
        pltpu.VMEM((3, 1, chans), F32),
        dma((tiles,)),
        dma((3, 3)),
        pltpu.VMEM((SPAN // 2 + 2, 2, SPAN, 3 * chans), BF16),
        pltpu.VMEM((SPAN, SPAN, chans), F32),
        pltpu.VMEM((S + 2, S // 2, 4 * chans), BF16),
        pltpu.VMEM((S + 2, S // 2, 4 * chans), BF16),
        pltpu.VMEM((S, S, chans), F32),
        pltpu.VMEM((S, S, chans), BF16),
        dma((S // PIECE,)),
    ]
    restored_shape = shaped(CAP, S, S, chans)
    sent_back, partial = pl.pallas_call(
        functools.partial(main_kernel, dims),
        out_shape=[shaped(tiles, dims.back_rows, SPAN, chans), restored_shape],
        in_specs=[smem] + [hbm] * (tiles + 6),
        out_specs=[hbm, hbm],
        scratch_shapes=restore_scratch
        + [pltpu.VMEM((tiles, dims.back_rows, SPAN, chans), BF16), dma((tiles,))],
        compiler_params=full,
        cost_estimate=cost(7e9, 8e6),
        name="restore_main",
    )(table, *got_main, *weights, *biases)
    got_back = swap(sent_back)

    restorations = pl.pallas_call(
        functools.partial(extra_kernel, dims),
        out_shape=restored_shape,
        in_specs=[smem] + [hbm] * 8,
        out_specs=hbm,
        scratch_shapes=restore_scratch,
        input_output_aliases={8: 0},
        compiler_params=full,
        cost_estimate=cost(6e9, 8e6),
        name="restore_extra",
    )(table, got_extra, *weights, *biases, partial)

    above, below, restorations = lax.optimization_barrier((above, below, restorations))
    assert bands % BANDS_AT_ONCE == 0
    decoded = pl.pallas_call(
        functools.partial(decode_kernel, dims),
        out_shape=shaped(*features.shape),
        in_specs=[hbm] * 5,
        out_specs=hbm,
        scratch_shapes=[
            pltpu.VMEM((bands, 2, cols, chans), BF16),
            pltpu.VMEM((bands, cols, chans), BF16),
            pltpu.VMEM((bands, cols, chans), BF16),
            pltpu.VMEM((3, 4, chans, 2 * chans), BF16),
            pltpu.VMEM((1, chans), F32),
            pltpu.VMEM((BANDS_AT_ONCE, 4, cols + 16, chans), F32),
            pltpu.VMEM((BANDS_AT_ONCE, 4, cols // 2, 4 * chans), BF16),
            pltpu.VMEM((BANDS_AT_ONCE, 2, cols, chans), F32),
            pltpu.VMEM((bands, 2, cols, chans), BF16),
            dma((bands,)),
            dma((3, bands)),
            dma((3,)),
        ],
        compiler_params=full,
        cost_estimate=cost(3e9, 6e6),
        name="decode",
    )(features, above, below, weights[0], biases[0])
    finished = pl.pallas_call(
        functools.partial(paste_kernel, dims),
        out_shape=shaped(*features.shape),
        in_specs=[smem, hbm, hbm],
        out_specs=hbm,
        scratch_shapes=[
            pltpu.VMEM((tiles, dims.back_rows, SPAN, chans), BF16),
            pltpu.VMEM((bands, 2, cols, chans), BF16),
            pltpu.VMEM((local_rows, cols, chans), F32),
            pltpu.VMEM((bands, 2, cols, chans), BF16),
            dma((1 + bands,)),
            dma((bands,)),
        ],
        compiler_params=full,
        cost_estimate=cost(0, 4e6),
        name="paste",
    )(table, got_back, decoded)
    return finished, restorations


def solution(mesh):
    return jax.shard_map(
        shards,
        mesh=mesh,
        in_specs=(
            P("sess", "tile", None, None),
            P(),
            P(),
            P(),
            P(),
            P(),
            P(),
            P(None, "sess"),
            P("sess"),
        ),
        out_specs=(P("sess", "tile", None, None), P(("sess", "tile"), None, None, None)),
        check_vma=False,
    )
```

```python
import functools

import jax
import jax.numpy as jnp
from jax import lax
from jax.experimental import pallas as pl
from jax.experimental.pallas import tpu as pltpu
from jax.sharding import PartitionSpec as P

S = 64
UNIT = 12
NCLS = 3
CAP = 2
PIECE = 16
BANDS_AT_ONCE = 2
SPAN = UNIT * (NCLS + 1)
BF16 = jnp.bfloat16
F32 = jnp.float32
I32 = jnp.int32
FULL_GRANT = 67000000
ROW, COL, SIDE, ROW2, COL2, SIDE2, PLACE = range(7)


def rows_within(window, band_rows, stride):
    return band_rows * (window // stride) + min(band_rows, window % stride)


class Dims:
    def __init__(self, features, tiles):
        self.bands, self.band_rows, self.cols, self.chans = features.shape
        self.tiles = tiles
        self.stride = tiles * self.band_rows
        self.shift = self.stride.bit_length() - 1
        self.local_rows = self.bands * self.band_rows
        self.rows = rows_within(SPAN + 2, self.band_rows, self.stride)
        self.back_rows = rows_within(SPAN, self.band_rows, self.stride)
        self.rim = -(-2 * self.rows // 16) * 16
        self.message = self.rows * SPAN + self.rim


def first_local(row, tile, dims):
    return ((row >> dims.shift) << 1) + jnp.clip((row & (dims.stride - 1)) - 2 * tile, 0, 2)


def global_row(local, tile, dims):
    return ((local >> 1) << dims.shift) + 2 * tile + (local & 1)


def silu(v):
    half = 0.5 * v
    return half + half * jnp.tanh(half)


def both(bias):
    return jnp.concatenate([bias, bias], -1)


class RowTaps:
    def __init__(self, source, bias, store, held, sems):
        chans = source.shape[-1]
        self.store = store
        self.held = held
        self.copies = (
            pltpu.make_async_copy(bias, held, sems.at[2]),
            pltpu.make_async_copy(source, store.at[0:3, :, :, 0:chans], sems.at[0]),
            pltpu.make_async_copy(source, store.at[1:4, :, :, chans : 2 * chans], sems.at[1]),
        )

    def start(self):
        for copy in self.copies:
            copy.start()
        chans = self.store.shape[2]
        none = jnp.zeros((3, chans, chans), BF16)
        self.store[3, :, :, 0:chans] = none
        self.store[0, :, :, chans : 2 * chans] = none

    def wait(self):
        for copy in self.copies:
            copy.wait()

    def bias(self):
        return both(self.held[...])

    def value(self):
        return self.store[...].reshape(-1, self.store.shape[-1])


class ColumnTaps(RowTaps):
    def __init__(self, source, bias, store, held, sems):
        chans = source.shape[-1]
        self.store = store
        self.held = held
        self.copies = (
            pltpu.make_async_copy(bias, held, sems.at[2]),
            pltpu.make_async_copy(source, store.at[:, 0:3, :, 0:chans], sems.at[0]),
            pltpu.make_async_copy(source, store.at[:, 1:4, :, chans : 2 * chans], sems.at[1]),
        )

    def start(self):
        for copy in self.copies:
            copy.start()
        chans = self.store.shape[2]
        none = jnp.zeros((3, chans, chans), BF16)
        self.store[:, 3, :, 0:chans] = none
        self.store[:, 0, :, chans : 2 * chans] = none


def two_chains(wide, taps):
    wide = wide.reshape(-1, wide.shape[-1])
    weight = taps.value()
    middle = weight.shape[0] // 2
    one = jnp.dot(wide[:, :middle], weight[:middle], preferred_element_type=F32)
    two = jnp.dot(wide[:, middle:], weight[middle:], preferred_element_type=F32)
    return one + two


def row_pairs(src, first, count, taps):
    parts = [
        src[pl.ds(first, count), 0],
        src[pl.ds(first, count), 1],
        src[pl.ds(first + 1, count), 0],
        src[pl.ds(first + 1, count), 1],
    ]
    return two_chains(jnp.concatenate(parts, -1), taps)


def column_pairs(src, first, count, taps):
    return two_chains(jnp.concatenate([src[pl.ds(first + a, count)] for a in range(3)], -1), taps)


def fill_canvas(dims, feat, held, canvas, sems):
    def copy(band):
        return pltpu.make_async_copy(feat.at[band], held.at[band], sems.at[band])

    for band in range(dims.bands):
        copy(band).start()

    def finish():
        edge = jnp.zeros((8, dims.chans), F32)
        for band in range(dims.bands):
            copy(band).wait()
            for i in range(2):
                row = 2 * band + i
                canvas[row, 0:8, :] = edge
                canvas[row, 8 + dims.cols : 16 + dims.cols, :] = edge
                canvas[row, 8 : 8 + dims.cols, :] = held[band, i].astype(F32)

    return finish


def pack_crops(dims, table, row_at, col_at, canvas, rim, staged, partner):
    me = lax.axis_index("tile")
    rim[...] = jnp.zeros_like(rim)

    @pl.loop(0, dims.tiles)
    def _(s):
        w = partner(s)
        row0 = table[row_at, w]
        col0 = table[col_at, w]
        start = first_local(jnp.maximum(row0 - 1, 0), me, dims)
        for i in range(dims.rows):
            row = jnp.minimum(start + i, dims.local_rows - 1)
            staged[s, i * SPAN : (i + 1) * SPAN, :] = canvas[row, pl.ds(col0 + 8, SPAN), :].astype(BF16)
            rim[2 * i : 2 * i + 1, :] = canvas[row, pl.ds(col0 + 7, 1), :]
            rim[2 * i + 1 : 2 * i + 2, :] = canvas[row, pl.ds(col0 + 8 + SPAN, 1), :]
        staged[s, dims.rows * SPAN :, :] = rim[...].astype(BF16)


def pack_kernel(
    dims, boxes_in, slots_in, feat, *refs
):
    sent, refs = refs[: dims.tiles], refs[dims.tiles :]
    sent_extra, table, last, leading, boxes, slots, main, extra, seconds, held, canvas, rim, staged, staged_extra, sems, feat_sems, sent_sems = refs
    me = lax.axis_index("tile")
    copies = (
        pltpu.make_async_copy(boxes_in, boxes, sems.at[0]),
        pltpu.make_async_copy(slots_in, slots, sems.at[1]),
    )
    for copy in copies:
        copy.start()
    finish = fill_canvas(dims, feat, held, canvas, feat_sems)
    for copy in copies:
        copy.wait()

    def first_pass(w, count):
        one = slots[CAP * w]
        two = slots[CAP * w + 1]
        full = (one >= 0) & (two >= 0)
        second = jnp.where(full, two, -1)
        main[w] = jnp.where(one >= 0, one, two)
        extra[w] = second
        seconds[count] = second
        return count + full.astype(I32)

    lax.fori_loop(0, dims.tiles, first_pass, jnp.int32(0))

    def second_pass(w, count):
        own = main[w]
        idle = own < 0
        crop = jnp.where(idle, seconds[count], own)
        table[ROW, w] = boxes[0, crop]
        table[COL, w] = boxes[1, crop]
        table[SIDE, w] = UNIT * (boxes[2, crop] + 2)
        other = jnp.maximum(extra[w], 0)
        table[ROW2, w] = boxes[0, other]
        table[COL2, w] = boxes[1, other]
        table[SIDE2, w] = jnp.where(extra[w] >= 0, UNIT * (boxes[2, other] + 2), 0)
        table[PLACE, w] = jnp.where(idle, 2, jnp.where(slots[CAP * w] >= 0, 0, 1))
        return count + idle.astype(I32)

    lax.fori_loop(0, dims.tiles, second_pass, jnp.int32(0))
    finish()
    edges = (
        pltpu.make_async_copy(held.at[:, 1], last, sems.at[2]),
        pltpu.make_async_copy(held.at[:, 0], leading, sems.at[3]),
    )
    for edge in edges:
        edge.start()
    pack_crops(dims, table, ROW, COL, canvas, rim, staged, lambda s: me ^ s)
    copies = [pltpu.make_async_copy(staged.at[s], sent[s], sent_sems.at[s]) for s in range(dims.tiles)]
    for copy in copies:
        copy.start()
    pack_crops(dims, table, ROW2, COL2, canvas, rim, staged_extra, lambda s: s)
    later = pltpu.make_async_copy(staged_extra, sent_extra, sems.at[0])
    later.start()
    for copy in copies:
        copy.wait()
    later.wait()
    for edge in edges:
        edge.wait()


def restore(dims, row0, length, arrival, source, got, taps, raw, decoded, wide, inner, mixed, delta, finish):
    chans = dims.chans
    above = row0 - 1
    pairs = SPAN // 2
    half = S // 2
    nothing = jnp.zeros((SPAN, 3 * chans), BF16)
    raw[0, 0] = nothing
    raw[pairs, 1] = nothing
    empty = jnp.zeros((half, 4 * chans), BF16)
    for store in (wide, inner):
        store[0] = empty
        store[S + 1] = empty

    @pl.loop(0, dims.tiles)
    def _(s):
        arrival(s).wait()
        e = source(s)
        start = first_local(jnp.maximum(above, 0), e, dims)
        rim = got[s, dims.rows * SPAN :, :].astype(F32)
        at = lax.broadcasted_iota(I32, (SPAN, chans), 0)
        for i in range(dims.rows):
            local = start + i
            place = global_row(local, e, dims) - above
            place = jnp.where((local < dims.local_rows) & (place < SPAN + 2), place, SPAN + 2)
            line = got[s, i * SPAN : (i + 1) * SPAN, :]
            wider = line.astype(F32)
            left = jnp.where(at == 0, rim[2 * i : 2 * i + 1], pltpu.roll(wider, 1, 0))
            right = jnp.where(at == SPAN - 1, rim[2 * i + 1 : 2 * i + 2], pltpu.roll(wider, SPAN - 1, 0))
            raw[place >> 1, place & 1] = jnp.concatenate([left.astype(BF16), line, right.astype(BF16)], -1)

    taps[1].start()
    taps[2].start()
    taps[0].wait()
    n = 8
    for first in range(0, pairs, n):
        total = silu(row_pairs(raw, first, n, taps[0]) + taps[0].bias())
        for k in range(n):
            part = total[k * SPAN : (k + 1) * SPAN]
            at = 2 * (first + k)
            upper = raw[first + k, 1, :, chans : 2 * chans].astype(F32) + part[:, :chans]
            lower = raw[first + k + 1, 0, :, chans : 2 * chans].astype(F32) + part[:, chans:]
            decoded[at] = upper.astype(BF16).astype(F32)
            decoded[at + 1] = lower.astype(BF16).astype(F32)

    lengthf = length.astype(F32)
    block = lax.broadcasted_iota(I32, (4, half, SPAN), 0)
    t = 2 * lax.broadcasted_iota(I32, (4, half, SPAN), 1) + block - 1
    j = lax.broadcasted_iota(I32, (4, half, SPAN), 2).astype(F32)
    spots = jnp.clip((t.astype(F32) + 0.5) * lengthf / S - 0.5, 0.0, lengthf - 1.0)
    across = jnp.where((t >= 0) & (t < S), jnp.maximum(0.0, 1.0 - jnp.abs(spots - j)), 0.0)
    across = across.reshape(4 * half, SPAN).astype(BF16)
    taps[1].wait()
    taps[2].wait()
    for m in range(S // 2):
        lines = []
        for parity in range(2):
            s = 2 * m + parity
            spot = jnp.clip((2 * s + 1) * length - S, 0, (length - 1) * 2 * S)
            low = spot >> 7
            part = (spot & 127).astype(F32) * (1.0 / (2 * S))
            high = jnp.minimum(low + 1, SPAN - 1)
            lines.append(((1.0 - part) * decoded[low] + part * decoded[high]).astype(BF16))
        cells = jnp.dot(across, jnp.concatenate(lines, -1), preferred_element_type=F32).astype(BF16)
        for parity in range(2):
            at = 2 * m + parity + 1
            for b in range(4):
                wide[at, :, b * chans : (b + 1) * chans] = cells[
                    b * half : (b + 1) * half, parity * chans : (parity + 1) * chans
                ]

    n = PIECE
    for first in range(0, S, n):
        total = silu(column_pairs(wide, first, n, taps[1]) + taps[1].bias())
        at = lax.broadcasted_iota(I32, (n, half, chans), 1)
        even = pltpu.roll(total[:, :chans], n * half - 1, 0).reshape(n, half, chans)
        odd = pltpu.roll(total[:, chans:], 1, 0).reshape(n, half, chans)
        rows = pl.ds(first + 1, n)
        inner[rows, :, 0:chans] = jnp.where(at == 0, 0.0, odd).astype(BF16)
        inner[rows, :, chans : 3 * chans] = total.astype(BF16).reshape(n, half, 2 * chans)
        inner[rows, :, 3 * chans :] = jnp.where(at == half - 1, 0.0, even).astype(BF16)

    for first in range(0, S, n):
        total = column_pairs(inner, first, n, taps[2]) + taps[2].bias()
        for k in range(n):
            mixed[first + k, pl.ds(0, half, stride=2), :] = total[k * half : (k + 1) * half, :chans]
            mixed[first + k, pl.ds(1, half, stride=2), :] = total[k * half : (k + 1) * half, chans:]
        delta[first : first + n] = mixed[first : first + n].astype(BF16)
        finish(first // PIECE)


def begin(dims, arrived, weights, biases, scratch):
    got, row_store, column_store, held, got_sems, tap_sems = scratch

    def arrival(s):
        return pltpu.make_async_copy(arrived[0], got.at[s], got_sems.at[s])

    for s in range(dims.tiles):
        pltpu.make_async_copy(arrived[s], got.at[s], got_sems.at[s]).start()
    taps = (
        RowTaps(weights[0], biases[0], row_store, held.at[0], tap_sems.at[0]),
        ColumnTaps(weights[1], biases[1], column_store.at[0], held.at[1], tap_sems.at[1]),
        ColumnTaps(weights[2], biases[2], column_store.at[1], held.at[2], tap_sems.at[2]),
    )
    taps[0].start()
    return arrival, taps


def main_kernel(dims, table, *refs):
    tiles, chans = dims.tiles, dims.chans
    arrived, refs = refs[:tiles], refs[tiles:]
    (dec_w, one_w, two_w, dec_b, one_b, two_b, sent, restored, got, row_store, column_store, held) = refs[:12]
    got_sems, tap_sems, raw, decoded, wide, inner, mixed, delta, sem, back, back_sems = refs[12:]
    me = lax.axis_index("tile")
    row0 = table[ROW, me]
    length = table[SIDE, me]
    place = table[PLACE, me]
    scratch = (got, row_store, column_store, held, got_sems, tap_sems)
    arrival, taps = begin(dims, arrived, (dec_w, one_w, two_w), (dec_b, one_b, two_b), scratch)
    restore(
        dims, row0, length, arrival, lambda s: me ^ s, got, taps,
        raw, decoded, wide, inner, mixed, delta, lambda piece: None,
    )

    @pl.when(place < CAP)
    def _():
        pltpu.make_async_copy(delta, restored.at[place], sem.at[0]).start()

    lengthf = length.astype(F32)
    t = lax.broadcasted_iota(I32, (SPAN, S), 0).astype(F32)
    s = lax.broadcasted_iota(I32, (SPAN, S), 1).astype(F32)
    spots = jnp.clip((t + 0.5) * S / lengthf - 0.5, 0.0, S - 1.0)
    lift = jnp.where(t < lengthf, jnp.maximum(0.0, 1.0 - jnp.abs(spots - s)), 0.0)
    coarse = lift.astype(BF16)
    lift = jnp.concatenate([coarse, (lift - coarse.astype(F32)).astype(BF16)], 0)
    scale = 1.0 / (2.0 * lengthf)
    group = 12

    @pl.loop(0, SPAN // 2 // group)
    def _(step):
        for k in range(group):
            lines = []
            for parity in range(2):
                h = 2 * (step * group + k) + parity
                spot = jnp.clip((2 * h + 1) * S - length, 0, (S - 1) * 2 * length)
                low = ((spot.astype(F32) + 0.5) * scale).astype(I32)
                part = (spot - low * 2 * length).astype(F32) * scale
                high = jnp.minimum(low + 1, S - 1)
                lines.append(((1.0 - part) * delta[low].astype(F32) + part * delta[high].astype(F32)).astype(BF16))
            patch = jnp.dot(lift, jnp.concatenate(lines, -1), preferred_element_type=F32)
            patch = (patch[:SPAN] + patch[SPAN:]).astype(BF16)
            for parity in range(2):
                row = row0 + 2 * (step * group + k) + parity
                dest = (row & (dims.stride - 1)) >> 1
                local = ((row >> dims.shift) << 1) + (row & 1)
                back[dest, local - first_local(row0, dest, dims)] = patch[:, parity * chans : (parity + 1) * chans]

    def leave(e):
        return pltpu.make_async_copy(back.at[e], sent.at[e], back_sems.at[e])

    for e in range(tiles):
        leave(e).start()
    for e in range(tiles):
        leave(e).wait()

    @pl.when(place < CAP)
    def _():
        pltpu.make_async_copy(delta, restored.at[place], sem.at[0]).wait()


def extra_kernel(
    dims, table, arrived, dec_w, one_w, two_w, dec_b, one_b, two_b, partial, restored,
    got, row_store, column_store, held, got_sems, tap_sems, raw, decoded, wide, inner, mixed, delta, sem,
):
    me = lax.axis_index("tile")
    row0 = table[ROW2, me]
    length = table[SIDE2, me]
    place = table[PLACE, me]

    def write(slot):
        copy = pltpu.make_async_copy(delta, restored.at[slot], sem.at[0])
        copy.start()
        copy.wait()

    @pl.when(length > 0)
    def _():
        scratch = (got, row_store, column_store, held, got_sems, tap_sems)
        arrival, taps = begin(dims, [arrived.at[s] for s in range(dims.tiles)], (dec_w, one_w, two_w), (dec_b, one_b, two_b), scratch)

        def leave(piece):
            rows = pl.ds(piece * PIECE, PIECE)
            return pltpu.make_async_copy(delta.at[rows], restored.at[1, rows], sem.at[piece])

        restore(
            dims, row0, length, arrival, lambda s: s, got, taps,
            raw, decoded, wide, inner, mixed, delta, lambda piece: leave(piece).start(),
        )
        for piece in range(S // PIECE):
            leave(piece).wait()

    @pl.when(length == 0)
    def _():
        delta[...] = jnp.zeros_like(delta)

        @pl.when(place != 0)
        def _():
            write(0)

        @pl.when(place != 1)
        def _():
            write(1)


def decode_kernel(
    dims, feat, above, below, weight, bias, finished,
    held, up, down, store, held_bias, lines, wide, mixed, out, sems, load_sems, tap_sems,
):
    me = lax.axis_index("tile")
    bands, chans, cols = dims.bands, dims.chans, dims.cols
    half = cols // 2
    taps = ColumnTaps(weight, bias, store, held_bias, tap_sems)
    def from_feat(band):
        return pltpu.make_async_copy(feat.at[band], held.at[band], load_sems.at[0, band])

    def from_above(band):
        return pltpu.make_async_copy(above.at[band], up.at[band], load_sems.at[1, band])

    def from_below(band):
        return pltpu.make_async_copy(below.at[band], down.at[band], load_sems.at[2, band])

    taps.start()
    from_below(0).start()
    for j in range(bands):
        from_feat(j).start()
        from_above(j).start()
        if j + 1 < bands:
            from_below(j + 1).start()

    def leave(band):
        return pltpu.make_async_copy(out.at[band], finished.at[band], sems.at[band])

    top = (me == 0).astype(I32)
    bottom = (me == dims.tiles - 1).astype(I32)
    edge = jnp.zeros((8, chans), F32)
    for k in range(lines.shape[0]):
        for a in range(4):
            lines[k, a, 0:8] = edge
            lines[k, a, 8 + cols :] = edge
    from_below(0).wait()
    taps.wait()

    def band(j, lines, wide, mixed):
        no_top = (top == 1) & (j == 0)
        no_bottom = (bottom == 1) & (j == bands - 1)
        over = up[jnp.maximum(j - top, 0)].astype(F32)
        under = down[jnp.minimum(j + bottom, bands - 1)].astype(F32)
        middle = slice(8, 8 + cols)
        lines[0, middle] = jnp.where(no_top, 0.0, over)
        lines[1, middle] = held[j, 0].astype(F32)
        lines[2, middle] = held[j, 1].astype(F32)
        lines[3, middle] = jnp.where(no_bottom, 0.0, under)
        for a in range(4):
            for b in range(4):
                wide[a, :, b * chans : (b + 1) * chans] = lines[a, pl.ds(7 + b, half, stride=2), :].astype(BF16)
        total = silu(column_pairs(wide, 0, 2, taps) + taps.bias())
        for i in range(2):
            part = total[i * half : (i + 1) * half]
            for b in range(2):
                here = lines[i + 1, pl.ds(8 + b, half, stride=2), :]
                mixed[i, pl.ds(b, half, stride=2), :] = here + part[:, b * chans : (b + 1) * chans]
            out[j, i] = mixed[i].astype(BF16)

    @pl.loop(0, bands // BANDS_AT_ONCE)
    def _(step):
        first = BANDS_AT_ONCE * step
        for k in range(BANDS_AT_ONCE):
            from_feat(first + k).wait()
            from_above(first + k).wait()
            if k + 1 < BANDS_AT_ONCE:
                from_below(first + k + 1).wait()

        @pl.when(first + BANDS_AT_ONCE < bands)
        def _():
            from_below(first + BANDS_AT_ONCE).wait()

        for k in range(BANDS_AT_ONCE):
            band(first + k, lines.at[k], wide.at[k], mixed.at[k])
        for k in range(BANDS_AT_ONCE):
            leave(first + k).start()

    for j in range(bands):
        leave(j).wait()


def paste_kernel(dims, table, back, decoded, finished, got, held, canvas, out, sems, load_sems):
    me = lax.axis_index("tile")
    patches = pltpu.make_async_copy(back, got, sems.at[0])
    patches.start()

    def load(band):
        return pltpu.make_async_copy(decoded.at[band], held.at[band], load_sems.at[band])

    def leave(band):
        return pltpu.make_async_copy(out.at[band], finished.at[band], sems.at[1 + band])

    for j in range(dims.bands):
        load(j).start()
    canvas[...] = jnp.zeros_like(canvas)
    patches.wait()

    @pl.loop(0, dims.tiles)
    def _(e):
        row0 = table[ROW, e]
        col0 = table[COL, e]
        length = table[SIDE, e]
        start = first_local(row0, me, dims)
        for i in range(dims.back_rows):
            local = start + i

            @pl.when((local < dims.local_rows) & (global_row(local, me, dims) - row0 < length))
            def _():
                canvas[local, pl.ds(col0, SPAN), :] += got[e, i].astype(F32)

    for j in range(dims.bands):
        load(j).wait()
        for i in range(2):
            out[j, i] = (canvas[2 * j + i] + held[j, i].astype(F32)).astype(BF16)
        leave(j).start()
    for j in range(dims.bands):
        leave(j).wait()


def shards(features, dec_weight, dec_bias, first_weight, first_bias, second_weight, second_bias, boxes, slots):
    tiles = lax.axis_size("tile")
    dims = Dims(features, tiles)
    bands, cols, chans, local_rows = dims.bands, dims.cols, dims.chans, dims.local_rows
    assert dims.band_rows == 2 and slots.shape[0] == CAP * tiles and boxes.shape[1] == tiles
    assert tiles & (tiles - 1) == 0

    smem = pl.BlockSpec(memory_space=pltpu.SMEM)
    hbm = pl.BlockSpec(memory_space=pl.ANY)
    full = pltpu.CompilerParams(vmem_limit_bytes=FULL_GRANT)
    dma = pltpu.SemaphoreType.DMA

    def cost(flops, moved):
        return pl.CostEstimate(flops=int(flops), bytes_accessed=int(moved), transcendentals=0)

    def shaped(*shape, kind=BF16):
        return jax.ShapeDtypeStruct(shape, kind)

    def swap(array):
        return lax.all_to_all(array, "tile", split_axis=0, concat_axis=0, tiled=True)

    pack_scratch = [
        pltpu.VMEM((bands, 2, cols, chans), BF16),
        pltpu.VMEM((local_rows, cols + 16, chans), F32),
        pltpu.VMEM((dims.rim, chans), F32),
        pltpu.VMEM((tiles, dims.message, chans), BF16),
        pltpu.VMEM((tiles, dims.message, chans), BF16),
        dma((4,)),
        dma((bands,)),
        dma((tiles,)),
    ]
    message = shaped(tiles, dims.message, chans)
    *sent_main, sent_extra, table, last, leading = pl.pallas_call(
        functools.partial(pack_kernel, dims),
        out_shape=[shaped(dims.message, chans)] * tiles
        + [message, shaped(7, tiles, kind=I32), shaped(bands, cols, chans), shaped(bands, cols, chans)],
        in_specs=[hbm, hbm, hbm],
        out_specs=[hbm] * (tiles + 1) + [smem, hbm, hbm],
        scratch_shapes=[
            pltpu.SMEM(boxes.shape, I32),
            pltpu.SMEM(slots.shape, I32),
            pltpu.SMEM((tiles,), I32),
            pltpu.SMEM((tiles,), I32),
            pltpu.SMEM((tiles + 1,), I32),
        ]
        + pack_scratch,
        compiler_params=full,
        cost_estimate=cost(0, 6e6),
        name="pack",
    )(boxes, slots, features)
    got_main = [sent_main[0]] + [None] * (tiles - 1)
    for s in [1] + sorted(range(2, tiles), key=lambda s: (-(s >> 1).bit_count(), -(s >> 1), s)):
        got_main[s] = lax.ppermute(sent_main[s], "tile", [(i, i ^ s) for i in range(tiles)])
    up = [(i, (i + 1) % tiles) for i in range(tiles)]
    above = lax.ppermute(last, "tile", up)
    below = lax.ppermute(leading, "tile", [(j, i) for i, j in up])

    got_extra = swap(sent_extra)

    weights = tuple(w.reshape(3, 3, chans, chans) for w in (dec_weight, first_weight, second_weight))
    biases = (dec_bias[None], first_bias[None], second_bias[None])
    restore_scratch = [
        pltpu.VMEM((tiles, dims.message, chans), BF16),
        pltpu.VMEM((4, 3, chans, 2 * chans), BF16),
        pltpu.VMEM((2, 3, 4, chans, 2 * chans), BF16),
        pltpu.VMEM((3, 1, chans), F32),
        dma((tiles,)),
        dma((3, 3)),
        pltpu.VMEM((SPAN // 2 + 2, 2, SPAN, 3 * chans), BF16),
        pltpu.VMEM((SPAN, SPAN, chans), F32),
        pltpu.VMEM((S + 2, S // 2, 4 * chans), BF16),
        pltpu.VMEM((S + 2, S // 2, 4 * chans), BF16),
        pltpu.VMEM((S, S, chans), F32),
        pltpu.VMEM((S, S, chans), BF16),
        dma((S // PIECE,)),
    ]
    restored_shape = shaped(CAP, S, S, chans)
    sent_back, partial = pl.pallas_call(
        functools.partial(main_kernel, dims),
        out_shape=[shaped(tiles, dims.back_rows, SPAN, chans), restored_shape],
        in_specs=[smem] + [hbm] * (tiles + 6),
        out_specs=[hbm, hbm],
        scratch_shapes=restore_scratch
        + [pltpu.VMEM((tiles, dims.back_rows, SPAN, chans), BF16), dma((tiles,))],
        compiler_params=full,
        cost_estimate=cost(7e9, 8e6),
        name="restore_main",
    )(table, *got_main, *weights, *biases)
    got_back = swap(sent_back)

    restorations = pl.pallas_call(
        functools.partial(extra_kernel, dims),
        out_shape=restored_shape,
        in_specs=[smem] + [hbm] * 8,
        out_specs=hbm,
        scratch_shapes=restore_scratch,
        input_output_aliases={8: 0},
        compiler_params=full,
        cost_estimate=cost(6e9, 8e6),
        name="restore_extra",
    )(table, got_extra, *weights, *biases, partial)

    above, below, restorations = lax.optimization_barrier((above, below, restorations))
    assert bands % BANDS_AT_ONCE == 0
    decoded = pl.pallas_call(
        functools.partial(decode_kernel, dims),
        out_shape=shaped(*features.shape),
        in_specs=[hbm] * 5,
        out_specs=hbm,
        scratch_shapes=[
            pltpu.VMEM((bands, 2, cols, chans), BF16),
            pltpu.VMEM((bands, cols, chans), BF16),
            pltpu.VMEM((bands, cols, chans), BF16),
            pltpu.VMEM((3, 4, chans, 2 * chans), BF16),
            pltpu.VMEM((1, chans), F32),
            pltpu.VMEM((BANDS_AT_ONCE, 4, cols + 16, chans), F32),
            pltpu.VMEM((BANDS_AT_ONCE, 4, cols // 2, 4 * chans), BF16),
            pltpu.VMEM((BANDS_AT_ONCE, 2, cols, chans), F32),
            pltpu.VMEM((bands, 2, cols, chans), BF16),
            dma((bands,)),
            dma((3, bands)),
            dma((3,)),
        ],
        compiler_params=full,
        cost_estimate=cost(3e9, 6e6),
        name="decode",
    )(features, above, below, weights[0], biases[0])
    finished = pl.pallas_call(
        functools.partial(paste_kernel, dims),
        out_shape=shaped(*features.shape),
        in_specs=[smem, hbm, hbm],
        out_specs=hbm,
        scratch_shapes=[
            pltpu.VMEM((tiles, dims.back_rows, SPAN, chans), BF16),
            pltpu.VMEM((bands, 2, cols, chans), BF16),
            pltpu.VMEM((local_rows, cols, chans), F32),
            pltpu.VMEM((bands, 2, cols, chans), BF16),
            dma((1 + bands,)),
            dma((bands,)),
        ],
        compiler_params=full,
        cost_estimate=cost(0, 4e6),
        name="paste",
    )(table, got_back, decoded)
    return finished, restorations


def solution(mesh):
    return jax.shard_map(
        shards,
        mesh=mesh,
        in_specs=(
            P("sess", "tile", None, None),
            P(),
            P(),
            P(),
            P(),
            P(),
            P(),
            P(None, "sess"),
            P("sess"),
        ),
        out_specs=(P("sess", "tile", None, None), P(("sess", "tile"), None, None, None)),
        check_vma=False,
    )
```
